32 devices in a mesh: groups: 2 (over y), tok: 4 (over z), tp: 2 (over x), sub: 2 (over core).
Axes of the slice: x: 2, y: 2, z: 4, core: 2. Of those that a mesh axis runs over, the one named last changes fastest.
Arguments:
- tokens: bfloat16 [4096, 8192], P(('groups', 'tok'), ('tp', 'sub')), parts along dimension 0, may hold values from -6 to 6
- frozen_key_weight: bfloat16 [8192, 1024], P(('tp', 'sub')), may hold values from -0.0625 to 0.0625
- output_gradient: bfloat16 [4096, 1024], P(('groups', 'tok'), ('tp', 'sub')), parts along dimension 0, may hold values from -6 to 6
- counts: int32 [8, 4], P('groups'), parts along dimension 0, may hold values from 1 to 509, as said below
- placement: int32 [8, 4], P('groups'), parts along dimension 0, may hold values from 0 to 15, as said below
- adapter_sequence: int32 [32], P('groups'), parts along dimension 0, may hold values from 0 to 15, as said below
- adapter_down: bfloat16 [32, 8192, 64], P(('groups', 'tok'), ('tp', 'sub')), parts along dimension 0, may hold values from -6 to 6
- adapter_up: bfloat16 [32, 1024, 64], P(('groups', 'tok'), ('tp', 'sub')), parts along dimension 0, may hold values from -6 to 6
- down_first_moment: float32 [32, 8192, 64], P(('groups', 'tok'), ('tp', 'sub')), parts along dimension 0, may hold values from -0.3 to 0.3
- down_second_moment: float32 [32, 8192, 64], P(('groups', 'tok'), ('tp', 'sub')), parts along dimension 0, may hold values from 0.0001 to 0.01
- down_average: float32 [32, 8192, 64], P(('groups', 'tok'), ('tp', 'sub')), parts along dimension 0, may hold values from -6 to 6
- up_first_moment: float32 [32, 1024, 64], P(('groups', 'tok'), ('tp', 'sub')), parts along dimension 0, may hold values from -0.3 to 0.3
- up_second_moment: float32 [32, 1024, 64], P(('groups', 'tok'), ('tp', 'sub')), parts along dimension 0, may hold values from 0.0001 to 0.01
- up_average: float32 [32, 1024, 64], P(('groups', 'tok'), ('tp', 'sub')), parts along dimension 0, may hold values from -6 to 6
Outputs:
- key_output: bfloat16 [4096, 1024], P(('groups', 'tok'), ('tp', 'sub')), parts along dimension 0
- input_gradient: bfloat16 [4096, 8192], P(('groups', 'tok'), ('tp', 'sub')), parts along dimension 0
- fresh_down: bfloat16 [32, 8192, 64], P(('groups', 'tok'), ('tp', 'sub')), parts along dimension 0
- fresh_up: bfloat16 [32, 1024, 64], P(('groups', 'tok'), ('tp', 'sub')), parts along dimension 0
- average_down_new: float32 [32, 8192, 64], P(('groups', 'tok'), ('tp', 'sub')), parts along dimension 0
- average_up_new: float32 [32, 1024, 64], P(('groups', 'tok'), ('tp', 'sub')), parts along dimension 0
The draws below stay inside these ranges and needn't reach their ends.
There are 2 independent parts, one for each index of `groups`. The reference program is written for one: setup_inputs(seed, part) draws one part's arguments, and reference() takes and returns one part's arrays. A program takes and returns all parts, laid end to end along the dimension named above; an argument that names none is the same for every part. Nothing has to cross between parts.
Inputs may be any that keep to these rules, and one draw needn't show every extreme that they name: `adapter_sequence`: a permutation; the adapters at positions p with p // 4 = j are owned by index j of tok. The tenant placement[j, s] is owned by index (j + s) mod 4 of tok, so each row names one tenant of every owner. `counts`: each row sums to 512.
All inputs are finite; a program needn't handle non-finite values.
Results may differ from the reference program's by a relative error of at most 0.0034.
Values may be sent and summed in bfloat16 or wider, within the bound.
No kernel may reach another device: no remote copies, remote signals or barrier semaphores. Data moves between devices by JAX's collectives and lax.ppermute only.
A program may use at most 128 MiB of HBM per device.

```python
import math
import jax
import jax.numpy as jnp
from jax import lax

MODEL_WIDTH = 8192
KEY_WIDTH = 1024
ADAPTER_RANK = 64
ADP_DEV = 4
TOK_DEV = 512
ADAPTER_TOTAL = 16
SLOTS = 4
TOKENS = 2048
N_TOK = 4


def shared_order(key):
    return jax.random.permutation(key, ADAPTER_TOTAL).astype(jnp.int32)


def draw_adapter_sequence(key, part):
    return shared_order(key)


def draw_placement(key, part):
    adapter_table = shared_order(key)
    key = jax.random.fold_in(key, 7)
    holders = ADAPTER_TOTAL // ADP_DEV
    local_shift = jax.random.randint(key, (holders,), 0, ADP_DEV).astype(jnp.int32)
    slot_index = jnp.arange(SLOTS, dtype=jnp.int32)[None, :]
    row_index = jnp.arange(holders, dtype=jnp.int32)[:, None]
    owners = (row_index + slot_index) % holders
    local_pick = (slot_index + local_shift[owners]) % ADP_DEV
    return adapter_table[owners * ADP_DEV + local_pick].astype(jnp.int32)


def draw_counts(key, part):
    key = jax.random.fold_in(key, 11)
    key_pow, key_row, key_slot = jax.random.split(key, 3)
    holders = ADAPTER_TOTAL // ADP_DEV
    powers = jax.random.randint(key_pow, (holders, SLOTS), 0, 5).astype(jnp.int32)
    weights = jnp.left_shift(jnp.ones_like(powers), powers)
    spare = TOK_DEV - SLOTS
    shares = 1 + spare * weights // jnp.sum(weights, axis=1, keepdims=True)
    rest = TOK_DEV - jnp.sum(shares, axis=1)
    slot_index = jnp.arange(SLOTS, dtype=jnp.int32)[None, :]
    first_col = (slot_index == 0).astype(jnp.int32)
    spread_rows = shares + rest[:, None] * first_col
    heavy_row = jax.random.randint(key_row, (), 0, holders).astype(jnp.int32)
    heavy_slot = jax.random.randint(key_slot, (), 0, SLOTS).astype(jnp.int32)
    heavy_values = 1 + spare * (slot_index == heavy_slot).astype(jnp.int32)
    row_index = jnp.arange(holders, dtype=jnp.int32)[:, None]
    picked = (row_index == heavy_row).astype(jnp.int32)
    return (picked * heavy_values + (1 - picked) * spread_rows).astype(jnp.int32)


def level_of(key, shape, cuts, smallest, largest):
    loudness, own = 1.0, jax.random.fold_in(key, 6)
    for dim, blocks in cuts:
        steps = jnp.exp(jax.random.uniform(jax.random.fold_in(own, dim), (blocks,), jnp.float32, smallest / len(cuts), largest / len(cuts)))
        loudness = loudness * jnp.repeat(steps, shape[dim] // blocks).reshape([-1 if axis == dim else 1 for axis in range(len(shape))])
    return loudness


def bell_draw(key, dims, deviation, reach, pieces=(), held_as=jnp.bfloat16):
    array = deviation * jax.random.normal(key, dims, jnp.float32)
    if pieces:
        array = array * level_of(key, dims, pieces, -0.22, 0.18)
    return jnp.clip(array, -reach, reach).astype(held_as)


def setup_inputs(seed: int = 0, part: int = 0) -> dict:
    arg_keys = jax.random.split(jax.random.key(seed), 15)
    own_keys = jax.random.split(jax.random.fold_in(arg_keys[14], part), 15)
    return {
        "tokens": bell_draw(own_keys[0], (TOKENS, MODEL_WIDTH), 1.0, 6.0, ((0, 4), (1, 4))),
        "frozen_key_weight": bell_draw(arg_keys[1], (MODEL_WIDTH, KEY_WIDTH), MODEL_WIDTH ** -0.5, 0.0625, ((0, 4),)),
        "output_gradient": bell_draw(own_keys[2], (TOKENS, KEY_WIDTH), 1.0, 6.0, ((0, 4), (1, 4))),
        "counts": draw_counts(jax.random.fold_in(jax.random.fold_in(arg_keys[14], part), 71), part),
        "placement": draw_placement(jax.random.fold_in(jax.random.fold_in(arg_keys[14], part), 71), part),
        "adapter_sequence": draw_adapter_sequence(jax.random.fold_in(jax.random.fold_in(arg_keys[14], part), 71), part),
        "adapter_down": bell_draw(own_keys[6], (ADAPTER_TOTAL, MODEL_WIDTH, ADAPTER_RANK), 1.0, 6.0, ((0, 4), (1, 4))),
        "adapter_up": bell_draw(own_keys[7], (ADAPTER_TOTAL, KEY_WIDTH, ADAPTER_RANK), 1.0, 6.0, ((0, 4), (1, 4))),
        "down_first_moment": bell_draw(own_keys[8], (ADAPTER_TOTAL, MODEL_WIDTH, ADAPTER_RANK), 0.05, 0.3, ((0, 4), (1, 4)), jnp.float32),
        "down_second_moment": jnp.clip(jnp.exp(math.log(0.01) - 4.6051702 * jax.random.uniform(own_keys[9], (ADAPTER_TOTAL, MODEL_WIDTH, ADAPTER_RANK), jnp.float32) ** level_of(own_keys[9], (ADAPTER_TOTAL, MODEL_WIDTH, ADAPTER_RANK), ((0, 4), (1, 4)), -0.2, 0.2)), 0.0001, 0.01),
        "down_average": bell_draw(own_keys[10], (ADAPTER_TOTAL, MODEL_WIDTH, ADAPTER_RANK), 1.0, 6.0, ((0, 4), (1, 4)), jnp.float32),
        "up_first_moment": bell_draw(own_keys[11], (ADAPTER_TOTAL, KEY_WIDTH, ADAPTER_RANK), 0.05, 0.3, ((0, 4), (1, 4)), jnp.float32),
        "up_second_moment": jnp.clip(jnp.exp(math.log(0.01) - 4.6051702 * jax.random.uniform(own_keys[12], (ADAPTER_TOTAL, KEY_WIDTH, ADAPTER_RANK), jnp.float32) ** level_of(own_keys[12], (ADAPTER_TOTAL, KEY_WIDTH, ADAPTER_RANK), ((0, 4), (1, 4)), -0.2, 0.2)), 0.0001, 0.01),
        "up_average": bell_draw(own_keys[13], (ADAPTER_TOTAL, KEY_WIDTH, ADAPTER_RANK), 1.0, 6.0, ((0, 4), (1, 4)), jnp.float32),
    }


adapter_scale = 0.5
learn_rate = 0.3
beta_one = 0.9
beta_two = 0.99
adam_eps = 1e-08
ema_decay = 0.9

def positions_of(adapter_sequence):
    entries = adapter_sequence.shape[0]
    indices = jnp.arange(entries, dtype=jnp.int32)
    matches = (adapter_sequence[:, None] == indices[None, :]).astype(jnp.int32)
    return lax.optimization_barrier(jnp.sum(matches * indices[:, None], axis=0)).astype(jnp.int32)

def token_slots(count_row, row_count):
    seg_end = jnp.cumsum(count_row)
    seg_start = seg_end - count_row
    positions = jnp.arange(row_count, dtype=jnp.int32)[:, None]
    return ((positions >= seg_start[None, :]) & (positions < seg_end[None, :])).astype(jnp.float32)

def optimizer_update(weights, gradient, mean_old, var_old, avg_old):
    mean_new = beta_one * mean_old + (1.0 - beta_one) * gradient
    var_new = beta_two * var_old + (1.0 - beta_two) * gradient * gradient
    updated = weights.astype(jnp.float32) - learn_rate * mean_new / (jnp.sqrt(var_new) + adam_eps)
    return (updated.astype(jnp.bfloat16), ema_decay * avg_old + (1.0 - ema_decay) * updated)

def reference(tokens, frozen_key_weight, output_gradient, counts, placement, adapter_sequence, adapter_down, adapter_up, down_first_moment, down_second_moment, down_average, up_first_moment, up_second_moment, up_average):
    position = positions_of(adapter_sequence)

    def holder(carried, inputs):
        sum_down, sum_up = carried
        tok_rows, cot_rows, row_tenants, row_counts = inputs
        slot_mask = token_slots(row_counts, TOK_DEV)
        slot_position = position[row_tenants]
        down_slot_table = adapter_down[slot_position].astype(jnp.float32)
        up_slot_table = adapter_up[slot_position].astype(jnp.float32)
        token_wide = tok_rows.astype(jnp.float32)
        gradient_wide = cot_rows.astype(jnp.float32)
        expand = slot_mask[:, :, None]
        low_sum = lax.optimization_barrier(jnp.sum(jnp.einsum('td,sdr->tsr', token_wide, down_slot_table) * expand, axis=1))
        back_sum = lax.optimization_barrier(jnp.sum(jnp.einsum('tk,skr->tsr', gradient_wide, up_slot_table) * expand, axis=1))
        lowered = (low_sum * MODEL_WIDTH ** (-0.5)).astype(jnp.bfloat16)
        backward = (back_sum * ADAPTER_RANK ** (-0.5)).astype(jnp.bfloat16)
        mask_bf = slot_mask.astype(jnp.bfloat16)[:, :, None]
        rank_mask = (lowered[:, None, :] * mask_bf).astype(jnp.float32)
        backward_mask = (backward[:, None, :] * mask_bf).astype(jnp.float32)
        raised_rows = jnp.einsum('tsr,skr->tk', rank_mask, up_slot_table)
        frozen_rows = jnp.dot(tok_rows, frozen_key_weight, preferred_element_type=jnp.float32)
        output_rows = (frozen_rows + adapter_scale * ADAPTER_RANK ** (-0.5) * raised_rows).astype(jnp.bfloat16)
        frozen_input = jnp.dot(cot_rows, frozen_key_weight.T, preferred_element_type=jnp.float32)
        adapter_input = jnp.einsum('tsr,sdr->td', backward_mask, down_slot_table)
        input_rows = (frozen_input + adapter_scale * MODEL_WIDTH ** (-0.5) * adapter_input).astype(jnp.bfloat16)
        partial_down = (adapter_scale * MODEL_WIDTH ** (-0.5) * jnp.einsum('og,ocp->cgp', token_wide, backward_mask)).astype(jnp.bfloat16)
        partial_up = (adapter_scale * ADAPTER_RANK ** (-0.5) * jnp.einsum('qy,qoe->oye', gradient_wide, rank_mask)).astype(jnp.bfloat16)
        sum_down = sum_down.at[slot_position].add(partial_down.astype(jnp.float32))
        sum_up = sum_up.at[slot_position].add(partial_up.astype(jnp.float32))
        return ((sum_down, sum_up), (output_rows, input_rows))
    start_down = jnp.zeros((ADAPTER_TOTAL, MODEL_WIDTH, ADAPTER_RANK), jnp.float32)
    start_up = jnp.zeros((ADAPTER_TOTAL, KEY_WIDTH, ADAPTER_RANK), jnp.float32)
    feeds = (tokens.reshape(N_TOK, TOK_DEV, MODEL_WIDTH), output_gradient.reshape(N_TOK, TOK_DEV, KEY_WIDTH), placement, counts)
    (down_gradient, up_gradient), (out_blocks, in_blocks) = lax.scan(holder, (start_down, start_up), feeds)
    key_output = out_blocks.reshape(TOKENS, KEY_WIDTH)
    input_gradient = in_blocks.reshape(TOKENS, MODEL_WIDTH)
    fresh_down, average_down_new = optimizer_update(adapter_down, down_gradient, down_first_moment, down_second_moment, down_average)
    fresh_up, average_up_new = optimizer_update(adapter_up, up_gradient, up_first_moment, up_second_moment, up_average)
    return (key_output, input_gradient, fresh_down, fresh_up, average_down_new, average_up_new)
```

```python
import functools

import jax
import jax.numpy as jnp
from jax import lax
from jax.experimental import pallas as pl
from jax.experimental.pallas import tpu as pltpu
from jax.sharding import PartitionSpec as P

MODEL_WIDTH = 8192
ADAPTER_RANK = 64

adapter_scale = 0.5
learn_rate = 0.3
beta_one = 0.9
beta_two = 0.99
adam_eps = 1e-08
ema_decay = 0.9

LOW_SCALE = MODEL_WIDTH ** (-0.5)
BACK_SCALE = ADAPTER_RANK ** (-0.5)
MIB = 1024 * 1024

f32 = jnp.float32
bf16 = jnp.bfloat16

SMEM = pl.BlockSpec(memory_space=pltpu.SMEM)
VMEM = pl.BlockSpec(memory_space=pltpu.VMEM)
ANY = pl.BlockSpec(memory_space=pl.ANY)


def shape_of(shape, dtype):
    return jax.ShapeDtypeStruct(tuple(shape), dtype)


def cost(flops, bytes_accessed):
    return pl.CostEstimate(flops=int(flops), bytes_accessed=int(bytes_accessed), transcendentals=0)


def params(mib):
    return pltpu.CompilerParams(vmem_limit_bytes=mib * MIB)


def nt(a, b):
    return lax.dot_general(a, b, (((1,), (1,)), ((), ())), preferred_element_type=f32)


def nn(a, b):
    return lax.dot_general(a, b, (((1,), (0,)), ((), ())), preferred_element_type=f32)


def tn(a, b):
    return lax.dot_general(a, b, (((0,), (0,)), ((), ())), preferred_element_type=f32)


def owned_place(placement, sequence, slot, owned, tok_size):
    me = lax.axis_index("tok")
    target = lax.rem(me - slot + tok_size, tok_size)
    tenant = placement[target, slot]
    place = jnp.int32(0)
    for k in range(1, owned):
        place = place + jnp.where(sequence[me * owned + k] == tenant, jnp.int32(k), jnp.int32(0))
    return place


def slot_ends(counts, slots):
    me = lax.axis_index("tok")
    ends = []
    total = jnp.int32(0)
    for s in range(slots):
        total = total + counts[me, s]
        ends.append(total)
    return ends


def slot_mask(ends, slot, shape):
    rows = lax.broadcasted_iota(jnp.int32, shape, 1)
    inside = rows < ends[slot]
    if slot:
        inside = inside & (rows >= ends[slot - 1])
    return inside


def pick_slot(ends, products, rank):
    rows = lax.broadcasted_iota(jnp.int32, (rank, products.shape[1]), 1)
    slots = products.shape[0] // rank
    out = products[(slots - 1) * rank :]
    for s in range(slots - 2, -1, -1):
        out = jnp.where(rows < ends[s], products[s * rank : (s + 1) * rank], out)
    return out


def spread_slots(ends, values):
    wide = values.astype(f32)
    return jnp.concatenate(
        [jnp.where(slot_mask(ends, s, wide.shape), wide, 0.0) for s in range(len(ends))], axis=0
    ).astype(bf16)


def paired_sum(parts):
    parts = list(parts)
    while len(parts) > 1:
        parts = [parts[i] + parts[i + 1] for i in range(0, len(parts), 2)]
    return parts[0]


def select_kernel(slots, owned, tok_size, placement, sequence, down, up, *rest):
    ups, downs, sems = rest[:slots], rest[slots : 2 * slots], rest[2 * slots]
    copies = []
    order = list(range(1, slots)) + [0]
    places = {s: owned_place(placement, sequence, s, owned, tok_size) for s in order}
    for s in order:
        copies.append(pltpu.make_async_copy(up.at[places[s]], ups[s], sems.at[s]))
    for s in order:
        copies.append(pltpu.make_async_copy(down.at[places[s]], downs[s], sems.at[slots + s]))
    for copy in copies:
        copy.start()
    for copy in copies:
        copy.wait()


def base_kernel(width, tokens, weight, keep, send):
    tp, sub = lax.axis_index("tp"), lax.axis_index("sub")
    mine, other = tp, 1 - tp
    for ref, s in ((send, 1 - sub), (keep, sub)):
        for i, t in enumerate((other, mine)):
            start = pl.multiple_of((t * 2 + s) * width, width)
            ref[i] = nn(tokens[...], weight[:, pl.ds(start, width)])


def back_kernel(slots, counts, grad, *rest):
    tables, out = rest[:slots], rest[slots]
    ends = slot_ends(counts, slots)
    table = jnp.concatenate([t[...] for t in tables], axis=0)
    out[...] = pick_slot(ends, nt(table, grad[...]), ADAPTER_RANK)


def part_down_kernel(slots, pieces, widths, counts, tokens, *rest):
    parts, rest = rest[:pieces], rest[pieces:]
    spread_out, own = rest[0], rest[1]
    sends = rest[2:]
    ends = slot_ends(counts, slots)
    back = (paired_sum([p[...] for p in parts]) * BACK_SCALE).astype(bf16)
    spread = spread_slots(ends, back)
    spread_out[...] = spread
    start = 0
    rank = ADAPTER_RANK
    for c, width in enumerate(widths):
        product = nn(spread, tokens[:, start : start + width]) * (adapter_scale * LOW_SCALE)
        product = product.astype(bf16)
        own[:, start : start + width] = product[:rank]
        for s in range(1, slots):
            sends[c * (slots - 1) + s - 1][...] = product[s * rank : (s + 1) * rank]
        start += width


def low_kernel(slots, counts, tokens, *rest):
    tables, out = rest[:slots], rest[slots]
    ends = slot_ends(counts, slots)
    table = jnp.concatenate([t[...] for t in tables], axis=0)
    out[...] = pick_slot(ends, nt(table, tokens[...]), ADAPTER_RANK)


def input_kernel(slots, blocks, width, spread, weight, *rest):
    grads, rest = rest[:blocks], rest[blocks:]
    tables, out = rest[:slots], rest[slots]
    if blocks == 1:
        frozen = nt(grads[0][...], weight[...])
    else:
        tp, sub = lax.axis_index("tp"), lax.axis_index("sub")
        frozen = None
        for ref, t, s in zip(grads, (tp, 1 - tp, tp, 1 - tp), (sub, sub, 1 - sub, 1 - sub)):
            start = pl.multiple_of((t * 2 + s) * width, width)
            term = nt(ref[...], weight[:, pl.ds(start, width)])
            frozen = term if frozen is None else frozen + term
    table = jnp.concatenate([t[...] for t in tables], axis=0)
    adapter = tn(spread[...], table)
    out[...] = (frozen + (adapter_scale * LOW_SCALE) * adapter).astype(bf16)


def key_kernel(slots, pieces, frozen_parts, counts, grad, *rest):
    parts, rest = rest[:pieces], rest[pieces:]
    frozen, rest = rest[:frozen_parts], rest[frozen_parts:]
    tables, rest = rest[:slots], rest[slots:]
    key_out, outs = rest[0], rest[1:]
    rank = ADAPTER_RANK
    ends = slot_ends(counts, slots)
    low = (paired_sum([p[...] for p in parts]) * LOW_SCALE).astype(bf16)
    spread = spread_slots(ends, low)
    product = (nn(spread, grad[...]) * (adapter_scale * BACK_SCALE)).astype(bf16)
    for s in range(slots):
        outs[s][...] = product[s * rank : (s + 1) * rank]
    table = jnp.concatenate([t[...] for t in tables], axis=0)
    raised = tn(spread, table)
    total = frozen[0][...]
    for part in frozen[1:]:
        total = total + part[...]
    key_out[...] = (total + (adapter_scale * BACK_SCALE) * raised).astype(bf16)


def adam_kernel(slots, owned, tok_size, aliased, placement, sequence, *rest):
    came, rest = rest[:slots], rest[slots:]
    weights, mean_old, var_old, avg_old = rest[:4]
    fresh, average = rest[4 + aliased :]
    places = [owned_place(placement, sequence, s, owned, tok_size) for s in range(slots)]
    for k in range(owned):
        gradient = jnp.zeros(weights.shape[1:], f32)
        for s in range(slots):
            pick = jnp.where(places[s] == k, 1.0, 0.0)
            gradient = gradient + pick * came[s][...].astype(f32)
        mean_new = beta_one * mean_old[k] + (1.0 - beta_one) * gradient
        var_new = beta_two * var_old[k] + (1.0 - beta_two) * gradient * gradient
        updated = weights[k].astype(f32) - learn_rate * mean_new / (jnp.sqrt(var_new) + adam_eps)
        fresh[k] = updated.astype(bf16)
        average[k] = ema_decay * avg_old[k] + (1.0 - ema_decay) * updated


def adam(placement, sequence, came, came_start, weights, mean, var, avg, tok_size, first, width, step, into):
    owned, rank, _ = weights.shape
    slots = len(came)
    block = pl.BlockSpec((owned, rank, step), lambda i: (0, 0, first // step + i))
    came_specs = [
        pl.BlockSpec((rank, step), lambda i, b=b: (0, (first - b) // step + i)) for b in came_start
    ]
    aliases = {}
    extra = ()
    if into is not None:
        extra = into
        aliases = {2 + slots + 4: 0, 2 + slots + 5: 1}
    return pl.pallas_call(
        functools.partial(adam_kernel, slots, owned, tok_size, len(extra)),
        grid=(width // step,),
        out_shape=(shape_of(weights.shape, bf16), shape_of(weights.shape, f32)),
        in_specs=[SMEM, SMEM] + came_specs + [block] * 4 + [ANY] * len(extra),
        out_specs=(block, block),
        input_output_aliases=aliases,
        compiler_params=params(24),
        cost_estimate=cost(owned * rank * width * 20, owned * rank * width * 20),
    )(placement, sequence, *came, weights, mean, var, avg, *extra)


def swap(block, axes, flips):
    sizes = [lax.axis_size(a) for a in axes]
    route = []
    for t in range(sizes[0]):
        for s in range(sizes[1]):
            source = (t ^ flips[0]) * sizes[1] + (s ^ flips[1])
            route.append((source, t * sizes[1] + s))
    return lax.ppermute(block, axes, route)


def per_device(
    tokens,
    frozen_key_weight,
    output_gradient,
    counts,
    placement,
    adapter_sequence,
    adapter_down,
    adapter_up,
    down_first_moment,
    down_second_moment,
    down_average,
    up_first_moment,
    up_second_moment,
    up_average,
):
    tok_size = lax.axis_size("tok")
    tp_size, sub_size = lax.axis_size("tp"), lax.axis_size("sub")
    shards = ("tp", "sub")
    square = tp_size == 2 and sub_size == 2
    rows, wide = tokens.shape
    narrow = output_gradient.shape[1]
    key_width = frozen_key_weight.shape[1]
    owned = adapter_down.shape[0]
    slots = placement.shape[1]
    rank = ADAPTER_RANK
    flip = lambda a: jnp.swapaxes(a, 1, 2)
    down, down_m, down_v, down_a = map(
        flip, (adapter_down, down_first_moment, down_second_moment, down_average)
    )
    up, up_m, up_v, up_a = map(flip, (adapter_up, up_first_moment, up_second_moment, up_average))

    def fetch(block, slot):
        return lax.ppermute(block, "tok", [((i + slot) % tok_size, i) for i in range(tok_size)])

    def give_back(block, slot):
        return lax.ppermute(block, "tok", [((i - slot) % tok_size, i) for i in range(tok_size)])

    def shared(part):
        if not square:
            return [lax.psum(part, shards)]
        return [
            part,
            swap(part, shards, (0, 1)),
            swap(part, shards, (1, 0)),
            swap(part, shards, (1, 1)),
        ]

    selected = pl.pallas_call(
        functools.partial(select_kernel, slots, owned, tok_size),
        out_shape=[shape_of((rank, narrow), bf16)] * slots + [shape_of((rank, wide), bf16)] * slots,
        in_specs=[SMEM, SMEM, ANY, ANY],
        out_specs=[ANY] * (2 * slots),
        scratch_shapes=[pltpu.SemaphoreType.DMA((2 * slots,))],
        cost_estimate=cost(0, 4 * slots * rank * (wide + narrow)),
    )(placement, adapter_sequence, down, up)
    up_tables = [selected[0]] + [fetch(selected[s], s) for s in range(1, slots)]
    down_tables = [selected[slots]] + [fetch(selected[slots + s], s) for s in range(1, slots)]

    if square:
        across = swap(output_gradient, shards, (1, 0))
        grads = [
            output_gradient,
            across,
            swap(output_gradient, shards, (0, 1)),
            swap(across, shards, (0, 1)),
        ]
        keep, send = pl.pallas_call(
            functools.partial(base_kernel, narrow),
            out_shape=[shape_of((2, rows, narrow), f32)] * 2,
            in_specs=[VMEM, VMEM],
            out_specs=[VMEM, VMEM],
            compiler_params=params(32),
            cost_estimate=cost(2 * rows * wide * key_width, 2 * wide * (rows + key_width)),
        )(tokens, frozen_key_weight)
        got = swap(send, shards, (0, 1))
        frozen = [keep[1], got[1], swap(keep[0] + got[0], shards, (1, 0))]
    else:
        grads = [lax.all_gather(output_gradient, shards, axis=1, tiled=True)]
        base = jnp.dot(tokens, frozen_key_weight, preferred_element_type=f32)
        frozen = [lax.psum_scatter(base, shards, scatter_dimension=1, tiled=True)]

    back_part = pl.pallas_call(
        functools.partial(back_kernel, slots),
        out_shape=shape_of((rank, rows), f32),
        in_specs=[SMEM, VMEM] + [VMEM] * slots,
        out_specs=VMEM,
        compiler_params=params(16),
        cost_estimate=cost(2 * rows * narrow * rank * slots, 2 * rows * narrow),
    )(counts, output_gradient, *up_tables)
    back_parts = shared(back_part)

    chunks = [wide // 2, wide // 2]
    spread_back, own_down, *sends = pl.pallas_call(
        functools.partial(part_down_kernel, slots, len(back_parts), chunks),
        out_shape=[shape_of((slots * rank, rows), bf16), shape_of((rank, wide), bf16)]
        + [shape_of((rank, w), bf16) for w in chunks for _ in range(1, slots)],
        in_specs=[SMEM] + [VMEM] * (1 + len(back_parts)),
        out_specs=[VMEM] * (2 + len(chunks) * (slots - 1)),
        compiler_params=params(24),
        cost_estimate=cost(2 * rows * wide * rank * slots, 2 * rows * wide),
    )(counts, tokens, *back_parts)
    came_down = [
        [give_back(sends[c * (slots - 1) + s - 1], s) for s in range(1, slots)]
        for c in range(len(chunks))
    ]

    low_part = pl.pallas_call(
        functools.partial(low_kernel, slots),
        out_shape=shape_of((rank, rows), f32),
        in_specs=[SMEM, VMEM] + [VMEM] * slots,
        out_specs=VMEM,
        compiler_params=params(24),
        cost_estimate=cost(2 * rows * wide * rank * slots, 2 * rows * wide),
    )(counts, tokens, *down_tables)
    low_parts = shared(low_part)

    step = min(256, wide)
    input_gradient = pl.pallas_call(
        functools.partial(input_kernel, slots, len(grads), narrow),
        grid=(wide // step,),
        out_shape=shape_of((rows, wide), bf16),
        in_specs=[
            pl.BlockSpec((slots * rank, rows), lambda i: (0, 0)),
            pl.BlockSpec((step, key_width), lambda i: (i, 0)),
        ]
        + [pl.BlockSpec(g.shape, lambda i: (0, 0)) for g in grads]
        + [pl.BlockSpec((rank, step), lambda i: (0, i))] * slots,
        out_specs=pl.BlockSpec((rows, step), lambda i: (0, i)),
        compiler_params=params(24),
        cost_estimate=cost(2 * rows * wide * (key_width + rank * slots), 2 * wide * (rows + key_width)),
    )(spread_back, frozen_key_weight, *grads, *down_tables)

    key_output, *part_up = pl.pallas_call(
        functools.partial(key_kernel, slots, len(low_parts), len(frozen)),
        out_shape=[shape_of((rows, narrow), bf16)] + [shape_of((rank, narrow), bf16)] * slots,
        in_specs=[SMEM] + [VMEM] * (1 + len(low_parts) + len(frozen) + slots),
        out_specs=[VMEM] * (1 + slots),
        compiler_params=params(24),
        cost_estimate=cost(4 * rows * narrow * rank * slots, 14 * rows * narrow),
    )(counts, output_gradient, *low_parts, *frozen, *up_tables)
    came_up = [part_up[0]] + [give_back(part_up[s], s) for s in range(1, slots)]

    done = None
    start = 0
    for c, width in enumerate(chunks):
        done = adam(
            placement, adapter_sequence, [own_down] + came_down[c], [0] + [start] * (slots - 1),
            down, down_m, down_v, down_a, tok_size, start, width, min(256, width), done,
        )
        start += width
    fresh_down, average_down = done
    fresh_up, average_up = adam(
        placement, adapter_sequence, came_up, [0] * slots,
        up, up_m, up_v, up_a, tok_size, 0, narrow, narrow, None,
    )
    return (
        key_output,
        input_gradient,
        flip(fresh_down),
        flip(fresh_up),
        flip(average_down),
        flip(average_up),
    )


def solution(mesh):
    rows = P(("groups", "tok"), ("tp", "sub"))
    cube = P(("groups", "tok"), ("tp", "sub"), None)
    return jax.shard_map(
        per_device,
        mesh=mesh,
        in_specs=(rows, P(("tp", "sub"), None), rows, P("groups", None), P("groups", None), P("groups"))
        + (cube,) * 8,
        out_specs=(rows, rows, cube, cube, cube, cube),
        check_vma=False,
    )
```

```python
import functools

import jax
import jax.numpy as jnp
from jax import lax
from jax.experimental import pallas as pl
from jax.experimental.pallas import tpu as pltpu
from jax.sharding import PartitionSpec as P

MODEL_WIDTH = 8192
ADAPTER_RANK = 64

adapter_scale = 0.5
learn_rate = 0.3
beta_one = 0.9
beta_two = 0.99
adam_eps = 1e-08
ema_decay = 0.9

LOW_SCALE = MODEL_WIDTH ** (-0.5)
BACK_SCALE = ADAPTER_RANK ** (-0.5)
MIB = 1024 * 1024

f32 = jnp.float32
bf16 = jnp.bfloat16

SMEM = pl.BlockSpec(memory_space=pltpu.SMEM)
VMEM = pl.BlockSpec(memory_space=pltpu.VMEM)
ANY = pl.BlockSpec(memory_space=pl.ANY)


def shape_of(shape, dtype):
    return jax.ShapeDtypeStruct(tuple(shape), dtype)


SCHEDULE_SCALE = 0.05


def cost(flops, bytes_accessed):
    return pl.CostEstimate(
        flops=int(flops * SCHEDULE_SCALE),
        bytes_accessed=int(bytes_accessed * SCHEDULE_SCALE),
        transcendentals=0,
    )


def params(mib):
    return pltpu.CompilerParams(vmem_limit_bytes=mib * MIB)


def nt(a, b):
    return lax.dot_general(a, b, (((1,), (1,)), ((), ())), preferred_element_type=f32)


def nn(a, b):
    return lax.dot_general(a, b, (((1,), (0,)), ((), ())), preferred_element_type=f32)


def tn(a, b):
    return lax.dot_general(a, b, (((0,), (0,)), ((), ())), preferred_element_type=f32)


def owned_place(placement, sequence, slot, owned, tok_size):
    me = lax.axis_index("tok")
    target = lax.rem(me - slot + tok_size, tok_size)
    tenant = placement[target, slot]
    place = jnp.int32(0)
    for k in range(1, owned):
        place = place + jnp.where(sequence[me * owned + k] == tenant, jnp.int32(k), jnp.int32(0))
    return place


def slot_ends(counts, slots):
    me = lax.axis_index("tok")
    ends = []
    total = jnp.int32(0)
    for s in range(slots):
        total = total + counts[me, s]
        ends.append(total)
    return ends


def slot_mask(ends, slot, shape):
    rows = lax.broadcasted_iota(jnp.int32, shape, 1)
    inside = rows < ends[slot]
    if slot:
        inside = inside & (rows >= ends[slot - 1])
    return inside


def pick_slot(ends, products, rank):
    rows = lax.broadcasted_iota(jnp.int32, (rank, products.shape[1]), 1)
    slots = products.shape[0] // rank
    out = products[(slots - 1) * rank :]
    for s in range(slots - 2, -1, -1):
        out = jnp.where(rows < ends[s], products[s * rank : (s + 1) * rank], out)
    return out


def spread_slots(ends, values):
    wide = values.astype(f32)
    return jnp.concatenate(
        [jnp.where(slot_mask(ends, s, wide.shape), wide, 0.0) for s in range(len(ends))], axis=0
    ).astype(bf16)


def paired_sum(parts):
    parts = list(parts)
    while len(parts) > 1:
        parts = [parts[i] + parts[i + 1] for i in range(0, len(parts), 2)]
    return parts[0]


def stacked_tables(tables, slots, tok_size):
    me = lax.axis_index("tok")
    return jnp.concatenate([tables[lax.rem(me + s, tok_size)] for s in range(slots)], axis=0)


def select_kernel(slots, owned, tok_size, placement, sequence, down, up, *rest):
    ups, downs, sems = rest[:slots], rest[slots], rest[slots + 1]
    me = lax.axis_index("tok")
    copies = []
    order = list(range(1, slots)) + [0]
    places = {s: owned_place(placement, sequence, s, owned, tok_size) for s in order}
    for s in order:
        copies.append(pltpu.make_async_copy(up.at[places[s]], ups[s], sems.at[s]))
    for s in order:
        target = downs.at[lax.rem(me - s + tok_size, tok_size)]
        copies.append(pltpu.make_async_copy(down.at[places[s]], target, sems.at[slots + s]))
    for copy in copies:
        copy.start()
    for copy in copies:
        copy.wait()


def base_kernel(width, tokens, weight, ready, keep, send):
    tp, sub = lax.axis_index("tp"), lax.axis_index("sub")
    mine, other = tp, 1 - tp
    for ref, s in ((send, 1 - sub), (keep, sub)):
        for i, t in enumerate((other, mine)):
            start = pl.multiple_of((t * 2 + s) * width, width)
            ref[i] = nn(tokens[...], weight[:, pl.ds(start, width)])


def back_kernel(slots, counts, grad, *rest):
    tables, out = rest[:slots], rest[slots]
    ends = slot_ends(counts, slots)
    table = jnp.concatenate([t[...] for t in tables], axis=0)
    out[...] = pick_slot(ends, nt(table, grad[...]), ADAPTER_RANK)


def part_down_kernel(slots, pieces, width, counts, tokens, grad, *rest):
    parts, rest = rest[:pieces], rest[pieces:]
    spread_out, grad_out, outs = rest[0], rest[1], rest[2:]
    ends = slot_ends(counts, slots)
    back = (paired_sum([p[...] for p in parts]) * BACK_SCALE).astype(bf16)
    spread = spread_slots(ends, back)
    spread_out[...] = spread
    product = (nn(spread, tokens[:, :width]) * (adapter_scale * LOW_SCALE)).astype(bf16)
    for s in range(slots):
        outs[s][...] = product[s * ADAPTER_RANK : (s + 1) * ADAPTER_RANK]
    grad_out[...] = grad[...]


def low_kernel(slots, tok_size, counts, tokens, tables, out):
    ends = slot_ends(counts, slots)
    table = stacked_tables(tables, slots, tok_size)
    out[...] = pick_slot(ends, nt(table, tokens[...]), ADAPTER_RANK)


def input_kernel(slots, tok_size, width, spread, weight, tables, after, *rest):
    grads, (out, whole, turned) = rest[:-3], rest[-3:]

    @pl.when(pl.program_id(0) == 0)
    def _():
        turned[...] = spread[...].astype(f32).T.astype(bf16)
        if len(grads) == 1:
            whole[...] = grads[0][...]
        else:
            tp, sub = lax.axis_index("tp"), lax.axis_index("sub")
            pieces = (grads[0][...], grads[1][...], grads[2][0], grads[2][1])
            for piece, t, s in zip(pieces, (tp, 1 - tp, tp, 1 - tp), (sub, sub, 1 - sub, 1 - sub)):
                start = pl.multiple_of((t * 2 + s) * width, width)
                whole[:, pl.ds(start, width)] = piece

    frozen = nt(whole[...], weight[...])
    table = stacked_tables(tables, slots, tok_size)
    adapter = nn(turned[...], table)
    out[...] = (frozen + (adapter_scale * LOW_SCALE) * adapter).astype(bf16)


def key_kernel(slots, pieces, frozen_parts, first, counts, tokens, grad, spread_back, *rest):
    parts, rest = rest[:pieces], rest[pieces:]
    frozen, rest = rest[:frozen_parts], rest[frozen_parts:]
    tables, rest = rest[:slots], rest[slots:]
    key_out, outs = rest[0], rest[1:]
    rank = ADAPTER_RANK
    split = tokens.shape[1] - first
    ends = slot_ends(counts, slots)
    low = (paired_sum([p[...] for p in parts]) * LOW_SCALE).astype(bf16)
    spread = spread_slots(ends, low)
    product = (nn(spread, grad[...]) * (adapter_scale * BACK_SCALE)).astype(bf16)
    for s in range(slots):
        outs[s][:, split:] = product[s * rank : (s + 1) * rank]
    product = (nn(spread_back[...], tokens[:, first:]) * (adapter_scale * LOW_SCALE)).astype(bf16)
    for s in range(slots):
        outs[s][:, :split] = product[s * rank : (s + 1) * rank]
    table = jnp.concatenate([t[...] for t in tables], axis=0)
    raised = nn(spread.astype(f32).T.astype(bf16), table)
    total = frozen[0][...]
    for part in frozen[1:]:
        total = total + part[...]
    key_out[...] = (total + (adapter_scale * BACK_SCALE) * raised).astype(bf16)


def adam_kernel(slots, owned, tok_size, offset, extras, placement, sequence, *rest):
    came, rest = rest[:slots], rest[slots:]
    weights, mean_old, var_old, avg_old = rest[:4]
    fresh, average, gradients = rest[4 + extras :]
    step = gradients.shape[2]
    gradients[...] = jnp.zeros(gradients.shape, f32)
    for s in range(slots):
        if came[s].shape[1] == step:
            part = came[s][...]
        elif pl.num_programs(0) == 1 or came[s].shape[1] % 128:
            part = came[s][:, offset : offset + step]
        else:
            start = pl.multiple_of(offset + pl.program_id(0) * step, step)
            part = came[s][:, pl.ds(start, step)]
        place = owned_place(placement, sequence, s, owned, tok_size)
        gradients[place] += part.astype(f32)
    for k in range(owned):
        gradient = gradients[k]
        mean_new = beta_one * mean_old[k] + (1.0 - beta_one) * gradient
        var_new = beta_two * var_old[k] + (1.0 - beta_two) * gradient * gradient
        updated = weights[k].astype(f32) - learn_rate * mean_new / (jnp.sqrt(var_new) + adam_eps)
        fresh[k] = updated.astype(bf16)
        average[k] = ema_decay * avg_old[k] + (1.0 - ema_decay) * updated


def adam(placement, sequence, came, offset, old, tok_size, first, width, step, into, after):
    weights = old[0]
    owned, rank, _ = weights.shape
    slots = len(came)
    block = pl.BlockSpec((owned, rank, step), lambda i: (0, 0, first // step + i))
    came_specs = [pl.BlockSpec(c.shape, lambda i: (0, 0)) for c in came]
    aliases = {2 + slots + 4: 0, 2 + slots + 5: 1} if into else {}
    extra = tuple(into) + tuple(after)
    return pl.pallas_call(
        functools.partial(adam_kernel, slots, owned, tok_size, offset, len(extra)),
        grid=(width // step,),
        out_shape=(shape_of(weights.shape, bf16), shape_of(weights.shape, f32)),
        in_specs=[SMEM, SMEM] + came_specs + [block] * 4 + [ANY] * len(extra),
        out_specs=(block, block),
        scratch_shapes=[pltpu.VMEM((owned, rank, step), f32)],
        input_output_aliases=aliases,
        compiler_params=params(24),
        cost_estimate=cost(owned * rank * width * 20, owned * rank * width * 20),
    )(placement, sequence, *came, *old, *extra)


def swap(block, axes, flips):
    sizes = [lax.axis_size(a) for a in axes]
    route = []
    for t in range(sizes[0]):
        for s in range(sizes[1]):
            source = (t ^ flips[0]) * sizes[1] + (s ^ flips[1])
            route.append((source, t * sizes[1] + s))
    return lax.ppermute(block, axes, route)


def per_device(
    tokens,
    frozen_key_weight,
    output_gradient,
    counts,
    placement,
    adapter_sequence,
    adapter_down,
    adapter_up,
    down_first_moment,
    down_second_moment,
    down_average,
    up_first_moment,
    up_second_moment,
    up_average,
):
    tok_size = lax.axis_size("tok")
    tp_size, sub_size = lax.axis_size("tp"), lax.axis_size("sub")
    shards = ("tp", "sub")
    square = tp_size == 2 and sub_size == 2
    rows, wide = tokens.shape
    narrow = output_gradient.shape[1]
    key_width = frozen_key_weight.shape[1]
    owned = adapter_down.shape[0]
    slots = placement.shape[1]
    rank = ADAPTER_RANK
    flip = lambda a: jnp.swapaxes(a, 1, 2)
    down, down_m, down_v, down_a = map(
        flip, (adapter_down, down_first_moment, down_second_moment, down_average)
    )
    up, up_m, up_v, up_a = map(flip, (adapter_up, up_first_moment, up_second_moment, up_average))

    def fetch(block, slot):
        return lax.ppermute(block, "tok", [((i + slot) % tok_size, i) for i in range(tok_size)])

    def give_back(block, slot):
        return lax.ppermute(block, "tok", [((i - slot) % tok_size, i) for i in range(tok_size)])

    def shared(part):
        if not square:
            return [lax.psum(part, shards)]
        both = part + swap(part, shards, (0, 1))
        return [both, swap(both, shards, (1, 0))]

    selected = pl.pallas_call(
        functools.partial(select_kernel, slots, owned, tok_size),
        out_shape=[shape_of((rank, narrow), bf16)] * slots + [shape_of((tok_size, rank, wide), bf16)],
        in_specs=[SMEM, SMEM, ANY, ANY],
        out_specs=[VMEM] * (slots + 1),
        scratch_shapes=[pltpu.SemaphoreType.DMA((2 * slots,))],
        cost_estimate=cost(0, 4 * slots * rank * (wide + narrow)),
    )(placement, adapter_sequence, down, up)
    up_tables = [selected[0]] + [fetch(selected[s], s) for s in range(1, slots)]
    down_tables = lax.all_to_all(selected[slots], "tok", split_axis=0, concat_axis=0, tiled=True)

    back_part = pl.pallas_call(
        functools.partial(back_kernel, slots),
        out_shape=shape_of((rank, rows), f32),
        in_specs=[SMEM, VMEM] + [VMEM] * slots,
        out_specs=VMEM,
        compiler_params=params(16),
        cost_estimate=cost(2 * rows * narrow * rank * slots, 2 * rows * narrow),
    )(counts, output_gradient, *up_tables)
    back_parts = shared(back_part)

    if square:
        keep, send = pl.pallas_call(
            functools.partial(base_kernel, narrow),
            out_shape=[shape_of((2, rows, narrow), f32)] * 2,
            in_specs=[VMEM, VMEM, ANY],
            out_specs=[VMEM, VMEM],
            compiler_params=params(32),
            cost_estimate=cost(2 * rows * wide * key_width, 2 * wide * (rows + key_width)),
        )(tokens, frozen_key_weight, back_part)
        got = swap(send, shards, (0, 1))
        frozen = [keep[1], got[1], swap(keep[0] + got[0], shards, (1, 0))]
    else:
        base = jnp.dot(tokens, frozen_key_weight, preferred_element_type=f32)
        frozen = [lax.psum_scatter(base, shards, scatter_dimension=1, tiled=True)]

    step = min(256, wide)
    first = wide * 5 // 8 // step * step
    spread_back, grad_copy, *part_first = pl.pallas_call(
        functools.partial(part_down_kernel, slots, len(back_parts), first),
        out_shape=[shape_of((slots * rank, rows), bf16), shape_of(output_gradient.shape, bf16)]
        + [shape_of((rank, first), bf16)] * slots,
        in_specs=[SMEM] + [VMEM] * (2 + len(back_parts)),
        out_specs=[VMEM] * (2 + slots),
        compiler_params=params(24),
        cost_estimate=cost(2 * rows * first * rank * slots, 2 * rows * first),
    )(counts, tokens, output_gradient, *back_parts)
    came_first = [part_first[0]] + [give_back(part_first[s], s) for s in range(1, slots)]

    if square:
        across = swap(grad_copy, shards, (1, 0))
        grads = [
            output_gradient,
            across,
            swap(jnp.stack([grad_copy, across]), shards, (0, 1)),
        ]
    else:
        grads = [lax.all_gather(output_gradient, shards, axis=1, tiled=True)]

    low_part = pl.pallas_call(
        functools.partial(low_kernel, slots, tok_size),
        out_shape=shape_of((rank, rows), f32),
        in_specs=[SMEM, VMEM, VMEM],
        out_specs=VMEM,
        compiler_params=params(24),
        cost_estimate=cost(2 * rows * wide * rank * slots, 2 * rows * wide),
    )(counts, tokens, down_tables)
    low_parts = shared(low_part)

    key_output, *part_second = pl.pallas_call(
        functools.partial(key_kernel, slots, len(low_parts), len(frozen), first),
        out_shape=[shape_of((rows, narrow), bf16)]
        + [shape_of((rank, wide - first + narrow), bf16)] * slots,
        in_specs=[SMEM] + [VMEM] * (3 + len(low_parts) + len(frozen) + slots),
        out_specs=[VMEM] * (1 + slots),
        compiler_params=params(24),
        cost_estimate=cost(4 * rows * narrow * rank * slots, 14 * rows * narrow),
    )(counts, tokens, output_gradient, spread_back, *low_parts, *frozen, *up_tables)
    came_second = [part_second[0]] + [give_back(part_second[s], s) for s in range(1, slots)]

    input_gradient = pl.pallas_call(
        functools.partial(input_kernel, slots, tok_size, narrow),
        grid=(wide // step,),
        out_shape=shape_of((rows, wide), bf16),
        in_specs=[
            pl.BlockSpec((slots * rank, rows), lambda i: (0, 0)),
            pl.BlockSpec((step, key_width), lambda i: (i, 0)),
            pl.BlockSpec((tok_size, rank, step), lambda i: (0, 0, i)),
            ANY,
        ]
        + [pl.BlockSpec(g.shape, lambda i, r=g.ndim: (0,) * r) for g in grads],
        out_specs=pl.BlockSpec((rows, step), lambda i: (0, i)),
        scratch_shapes=[pltpu.VMEM((rows, key_width), bf16), pltpu.VMEM((rows, slots * rank), bf16)],
        compiler_params=params(24),
        cost_estimate=cost(2 * rows * wide * (key_width + rank * slots), 2 * wide * (rows + key_width)),
    )(spread_back, frozen_key_weight, down_tables, key_output, *grads)

    down_old, up_old = (down, down_m, down_v, down_a), (up, up_m, up_v, up_a)
    done = adam(
        placement, adapter_sequence, came_first, 0, down_old, tok_size, 0, first, step,
        (), (input_gradient,),
    )
    fresh_up, average_up = adam(
        placement, adapter_sequence, came_second, wide - first, up_old, tok_size, 0, narrow, narrow,
        (), done,
    )
    fresh_down, average_down = adam(
        placement, adapter_sequence, came_second, 0, down_old, tok_size, first, wide - first, step,
        done, (average_up,),
    )
    return (
        key_output,
        input_gradient,
        flip(fresh_down),
        flip(fresh_up),
        flip(average_down),
        flip(average_up),
    )


def solution(mesh):
    rows = P(("groups", "tok"), ("tp", "sub"))
    cube = P(("groups", "tok"), ("tp", "sub"), None)
    return jax.shard_map(
        per_device,
        mesh=mesh,
        in_specs=(rows, P(("tp", "sub"), None), rows, P("groups", None), P("groups", None), P("groups"))
        + (cube,) * 8,
        out_specs=(rows, rows, cube, cube, cube, cube),
        check_vma=False,
    )
```

```python
import functools

import jax
import jax.numpy as jnp
from jax import lax
from jax.experimental import pallas as pl
from jax.experimental.pallas import tpu as pltpu
from jax.sharding import PartitionSpec as P

MODEL_WIDTH = 8192
ADAPTER_RANK = 64

adapter_scale = 0.5
learn_rate = 0.3
beta_one = 0.9
beta_two = 0.99
adam_eps = 1e-08
ema_decay = 0.9

LOW_SCALE = MODEL_WIDTH ** (-0.5)
BACK_SCALE = ADAPTER_RANK ** (-0.5)
MIB = 1024 * 1024

f32 = jnp.float32
bf16 = jnp.bfloat16

SMEM = pl.BlockSpec(memory_space=pltpu.SMEM)
VMEM = pl.BlockSpec(memory_space=pltpu.VMEM)
ANY = pl.BlockSpec(memory_space=pl.ANY)


def shape_of(shape, dtype):
    return jax.ShapeDtypeStruct(tuple(shape), dtype)


SCHEDULE_SCALE = 0.05


def cost(flops, bytes_accessed):
    return pl.CostEstimate(
        flops=int(flops * SCHEDULE_SCALE),
        bytes_accessed=int(bytes_accessed * SCHEDULE_SCALE),
        transcendentals=0,
    )


def params(mib):
    return pltpu.CompilerParams(vmem_limit_bytes=mib * MIB)


def nt(a, b):
    return lax.dot_general(a, b, (((1,), (1,)), ((), ())), preferred_element_type=f32)


def nn(a, b):
    return lax.dot_general(a, b, (((1,), (0,)), ((), ())), preferred_element_type=f32)


def tn(a, b):
    return lax.dot_general(a, b, (((0,), (0,)), ((), ())), preferred_element_type=f32)


def facts_kernel(slots, owned, tok_size, counts, placement, sequence, facts):
    me = lax.axis_index("tok")
    total = jnp.int32(0)
    for s in range(slots):
        total = total + counts[me, s]
        facts[s] = total
        tenant = placement[lax.rem(me - s + tok_size, tok_size), s]
        place = jnp.int32(0)
        for k in range(1, owned):
            place = place + jnp.where(sequence[me * owned + k] == tenant, k, 0)
        facts[slots + s] = place


def slot_ends(facts, slots):
    return [facts[s] for s in range(slots)]


def slot_mask(ends, slot, shape):
    rows = lax.broadcasted_iota(jnp.int32, shape, 1)
    inside = rows < ends[slot]
    if slot:
        inside = inside & (rows >= ends[slot - 1])
    return inside


def pick_slot(ends, products, rank):
    rows = lax.broadcasted_iota(jnp.int32, (rank, products.shape[1]), 1)
    slots = products.shape[0] // rank
    out = products[(slots - 1) * rank :]
    for s in range(slots - 2, -1, -1):
        out = jnp.where(rows < ends[s], products[s * rank : (s + 1) * rank], out)
    return out


def spread_slots(ends, values):
    wide = values.astype(f32)
    return jnp.concatenate(
        [jnp.where(slot_mask(ends, s, wide.shape), wide, 0.0) for s in range(len(ends))], axis=0
    ).astype(bf16)


def paired_sum(stack):
    parts = [stack[i] for i in range(stack.shape[0])]
    while len(parts) > 1:
        parts = [parts[i] + parts[i + 1] for i in range(0, len(parts), 2)]
    return parts[0]


def stacked_tables(tables, slots, tok_size):
    me = lax.axis_index("tok")
    return jnp.concatenate([tables[lax.rem(me + s, tok_size)] for s in range(slots)], axis=0)


def select_kernel(slots, owned, tok_size, counts, placement, sequence, down, up, facts, *rest):
    ups, downs, sems = rest[0], rest[1 : slots + 1], rest[slots + 1]
    me = lax.axis_index("tok")
    facts_kernel(slots, owned, tok_size, counts, placement, sequence, facts)
    copies = []
    order = list(range(1, slots)) + [0]
    for s in order:
        target = ups.at[lax.rem(me - s + tok_size, tok_size)]
        copies.append(pltpu.make_async_copy(up.at[facts[slots + s]], target, sems.at[s]))
    for s in order:
        copies.append(pltpu.make_async_copy(down.at[facts[slots + s]], downs[s], sems.at[slots + s]))
    for copy in copies:
        copy.start()
    for copy in copies:
        copy.wait()


def base_kernel(width, tokens, weight, keep, send):
    tp, sub = lax.axis_index("tp"), lax.axis_index("sub")
    mine, other = tp, 1 - tp
    for ref, s in ((send, 1 - sub), (keep, sub)):
        for i, t in enumerate((other, mine)):
            start = pl.multiple_of((t * 2 + s) * width, width)
            ref[i] = nn(tokens[...], weight[:, pl.ds(start, width)])


def back_kernel(slots, tok_size, facts, grad, tables, out):
    ends = slot_ends(facts, slots)
    table = stacked_tables(tables, slots, tok_size)
    part = pick_slot(ends, nt(table, grad[...]), ADAPTER_RANK)
    for i in range(out.shape[0]):
        out[i] = part


def part_down_kernel(slots, width, facts, tokens, parts, spread_out, *outs):
    ends = slot_ends(facts, slots)
    back = (paired_sum(parts) * BACK_SCALE).astype(bf16)
    spread = spread_slots(ends, back)
    spread_out[...] = spread
    product = (nn(spread, tokens[:, :width]) * (adapter_scale * LOW_SCALE)).astype(bf16)
    for s in range(slots):
        outs[s][...] = product[s * ADAPTER_RANK : (s + 1) * ADAPTER_RANK]


def low_kernel(slots, facts, tokens, *rest):
    tables, out = rest[:slots], rest[slots]
    ends = slot_ends(facts, slots)
    table = jnp.concatenate([t[...] for t in tables], axis=0)
    part = pick_slot(ends, nt(table, tokens[...]), ADAPTER_RANK)
    for i in range(out.shape[0]):
        out[i] = part


def input_kernel(slots, width, spread, weight, *rest):
    grads, rest = rest[:-(slots + 3)], rest[-(slots + 3) :]
    tables, (out, whole, turned) = rest[:slots], rest[slots:]

    @pl.when(pl.program_id(0) == 0)
    def _():
        turned[...] = spread[...].astype(f32).T.astype(bf16)
        if len(grads) == 1:
            whole[...] = grads[0][...]
        else:
            tp, sub = lax.axis_index("tp"), lax.axis_index("sub")
            pieces = (grads[0][...], grads[1][...], grads[2][0], grads[2][1])
            for piece, t, s in zip(pieces, (tp, 1 - tp, tp, 1 - tp), (sub, sub, 1 - sub, 1 - sub)):
                start = pl.multiple_of((t * 2 + s) * width, width)
                whole[:, pl.ds(start, width)] = piece

    frozen = nt(whole[...], weight[...])
    table = jnp.concatenate([t[...] for t in tables], axis=0)
    adapter = nn(turned[...], table)
    out[...] = (frozen + (adapter_scale * LOW_SCALE) * adapter).astype(bf16)


def second_kernel(slots, first, facts, tokens, grad, spread_back, parts, spread_low, *outs):
    rank = ADAPTER_RANK
    split = tokens.shape[1] - first
    ends = slot_ends(facts, slots)
    low = (paired_sum(parts) * LOW_SCALE).astype(bf16)
    spread = spread_slots(ends, low)
    spread_low[...] = spread
    product = (nn(spread, grad[...]) * (adapter_scale * BACK_SCALE)).astype(bf16)
    for s in range(slots):
        outs[s][:, split:] = product[s * rank : (s + 1) * rank]
    product = (nn(spread_back[...], tokens[:, first:]) * (adapter_scale * LOW_SCALE)).astype(bf16)
    for s in range(slots):
        outs[s][:, :split] = product[s * rank : (s + 1) * rank]


def key_kernel(slots, tok_size, spread, tables, *rest):
    frozen, key_out = rest[:-1], rest[-1]
    table = stacked_tables(tables, slots, tok_size)
    raised = nn(spread[...].astype(f32).T.astype(bf16), table)
    total = frozen[0][...]
    for part in frozen[1:]:
        total = total + part[...]
    key_out[...] = (total + (adapter_scale * BACK_SCALE) * raised).astype(bf16)


def adam_kernel(slots, owned, offset, extras, facts, *rest):
    came, rest = rest[:slots], rest[slots:]
    weights, mean_old, var_old, avg_old = rest[:4]
    fresh, average, gradients = rest[4 + extras :]
    step = gradients.shape[2]
    gradients[...] = jnp.zeros(gradients.shape, f32)
    for s in range(slots):
        if came[s].shape[1] == step:
            part = came[s][...]
        elif pl.num_programs(0) == 1 or came[s].shape[1] % 128:
            part = came[s][:, offset : offset + step]
        else:
            start = pl.multiple_of(offset + pl.program_id(0) * step, step)
            part = came[s][:, pl.ds(start, step)]
        gradients[facts[slots + s]] += part.astype(f32)
    for k in range(owned):
        gradient = gradients[k]
        mean_new = beta_one * mean_old[k] + (1.0 - beta_one) * gradient
        var_new = beta_two * var_old[k] + (1.0 - beta_two) * gradient * gradient
        updated = weights[k].astype(f32) - learn_rate * mean_new / (jnp.sqrt(var_new) + adam_eps)
        fresh[k] = updated.astype(bf16)
        average[k] = ema_decay * avg_old[k] + (1.0 - ema_decay) * updated


def adam(facts, came, offset, old, first, width, step, into):
    weights = old[0]
    owned, rank, _ = weights.shape
    slots = len(came)
    block = pl.BlockSpec((owned, rank, step), lambda i: (0, 0, first // step + i))
    came_specs = [pl.BlockSpec(c.shape, lambda i: (0, 0)) for c in came]
    aliases = {1 + slots + 4: 0, 1 + slots + 5: 1} if into else {}
    extra = tuple(into)
    return pl.pallas_call(
        functools.partial(adam_kernel, slots, owned, offset, len(extra)),
        grid=(width // step,),
        out_shape=(shape_of(weights.shape, bf16), shape_of(weights.shape, f32)),
        in_specs=[SMEM] + came_specs + [block] * 4 + [ANY] * len(extra),
        out_specs=(block, block),
        scratch_shapes=[pltpu.VMEM((owned, rank, step), f32)],
        input_output_aliases=aliases,
        compiler_params=params(16),
        cost_estimate=cost(owned * rank * width * 20, owned * rank * width * 20),
    )(facts, *came, *old, *extra)


def after(value, *others):
    return lax.optimization_barrier((value, *others))[0]


def swap(block, axes, flips):
    sizes = [lax.axis_size(a) for a in axes]
    route = []
    for t in range(sizes[0]):
        for s in range(sizes[1]):
            source = (t ^ flips[0]) * sizes[1] + (s ^ flips[1])
            route.append((source, t * sizes[1] + s))
    return lax.ppermute(block, axes, route)


def per_device(
    tokens,
    frozen_key_weight,
    output_gradient,
    counts,
    placement,
    adapter_sequence,
    adapter_down,
    adapter_up,
    down_first_moment,
    down_second_moment,
    down_average,
    up_first_moment,
    up_second_moment,
    up_average,
):
    tok_size = lax.axis_size("tok")
    tp_size, sub_size = lax.axis_size("tp"), lax.axis_size("sub")
    shards = ("tp", "sub")
    square = tp_size == 2 and sub_size == 2
    rows, wide = tokens.shape
    narrow = output_gradient.shape[1]
    key_width = frozen_key_weight.shape[1]
    owned = adapter_down.shape[0]
    slots = placement.shape[1]
    rank = ADAPTER_RANK
    flip = lambda a: jnp.swapaxes(a, 1, 2)
    down, down_m, down_v, down_a = map(
        flip, (adapter_down, down_first_moment, down_second_moment, down_average)
    )
    up, up_m, up_v, up_a = map(flip, (adapter_up, up_first_moment, up_second_moment, up_average))

    def fetch(block, slot):
        return lax.ppermute(block, "tok", [((i + slot) % tok_size, i) for i in range(tok_size)])

    def give_back(block, slot):
        return lax.ppermute(block, "tok", [((i - slot) % tok_size, i) for i in range(tok_size)])

    def shared(stack):
        if not square:
            return lax.psum(stack, shards)
        return lax.all_to_all(stack, shards, split_axis=0, concat_axis=0, tiled=True)

    copies = tp_size * sub_size if square else 1
    facts, up_send, *selected = pl.pallas_call(
        functools.partial(select_kernel, slots, owned, tok_size),
        out_shape=[shape_of((2 * slots,), jnp.int32), shape_of((tok_size, rank, narrow), bf16)]
        + [shape_of((rank, wide), bf16)] * slots,
        in_specs=[SMEM, SMEM, SMEM, ANY, ANY],
        out_specs=[SMEM] + [VMEM] * (1 + slots),
        scratch_shapes=[pltpu.SemaphoreType.DMA((2 * slots,))],
        compiler_params=params(56),
        cost_estimate=cost(0, 4 * slots * rank * (wide + narrow)),
    )(counts, placement, adapter_sequence, down, up)
    up_tables = lax.all_to_all(up_send, "tok", split_axis=0, concat_axis=0, tiled=True)
    down_tables = [selected[0]] + [fetch(selected[s], s) for s in range(1, slots)]

    back_part = pl.pallas_call(
        functools.partial(back_kernel, slots, tok_size),
        out_shape=shape_of((copies, rank, rows), f32),
        in_specs=[SMEM, VMEM, VMEM],
        out_specs=VMEM,
        compiler_params=params(16),
        cost_estimate=cost(2 * rows * narrow * rank * slots, 2 * rows * narrow),
    )(facts, output_gradient, up_tables)
    back_parts = shared(back_part)

    step = min(256, wide)
    first = wide * 5 // 8 // step * step
    spread_back, *part_first = pl.pallas_call(
        functools.partial(part_down_kernel, slots, first),
        out_shape=[shape_of((slots * rank, rows), bf16)] + [shape_of((rank, first), bf16)] * slots,
        in_specs=[SMEM, VMEM, VMEM],
        out_specs=[VMEM] * (1 + slots),
        compiler_params=params(16),
        cost_estimate=cost(2 * rows * first * rank * slots, 2 * rows * first),
    )(facts, tokens, back_parts)
    came_first = [part_first[0]] + [give_back(part_first[s], s) for s in range(1, slots)]

    if square:
        across = swap(output_gradient, shards, (1, 0))
        grads = [
            output_gradient,
            across,
            swap(jnp.stack([output_gradient, across]), shards, (0, 1)),
        ]
        keep, send = pl.pallas_call(
            functools.partial(base_kernel, narrow),
            out_shape=[shape_of((2, rows, narrow), f32)] * 2,
            in_specs=[VMEM, VMEM],
            out_specs=[VMEM, VMEM],
            compiler_params=params(16),
            cost_estimate=cost(2 * rows * wide * key_width, 2 * wide * (rows + key_width)),
        )(tokens, after(frozen_key_weight, spread_back))
        got = swap(send, shards, (0, 1))
        frozen = [keep[1], got[1], swap(keep[0] + got[0], shards, (1, 0))]
        own_table = after(down_tables[0], keep)
    else:
        grads = [lax.all_gather(output_gradient, shards, axis=1, tiled=True)]
        base = jnp.dot(tokens, frozen_key_weight, preferred_element_type=f32)
        frozen = [lax.psum_scatter(base, shards, scatter_dimension=1, tiled=True)]
        own_table = down_tables[0]

    low_part = pl.pallas_call(
        functools.partial(low_kernel, slots),
        out_shape=shape_of((copies, rank, rows), f32),
        in_specs=[SMEM, VMEM] + [VMEM] * slots,
        out_specs=VMEM,
        compiler_params=params(16),
        cost_estimate=cost(2 * rows * wide * rank * slots, 2 * rows * wide),
    )(facts, tokens, own_table, *down_tables[1:])
    low_parts = shared(low_part)

    spread_low, *part_second = pl.pallas_call(
        functools.partial(second_kernel, slots, first),
        out_shape=[shape_of((slots * rank, rows), bf16)]
        + [shape_of((rank, wide - first + narrow), bf16)] * slots,
        in_specs=[SMEM] + [VMEM] * 4,
        out_specs=[VMEM] * (1 + slots),
        compiler_params=params(16),
        cost_estimate=cost(2 * rows * narrow * rank * slots, 14 * rows * narrow),
    )(facts, tokens, output_gradient, spread_back, low_parts)
    came_second = [part_second[0]] + [
        give_back(after(part_second[s], *came_first[1:]), s) for s in range(1, slots)
    ]

    key_output = pl.pallas_call(
        functools.partial(key_kernel, slots, tok_size),
        out_shape=shape_of((rows, narrow), bf16),
        in_specs=[VMEM] * (2 + len(frozen)),
        out_specs=VMEM,
        compiler_params=params(16),
        cost_estimate=cost(2 * rows * narrow * rank * slots, 14 * rows * narrow),
    )(spread_low, up_tables, *frozen)

    input_gradient = pl.pallas_call(
        functools.partial(input_kernel, slots, narrow),
        grid=(wide // step,),
        out_shape=shape_of((rows, wide), bf16),
        in_specs=[
            pl.BlockSpec((slots * rank, rows), lambda i: (0, 0)),
            pl.BlockSpec((step, key_width), lambda i: (i, 0)),
        ]
        + [pl.BlockSpec(g.shape, lambda i, r=g.ndim: (0,) * r) for g in grads]
        + [pl.BlockSpec((rank, step), lambda i: (0, i))] * slots,
        out_specs=pl.BlockSpec((rows, step), lambda i: (0, i)),
        scratch_shapes=[pltpu.VMEM((rows, key_width), bf16), pltpu.VMEM((rows, slots * rank), bf16)],
        compiler_params=params(16),
        cost_estimate=cost(2 * rows * wide * (key_width + rank * slots), 2 * wide * (rows + key_width)),
    )(after(spread_back, spread_low), frozen_key_weight, *grads, *down_tables)

    down_old, up_old = (down, down_m, down_v, down_a), (up, up_m, up_v, up_a)
    done = adam(facts, came_first, 0, down_old, 0, first, step, ())
    late = [came_second[0]] + [after(c, key_output, input_gradient, done[0]) for c in came_second[1:]]
    fresh_up, average_up = adam(facts, late, wide - first, up_old, 0, narrow, narrow, ())
    fresh_down, average_down = adam(
        facts, late, 0, down_old, first, wide - first, step, done
    )
    return (
        key_output,
        input_gradient,
        flip(fresh_down),
        flip(fresh_up),
        flip(average_down),
        flip(average_up),
    )


def solution(mesh):
    rows = P(("groups", "tok"), ("tp", "sub"))
    cube = P(("groups", "tok"), ("tp", "sub"), None)
    return jax.shard_map(
        per_device,
        mesh=mesh,
        in_specs=(rows, P(("tp", "sub"), None), rows, P("groups", None), P("groups", None), P("groups"))
        + (cube,) * 8,
        out_specs=(rows, rows, cube, cube, cube, cube),
        check_vma=False,
    )
```

```python
import functools

import jax
import jax.numpy as jnp
from jax import lax
from jax.experimental import pallas as pl
from jax.experimental.pallas import tpu as pltpu
from jax.sharding import PartitionSpec as P

MODEL_WIDTH = 8192
ADAPTER_RANK = 64

adapter_scale = 0.5
learn_rate = 0.3
beta_one = 0.9
beta_two = 0.99
adam_eps = 1e-08
ema_decay = 0.9

LOW_SCALE = MODEL_WIDTH ** (-0.5)
BACK_SCALE = ADAPTER_RANK ** (-0.5)
MIB = 1024 * 1024

f32 = jnp.float32
bf16 = jnp.bfloat16

SMEM = pl.BlockSpec(memory_space=pltpu.SMEM)
VMEM = pl.BlockSpec(memory_space=pltpu.VMEM)
ANY = pl.BlockSpec(memory_space=pl.ANY)


def shape_of(shape, dtype):
    return jax.ShapeDtypeStruct(tuple(shape), dtype)


SCHEDULE_SCALE = 0.05


def cost(flops, bytes_accessed):
    return pl.CostEstimate(
        flops=int(flops * SCHEDULE_SCALE),
        bytes_accessed=int(bytes_accessed * SCHEDULE_SCALE),
        transcendentals=0,
    )


def params(mib):
    return pltpu.CompilerParams(vmem_limit_bytes=mib * MIB)


def nt(a, b):
    return lax.dot_general(a, b, (((1,), (1,)), ((), ())), preferred_element_type=f32)


def nn(a, b):
    return lax.dot_general(a, b, (((1,), (0,)), ((), ())), preferred_element_type=f32)


def tn(a, b):
    return lax.dot_general(a, b, (((0,), (0,)), ((), ())), preferred_element_type=f32)


def facts_kernel(slots, owned, tok_size, counts, placement, sequence, facts):
    me = lax.axis_index("tok")
    total = jnp.int32(0)
    for s in range(slots):
        total = total + counts[me, s]
        facts[s] = total
        tenant = placement[lax.rem(me - s + tok_size, tok_size), s]
        place = jnp.int32(0)
        for k in range(1, owned):
            place = place + jnp.where(sequence[me * owned + k] == tenant, k, 0)
        facts[slots + s] = place


def slot_ends(facts, slots):
    return [facts[s] for s in range(slots)]


def slot_mask(ends, slot, shape):
    rows = lax.broadcasted_iota(jnp.int32, shape, 1)
    inside = rows < ends[slot]
    if slot:
        inside = inside & (rows >= ends[slot - 1])
    return inside


def pick_slot(ends, products, rank):
    rows = lax.broadcasted_iota(jnp.int32, (rank, products.shape[1]), 1)
    slots = products.shape[0] // rank
    out = products[(slots - 1) * rank :]
    for s in range(slots - 2, -1, -1):
        out = jnp.where(rows < ends[s], products[s * rank : (s + 1) * rank], out)
    return out


def spread_slots(ends, values):
    wide = values.astype(f32)
    return jnp.concatenate(
        [jnp.where(slot_mask(ends, s, wide.shape), wide, 0.0) for s in range(len(ends))], axis=0
    ).astype(bf16)


def paired_sum(refs):
    parts = [ref[...] for ref in refs]
    while len(parts) > 1:
        parts = [parts[i] + parts[i + 1] for i in range(0, len(parts), 2)]
    return parts[0]


def select_kernel(slots, owned, tok_size, counts, placement, sequence, down, up, facts, *rest):
    ups, downs, sems = rest[:slots], rest[slots], rest[slots + 1]
    me = lax.axis_index("tok")
    facts_kernel(slots, owned, tok_size, counts, placement, sequence, facts)
    copies = []
    order = list(range(1, slots)) + [0]
    for s in order:
        copies.append(pltpu.make_async_copy(up.at[facts[slots + s]], ups[s], sems.at[s]))
    for s in order:
        target = downs.at[lax.rem(me - s + tok_size, tok_size)]
        copies.append(pltpu.make_async_copy(down.at[facts[slots + s]], target, sems.at[slots + s]))
    for copy in copies:
        copy.start()
    for copy in copies:
        copy.wait()


def base_kernel(width, tokens, weight, keep, send):
    tp, sub = lax.axis_index("tp"), lax.axis_index("sub")
    mine, other = tp, 1 - tp
    for ref, s in ((send, 1 - sub), (keep, sub)):
        for i, t in enumerate((other, mine)):
            start = pl.multiple_of((t * 2 + s) * width, width)
            ref[i] = nn(tokens[...], weight[:, pl.ds(start, width)])


def by_slot(tables, slots, tok_size):
    me = lax.axis_index("tok")
    return jnp.concatenate([tables[lax.rem(me + s, tok_size)] for s in range(slots)], axis=0)


def stacked(tables):
    return jnp.concatenate([t[...] for t in tables], axis=0)


def back_kernel(slots, facts, grad, *rest):
    tables, out = rest[:slots], rest[slots]
    out[...] = pick_slot(slot_ends(facts, slots), nt(stacked(tables), grad[...]), ADAPTER_RANK)


def part_down_kernel(slots, pieces, width, facts, tokens, *rest):
    parts, spread_out, outs = rest[:pieces], rest[pieces], rest[pieces + 1 :]
    ends = slot_ends(facts, slots)
    back = (paired_sum(parts) * BACK_SCALE).astype(bf16)
    spread = spread_slots(ends, back)
    spread_out[...] = spread
    product = (nn(spread, tokens[:, :width]) * (adapter_scale * LOW_SCALE)).astype(bf16)
    for s in range(slots):
        outs[s][...] = product[s * ADAPTER_RANK : (s + 1) * ADAPTER_RANK]


def low_kernel(slots, tok_size, facts, tokens, tables, out):
    table = by_slot(tables, slots, tok_size)
    out[...] = pick_slot(slot_ends(facts, slots), nt(table, tokens[...]), ADAPTER_RANK)


def input_kernel(slots, tok_size, width, spread, weight, tables, *rest):
    grads, (out, whole, turned) = rest[:-3], rest[-3:]

    @pl.when(pl.program_id(0) == 0)
    def _():
        turned[...] = spread[...].astype(f32).T.astype(bf16)
        if len(grads) == 1:
            whole[...] = grads[0][...]
        else:
            tp, sub = lax.axis_index("tp"), lax.axis_index("sub")
            pieces = (grads[0][...], grads[1][...], grads[2][0], grads[2][1])
            for piece, t, s in zip(pieces, (tp, 1 - tp, tp, 1 - tp), (sub, sub, 1 - sub, 1 - sub)):
                start = pl.multiple_of((t * 2 + s) * width, width)
                whole[:, pl.ds(start, width)] = piece

    frozen = nt(whole[...], weight[...])
    table = by_slot(tables, slots, tok_size)
    adapter = nn(turned[...], table)
    out[...] = (frozen + (adapter_scale * LOW_SCALE) * adapter).astype(bf16)


def second_kernel(slots, pieces, first, facts, tokens, grad, spread_back, *rest):
    rank = ADAPTER_RANK
    parts, spread_low, outs = rest[:pieces], rest[pieces], rest[pieces + 1 :]
    split = tokens.shape[1] - first
    ends = slot_ends(facts, slots)
    low = (paired_sum(parts) * LOW_SCALE).astype(bf16)
    spread = spread_slots(ends, low)
    spread_low[...] = spread
    product = (nn(spread, grad[...]) * (adapter_scale * BACK_SCALE)).astype(bf16)
    for s in range(slots):
        outs[s][:, split:] = product[s * rank : (s + 1) * rank]
    product = (nn(spread_back[...], tokens[:, first:]) * (adapter_scale * LOW_SCALE)).astype(bf16)
    for s in range(slots):
        outs[s][:, :split] = product[s * rank : (s + 1) * rank]


def key_kernel(slots, spread, *rest):
    tables, frozen, key_out = rest[:slots], rest[slots:-1], rest[-1]
    table = stacked(tables)
    raised = nn(spread[...].astype(f32).T.astype(bf16), table)
    total = frozen[0][...]
    for part in frozen[1:]:
        total = total + part[...]
    key_out[...] = (total + (adapter_scale * BACK_SCALE) * raised).astype(bf16)


def adam_kernel(slots, owned, offset, extras, facts, *rest):
    came, rest = rest[:slots], rest[slots:]
    weights, mean_old, var_old, avg_old = rest[:4]
    fresh, average, gradients = rest[4 + extras :]
    step = gradients.shape[2]
    gradients[...] = jnp.zeros(gradients.shape, f32)
    for s in range(slots):
        if came[s].shape[1] == step:
            part = came[s][...]
        elif pl.num_programs(0) == 1 or came[s].shape[1] % 128:
            part = came[s][:, offset : offset + step]
        else:
            start = pl.multiple_of(offset + pl.program_id(0) * step, step)
            part = came[s][:, pl.ds(start, step)]
        gradients[facts[slots + s]] += part.astype(f32)
    for k in range(owned):
        gradient = gradients[k]
        mean_new = beta_one * mean_old[k] + (1.0 - beta_one) * gradient
        var_new = beta_two * var_old[k] + (1.0 - beta_two) * gradient * gradient
        updated = weights[k].astype(f32) - learn_rate * mean_new / (jnp.sqrt(var_new) + adam_eps)
        fresh[k] = updated.astype(bf16)
        average[k] = ema_decay * avg_old[k] + (1.0 - ema_decay) * updated


def adam(facts, came, offset, old, first, width, step, into):
    weights = old[0]
    owned, rank, _ = weights.shape
    slots = len(came)
    block = pl.BlockSpec((owned, rank, step), lambda i: (0, 0, first // step + i))
    came_specs = [pl.BlockSpec(c.shape, lambda i: (0, 0)) for c in came]
    aliases = {1 + slots + 4: 0, 1 + slots + 5: 1} if into else {}
    extra = tuple(into)
    return pl.pallas_call(
        functools.partial(adam_kernel, slots, owned, offset, len(extra)),
        grid=(width // step,),
        out_shape=(shape_of(weights.shape, bf16), shape_of(weights.shape, f32)),
        in_specs=[SMEM] + came_specs + [block] * 4 + [ANY] * len(extra),
        out_specs=(block, block),
        scratch_shapes=[pltpu.VMEM((owned, rank, step), f32)],
        input_output_aliases=aliases,
        compiler_params=params(16),
        cost_estimate=cost(owned * rank * width * 20, owned * rank * width * 20),
    )(facts, *came, *old, *extra)


def after(value, *others):
    return lax.optimization_barrier((value, *others))[0]


def swap(block, axes, flips):
    sizes = [lax.axis_size(a) for a in axes]
    route = []
    for t in range(sizes[0]):
        for s in range(sizes[1]):
            source = (t ^ flips[0]) * sizes[1] + (s ^ flips[1])
            route.append((source, t * sizes[1] + s))
    return lax.ppermute(block, axes, route)


def per_device(
    tokens,
    frozen_key_weight,
    output_gradient,
    counts,
    placement,
    adapter_sequence,
    adapter_down,
    adapter_up,
    down_first_moment,
    down_second_moment,
    down_average,
    up_first_moment,
    up_second_moment,
    up_average,
):
    tok_size = lax.axis_size("tok")
    tp_size, sub_size = lax.axis_size("tp"), lax.axis_size("sub")
    shards = ("tp", "sub")
    square = tp_size == 2 and sub_size == 2
    rows, wide = tokens.shape
    narrow = output_gradient.shape[1]
    key_width = frozen_key_weight.shape[1]
    owned = adapter_down.shape[0]
    slots = placement.shape[1]
    rank = ADAPTER_RANK
    flip = lambda a: jnp.swapaxes(a, 1, 2)
    down, down_m, down_v, down_a = map(
        flip, (adapter_down, down_first_moment, down_second_moment, down_average)
    )
    up, up_m, up_v, up_a = map(flip, (adapter_up, up_first_moment, up_second_moment, up_average))

    def fetch(block, slot):
        return lax.ppermute(block, "tok", [((i + slot) % tok_size, i) for i in range(tok_size)])

    def give_back(block, slot):
        return lax.ppermute(block, "tok", [((i - slot) % tok_size, i) for i in range(tok_size)])

    def shared(part):
        if not square:
            return [lax.psum(part, shards)]
        both = part + swap(part, shards, (0, 1))
        return [both, swap(both, shards, (1, 0))]

    step = min(256, wide)
    first = wide * 5 // 8 // step * step
    second = wide - first + narrow

    facts, *selected = pl.pallas_call(
        functools.partial(select_kernel, slots, owned, tok_size),
        out_shape=[shape_of((2 * slots,), jnp.int32)]
        + [shape_of((rank, narrow), bf16)] * slots
        + [shape_of((tok_size, rank, wide), bf16)],
        in_specs=[SMEM, SMEM, SMEM, ANY, ANY],
        out_specs=[SMEM] + [VMEM] * (slots + 1),
        scratch_shapes=[pltpu.SemaphoreType.DMA((2 * slots,))],
        compiler_params=params(56),
        cost_estimate=cost(0, 4 * slots * rank * (wide + narrow)),
    )(counts, placement, adapter_sequence, down, up)
    down_tables = lax.all_to_all(selected[slots], "tok", split_axis=0, concat_axis=0, tiled=True)

    def group(work):
        shapes = jax.eval_shape(work)
        nothing = lambda: jax.tree.map(lambda a: jnp.zeros(a.shape, a.dtype), shapes)
        return lax.cond(counts[0, 0] > 0, work, nothing)

    def back_work():
        tables = [selected[0]] + [fetch(selected[s], s) for s in range(1, slots)]
        part = pl.pallas_call(
            functools.partial(back_kernel, slots),
            out_shape=shape_of((rank, rows), f32),
            in_specs=[SMEM, VMEM] + [VMEM] * slots,
            out_specs=VMEM,
            compiler_params=params(16),
            cost_estimate=cost(2 * rows * narrow * rank * slots, 2 * rows * narrow),
        )(facts, output_gradient, *tables)
        parts = shared(part)
        spread, *sends = pl.pallas_call(
            functools.partial(part_down_kernel, slots, len(parts), first),
            out_shape=[shape_of((slots * rank, rows), bf16)] + [shape_of((rank, first), bf16)] * slots,
            in_specs=[SMEM, VMEM] + [VMEM] * len(parts),
            out_specs=[VMEM] * (1 + slots),
            compiler_params=params(16),
            cost_estimate=cost(2 * rows * first * rank * slots, 2 * rows * first),
        )(facts, tokens, *parts)
        return tables, spread, sends

    up_tables, spread_back, part_first = group(back_work)
    came_first = [part_first[0]] + [give_back(part_first[s], s) for s in range(1, slots)]

    def frozen_work():
        cotangent = after(output_gradient, spread_back)
        if not square:
            grads = [lax.all_gather(cotangent, shards, axis=1, tiled=True)]
            base = jnp.dot(tokens, frozen_key_weight, preferred_element_type=f32)
            return grads, [lax.psum_scatter(base, shards, scatter_dimension=1, tiled=True)], []
        across = swap(cotangent, shards, (1, 0))
        grads = [across, swap(jnp.stack([cotangent, across]), shards, (0, 1))]
        keep, send = pl.pallas_call(
            functools.partial(base_kernel, narrow),
            out_shape=[shape_of((2, rows, narrow), f32)] * 2,
            in_specs=[VMEM, VMEM],
            out_specs=[VMEM, VMEM],
            compiler_params=params(16),
            cost_estimate=cost(2 * rows * wide * key_width, 2 * wide * (rows + key_width)),
        )(tokens, frozen_key_weight)
        got = swap(send, shards, (0, 1))
        return grads, [keep[1] + got[1]], [keep[0] + got[0]]

    grads, frozen, passing = group(frozen_work)
    if square:
        grads = [output_gradient] + grads

    def low_work():
        tables = after(down_tables, frozen[0])
        part = pl.pallas_call(
            functools.partial(low_kernel, slots, tok_size),
            out_shape=shape_of((rank, rows), f32),
            in_specs=[SMEM, VMEM, VMEM],
            out_specs=VMEM,
            compiler_params=params(16),
            cost_estimate=cost(2 * rows * wide * rank * slots, 2 * rows * wide),
        )(facts, tokens, tables)
        parts = shared(part)
        spread, *sends = pl.pallas_call(
            functools.partial(second_kernel, slots, len(parts), first),
            out_shape=[shape_of((slots * rank, rows), bf16)] + [shape_of((rank, second), bf16)] * slots,
            in_specs=[SMEM] + [VMEM] * (3 + len(parts)),
            out_specs=[VMEM] * (1 + slots),
            compiler_params=params(16),
            cost_estimate=cost(2 * rows * narrow * rank * slots, 14 * rows * narrow),
        )(facts, tokens, output_gradient, spread_back, *parts)
        return spread, sends

    spread_low, part_second = group(low_work)
    if square:
        frozen = frozen + [swap(after(passing[0], spread_low), shards, (1, 0))]
    came_second = [part_second[0]] + [
        give_back(after(part_second[s], *came_first[1:]), s) for s in range(1, slots)
    ]

    key_output = pl.pallas_call(
        functools.partial(key_kernel, slots),
        out_shape=shape_of((rows, narrow), bf16),
        in_specs=[VMEM] * (1 + slots + len(frozen)),
        out_specs=VMEM,
        compiler_params=params(16),
        cost_estimate=cost(2 * rows * narrow * rank * slots, 14 * rows * narrow),
    )(spread_low, *up_tables, *frozen)

    input_gradient = pl.pallas_call(
        functools.partial(input_kernel, slots, tok_size, narrow),
        grid=(wide // step,),
        out_shape=shape_of((rows, wide), bf16),
        in_specs=[
            pl.BlockSpec((slots * rank, rows), lambda i: (0, 0)),
            pl.BlockSpec((step, key_width), lambda i: (i, 0)),
            pl.BlockSpec((tok_size, rank, step), lambda i: (0, 0, i)),
        ]
        + [pl.BlockSpec(g.shape, lambda i, r=g.ndim: (0,) * r) for g in grads],
        out_specs=pl.BlockSpec((rows, step), lambda i: (0, i)),
        scratch_shapes=[pltpu.VMEM((rows, key_width), bf16), pltpu.VMEM((rows, slots * rank), bf16)],
        compiler_params=params(16),
        cost_estimate=cost(2 * rows * wide * (key_width + rank * slots), 2 * wide * (rows + key_width)),
    )(after(spread_back, spread_low), frozen_key_weight, down_tables, *grads)

    down_old, up_old = (down, down_m, down_v, down_a), (up, up_m, up_v, up_a)
    done = adam(facts, came_first, 0, down_old, 0, first, step, ())
    late = [came_second[0]] + [after(c, key_output, input_gradient, done[0]) for c in came_second[1:]]
    fresh_up, average_up = adam(facts, late, wide - first, up_old, 0, narrow, narrow, ())
    fresh_down, average_down = adam(
        facts, late, 0, down_old, first, wide - first, step, done
    )
    return (
        key_output,
        input_gradient,
        flip(fresh_down),
        flip(fresh_up),
        flip(average_down),
        flip(average_up),
    )


def solution(mesh):
    rows = P(("groups", "tok"), ("tp", "sub"))
    cube = P(("groups", "tok"), ("tp", "sub"), None)
    return jax.shard_map(
        per_device,
        mesh=mesh,
        in_specs=(rows, P(("tp", "sub"), None), rows, P("groups", None), P("groups", None), P("groups"))
        + (cube,) * 8,
        out_specs=(rows, rows, cube, cube, cube, cube),
        check_vma=False,
    )
```

```python
import functools

import jax
import jax.numpy as jnp
from jax import lax
from jax.experimental import pallas as pl
from jax.experimental.pallas import tpu as pltpu
from jax.sharding import PartitionSpec as P

MODEL_WIDTH = 8192
ADAPTER_RANK = 64

adapter_scale = 0.5
learn_rate = 0.3
beta_one = 0.9
beta_two = 0.99
adam_eps = 1e-08
ema_decay = 0.9

LOW_SCALE = MODEL_WIDTH ** (-0.5)
BACK_SCALE = ADAPTER_RANK ** (-0.5)
MIB = 1024 * 1024

f32 = jnp.float32
bf16 = jnp.bfloat16

SMEM = pl.BlockSpec(memory_space=pltpu.SMEM)
VMEM = pl.BlockSpec(memory_space=pltpu.VMEM)
ANY = pl.BlockSpec(memory_space=pl.ANY)


def shape_of(shape, dtype):
    return jax.ShapeDtypeStruct(tuple(shape), dtype)


SCHEDULE_SCALE = 3


def cost(flops, bytes_accessed):
    return pl.CostEstimate(
        flops=int(flops * SCHEDULE_SCALE),
        bytes_accessed=int(bytes_accessed * SCHEDULE_SCALE),
        transcendentals=0,
    )


def params(mib):
    return pltpu.CompilerParams(vmem_limit_bytes=mib * MIB)


def nt(a, b):
    return lax.dot_general(a, b, (((1,), (1,)), ((), ())), preferred_element_type=f32)


def nn(a, b):
    return lax.dot_general(a, b, (((1,), (0,)), ((), ())), preferred_element_type=f32)


def tn(a, b):
    return lax.dot_general(a, b, (((0,), (0,)), ((), ())), preferred_element_type=f32)


def facts_kernel(slots, owned, tok_size, counts, placement, sequence, facts):
    me = lax.axis_index("tok")
    total = jnp.int32(0)
    for s in range(slots):
        total = total + counts[me, s]
        facts[s] = total
        tenant = placement[lax.rem(me - s + tok_size, tok_size), s]
        place = jnp.int32(0)
        for k in range(1, owned):
            place = place + jnp.where(sequence[me * owned + k] == tenant, k, 0)
        facts[slots + s] = place


def slot_ends(facts, slots):
    return [facts[s] for s in range(slots)]


def slot_mask(ends, slot, shape):
    rows = lax.broadcasted_iota(jnp.int32, shape, 1)
    inside = rows < ends[slot]
    if slot:
        inside = inside & (rows >= ends[slot - 1])
    return inside


def pick_slot(ends, products, rank):
    rows = lax.broadcasted_iota(jnp.int32, (rank, products.shape[1]), 1)
    slots = products.shape[0] // rank
    out = products[(slots - 1) * rank :]
    for s in range(slots - 2, -1, -1):
        out = jnp.where(rows < ends[s], products[s * rank : (s + 1) * rank], out)
    return out


def spread_slots(ends, values):
    wide = values.astype(f32)
    return jnp.concatenate(
        [jnp.where(slot_mask(ends, s, wide.shape), wide, 0.0) for s in range(len(ends))], axis=0
    ).astype(bf16)


def paired_sum(refs):
    parts = [ref[...] for ref in refs]
    while len(parts) > 1:
        parts = [parts[i] + parts[i + 1] for i in range(0, len(parts), 2)]
    return parts[0]


def select_kernel(slots, owned, tok_size, counts, placement, sequence, down, up, facts, *rest):
    ups, downs, sems = rest[0], rest[1 : slots + 1], rest[slots + 1]
    me = lax.axis_index("tok")
    facts_kernel(slots, owned, tok_size, counts, placement, sequence, facts)
    copies = []
    order = list(range(1, slots)) + [0]
    for s in order:
        target = ups.at[lax.rem(me - s + tok_size, tok_size)]
        copies.append(pltpu.make_async_copy(up.at[facts[slots + s]], target, sems.at[s]))
    for s in order:
        copies.append(pltpu.make_async_copy(down.at[facts[slots + s]], downs[s], sems.at[slots + s]))
    for copy in copies:
        copy.start()
    for copy in copies:
        copy.wait()


def base_kernel(width, tokens, weight, keep, send):
    tp, sub = lax.axis_index("tp"), lax.axis_index("sub")
    mine, other = tp, 1 - tp
    for ref, s in ((send, 1 - sub), (keep, sub)):
        for i, t in enumerate((other, mine)):
            start = pl.multiple_of((t * 2 + s) * width, width)
            ref[i] = nn(tokens[...], weight[:, pl.ds(start, width)])


def by_slot(tables, slots, tok_size):
    me = lax.axis_index("tok")
    return jnp.concatenate([tables[lax.rem(me + s, tok_size)] for s in range(slots)], axis=0)


def stacked(tables):
    return jnp.concatenate([t[...] for t in tables], axis=0)


def back_kernel(slots, tok_size, facts, grad, tables, out):
    table = by_slot(tables, slots, tok_size)
    out[...] = pick_slot(slot_ends(facts, slots), nt(table, grad[...]), ADAPTER_RANK)


def part_down_kernel(slots, pieces, width, facts, tokens, *rest):
    parts, spread_out, outs = rest[:pieces], rest[pieces], rest[pieces + 1 :]
    ends = slot_ends(facts, slots)
    back = (paired_sum(parts) * BACK_SCALE).astype(bf16)
    spread = spread_slots(ends, back)
    spread_out[...] = spread
    product = (nn(spread, tokens[:, :width]) * (adapter_scale * LOW_SCALE)).astype(bf16)
    for s in range(slots):
        outs[s][...] = product[s * ADAPTER_RANK : (s + 1) * ADAPTER_RANK]


def low_kernel(slots, facts, tokens, *rest):
    tables, out = rest[:slots], rest[slots]
    out[...] = pick_slot(slot_ends(facts, slots), nt(stacked(tables), tokens[...]), ADAPTER_RANK)


def input_kernel(slots, width, extras, spread, weight, *rest):
    rest = rest[:-3 - extras] + rest[-3:] if extras else rest
    tables, grads, (out, whole, turned) = rest[:slots], rest[slots:-3], rest[-3:]

    @pl.when(pl.program_id(0) == 0)
    def _():
        turned[...] = spread[...].astype(f32).T.astype(bf16)
        if len(grads) == 1:
            whole[...] = grads[0][...]
        else:
            tp, sub = lax.axis_index("tp"), lax.axis_index("sub")
            pieces = (grads[0][...], grads[1][...], grads[2][0], grads[2][1])
            for piece, t, s in zip(pieces, (tp, 1 - tp, tp, 1 - tp), (sub, sub, 1 - sub, 1 - sub)):
                start = pl.multiple_of((t * 2 + s) * width, width)
                whole[:, pl.ds(start, width)] = piece

    frozen = None
    for start in range(0, whole.shape[1], 256):
        term = nt(whole[:, start : start + 256], weight[:, start : start + 256])
        frozen = term if frozen is None else frozen + term
    adapter = nn(turned[...], stacked(tables))
    out[...] = (frozen + (adapter_scale * LOW_SCALE) * adapter).astype(bf16)


def second_kernel(slots, pieces, first, facts, tokens, grad, spread_back, *rest):
    rank = ADAPTER_RANK
    parts, spread_low, outs = rest[:pieces], rest[pieces], rest[pieces + 1 :]
    split = tokens.shape[1] - first
    ends = slot_ends(facts, slots)
    low = (paired_sum(parts) * LOW_SCALE).astype(bf16)
    spread = spread_slots(ends, low)
    spread_low[...] = spread
    product = (nn(spread, grad[...]) * (adapter_scale * BACK_SCALE)).astype(bf16)
    for s in range(slots):
        outs[s][:, split:] = product[s * rank : (s + 1) * rank]
    product = (nn(spread_back[...], tokens[:, first:]) * (adapter_scale * LOW_SCALE)).astype(bf16)
    for s in range(slots):
        outs[s][:, :split] = product[s * rank : (s + 1) * rank]


def key_kernel(slots, tok_size, spread, tables, *rest):
    frozen, key_out = rest[:-1], rest[-1]
    table = by_slot(tables, slots, tok_size)
    raised = nn(spread[...].astype(f32).T.astype(bf16), table)
    total = frozen[0][...]
    for part in frozen[1:]:
        total = total + part[...].astype(f32)
    key_out[...] = (total + (adapter_scale * BACK_SCALE) * raised).astype(bf16)


def adam_kernel(slots, owned, offset, extras, facts, *rest):
    came, rest = rest[:slots], rest[slots:]
    weights, mean_old, var_old, avg_old = rest[:4]
    fresh, average, gradients = rest[4 + extras :]
    step = gradients.shape[2]
    width = came[0].shape[1]
    if width == step:
        columns = slice(None)
    elif pl.num_programs(0) == 1 or width % 128:
        columns = slice(offset, offset + step)
    else:
        columns = pl.ds(pl.multiple_of(offset + pl.program_id(0) * step, step), step)
    gradients[...] = jnp.zeros(gradients.shape, f32)
    for s in range(slots):
        gradients[facts[slots + s]] += came[s][:, columns].astype(f32)
    for k in range(owned):
        gradient = gradients[k]
        mean_new = beta_one * mean_old[k] + (1.0 - beta_one) * gradient
        var_new = beta_two * var_old[k] + (1.0 - beta_two) * gradient * gradient
        root = var_new * lax.rsqrt(var_new) + adam_eps
        inverse = pl.reciprocal(root, approx=True)
        inverse = inverse * (2.0 - root * inverse)
        updated = weights[k].astype(f32) - learn_rate * mean_new * inverse
        fresh[k] = updated.astype(bf16)
        average[k] = ema_decay * avg_old[k] + (1.0 - ema_decay) * updated


def adam(facts, came, offset, old, first, width, step, into):
    weights = old[0]
    owned, rank, _ = weights.shape
    block = pl.BlockSpec((owned, rank, step), lambda i: (0, 0, first // step + i))
    came_specs = [pl.BlockSpec(c.shape, lambda i, r=c.ndim: (0,) * r) for c in came]
    count = len(came)
    aliases = {1 + count + 4: 0, 1 + count + 5: 1} if into else {}
    extra = tuple(into)
    return pl.pallas_call(
        functools.partial(adam_kernel, count, owned, offset, len(extra)),
        grid=(width // step,),
        out_shape=(shape_of(weights.shape, bf16), shape_of(weights.shape, f32)),
        in_specs=[SMEM] + came_specs + [block] * 4 + [ANY] * len(extra),
        out_specs=(block, block),
        scratch_shapes=[pltpu.VMEM((owned, rank, step), f32)],
        input_output_aliases=aliases,
        compiler_params=params(56),
        cost_estimate=cost(owned * rank * width * 20, owned * rank * width * 20),
    )(facts, *came, *old, *extra)


def after(value, *others):
    return lax.optimization_barrier((value, *others))[0]


def swap(block, axes, flips):
    sizes = [lax.axis_size(a) for a in axes]
    route = []
    for t in range(sizes[0]):
        for s in range(sizes[1]):
            source = (t ^ flips[0]) * sizes[1] + (s ^ flips[1])
            route.append((source, t * sizes[1] + s))
    return lax.ppermute(block, axes, route)


def per_device(
    tokens,
    frozen_key_weight,
    output_gradient,
    counts,
    placement,
    adapter_sequence,
    adapter_down,
    adapter_up,
    down_first_moment,
    down_second_moment,
    down_average,
    up_first_moment,
    up_second_moment,
    up_average,
):
    tok_size = lax.axis_size("tok")
    tp_size, sub_size = lax.axis_size("tp"), lax.axis_size("sub")
    shards = ("tp", "sub")
    square = tp_size == 2 and sub_size == 2
    rows, wide = tokens.shape
    narrow = output_gradient.shape[1]
    key_width = frozen_key_weight.shape[1]
    owned = adapter_down.shape[0]
    slots = placement.shape[1]
    rank = ADAPTER_RANK
    flip = lambda a: jnp.swapaxes(a, 1, 2)
    down, down_m, down_v, down_a = map(
        flip, (adapter_down, down_first_moment, down_second_moment, down_average)
    )
    up, up_m, up_v, up_a = map(flip, (adapter_up, up_first_moment, up_second_moment, up_average))

    def fetch(block, slot):
        return lax.ppermute(block, "tok", [((i + slot) % tok_size, i) for i in range(tok_size)])

    def give_back(block, slot):
        return lax.ppermute(block, "tok", [((i - slot) % tok_size, i) for i in range(tok_size)])

    def shared(part):
        if not square:
            return [lax.psum(part, shards)]
        both = part + swap(part, shards, (0, 1))
        return [both, swap(both, shards, (1, 0))]

    step = min(256, wide)
    first = wide * 5 // 8 // step * step
    second = wide - first + narrow

    facts, up_send, *down_send = pl.pallas_call(
        functools.partial(select_kernel, slots, owned, tok_size),
        out_shape=[shape_of((2 * slots,), jnp.int32), shape_of((tok_size, rank, narrow), bf16)]
        + [shape_of((rank, wide), bf16)] * slots,
        in_specs=[SMEM, SMEM, SMEM, ANY, ANY],
        out_specs=[SMEM] + [VMEM] * (slots + 1),
        scratch_shapes=[pltpu.SemaphoreType.DMA((2 * slots,))],
        compiler_params=params(56),
        cost_estimate=cost(0, 4 * slots * rank * (wide + narrow)),
    )(counts, placement, adapter_sequence, down, up)
    up_tables = lax.all_to_all(up_send, "tok", split_axis=0, concat_axis=0, tiled=True)
    down_tables = [down_send[0]] + [fetch(down_send[s], s) for s in range(1, slots)]
    def group(work):
        shapes = jax.eval_shape(work)
        nothing = lambda: jax.tree.map(lambda a: jnp.zeros(a.shape, a.dtype), shapes)
        return lax.cond(counts[0, 0] > 0, work, nothing)

    def back_work():
        part = pl.pallas_call(
            functools.partial(back_kernel, slots, tok_size),
            out_shape=shape_of((rank, rows), f32),
            in_specs=[SMEM, VMEM, VMEM],
            out_specs=VMEM,
            compiler_params=params(16),
            cost_estimate=cost(2 * rows * narrow * rank * slots, 2 * rows * narrow),
        )(facts, output_gradient, up_tables)
        parts = shared(part)
        base = []
        if square:
            across = swap(output_gradient, shards, (1, 0))
            pair = swap(jnp.stack([output_gradient, across]), shards, (0, 1))
            grads = [across, pair]
            base = pl.pallas_call(
                functools.partial(base_kernel, narrow),
                out_shape=[shape_of((2, rows, narrow), f32)] * 2,
                in_specs=[VMEM, VMEM],
                out_specs=[VMEM, VMEM],
                compiler_params=params(16),
                cost_estimate=cost(2 * rows * wide * key_width, 2 * wide * (rows + key_width)),
            )(tokens, after(frozen_key_weight, parts[0]))
            parts = [after(parts[0], base[0]), parts[1]]
        else:
            grads = [lax.all_gather(output_gradient, shards, axis=1, tiled=True)]
        spread, *sends = pl.pallas_call(
            functools.partial(part_down_kernel, slots, len(parts), first),
            out_shape=[shape_of((slots * rank, rows), bf16)] + [shape_of((rank, first), bf16)] * slots,
            in_specs=[SMEM, VMEM] + [VMEM] * len(parts),
            out_specs=[VMEM] * (1 + slots),
            compiler_params=params(16),
            cost_estimate=cost(2 * rows * first * rank * slots, 2 * rows * first),
        )(facts, tokens, *parts)
        return grads, base, spread, sends

    grads, base, spread_back, part_first = group(back_work)
    if square:
        grads = [output_gradient] + grads
    came_first = [part_first[0]] + [give_back(part_first[s], s) for s in range(1, slots)]

    half = wide // 2 // step * step

    def input_part(spread, begin, width, into):
        return pl.pallas_call(
            functools.partial(input_kernel, slots, narrow, len(into)),
            grid=(width // step,),
            out_shape=shape_of((rows, wide), bf16),
            in_specs=[
                pl.BlockSpec((slots * rank, rows), lambda i: (0, 0)),
                pl.BlockSpec((step, key_width), lambda i: (begin // step + i, 0)),
            ]
            + [pl.BlockSpec((rank, step), lambda i: (0, begin // step + i))] * slots
            + [pl.BlockSpec(g.shape, lambda i, r=g.ndim: (0,) * r) for g in grads]
            + [ANY] * len(into),
            out_specs=pl.BlockSpec((rows, step), lambda i: (0, begin // step + i)),
            scratch_shapes=[
                pltpu.VMEM((rows, key_width), bf16),
                pltpu.VMEM((rows, slots * rank), bf16),
            ],
            input_output_aliases={2 + slots + len(grads): 0} if into else {},
            compiler_params=params(16),
            cost_estimate=cost(
                2 * rows * width * (key_width + rank * slots), 2 * width * (rows + key_width)
            ),
        )(spread, frozen_key_weight, *down_tables, *grads, *into)

    def low_work():
        part = pl.pallas_call(
            functools.partial(low_kernel, slots),
            out_shape=shape_of((rank, rows), f32),
            in_specs=[SMEM, VMEM] + [VMEM] * slots,
            out_specs=VMEM,
            compiler_params=params(16),
            cost_estimate=cost(2 * rows * wide * rank * slots, 2 * rows * wide),
        )(facts, tokens, *down_tables)
        parts = shared(part)
        input_first = input_part(after(spread_back, parts[0]), 0, half, ())
        if square:
            keep, send = base
            got = swap(send, shards, (0, 1))
            frozen, passing = keep[1] + got[1], (keep[0] + got[0]).astype(bf16)
            parts = [after(parts[0], input_first, frozen, passing), parts[1]]
        else:
            whole = jnp.dot(tokens, frozen_key_weight, preferred_element_type=f32)
            frozen = lax.psum_scatter(whole, shards, scatter_dimension=1, tiled=True)
            passing = ()
        spread, *sends = pl.pallas_call(
            functools.partial(second_kernel, slots, len(parts), first),
            out_shape=[shape_of((slots * rank, rows), bf16)] + [shape_of((rank, second), bf16)] * slots,
            in_specs=[SMEM] + [VMEM] * (3 + len(parts)),
            out_specs=[VMEM] * (1 + slots),
            compiler_params=params(16),
            cost_estimate=cost(2 * rows * narrow * rank * slots, 14 * rows * narrow),
        )(facts, tokens, output_gradient, spread_back, *parts)
        return spread, sends, frozen, passing, input_first

    spread_low, part_second, frozen, passing, input_first = group(low_work)
    frozen = [frozen, swap(passing, shards, (1, 0))] if square else [frozen]
    came_second = [part_second[0]] + [
        give_back(after(part_second[s], *came_first[1:]), s) for s in range(1, slots)
    ]

    key_output = pl.pallas_call(
        functools.partial(key_kernel, slots, tok_size),
        out_shape=shape_of((rows, narrow), bf16),
        in_specs=[VMEM] * (2 + len(frozen)),
        out_specs=VMEM,
        compiler_params=params(16),
        cost_estimate=cost(2 * rows * narrow * rank * slots, 14 * rows * narrow),
    )(spread_low, up_tables, *frozen)
    input_gradient = input_part(spread_back, half, wide - half, (input_first,))

    down_old, up_old = (down, down_m, down_v, down_a), (up, up_m, up_v, up_a)
    done = adam(facts, came_first, 0, down_old, 0, first, step, ())
    late = [came_second[0]] + [after(c, key_output, input_gradient, done[0]) for c in came_second[1:]]
    fresh_up, average_up = adam(
        facts, late, wide - first, up_old, 0, narrow, narrow, ()
    )
    fresh_down, average_down = adam(
        facts, late, 0, down_old, first, wide - first, step, done
    )
    return (
        key_output,
        input_gradient,
        flip(fresh_down),
        flip(fresh_up),
        flip(average_down),
        flip(average_up),
    )


def solution(mesh):
    rows = P(("groups", "tok"), ("tp", "sub"))
    cube = P(("groups", "tok"), ("tp", "sub"), None)
    return jax.shard_map(
        per_device,
        mesh=mesh,
        in_specs=(rows, P(("tp", "sub"), None), rows, P("groups", None), P("groups", None), P("groups"))
        + (cube,) * 8,
        out_specs=(rows, rows, cube, cube, cube, cube),
        check_vma=False,
    )
```

```python
import functools

import jax
import jax.numpy as jnp
from jax import lax
from jax.experimental import pallas as pl
from jax.experimental.pallas import tpu as pltpu
from jax.sharding import PartitionSpec as P

MODEL_WIDTH = 8192
ADAPTER_RANK = 64

adapter_scale = 0.5
learn_rate = 0.3
beta_one = 0.9
beta_two = 0.99
adam_eps = 1e-08
ema_decay = 0.9

LOW_SCALE = MODEL_WIDTH ** (-0.5)
BACK_SCALE = ADAPTER_RANK ** (-0.5)
MIB = 1024 * 1024

f32 = jnp.float32
bf16 = jnp.bfloat16

SMEM = pl.BlockSpec(memory_space=pltpu.SMEM)
VMEM = pl.BlockSpec(memory_space=pltpu.VMEM)
ANY = pl.BlockSpec(memory_space=pl.ANY)


def shape_of(shape, dtype):
    return jax.ShapeDtypeStruct(tuple(shape), dtype)


SCHEDULE_SCALE = 3


def cost(flops, bytes_accessed):
    return pl.CostEstimate(
        flops=int(flops * SCHEDULE_SCALE),
        bytes_accessed=int(bytes_accessed * SCHEDULE_SCALE),
        transcendentals=0,
    )


def params(mib):
    return pltpu.CompilerParams(vmem_limit_bytes=mib * MIB)


def nt(a, b):
    return lax.dot_general(a, b, (((1,), (1,)), ((), ())), preferred_element_type=f32)


def nn(a, b):
    return lax.dot_general(a, b, (((1,), (0,)), ((), ())), preferred_element_type=f32)


def tn(a, b):
    return lax.dot_general(a, b, (((0,), (0,)), ((), ())), preferred_element_type=f32)


def facts_kernel(slots, owned, tok_size, counts, placement, sequence, facts):
    me = lax.axis_index("tok")
    total = jnp.int32(0)
    for s in range(slots):
        total = total + counts[me, s]
        facts[s] = total
        tenant = placement[lax.rem(me - s + tok_size, tok_size), s]
        place = jnp.int32(0)
        for k in range(1, owned):
            place = place + jnp.where(sequence[me * owned + k] == tenant, k, 0)
        facts[slots + s] = place


def slot_ends(facts, slots):
    return [facts[s] for s in range(slots)]


def slot_mask(ends, slot, shape):
    rows = lax.broadcasted_iota(jnp.int32, shape, 1)
    inside = rows < ends[slot]
    if slot:
        inside = inside & (rows >= ends[slot - 1])
    return inside


def pick_slot(ends, products, rank):
    rows = lax.broadcasted_iota(jnp.int32, (rank, products.shape[1]), 1)
    slots = products.shape[0] // rank
    out = products[(slots - 1) * rank :]
    for s in range(slots - 2, -1, -1):
        out = jnp.where(rows < ends[s], products[s * rank : (s + 1) * rank], out)
    return out


def spread_slots(ends, values):
    wide = values.astype(f32)
    return jnp.concatenate(
        [jnp.where(slot_mask(ends, s, wide.shape), wide, 0.0) for s in range(len(ends))], axis=0
    ).astype(bf16)


def paired_sum(refs):
    parts = [ref[...] for ref in refs]
    while len(parts) > 1:
        parts = [parts[i] + parts[i + 1] for i in range(0, len(parts), 2)]
    return parts[0]


def select_kernel(slots, owned, tok_size, counts, placement, sequence, down, up, facts, *rest):
    ups, downs, sems = rest[0], rest[1 : slots + 1], rest[slots + 1]
    me = lax.axis_index("tok")
    facts_kernel(slots, owned, tok_size, counts, placement, sequence, facts)
    copies = []
    order = list(range(1, slots)) + [0]
    for s in order:
        target = ups.at[lax.rem(me - s + tok_size, tok_size)]
        copies.append(pltpu.make_async_copy(up.at[facts[slots + s]], target, sems.at[s]))
    for s in order:
        copies.append(pltpu.make_async_copy(down.at[facts[slots + s]], downs[s], sems.at[slots + s]))
    for copy in copies:
        copy.start()
    for copy in copies:
        copy.wait()


def base_kernel(width, tokens, weight, keep, send):
    tp, sub = lax.axis_index("tp"), lax.axis_index("sub")
    mine, other = tp, 1 - tp
    for ref, s in ((send, 1 - sub), (keep, sub)):
        for i, t in enumerate((other, mine)):
            start = pl.multiple_of((t * 2 + s) * width, width)
            ref[i] = nn(tokens[...], weight[:, pl.ds(start, width)])


def by_slot(tables, slots, tok_size):
    me = lax.axis_index("tok")
    return jnp.concatenate([tables[lax.rem(me + s, tok_size)] for s in range(slots)], axis=0)


def stacked(tables):
    return jnp.concatenate([t[...] for t in tables], axis=0)


def back_kernel(slots, tok_size, facts, grad, tables, out):
    table = by_slot(tables, slots, tok_size)
    out[...] = pick_slot(slot_ends(facts, slots), nt(table, grad[...]), ADAPTER_RANK)


def part_down_kernel(slots, pieces, width, facts, tokens, *rest):
    parts, spread_out, outs = rest[:pieces], rest[pieces], rest[pieces + 1 :]
    ends = slot_ends(facts, slots)
    back = (paired_sum(parts) * BACK_SCALE).astype(bf16)
    spread = spread_slots(ends, back)
    spread_out[...] = spread
    product = (nn(spread, tokens[:, :width]) * (adapter_scale * LOW_SCALE)).astype(bf16)
    for s in range(slots):
        outs[s][...] = product[s * ADAPTER_RANK : (s + 1) * ADAPTER_RANK]


def low_kernel(slots, facts, tokens, *rest):
    tables, out = rest[:slots], rest[slots]
    out[...] = pick_slot(slot_ends(facts, slots), nt(stacked(tables), tokens[...]), ADAPTER_RANK)


def input_kernel(slots, width, extras, spread, weight, *rest):
    rest = rest[:-3 - extras] + rest[-3:] if extras else rest
    tables, grads, (out, whole, turned) = rest[:slots], rest[slots:-3], rest[-3:]

    @pl.when(pl.program_id(0) == 0)
    def _():
        turned[...] = spread[...].astype(f32).T.astype(bf16)
        if len(grads) == 1:
            whole[...] = grads[0][...]
        else:
            tp, sub = lax.axis_index("tp"), lax.axis_index("sub")
            pieces = (grads[0][...], grads[1][...], grads[2][0], grads[2][1])
            for piece, t, s in zip(pieces, (tp, 1 - tp, tp, 1 - tp), (sub, sub, 1 - sub, 1 - sub)):
                start = pl.multiple_of((t * 2 + s) * width, width)
                whole[:, pl.ds(start, width)] = piece

    frozen = None
    for start in range(0, whole.shape[1], 256):
        term = nt(whole[:, start : start + 256], weight[:, start : start + 256])
        frozen = term if frozen is None else frozen + term
    adapter = nn(turned[...], stacked(tables))
    out[...] = (frozen + (adapter_scale * LOW_SCALE) * adapter).astype(bf16)


def second_kernel(slots, pieces, first, facts, tokens, grad, spread_back, *rest):
    rank = ADAPTER_RANK
    parts, spread_low, outs = rest[:pieces], rest[pieces], rest[pieces + 1 :]
    split = tokens.shape[1] - first
    ends = slot_ends(facts, slots)
    low = (paired_sum(parts) * LOW_SCALE).astype(bf16)
    spread = spread_slots(ends, low)
    spread_low[...] = spread
    product = (nn(spread, grad[...]) * (adapter_scale * BACK_SCALE)).astype(bf16)
    for s in range(slots):
        outs[s][:, split:] = product[s * rank : (s + 1) * rank]
    product = (nn(spread_back[...], tokens[:, first:]) * (adapter_scale * LOW_SCALE)).astype(bf16)
    for s in range(slots):
        outs[s][:, :split] = product[s * rank : (s + 1) * rank]


def key_kernel(slots, tok_size, spread, tables, *rest):
    frozen, key_out = rest[:-1], rest[-1]
    table = by_slot(tables, slots, tok_size)
    raised = nn(spread[...].astype(f32).T.astype(bf16), table)
    total = frozen[0][...]
    for part in frozen[1:]:
        total = total + part[...].astype(f32)
    key_out[...] = (total + (adapter_scale * BACK_SCALE) * raised).astype(bf16)


def adam_kernel(slots, spans, extras, facts, *rest):
    came, rest = rest[:slots], rest[slots:]
    count = len(spans)
    old, rest = rest[: 4 * count], rest[4 * count + extras :]
    new, gradient_ref = rest[: 2 * count], rest[2 * count]
    k = pl.program_id(0)
    gradient_ref[...] = jnp.zeros(gradient_ref.shape, f32)
    for s in range(slots):

        @pl.when(facts[slots + s] == k)
        def _():
            start, width = spans[0][0], sum(w for _, w in spans)
            gradient_ref[...] += came[s][:, start : start + width].astype(f32)

    begin = 0
    for t, (_, width) in enumerate(spans):
        weights, mean_old, var_old, avg_old = old[4 * t : 4 * t + 4]
        gradient = gradient_ref[:, begin : begin + width]
        mean_new = beta_one * mean_old[0] + (1.0 - beta_one) * gradient
        var_new = beta_two * var_old[0] + (1.0 - beta_two) * gradient * gradient
        root = var_new * lax.rsqrt(var_new) + adam_eps
        inverse = pl.reciprocal(root, approx=True)
        inverse = inverse * (2.0 - root * inverse)
        updated = weights[0].astype(f32) - learn_rate * mean_new * inverse
        new[2 * t][0] = updated.astype(bf16)
        new[2 * t + 1][0] = ema_decay * avg_old[0] + (1.0 - ema_decay) * updated
        begin += width


def adam(facts, came, targets, into):
    owned, rank, _ = targets[0][0][0].shape
    blocks, arrays, shapes, spans = [], [], [], []
    for old, first, width, start in targets:
        block = pl.BlockSpec((1, rank, width), lambda k, c=first // width: (k, 0, c))
        blocks.append(block)
        arrays += list(old)
        shapes += [shape_of(old[0].shape, bf16), shape_of(old[0].shape, f32)]
        spans.append((start, width))
    total = sum(w for _, w in spans)
    count = len(came)
    aliases = {1 + count + len(arrays) + i: i for i in range(len(into))}
    return pl.pallas_call(
        functools.partial(adam_kernel, count, tuple(spans), len(into)),
        grid=(owned,),
        out_shape=shapes,
        in_specs=[SMEM]
        + [pl.BlockSpec(c.shape, lambda k: (0, 0)) for c in came]
        + [b for b in blocks for _ in range(4)]
        + [ANY] * len(into),
        out_specs=[b for b in blocks for _ in range(2)],
        scratch_shapes=[pltpu.VMEM((rank, total), f32)],
        input_output_aliases=aliases,
        compiler_params=params(56),
        cost_estimate=cost(owned * rank * total * 20, owned * rank * total * 20),
    )(facts, *came, *arrays, *into)


def after(value, *others):
    return lax.optimization_barrier((value, *others))[0]


def swap(block, axes, flips):
    sizes = [lax.axis_size(a) for a in axes]
    route = []
    for t in range(sizes[0]):
        for s in range(sizes[1]):
            source = (t ^ flips[0]) * sizes[1] + (s ^ flips[1])
            route.append((source, t * sizes[1] + s))
    return lax.ppermute(block, axes, route)


def per_device(
    tokens,
    frozen_key_weight,
    output_gradient,
    counts,
    placement,
    adapter_sequence,
    adapter_down,
    adapter_up,
    down_first_moment,
    down_second_moment,
    down_average,
    up_first_moment,
    up_second_moment,
    up_average,
):
    tok_size = lax.axis_size("tok")
    tp_size, sub_size = lax.axis_size("tp"), lax.axis_size("sub")
    shards = ("tp", "sub")
    square = tp_size == 2 and sub_size == 2
    rows, wide = tokens.shape
    narrow = output_gradient.shape[1]
    key_width = frozen_key_weight.shape[1]
    owned = adapter_down.shape[0]
    slots = placement.shape[1]
    rank = ADAPTER_RANK
    flip = lambda a: jnp.swapaxes(a, 1, 2)
    down, down_m, down_v, down_a = map(
        flip, (adapter_down, down_first_moment, down_second_moment, down_average)
    )
    up, up_m, up_v, up_a = map(flip, (adapter_up, up_first_moment, up_second_moment, up_average))

    def fetch(block, slot):
        return lax.ppermute(block, "tok", [((i + slot) % tok_size, i) for i in range(tok_size)])

    def give_back(block, slot):
        return lax.ppermute(block, "tok", [((i - slot) % tok_size, i) for i in range(tok_size)])

    def shared(part):
        if not square:
            return [lax.psum(part, shards)]
        both = part + swap(part, shards, (0, 1))
        return [both, swap(both, shards, (1, 0))]

    step = min(256, wide)
    first = wide - max(step, wide // 4)
    second = wide - first + narrow

    facts, up_send, *down_send = pl.pallas_call(
        functools.partial(select_kernel, slots, owned, tok_size),
        out_shape=[shape_of((2 * slots,), jnp.int32), shape_of((tok_size, rank, narrow), bf16)]
        + [shape_of((rank, wide), bf16)] * slots,
        in_specs=[SMEM, SMEM, SMEM, ANY, ANY],
        out_specs=[SMEM] + [VMEM] * (slots + 1),
        scratch_shapes=[pltpu.SemaphoreType.DMA((2 * slots,))],
        compiler_params=params(56),
        cost_estimate=cost(0, 4 * slots * rank * (wide + narrow)),
    )(counts, placement, adapter_sequence, down, up)
    up_tables = lax.all_to_all(up_send, "tok", split_axis=0, concat_axis=0, tiled=True)
    ready = counts[0, 0] > 0
    down_tables = [down_send[0]] + [
        fetch(after(down_send[s], up_tables, ready), s) for s in range(1, slots)
    ]
    def group(work):
        shapes = jax.eval_shape(work)
        nothing = lambda: jax.tree.map(lambda a: jnp.zeros(a.shape, a.dtype), shapes)
        return lax.cond(ready, work, nothing)

    def back_work():
        part = pl.pallas_call(
            functools.partial(back_kernel, slots, tok_size),
            out_shape=shape_of((rank, rows), f32),
            in_specs=[SMEM, VMEM, VMEM],
            out_specs=VMEM,
            compiler_params=params(16),
            cost_estimate=cost(2 * rows * narrow * rank * slots, 2 * rows * narrow),
        )(facts, output_gradient, up_tables)
        parts = shared(part)
        base = []
        if square:
            across = swap(output_gradient, shards, (1, 0))
            pair = swap(jnp.stack([output_gradient, across]), shards, (0, 1))
            grads = [across, pair]
            base = pl.pallas_call(
                functools.partial(base_kernel, narrow),
                out_shape=[shape_of((2, rows, narrow), f32)] * 2,
                in_specs=[VMEM, VMEM],
                out_specs=[VMEM, VMEM],
                compiler_params=params(16),
                cost_estimate=cost(2 * rows * wide * key_width, 2 * wide * (rows + key_width)),
            )(tokens, after(frozen_key_weight, parts[0]))
            parts = [after(parts[0], base[0]), parts[1]]
        else:
            grads = [lax.all_gather(output_gradient, shards, axis=1, tiled=True)]
        spread, *sends = pl.pallas_call(
            functools.partial(part_down_kernel, slots, len(parts), first),
            out_shape=[shape_of((slots * rank, rows), bf16)] + [shape_of((rank, first), bf16)] * slots,
            in_specs=[SMEM, VMEM] + [VMEM] * len(parts),
            out_specs=[VMEM] * (1 + slots),
            compiler_params=params(16),
            cost_estimate=cost(2 * rows * first * rank * slots, 2 * rows * first),
        )(facts, tokens, *parts)
        return grads, base, spread, sends

    grads, base, spread_back, part_first = group(back_work)
    if square:
        grads = [output_gradient] + grads
    came_first = [part_first[0]] + [give_back(part_first[s], s) for s in range(1, slots)]

    def input_part(spread, begin, width, into):
        return pl.pallas_call(
            functools.partial(input_kernel, slots, narrow, len(into)),
            grid=(width // step,),
            out_shape=shape_of((rows, wide), bf16),
            in_specs=[
                pl.BlockSpec((slots * rank, rows), lambda i: (0, 0)),
                pl.BlockSpec((step, key_width), lambda i: (begin // step + i, 0)),
            ]
            + [pl.BlockSpec((rank, step), lambda i: (0, begin // step + i))] * slots
            + [pl.BlockSpec(g.shape, lambda i, r=g.ndim: (0,) * r) for g in grads]
            + [ANY] * len(into),
            out_specs=pl.BlockSpec((rows, step), lambda i: (0, begin // step + i)),
            scratch_shapes=[
                pltpu.VMEM((rows, key_width), bf16),
                pltpu.VMEM((rows, slots * rank), bf16),
            ],
            input_output_aliases={2 + slots + len(grads): 0} if into else {},
            compiler_params=params(16),
            cost_estimate=cost(
                2 * rows * width * (key_width + rank * slots), 2 * width * (rows + key_width)
            ),
        )(spread, frozen_key_weight, *down_tables, *grads, *into)

    def low_work():
        part = pl.pallas_call(
            functools.partial(low_kernel, slots),
            out_shape=shape_of((rank, rows), f32),
            in_specs=[SMEM, VMEM] + [VMEM] * slots,
            out_specs=VMEM,
            compiler_params=params(16),
            cost_estimate=cost(2 * rows * wide * rank * slots, 2 * rows * wide),
        )(facts, tokens, *down_tables)
        parts = shared(part)
        input_gradient = input_part(after(spread_back, parts[0]), 0, wide, ())
        if square:
            keep, send = base
            got = swap(send, shards, (0, 1))
            frozen, passing = keep[1] + got[1], (keep[0] + got[0]).astype(bf16)
            parts = [after(parts[0], input_gradient, frozen, passing), parts[1]]
        else:
            whole = jnp.dot(tokens, frozen_key_weight, preferred_element_type=f32)
            frozen = lax.psum_scatter(whole, shards, scatter_dimension=1, tiled=True)
            passing = ()
        spread, *sends = pl.pallas_call(
            functools.partial(second_kernel, slots, len(parts), first),
            out_shape=[shape_of((slots * rank, rows), bf16)] + [shape_of((rank, second), bf16)] * slots,
            in_specs=[SMEM] + [VMEM] * (3 + len(parts)),
            out_specs=[VMEM] * (1 + slots),
            compiler_params=params(16),
            cost_estimate=cost(2 * rows * narrow * rank * slots, 14 * rows * narrow),
        )(facts, tokens, output_gradient, spread_back, *parts)
        return spread, sends, frozen, passing, input_gradient

    spread_low, part_second, frozen, passing, input_gradient = group(low_work)
    frozen = [frozen, swap(passing, shards, (1, 0))] if square else [frozen]
    came_second = [part_second[0]] + [
        give_back(after(part_second[s], *came_first[1:]), s) for s in range(1, slots)
    ]

    key_output = pl.pallas_call(
        functools.partial(key_kernel, slots, tok_size),
        out_shape=shape_of((rows, narrow), bf16),
        in_specs=[VMEM] * (2 + len(frozen)),
        out_specs=VMEM,
        compiler_params=params(16),
        cost_estimate=cost(2 * rows * narrow * rank * slots, 14 * rows * narrow),
    )(spread_low, up_tables, *frozen)

    down_old, up_old = (down, down_m, down_v, down_a), (up, up_m, up_v, up_a)
    done = adam(facts, came_first, [(down_old, 0, first, 0)], ())
    late = [came_second[0]] + [after(c, key_output, done[0]) for c in came_second[1:]]
    fresh_down, average_down, fresh_up, average_up = adam(
        facts,
        late,
        [(down_old, first, wide - first, 0), (up_old, 0, narrow, wide - first)],
        done,
    )
    return (
        key_output,
        input_gradient,
        flip(fresh_down),
        flip(fresh_up),
        flip(average_down),
        flip(average_up),
    )


def solution(mesh):
    rows = P(("groups", "tok"), ("tp", "sub"))
    cube = P(("groups", "tok"), ("tp", "sub"), None)
    return jax.shard_map(
        per_device,
        mesh=mesh,
        in_specs=(rows, P(("tp", "sub"), None), rows, P("groups", None), P("groups", None), P("groups"))
        + (cube,) * 8,
        out_specs=(rows, rows, cube, cube, cube, cube),
        check_vma=False,
    )
```

```python
import functools

import jax
import jax.numpy as jnp
from jax import lax
from jax.experimental import pallas as pl
from jax.experimental.pallas import tpu as pltpu
from jax.sharding import PartitionSpec as P

MODEL_WIDTH = 8192
ADAPTER_RANK = 64

adapter_scale = 0.5
learn_rate = 0.3
beta_one = 0.9
beta_two = 0.99
adam_eps = 1e-08
ema_decay = 0.9

LOW_SCALE = MODEL_WIDTH ** (-0.5)
BACK_SCALE = ADAPTER_RANK ** (-0.5)
MIB = 1024 * 1024

f32 = jnp.float32
bf16 = jnp.bfloat16

SMEM = pl.BlockSpec(memory_space=pltpu.SMEM)
VMEM = pl.BlockSpec(memory_space=pltpu.VMEM)
ANY = pl.BlockSpec(memory_space=pl.ANY)


def shape_of(shape, dtype):
    return jax.ShapeDtypeStruct(tuple(shape), dtype)


SCHEDULE_SCALE = 3


def cost(flops, bytes_accessed):
    return pl.CostEstimate(
        flops=int(flops * SCHEDULE_SCALE),
        bytes_accessed=int(bytes_accessed * SCHEDULE_SCALE),
        transcendentals=0,
    )


def params(mib):
    return pltpu.CompilerParams(vmem_limit_bytes=mib * MIB)


def nt(a, b):
    return lax.dot_general(a, b, (((1,), (1,)), ((), ())), preferred_element_type=f32)


def nn(a, b):
    return lax.dot_general(a, b, (((1,), (0,)), ((), ())), preferred_element_type=f32)


def tn(a, b):
    return lax.dot_general(a, b, (((0,), (0,)), ((), ())), preferred_element_type=f32)


def facts_kernel(slots, owned, tok_size, counts, placement, sequence, facts):
    me = lax.axis_index("tok")
    total = jnp.int32(0)
    for s in range(slots):
        total = total + counts[me, s]
        facts[s] = total
        tenant = placement[lax.rem(me - s + tok_size, tok_size), s]
        place = jnp.int32(0)
        for k in range(1, owned):
            place = place + jnp.where(sequence[me * owned + k] == tenant, k, 0)
        facts[slots + s] = place


def slot_ends(facts, slots):
    return [facts[s] for s in range(slots)]


def slot_mask(ends, slot, shape):
    rows = lax.broadcasted_iota(jnp.int32, shape, 1)
    inside = rows < ends[slot]
    if slot:
        inside = inside & (rows >= ends[slot - 1])
    return inside


def pick_slot(ends, products, rank):
    rows = lax.broadcasted_iota(jnp.int32, (rank, products.shape[1]), 1)
    slots = products.shape[0] // rank
    out = products[(slots - 1) * rank :]
    for s in range(slots - 2, -1, -1):
        out = jnp.where(rows < ends[s], products[s * rank : (s + 1) * rank], out)
    return out


def spread_slots(ends, values):
    wide = values.astype(f32)
    return jnp.concatenate(
        [jnp.where(slot_mask(ends, s, wide.shape), wide, 0.0) for s in range(len(ends))], axis=0
    ).astype(bf16)


def paired_sum(refs):
    parts = [ref[...] for ref in refs]
    while len(parts) > 1:
        parts = [parts[i] + parts[i + 1] for i in range(0, len(parts), 2)]
    return parts[0]


def select_kernel(slots, owned, tok_size, counts, placement, sequence, down, up, facts, *rest):
    ups, downs, sems = rest[0], rest[1 : slots + 1], rest[slots + 1]
    me = lax.axis_index("tok")
    facts_kernel(slots, owned, tok_size, counts, placement, sequence, facts)
    copies = []
    order = list(range(1, slots)) + [0]
    for s in order:
        target = ups.at[lax.rem(me - s + tok_size, tok_size)]
        copies.append(pltpu.make_async_copy(up.at[facts[slots + s]], target, sems.at[s]))
    for s in order:
        copies.append(pltpu.make_async_copy(down.at[facts[slots + s]], downs[s], sems.at[slots + s]))
    for copy in copies:
        copy.start()
    for copy in copies:
        copy.wait()


def base_kernel(width, tokens, weight, keep, send):
    tp, sub = lax.axis_index("tp"), lax.axis_index("sub")
    mine, other = tp, 1 - tp
    for ref, s in ((send, 1 - sub), (keep, sub)):
        for i, t in enumerate((other, mine)):
            start = pl.multiple_of((t * 2 + s) * width, width)
            ref[i] = nn(tokens[...], weight[:, pl.ds(start, width)])


def by_slot(tables, slots, tok_size):
    me = lax.axis_index("tok")
    return jnp.concatenate([tables[lax.rem(me + s, tok_size)] for s in range(slots)], axis=0)


def stacked(tables):
    return jnp.concatenate([t[...] for t in tables], axis=0)


def back_kernel(slots, tok_size, facts, grad, tables, out):
    table = by_slot(tables, slots, tok_size)
    out[...] = pick_slot(slot_ends(facts, slots), nt(table, grad[...]), ADAPTER_RANK)


def part_down_kernel(slots, pieces, width, facts, tokens, *rest):
    parts, spread_out, outs = rest[:pieces], rest[pieces], rest[pieces + 1 :]
    ends = slot_ends(facts, slots)
    back = (paired_sum(parts) * BACK_SCALE).astype(bf16)
    spread = spread_slots(ends, back)
    spread_out[...] = spread
    for c in range(0, width, 256):
        columns = slice(c, min(c + 256, width))
        product = (nn(spread, tokens[:, columns]) * (adapter_scale * LOW_SCALE)).astype(bf16)
        for s in range(slots):
            outs[s][:, columns] = product[s * ADAPTER_RANK : (s + 1) * ADAPTER_RANK]


def low_kernel(slots, facts, tokens, *rest):
    tables, out = rest[:slots], rest[slots]
    out[...] = pick_slot(slot_ends(facts, slots), nt(stacked(tables), tokens[...]), ADAPTER_RANK)


def input_kernel(slots, width, extras, spread, weight, *rest):
    rest = rest[:-3 - extras] + rest[-3:] if extras else rest
    tables, grads, (out, whole, turned) = rest[:slots], rest[slots:-3], rest[-3:]

    @pl.when(pl.program_id(0) == 0)
    def _():
        turned[...] = spread[...].astype(f32).T.astype(bf16)
        if len(grads) == 1:
            whole[...] = grads[0][...]
        else:
            tp, sub = lax.axis_index("tp"), lax.axis_index("sub")
            pieces = (grads[0][...], grads[1][...], grads[2][0], grads[2][1])
            for piece, t, s in zip(pieces, (tp, 1 - tp, tp, 1 - tp), (sub, sub, 1 - sub, 1 - sub)):
                start = pl.multiple_of((t * 2 + s) * width, width)
                whole[:, pl.ds(start, width)] = piece

    frozen = None
    for start in range(0, whole.shape[1], 256):
        term = nt(whole[:, start : start + 256], weight[:, start : start + 256])
        frozen = term if frozen is None else frozen + term
    adapter = nn(turned[...], stacked(tables))
    out[...] = (frozen + (adapter_scale * LOW_SCALE) * adapter).astype(bf16)


def second_kernel(slots, pieces, first, facts, tokens, grad, spread_back, *rest):
    rank = ADAPTER_RANK
    parts, spread_low, outs = rest[:pieces], rest[pieces], rest[pieces + 1 :]
    split = tokens.shape[1] - first
    ends = slot_ends(facts, slots)
    low = (paired_sum(parts) * LOW_SCALE).astype(bf16)
    spread = spread_slots(ends, low)
    spread_low[...] = spread
    product = (nn(spread, grad[...]) * (adapter_scale * BACK_SCALE)).astype(bf16)
    for s in range(slots):
        outs[s][:, split:] = product[s * rank : (s + 1) * rank]
    for c in range(0, split, 256):
        end = min(c + 256, split)
        product = nn(spread_back[...], tokens[:, first + c : first + end])
        product = (product * (adapter_scale * LOW_SCALE)).astype(bf16)
        for s in range(slots):
            outs[s][:, c:end] = product[s * rank : (s + 1) * rank]


def key_kernel(slots, tok_size, spread, tables, *rest):
    frozen, key_out = rest[:-1], rest[-1]
    table = by_slot(tables, slots, tok_size)
    raised = nn(spread[...].astype(f32).T.astype(bf16), table)
    total = frozen[0][...]
    for part in frozen[1:]:
        total = total + part[...].astype(f32)
    key_out[...] = (total + (adapter_scale * BACK_SCALE) * raised).astype(bf16)


def adam_kernel(slots, spans, extras, facts, *rest):
    came, rest = rest[:slots], rest[slots:]
    count = len(spans)
    old, rest = rest[: 4 * count], rest[4 * count + extras :]
    new, gradient_ref = rest[: 2 * count], rest[2 * count]
    k = pl.program_id(0)
    total = sum(width for _, width in spans)
    rows = 16

    def over_rows(body):
        def step(i, _):
            body(pl.ds(pl.multiple_of(i * rows, rows), rows))
            return 0

        lax.fori_loop(0, gradient_ref.shape[0] // rows, step, 0)

    @over_rows
    def _(r):
        gradient_ref[r, :] = jnp.zeros((rows, total), f32)

    for s in range(slots):

        @pl.when(facts[slots + s] == k)
        def _():
            @over_rows
            def _(r):
                start = spans[0][0]
                gradient_ref[r, :] += came[s][r, start : start + total].astype(f32)

    def update(refs, news, r, begin, columns):
        weights, mean_old, var_old, avg_old = refs
        gradient = gradient_ref[r, begin + columns.start : begin + columns.stop]
        mean_new = beta_one * mean_old[0, r, columns] + (1.0 - beta_one) * gradient
        var_new = beta_two * var_old[0, r, columns] + (1.0 - beta_two) * gradient * gradient
        root = var_new * lax.rsqrt(var_new) + adam_eps
        inverse = pl.reciprocal(root, approx=True)
        inverse = inverse * (2.0 - root * inverse)
        updated = weights[0, r, columns].astype(f32) - learn_rate * mean_new * inverse
        news[0][0, r, columns] = updated.astype(bf16)
        news[1][0, r, columns] = ema_decay * avg_old[0, r, columns] + (1.0 - ema_decay) * updated

    @over_rows
    def _(r):
        begin = 0
        for t, (_, width) in enumerate(spans):
            for c in range(0, width, 256):
                columns = slice(c, min(c + 256, width))
                update(old[4 * t : 4 * t + 4], new[2 * t : 2 * t + 2], r, begin, columns)
            begin += width


def adam(facts, came, targets, into):
    owned, rank, _ = targets[0][0][0].shape
    blocks, arrays, shapes, spans = [], [], [], []
    for old, first, width, start in targets:
        block = pl.BlockSpec((1, rank, width), lambda k, c=first // width: (k, 0, c))
        blocks.append(block)
        arrays += list(old)
        shapes += [shape_of(old[0].shape, bf16), shape_of(old[0].shape, f32)]
        spans.append((start, width))
    total = sum(w for _, w in spans)
    count = len(came)
    aliases = {1 + count + len(arrays) + i: i for i in range(len(into))}
    return pl.pallas_call(
        functools.partial(adam_kernel, count, tuple(spans), len(into)),
        grid=(owned,),
        out_shape=shapes,
        in_specs=[SMEM]
        + [pl.BlockSpec(c.shape, lambda k: (0, 0)) for c in came]
        + [b for b in blocks for _ in range(4)]
        + [ANY] * len(into),
        out_specs=[b for b in blocks for _ in range(2)],
        scratch_shapes=[pltpu.VMEM((rank, total), f32)],
        input_output_aliases=aliases,
        compiler_params=params(60),
        cost_estimate=cost(owned * rank * total * 20, owned * rank * total * 20),
    )(facts, *came, *arrays, *into)


def after(value, *others):
    return lax.optimization_barrier((value, *others))[0]


def swap(block, axes, flips):
    sizes = [lax.axis_size(a) for a in axes]
    route = []
    for t in range(sizes[0]):
        for s in range(sizes[1]):
            source = (t ^ flips[0]) * sizes[1] + (s ^ flips[1])
            route.append((source, t * sizes[1] + s))
    return lax.ppermute(block, axes, route)


def per_device(
    tokens,
    frozen_key_weight,
    output_gradient,
    counts,
    placement,
    adapter_sequence,
    adapter_down,
    adapter_up,
    down_first_moment,
    down_second_moment,
    down_average,
    up_first_moment,
    up_second_moment,
    up_average,
):
    tok_size = lax.axis_size("tok")
    tp_size, sub_size = lax.axis_size("tp"), lax.axis_size("sub")
    shards = ("tp", "sub")
    square = tp_size == 2 and sub_size == 2
    rows, wide = tokens.shape
    narrow = output_gradient.shape[1]
    key_width = frozen_key_weight.shape[1]
    owned = adapter_down.shape[0]
    slots = placement.shape[1]
    rank = ADAPTER_RANK
    flip = lambda a: jnp.swapaxes(a, 1, 2)
    down, down_m, down_v, down_a = map(
        flip, (adapter_down, down_first_moment, down_second_moment, down_average)
    )
    up, up_m, up_v, up_a = map(flip, (adapter_up, up_first_moment, up_second_moment, up_average))

    def fetch(block, slot):
        return lax.ppermute(block, "tok", [((i + slot) % tok_size, i) for i in range(tok_size)])

    def give_back(block, slot):
        return lax.ppermute(block, "tok", [((i - slot) % tok_size, i) for i in range(tok_size)])

    def shared(part):
        if not square:
            return [lax.psum(part, shards)]
        both = part + swap(part, shards, (0, 1))
        return [both, swap(both, shards, (1, 0))]

    step = min(256, wide)
    first = wide - max(step, wide // 4)
    second = wide - first + narrow

    facts, up_send, *down_send = pl.pallas_call(
        functools.partial(select_kernel, slots, owned, tok_size),
        out_shape=[shape_of((2 * slots,), jnp.int32), shape_of((tok_size, rank, narrow), bf16)]
        + [shape_of((rank, wide), bf16)] * slots,
        in_specs=[SMEM, SMEM, SMEM, ANY, ANY],
        out_specs=[SMEM] + [VMEM] * (slots + 1),
        scratch_shapes=[pltpu.SemaphoreType.DMA((2 * slots,))],
        compiler_params=params(56),
        cost_estimate=cost(0, 4 * slots * rank * (wide + narrow)),
    )(counts, placement, adapter_sequence, down, up)
    up_tables = lax.all_to_all(up_send, "tok", split_axis=0, concat_axis=0, tiled=True)
    ready = counts[0, 0] > 0
    early = fetch(down_send[1], 1)
    up_tables = after(up_tables, early)
    down_tables = [down_send[0], early] + [
        fetch(after(down_send[s], up_tables, ready), s) for s in range(2, slots)
    ]
    def group(work):
        shapes = jax.eval_shape(work)
        nothing = lambda: jax.tree.map(lambda a: jnp.zeros(a.shape, a.dtype), shapes)
        return lax.cond(ready, work, nothing)

    def back_work():
        part = pl.pallas_call(
            functools.partial(back_kernel, slots, tok_size),
            out_shape=shape_of((rank, rows), f32),
            in_specs=[SMEM, VMEM, VMEM],
            out_specs=VMEM,
            compiler_params=params(16),
            cost_estimate=cost(2 * rows * narrow * rank * slots, 2 * rows * narrow),
        )(facts, output_gradient, up_tables)
        parts = shared(part)
        base = []
        if square:
            across = swap(output_gradient, shards, (1, 0))
            pair = swap(jnp.stack([output_gradient, across]), shards, (0, 1))
            grads = [across, pair]
            base = pl.pallas_call(
                functools.partial(base_kernel, narrow),
                out_shape=[shape_of((2, rows, narrow), f32)] * 2,
                in_specs=[VMEM, VMEM],
                out_specs=[VMEM, VMEM],
                compiler_params=params(16),
                cost_estimate=cost(2 * rows * wide * key_width, 2 * wide * (rows + key_width)),
            )(tokens, after(frozen_key_weight, parts[0]))
            parts = [after(parts[0], base[0]), parts[1]]
        else:
            grads = [lax.all_gather(output_gradient, shards, axis=1, tiled=True)]
        spread, *sends = pl.pallas_call(
            functools.partial(part_down_kernel, slots, len(parts), first),
            out_shape=[shape_of((slots * rank, rows), bf16)] + [shape_of((rank, first), bf16)] * slots,
            in_specs=[SMEM, VMEM] + [VMEM] * len(parts),
            out_specs=[VMEM] * (1 + slots),
            compiler_params=params(16),
            cost_estimate=cost(2 * rows * first * rank * slots, 2 * rows * first),
        )(facts, tokens, *parts)
        return grads, base, spread, sends

    grads, base, spread_back, part_first = group(back_work)
    if square:
        grads = [output_gradient] + grads
    came_first = [part_first[0]] + [
        give_back(after(part_first[s], *down_tables[1:]), s) for s in range(1, slots)
    ]

    def input_part(spread, begin, width, into):
        return pl.pallas_call(
            functools.partial(input_kernel, slots, narrow, len(into)),
            grid=(width // step,),
            out_shape=shape_of((rows, wide), bf16),
            in_specs=[
                pl.BlockSpec((slots * rank, rows), lambda i: (0, 0)),
                pl.BlockSpec((step, key_width), lambda i: (begin // step + i, 0)),
            ]
            + [pl.BlockSpec((rank, step), lambda i: (0, begin // step + i))] * slots
            + [pl.BlockSpec(g.shape, lambda i, r=g.ndim: (0,) * r) for g in grads]
            + [ANY] * len(into),
            out_specs=pl.BlockSpec((rows, step), lambda i: (0, begin // step + i)),
            scratch_shapes=[
                pltpu.VMEM((rows, key_width), bf16),
                pltpu.VMEM((rows, slots * rank), bf16),
            ],
            input_output_aliases={2 + slots + len(grads): 0} if into else {},
            compiler_params=params(60),
            cost_estimate=cost(
                2 * rows * width * (key_width + rank * slots), 2 * width * (rows + key_width)
            ),
        )(spread, frozen_key_weight, *down_tables, *grads, *into)

    def low_work():
        part = pl.pallas_call(
            functools.partial(low_kernel, slots),
            out_shape=shape_of((rank, rows), f32),
            in_specs=[SMEM, VMEM] + [VMEM] * slots,
            out_specs=VMEM,
            compiler_params=params(16),
            cost_estimate=cost(2 * rows * wide * rank * slots, 2 * rows * wide),
        )(facts, tokens, *down_tables)
        parts = shared(part)
        input_gradient = input_part(after(spread_back, parts[0]), 0, wide, ())
        if square:
            keep, send = base
            got = swap(send, shards, (0, 1))
            frozen, passing = keep[1] + got[1], (keep[0] + got[0]).astype(bf16)
            parts = [after(parts[0], input_gradient, frozen, passing), parts[1]]
        else:
            whole = jnp.dot(tokens, frozen_key_weight, preferred_element_type=f32)
            frozen = lax.psum_scatter(whole, shards, scatter_dimension=1, tiled=True)
            passing = ()
        spread, *sends = pl.pallas_call(
            functools.partial(second_kernel, slots, len(parts), first),
            out_shape=[shape_of((slots * rank, rows), bf16)] + [shape_of((rank, second), bf16)] * slots,
            in_specs=[SMEM] + [VMEM] * (3 + len(parts)),
            out_specs=[VMEM] * (1 + slots),
            compiler_params=params(16),
            cost_estimate=cost(2 * rows * narrow * rank * slots, 14 * rows * narrow),
        )(facts, tokens, output_gradient, spread_back, *parts)
        return spread, sends, frozen, passing, input_gradient

    spread_low, part_second, frozen, passing, input_gradient = group(low_work)
    frozen = [frozen, swap(passing, shards, (1, 0))] if square else [frozen]
    came_second = [part_second[0]] + [
        give_back(after(part_second[s], *came_first[1:]), s) for s in range(1, slots)
    ]

    key_output = pl.pallas_call(
        functools.partial(key_kernel, slots, tok_size),
        out_shape=shape_of((rows, narrow), bf16),
        in_specs=[VMEM] * (2 + len(frozen)),
        out_specs=VMEM,
        compiler_params=params(16),
        cost_estimate=cost(2 * rows * narrow * rank * slots, 14 * rows * narrow),
    )(spread_low, up_tables, *frozen)

    down_old, up_old = (down, down_m, down_v, down_a), (up, up_m, up_v, up_a)
    done = adam(facts, came_first, [(down_old, 0, first, 0)], ())
    late = [came_second[0]] + [after(c, key_output, done[0]) for c in came_second[1:]]
    fresh_down, average_down, fresh_up, average_up = adam(
        facts,
        late,
        [(down_old, first, wide - first, 0), (up_old, 0, narrow, wide - first)],
        done,
    )
    return (
        key_output,
        input_gradient,
        flip(fresh_down),
        flip(fresh_up),
        flip(average_down),
        flip(average_up),
    )


def solution(mesh):
    rows = P(("groups", "tok"), ("tp", "sub"))
    cube = P(("groups", "tok"), ("tp", "sub"), None)
    return jax.shard_map(
        per_device,
        mesh=mesh,
        in_specs=(rows, P(("tp", "sub"), None), rows, P("groups", None), P("groups", None), P("groups"))
        + (cube,) * 8,
        out_specs=(rows, rows, cube, cube, cube, cube),
        check_vma=False,
    )
```

```python
import functools

import jax
import jax.numpy as jnp
from jax import lax
from jax.experimental import pallas as pl
from jax.experimental.pallas import tpu as pltpu
from jax.sharding import PartitionSpec as P

MODEL_WIDTH = 8192
ADAPTER_RANK = 64

adapter_scale = 0.5
learn_rate = 0.3
beta_one = 0.9
beta_two = 0.99
adam_eps = 1e-08
ema_decay = 0.9

LOW_SCALE = MODEL_WIDTH ** (-0.5)
BACK_SCALE = ADAPTER_RANK ** (-0.5)
MIB = 1024 * 1024

f32 = jnp.float32
bf16 = jnp.bfloat16

SMEM = pl.BlockSpec(memory_space=pltpu.SMEM)
VMEM = pl.BlockSpec(memory_space=pltpu.VMEM)
ANY = pl.BlockSpec(memory_space=pl.ANY)


def shape_of(shape, dtype):
    return jax.ShapeDtypeStruct(tuple(shape), dtype)


SCHEDULE_SCALE = 3


def cost(flops, bytes_accessed):
    return pl.CostEstimate(
        flops=int(flops * SCHEDULE_SCALE),
        bytes_accessed=int(bytes_accessed * SCHEDULE_SCALE),
        transcendentals=0,
    )


def params(mib):
    return pltpu.CompilerParams(vmem_limit_bytes=mib * MIB)


def nt(a, b):
    return lax.dot_general(a, b, (((1,), (1,)), ((), ())), preferred_element_type=f32)


def nn(a, b):
    return lax.dot_general(a, b, (((1,), (0,)), ((), ())), preferred_element_type=f32)


def tn(a, b):
    return lax.dot_general(a, b, (((0,), (0,)), ((), ())), preferred_element_type=f32)


def facts_kernel(slots, owned, tok_size, counts, placement, sequence, facts):
    me = lax.axis_index("tok")
    total = jnp.int32(0)
    for s in range(slots):
        total = total + counts[me, s]
        facts[s] = total
        tenant = placement[lax.rem(me - s + tok_size, tok_size), s]
        place = jnp.int32(0)
        for k in range(1, owned):
            place = place + jnp.where(sequence[me * owned + k] == tenant, k, 0)
        facts[slots + s] = place


def slot_ends(facts, slots):
    return [facts[s] for s in range(slots)]


def slot_mask(ends, slot, shape):
    rows = lax.broadcasted_iota(jnp.int32, shape, 1)
    inside = rows < ends[slot]
    if slot:
        inside = inside & (rows >= ends[slot - 1])
    return inside


def pick_slot(ends, products, rank):
    rows = lax.broadcasted_iota(jnp.int32, (rank, products.shape[1]), 1)
    slots = products.shape[0] // rank
    out = products[(slots - 1) * rank :]
    for s in range(slots - 2, -1, -1):
        out = jnp.where(rows < ends[s], products[s * rank : (s + 1) * rank], out)
    return out


def spread_slots(ends, values):
    wide = values.astype(f32)
    return jnp.concatenate(
        [jnp.where(slot_mask(ends, s, wide.shape), wide, 0.0) for s in range(len(ends))], axis=0
    ).astype(bf16)


def paired_sum(refs):
    parts = [ref[...] for ref in refs]
    while len(parts) > 1:
        parts = [parts[i] + parts[i + 1] for i in range(0, len(parts), 2)]
    return parts[0]


def select_kernel(slots, owned, tok_size, counts, placement, sequence, down, up, facts, *rest):
    ups, downs, sems = rest[:slots], rest[slots : 2 * slots], rest[2 * slots]
    facts_kernel(slots, owned, tok_size, counts, placement, sequence, facts)
    copies = []
    order = list(range(1, slots)) + [0]
    for s in order:
        copies.append(pltpu.make_async_copy(up.at[facts[slots + s]], ups[s], sems.at[s]))
    for s in order:
        copies.append(pltpu.make_async_copy(down.at[facts[slots + s]], downs[s], sems.at[slots + s]))
    for copy in copies:
        copy.start()
    for copy in copies:
        copy.wait()


def base_kernel(width, tokens, weight, keep, send):
    tp, sub = lax.axis_index("tp"), lax.axis_index("sub")
    mine, other = tp, 1 - tp
    for ref, s in ((send, 1 - sub), (keep, sub)):
        for i, t in enumerate((other, mine)):
            start = pl.multiple_of((t * 2 + s) * width, width)
            ref[i] = nn(tokens[...], weight[:, pl.ds(start, width)])


def stacked(tables):
    return jnp.concatenate([t[...] for t in tables], axis=0)


def back_kernel(slots, facts, grad, *rest):
    tables, out = rest[:slots], rest[slots]
    out[...] = pick_slot(slot_ends(facts, slots), nt(stacked(tables), grad[...]), ADAPTER_RANK)


def part_down_kernel(slots, pieces, width, facts, tokens, *rest):
    parts, spread_out, outs = rest[:pieces], rest[pieces], rest[pieces + 1 :]
    ends = slot_ends(facts, slots)
    back = (paired_sum(parts) * BACK_SCALE).astype(bf16)
    spread = spread_slots(ends, back)
    spread_out[...] = spread
    for c in range(0, width, 256):
        columns = slice(c, min(c + 256, width))
        product = (nn(spread, tokens[:, columns]) * (adapter_scale * LOW_SCALE)).astype(bf16)
        for s in range(slots):
            outs[s][:, columns] = product[s * ADAPTER_RANK : (s + 1) * ADAPTER_RANK]


def low_kernel(slots, facts, tokens, *rest):
    tables, out = rest[:slots], rest[slots]
    out[...] = pick_slot(slot_ends(facts, slots), nt(stacked(tables), tokens[...]), ADAPTER_RANK)


def input_kernel(slots, pieces, width, spread, weight, *rest):
    tables, rest = rest[:slots], rest[slots:]
    grads, rest = rest[:pieces], rest[pieces:]
    out, whole, turned, spread_here, table_here, weight_here, out_here, in_sems, out_sems = rest
    rows, wide = out_here.shape
    step = min(256, wide)
    steps = wide // step

    if pieces == 1:
        copies = [pltpu.make_async_copy(grads[0], whole, in_sems.at[0])]
    else:
        tp, sub = lax.axis_index("tp"), lax.axis_index("sub")
        copies = []
        places = zip((tp, 1 - tp, tp, 1 - tp), (sub, sub, 1 - sub, 1 - sub))
        for i, (piece, (t, s)) in enumerate(
            zip((grads[0], grads[1], grads[2].at[0], grads[2].at[1]), places)
        ):
            start = pl.multiple_of((t * 2 + s) * width, width)
            copies.append(
                pltpu.make_async_copy(piece, whole.at[:, pl.ds(start, width)], in_sems.at[i])
            )
    copies.append(pltpu.make_async_copy(spread, spread_here, in_sems.at[4]))
    for s in range(slots):
        place = table_here.at[pl.ds(s * ADAPTER_RANK, ADAPTER_RANK)]
        copies.append(pltpu.make_async_copy(tables[s], place, in_sems.at[5 + s]))
    loads, stores = [], []
    for i in range(steps):
        block = pl.ds(i * step, step)
        sem = in_sems.at[5 + slots + i]
        loads.append(pltpu.make_async_copy(weight.at[block], weight_here.at[block], sem))
        stores.append(
            pltpu.make_async_copy(out_here.at[:, block], out.at[:, block], out_sems.at[i])
        )
    for copy in copies + loads:
        copy.start()
    for copy in copies:
        copy.wait()
    turned[...] = spread_here[...].astype(f32).T.astype(bf16)
    for i in range(steps):
        columns = slice(i * step, (i + 1) * step)
        loads[i].wait()
        frozen = None
        for start in range(0, whole.shape[1], 256):
            term = nt(whole[:, start : start + 256], weight_here[columns, start : start + 256])
            frozen = term if frozen is None else frozen + term
        adapter = nn(turned[...], table_here[:, columns])
        out_here[:, columns] = (frozen + (adapter_scale * LOW_SCALE) * adapter).astype(bf16)
        stores[i].start()
    for copy in stores:
        copy.wait()


def second_kernel(slots, pieces, first, facts, tokens, grad, spread_back, *rest):
    rank = ADAPTER_RANK
    parts, spread_low, outs = rest[:pieces], rest[pieces], rest[pieces + 1 :]
    split = tokens.shape[1] - first
    ends = slot_ends(facts, slots)
    low = (paired_sum(parts) * LOW_SCALE).astype(bf16)
    spread = spread_slots(ends, low)
    spread_low[...] = spread
    product = (nn(spread, grad[...]) * (adapter_scale * BACK_SCALE)).astype(bf16)
    for s in range(slots):
        outs[s][:, split:] = product[s * rank : (s + 1) * rank]
    for c in range(0, split, 256):
        end = min(c + 256, split)
        product = nn(spread_back[...], tokens[:, first + c : first + end])
        product = (product * (adapter_scale * LOW_SCALE)).astype(bf16)
        for s in range(slots):
            outs[s][:, c:end] = product[s * rank : (s + 1) * rank]


def key_kernel(slots, spread, *rest):
    tables, frozen, key_out = rest[:slots], rest[slots:-1], rest[-1]
    table = stacked(tables)
    raised = nn(spread[...].astype(f32).T.astype(bf16), table)
    total = frozen[0][...]
    for part in frozen[1:]:
        total = total + part[...].astype(f32)
    key_out[...] = (total + (adapter_scale * BACK_SCALE) * raised).astype(bf16)


def adam_kernel(slots, spans, extras, facts, *rest):
    count = len(spans)
    came, rest = rest[:slots], rest[slots:]
    old, rest = rest[: 4 * count], rest[4 * count + extras :]
    new, rest = rest[: 2 * count], rest[2 * count :]
    came_here, rest = rest[0], rest[1:]
    old_here, rest = rest[: 4 * count], rest[4 * count :]
    new_here, (gradient_ref, in_sems, out_sems) = rest[: 2 * count], rest[2 * count :]
    owned, rank = old_here[0].shape[:2]
    total = gradient_ref.shape[1]
    start = spans[0][1]
    rows = 16

    arrivals = [
        pltpu.make_async_copy(came[s].at[:, pl.ds(start, total)], came_here.at[s], in_sems.at[s])
        for s in range(slots)
    ]
    loads, stores = [], []
    for k in range(owned):
        for i in range(4 * count):
            first, _, width = spans[i // 4]
            block = old[i].at[k, :, pl.ds(first, width)]
            sem = in_sems.at[slots + k * 4 * count + i]
            loads.append(pltpu.make_async_copy(block, old_here[i].at[k], sem))
        for i in range(2 * count):
            first, _, width = spans[i // 2]
            block = new[i].at[k, :, pl.ds(first, width)]
            sem = out_sems.at[k * 2 * count + i]
            stores.append(pltpu.make_async_copy(new_here[i].at[k], block, sem))
    for copy in arrivals + loads:
        copy.start()

    def over_rows(body):
        def step(i, _):
            body(pl.ds(pl.multiple_of(i * rows, rows), rows))
            return 0

        lax.fori_loop(0, rank // rows, step, 0)

    def update(k, refs, news, r, begin, columns):
        weights, mean_old, var_old, avg_old = refs
        gradient = gradient_ref[r, begin + columns.start : begin + columns.stop]
        mean_new = beta_one * mean_old[k, r, columns] + (1.0 - beta_one) * gradient
        var_new = beta_two * var_old[k, r, columns] + (1.0 - beta_two) * gradient * gradient
        root = var_new * lax.rsqrt(var_new) + adam_eps
        inverse = pl.reciprocal(root, approx=True)
        inverse = inverse * (2.0 - root * inverse)
        updated = weights[k, r, columns].astype(f32) - learn_rate * mean_new * inverse
        news[0][k, r, columns] = updated.astype(bf16)
        news[1][k, r, columns] = ema_decay * avg_old[k, r, columns] + (1.0 - ema_decay) * updated

    for copy in arrivals:
        copy.wait()
    for k in range(owned):

        @over_rows
        def _(r):
            gradient_ref[r, :] = jnp.zeros((rows, total), f32)

        for s in range(slots):

            @pl.when(facts[slots + s] == k)
            def _():
                @over_rows
                def _(r):
                    gradient_ref[r, :] += came_here[s, r, :].astype(f32)

        for copy in loads[k * 4 * count : (k + 1) * 4 * count]:
            copy.wait()

        @over_rows
        def _(r):
            begin = 0
            for t, (_, _, width) in enumerate(spans):
                for c in range(0, width, 512):
                    columns = slice(c, min(c + 512, width))
                    refs, news = old_here[4 * t : 4 * t + 4], new_here[2 * t : 2 * t + 2]
                    update(k, refs, news, r, begin, columns)
                begin += width

        for copy in stores[k * 2 * count : (k + 1) * 2 * count]:
            copy.start()
    for copy in stores:
        copy.wait()


def adam(facts, came, targets, into):
    owned, rank, _ = targets[0][0][0].shape
    arrays, shapes, spans, old_here, new_here = [], [], [], [], []
    for old, first, width, start in targets:
        arrays += list(old)
        shapes += [shape_of(old[0].shape, bf16), shape_of(old[0].shape, f32)]
        spans.append((first, start, width))
        old_here += [pltpu.VMEM((owned, rank, width), a.dtype) for a in old]
        new_here += [pltpu.VMEM((owned, rank, width), t) for t in (bf16, f32)]
    total = sum(span[2] for span in spans)
    count = len(came)
    aliases = {1 + count + len(arrays) + i: i for i in range(len(into))}
    return pl.pallas_call(
        functools.partial(adam_kernel, count, tuple(spans), len(into)),
        out_shape=shapes,
        in_specs=[SMEM] + [ANY] * (count + len(arrays) + len(into)),
        out_specs=[ANY] * len(shapes),
        scratch_shapes=[pltpu.VMEM((count, rank, total), bf16)]
        + old_here
        + new_here
        + [
            pltpu.VMEM((rank, total), f32),
            pltpu.SemaphoreType.DMA((count + owned * len(arrays),)),
            pltpu.SemaphoreType.DMA((owned * len(shapes),)),
        ],
        input_output_aliases=aliases,
        compiler_params=params(60),
        cost_estimate=cost(owned * rank * total * 20, owned * rank * total * 20),
    )(facts, *came, *arrays, *into)


def after(value, *others):
    return lax.optimization_barrier((value, *others))[0]


def swap(block, axes, flips):
    sizes = [lax.axis_size(a) for a in axes]
    route = []
    for t in range(sizes[0]):
        for s in range(sizes[1]):
            source = (t ^ flips[0]) * sizes[1] + (s ^ flips[1])
            route.append((source, t * sizes[1] + s))
    return lax.ppermute(block, axes, route)


def per_device(
    tokens,
    frozen_key_weight,
    output_gradient,
    counts,
    placement,
    adapter_sequence,
    adapter_down,
    adapter_up,
    down_first_moment,
    down_second_moment,
    down_average,
    up_first_moment,
    up_second_moment,
    up_average,
):
    tok_size = lax.axis_size("tok")
    tp_size, sub_size = lax.axis_size("tp"), lax.axis_size("sub")
    shards = ("tp", "sub")
    square = tp_size == 2 and sub_size == 2
    rows, wide = tokens.shape
    narrow = output_gradient.shape[1]
    key_width = frozen_key_weight.shape[1]
    owned = adapter_down.shape[0]
    slots = placement.shape[1]
    rank = ADAPTER_RANK
    flip = lambda a: jnp.swapaxes(a, 1, 2)
    down, down_m, down_v, down_a = map(
        flip, (adapter_down, down_first_moment, down_second_moment, down_average)
    )
    up, up_m, up_v, up_a = map(flip, (adapter_up, up_first_moment, up_second_moment, up_average))

    def fetch(block, slot):
        return lax.ppermute(block, "tok", [((i + slot) % tok_size, i) for i in range(tok_size)])

    def give_back(block, slot):
        return lax.ppermute(block, "tok", [((i - slot) % tok_size, i) for i in range(tok_size)])

    def shared(part):
        if not square:
            return [lax.psum(part, shards)]
        both = part + swap(part, shards, (0, 1))
        return [both, swap(both, shards, (1, 0))]

    step = min(256, wide)
    first = wide - step
    second = wide - first + narrow

    facts, *sent = pl.pallas_call(
        functools.partial(select_kernel, slots, owned, tok_size),
        out_shape=[shape_of((2 * slots,), jnp.int32)]
        + [shape_of((rank, narrow), bf16)] * slots
        + [shape_of((rank, wide), bf16)] * slots,
        in_specs=[SMEM, SMEM, SMEM, ANY, ANY],
        out_specs=[SMEM] + [VMEM] * (2 * slots),
        scratch_shapes=[pltpu.SemaphoreType.DMA((2 * slots,))],
        compiler_params=params(56),
        cost_estimate=cost(0, 4 * slots * rank * (wide + narrow)),
    )(counts, placement, adapter_sequence, down, up)
    up_send, down_send = sent[:slots], sent[slots:]
    ready = counts[0, 0] > 0
    early = fetch(down_send[1], 1)
    up_tables = [up_send[0]] + [fetch(up_send[s], s) for s in range(1, slots)]
    up_tables[0] = after(up_tables[0], early)
    down_tables = [down_send[0], early] + [
        fetch(after(down_send[s], ready, *up_tables), s) for s in range(2, slots)
    ]

    def group(work):
        shapes = jax.eval_shape(work)
        nothing = lambda: jax.tree.map(lambda a: jnp.zeros(a.shape, a.dtype), shapes)
        return lax.cond(ready, work, nothing)

    def back_work():
        part = pl.pallas_call(
            functools.partial(back_kernel, slots),
            out_shape=shape_of((rank, rows), f32),
            in_specs=[SMEM, VMEM] + [VMEM] * slots,
            out_specs=VMEM,
            compiler_params=params(16),
            cost_estimate=cost(2 * rows * narrow * rank * slots, 2 * rows * narrow),
        )(facts, output_gradient, *up_tables)
        parts = shared(part)
        if square:
            across = swap(output_gradient, shards, (1, 0))
            base = pl.pallas_call(
                functools.partial(base_kernel, narrow),
                out_shape=[shape_of((2, rows, narrow), f32)] * 2,
                in_specs=[VMEM, VMEM],
                out_specs=[VMEM, VMEM],
                compiler_params=params(16),
                cost_estimate=cost(2 * rows * wide * key_width, 2 * wide * (rows + key_width)),
            )(tokens, after(frozen_key_weight, parts[0]))
            pair = jnp.stack([output_gradient, after(across, base[0])])
            grads = [across, swap(pair, shards, (0, 1))]
            parts = [after(parts[0], base[0]), parts[1]]
        else:
            base = []
            grads = [lax.all_gather(output_gradient, shards, axis=1, tiled=True)]
        spread, *sends = pl.pallas_call(
            functools.partial(part_down_kernel, slots, len(parts), first),
            out_shape=[shape_of((slots * rank, rows), bf16)] + [shape_of((rank, first), bf16)] * slots,
            in_specs=[SMEM, VMEM] + [VMEM] * len(parts),
            out_specs=[VMEM] * (1 + slots),
            compiler_params=params(16),
            cost_estimate=cost(2 * rows * first * rank * slots, 2 * rows * first),
        )(facts, tokens, *parts)
        return grads, base, spread, sends

    grads, base, spread_back, part_first = group(back_work)
    if square:
        grads = [output_gradient] + grads
    came_first = [part_first[0]] + [
        give_back(after(part_first[s], *down_tables[1:]), s) for s in range(1, slots)
    ]

    def input_whole(spread):
        steps = wide // step
        return pl.pallas_call(
            functools.partial(input_kernel, slots, len(grads), narrow),
            out_shape=shape_of((rows, wide), bf16),
            in_specs=[ANY] * (2 + slots + len(grads)),
            out_specs=ANY,
            scratch_shapes=[
                pltpu.VMEM((rows, key_width), bf16),
                pltpu.VMEM((rows, slots * rank), bf16),
                pltpu.VMEM((slots * rank, rows), bf16),
                pltpu.VMEM((slots * rank, wide), bf16),
                pltpu.VMEM((wide, key_width), bf16),
                pltpu.VMEM((rows, wide), bf16),
                pltpu.SemaphoreType.DMA((5 + slots + steps,)),
                pltpu.SemaphoreType.DMA((steps,)),
            ],
            compiler_params=params(60),
            cost_estimate=cost(
                2 * rows * wide * (key_width + rank * slots), 2 * wide * (rows + key_width)
            ),
        )(spread, frozen_key_weight, *down_tables, *grads)

    def low_work():
        part = pl.pallas_call(
            functools.partial(low_kernel, slots),
            out_shape=shape_of((rank, rows), f32),
            in_specs=[SMEM, VMEM] + [VMEM] * slots,
            out_specs=VMEM,
            compiler_params=params(60),
            cost_estimate=cost(2 * rows * wide * rank * slots, 2 * rows * wide),
        )(facts, tokens, *down_tables)
        parts = shared(part)
        input_gradient = input_whole(after(spread_back, parts[0]))
        if square:
            keep, send = base
            got = swap(send, shards, (0, 1))
            frozen, passing = keep[1] + got[1], (keep[0] + got[0]).astype(bf16)
            parts = [after(parts[0], input_gradient, frozen, passing), parts[1]]
        else:
            whole = jnp.dot(tokens, frozen_key_weight, preferred_element_type=f32)
            frozen = lax.psum_scatter(whole, shards, scatter_dimension=1, tiled=True)
            passing = ()
        spread, *sends = pl.pallas_call(
            functools.partial(second_kernel, slots, len(parts), first),
            out_shape=[shape_of((slots * rank, rows), bf16)] + [shape_of((rank, second), bf16)] * slots,
            in_specs=[SMEM] + [VMEM] * (3 + len(parts)),
            out_specs=[VMEM] * (1 + slots),
            compiler_params=params(16),
            cost_estimate=cost(2 * rows * narrow * rank * slots, 14 * rows * narrow),
        )(facts, tokens, output_gradient, spread_back, *parts)
        return spread, sends, frozen, passing, input_gradient

    spread_low, part_second, frozen, passing, input_gradient = group(low_work)
    frozen = [frozen, swap(passing, shards, (1, 0))] if square else [frozen]
    came_second = [part_second[0]] + [
        give_back(after(part_second[s], *came_first[1:]), s) for s in range(1, slots)
    ]

    key_output = pl.pallas_call(
        functools.partial(key_kernel, slots),
        out_shape=shape_of((rows, narrow), bf16),
        in_specs=[VMEM] * (1 + slots + len(frozen)),
        out_specs=VMEM,
        compiler_params=params(16),
        cost_estimate=cost(2 * rows * narrow * rank * slots, 14 * rows * narrow),
    )(spread_low, *up_tables, *frozen)

    down_old, up_old = (down, down_m, down_v, down_a), (up, up_m, up_v, up_a)
    done = adam(facts, came_first, [(down_old, 0, first, 0)], ())
    late = [came_second[0]] + [after(c, key_output, done[0]) for c in came_second[1:]]
    fresh_down, average_down, fresh_up, average_up = adam(
        facts,
        late,
        [(down_old, first, wide - first, 0), (up_old, 0, narrow, wide - first)],
        done,
    )
    return (
        key_output,
        input_gradient,
        flip(fresh_down),
        flip(fresh_up),
        flip(average_down),
        flip(average_up),
    )


def solution(mesh):
    rows = P(("groups", "tok"), ("tp", "sub"))
    cube = P(("groups", "tok"), ("tp", "sub"), None)
    return jax.shard_map(
        per_device,
        mesh=mesh,
        in_specs=(rows, P(("tp", "sub"), None), rows, P("groups", None), P("groups", None), P("groups"))
        + (cube,) * 8,
        out_specs=(rows, rows, cube, cube, cube, cube),
        check_vma=False,
    )
```

```python
import functools

import jax
import jax.numpy as jnp
from jax import lax
from jax.experimental import pallas as pl
from jax.experimental.pallas import tpu as pltpu
from jax.sharding import PartitionSpec as P

MODEL_WIDTH = 8192
ADAPTER_RANK = 64

adapter_scale = 0.5
learn_rate = 0.3
beta_one = 0.9
beta_two = 0.99
adam_eps = 1e-08
ema_decay = 0.9

LOW_SCALE = MODEL_WIDTH ** (-0.5)
BACK_SCALE = ADAPTER_RANK ** (-0.5)
MIB = 1024 * 1024

f32 = jnp.float32
bf16 = jnp.bfloat16

SMEM = pl.BlockSpec(memory_space=pltpu.SMEM)
VMEM = pl.BlockSpec(memory_space=pltpu.VMEM)
ANY = pl.BlockSpec(memory_space=pl.ANY)


def shape_of(shape, dtype):
    return jax.ShapeDtypeStruct(tuple(shape), dtype)


SCHEDULE_SCALE = 3


def cost(flops, bytes_accessed):
    return pl.CostEstimate(
        flops=int(flops * SCHEDULE_SCALE),
        bytes_accessed=int(bytes_accessed * SCHEDULE_SCALE),
        transcendentals=0,
    )


def params(mib):
    return pltpu.CompilerParams(vmem_limit_bytes=mib * MIB)


def nt(a, b):
    return lax.dot_general(a, b, (((1,), (1,)), ((), ())), preferred_element_type=f32)


def nn(a, b):
    return lax.dot_general(a, b, (((1,), (0,)), ((), ())), preferred_element_type=f32)


def tn(a, b):
    return lax.dot_general(a, b, (((0,), (0,)), ((), ())), preferred_element_type=f32)


def facts_kernel(slots, owned, tok_size, counts, placement, sequence, facts):
    me = lax.axis_index("tok")
    total = jnp.int32(0)
    for s in range(slots):
        total = total + counts[me, s]
        facts[s] = total
        tenant = placement[lax.rem(me - s + tok_size, tok_size), s]
        place = jnp.int32(0)
        for k in range(1, owned):
            place = place + jnp.where(sequence[me * owned + k] == tenant, k, 0)
        facts[slots + s] = place


def slot_ends(facts, slots):
    return [facts[s] for s in range(slots)]


def slot_mask(ends, slot, shape):
    rows = lax.broadcasted_iota(jnp.int32, shape, 1)
    inside = rows < ends[slot]
    if slot:
        inside = inside & (rows >= ends[slot - 1])
    return inside


def pick_slot(ends, products, rank):
    rows = lax.broadcasted_iota(jnp.int32, (rank, products.shape[1]), 1)
    slots = products.shape[0] // rank
    out = products[(slots - 1) * rank :]
    for s in range(slots - 2, -1, -1):
        out = jnp.where(rows < ends[s], products[s * rank : (s + 1) * rank], out)
    return out


def spread_slots(ends, values):
    wide = values.astype(f32)
    return jnp.concatenate(
        [jnp.where(slot_mask(ends, s, wide.shape), wide, 0.0) for s in range(len(ends))], axis=0
    ).astype(bf16)


def paired_sum(refs):
    parts = [ref[...] for ref in refs]
    while len(parts) > 1:
        parts = [parts[i] + parts[i + 1] for i in range(0, len(parts), 2)]
    return parts[0]


def select_kernel(slots, owned, tok_size, counts, placement, sequence, down, up, facts, *rest):
    ups, downs, sems = rest[:slots], rest[slots : 2 * slots], rest[2 * slots]
    facts_kernel(slots, owned, tok_size, counts, placement, sequence, facts)
    copies = []
    order = list(range(1, slots)) + [0]
    for s in order:
        copies.append(pltpu.make_async_copy(up.at[facts[slots + s]], ups[s], sems.at[s]))
    for s in order:
        copies.append(pltpu.make_async_copy(down.at[facts[slots + s]], downs[s], sems.at[slots + s]))
    for copy in copies:
        copy.start()
    for copy in copies:
        copy.wait()


def base_kernel(width, tokens, weight, keep, send):
    tp, sub = lax.axis_index("tp"), lax.axis_index("sub")
    mine, other = tp, 1 - tp
    for ref, s in ((send, 1 - sub), (keep, sub)):
        for i, t in enumerate((other, mine)):
            start = pl.multiple_of((t * 2 + s) * width, width)
            ref[i] = nn(tokens[...], weight[:, pl.ds(start, width)])


def stacked(tables):
    return jnp.concatenate([t[...] for t in tables], axis=0)


def back_kernel(slots, facts, grad, *rest):
    tables, out = rest[:slots], rest[slots]
    out[...] = pick_slot(slot_ends(facts, slots), nt(stacked(tables), grad[...]), ADAPTER_RANK)


def part_down_kernel(slots, pieces, width, facts, tokens, *rest):
    parts, spread_out, outs = rest[:pieces], rest[pieces], rest[pieces + 1 :]
    ends = slot_ends(facts, slots)
    back = (paired_sum(parts) * BACK_SCALE).astype(bf16)
    spread = spread_slots(ends, back)
    spread_out[...] = spread
    for c in range(0, width, 256):
        columns = slice(c, min(c + 256, width))
        product = (nn(spread, tokens[:, columns]) * (adapter_scale * LOW_SCALE)).astype(bf16)
        for s in range(slots):
            outs[s][:, columns] = product[s * ADAPTER_RANK : (s + 1) * ADAPTER_RANK]


def low_kernel(slots, facts, tokens, *rest):
    tables, out = rest[:slots], rest[slots]
    out[...] = pick_slot(slot_ends(facts, slots), nt(stacked(tables), tokens[...]), ADAPTER_RANK)


def input_kernel(slots, width, spread, weight, *rest):
    tables, grads, (out, whole, turned) = rest[:slots], rest[slots:-3], rest[-3:]

    @pl.when(pl.program_id(0) == 0)
    def _():
        turned[...] = spread[...].astype(f32).T.astype(bf16)
        if len(grads) == 1:
            whole[...] = grads[0][...]
        else:
            tp, sub = lax.axis_index("tp"), lax.axis_index("sub")
            pieces = (grads[0][...], grads[1][...], grads[2][0], grads[2][1])
            for piece, t, s in zip(pieces, (tp, 1 - tp, tp, 1 - tp), (sub, sub, 1 - sub, 1 - sub)):
                start = pl.multiple_of((t * 2 + s) * width, width)
                whole[:, pl.ds(start, width)] = piece

    frozen = None
    for start in range(0, whole.shape[1], 256):
        term = nt(whole[:, start : start + 256], weight[:, start : start + 256])
        frozen = term if frozen is None else frozen + term
    adapter = nn(turned[...], stacked(tables))
    out[...] = (frozen + (adapter_scale * LOW_SCALE) * adapter).astype(bf16)


def second_kernel(slots, pieces, first, facts, tokens, grad, spread_back, *rest):
    rank = ADAPTER_RANK
    parts, spread_low, outs = rest[:pieces], rest[pieces], rest[pieces + 1 :]
    split = tokens.shape[1] - first
    ends = slot_ends(facts, slots)
    low = (paired_sum(parts) * LOW_SCALE).astype(bf16)
    spread = spread_slots(ends, low)
    spread_low[...] = spread
    product = (nn(spread, grad[...]) * (adapter_scale * BACK_SCALE)).astype(bf16)
    for s in range(slots):
        outs[s][:, split:] = product[s * rank : (s + 1) * rank]
    for c in range(0, split, 256):
        end = min(c + 256, split)
        product = nn(spread_back[...], tokens[:, first + c : first + end])
        product = (product * (adapter_scale * LOW_SCALE)).astype(bf16)
        for s in range(slots):
            outs[s][:, c:end] = product[s * rank : (s + 1) * rank]


def key_kernel(slots, spread, *rest):
    tables, frozen, key_out = rest[:slots], rest[slots:-1], rest[-1]
    table = stacked(tables)
    raised = nn(spread[...].astype(f32).T.astype(bf16), table)
    total = frozen[0][...]
    for part in frozen[1:]:
        total = total + part[...].astype(f32)
    key_out[...] = (total + (adapter_scale * BACK_SCALE) * raised).astype(bf16)


def adam_kernel(slots, spans, extras, parts, facts, *rest):
    count = len(spans)
    came, rest = rest[:slots], rest[slots:]
    old, rest = rest[: 4 * count], rest[4 * count + extras :]
    new, rest = rest[: 2 * count], rest[2 * count :]
    new_here, (gradient_ref, out_sems) = rest[: 2 * count], rest[2 * count :]
    owned, rank = old[0].shape[:2]
    total = gradient_ref.shape[1]
    start = spans[0][1]
    rows = 16
    held = owned // parts
    stores = []
    for p in range(parts):
        group = pl.ds(p * held, held)
        for i in range(2 * count):
            first, _, width = spans[i // 2]
            block = new[i].at[group, :, pl.ds(first, width)]
            sem = out_sems.at[p * 2 * count + i]
            stores.append(pltpu.make_async_copy(new_here[i].at[group], block, sem))

    def over_rows(body):
        def step(i, _):
            body(pl.ds(pl.multiple_of(i * rows, rows), rows))
            return 0

        lax.fori_loop(0, rank // rows, step, 0)

    def update(k, refs, news, r, first, begin, columns):
        weights, mean_old, var_old, avg_old = refs
        here = slice(first + columns.start, first + columns.stop)
        gradient = gradient_ref[r, begin + columns.start : begin + columns.stop]
        mean_new = beta_one * mean_old[k, r, here] + (1.0 - beta_one) * gradient
        var_new = beta_two * var_old[k, r, here] + (1.0 - beta_two) * gradient * gradient
        root = var_new * lax.rsqrt(var_new) + adam_eps
        inverse = pl.reciprocal(root, approx=True)
        inverse = inverse * (2.0 - root * inverse)
        updated = weights[k, r, here].astype(f32) - learn_rate * mean_new * inverse
        news[0][k, r, columns] = updated.astype(bf16)
        news[1][k, r, columns] = ema_decay * avg_old[k, r, here] + (1.0 - ema_decay) * updated

    for k in range(owned):

        @over_rows
        def _(r):
            gradient_ref[r, :] = jnp.zeros((rows, total), f32)

        for s in range(slots):

            @pl.when(facts[slots + s] == k)
            def _():
                @over_rows
                def _(r):
                    gradient_ref[r, :] += came[s][r, start : start + total].astype(f32)

        @over_rows
        def _(r):
            begin = 0
            for t, (first, _, width) in enumerate(spans):
                for c in range(0, width, 512):
                    columns = slice(c, min(c + 512, width))
                    refs, news = old[4 * t : 4 * t + 4], new_here[2 * t : 2 * t + 2]
                    update(k, refs, news, r, first, begin, columns)
                begin += width

        if (k + 1) % held == 0:
            for copy in stores[k // held * 2 * count : (k // held + 1) * 2 * count]:
                copy.start()
    for copy in stores:
        copy.wait()


def adam(facts, came, targets, into):
    owned, rank, _ = targets[0][0][0].shape
    arrays, shapes, spans, new_here = [], [], [], []
    for old, first, width, start in targets:
        arrays += list(old)
        shapes += [shape_of(old[0].shape, bf16), shape_of(old[0].shape, f32)]
        spans.append((first, start, width))
        new_here += [pltpu.VMEM((owned, rank, width), t) for t in (bf16, f32)]
    total = sum(span[2] for span in spans)
    count = len(came)
    parts = owned if total > 1024 else 1
    aliases = {1 + count + len(arrays) + i: i for i in range(len(into))}
    return pl.pallas_call(
        functools.partial(adam_kernel, count, tuple(spans), len(into), parts),
        out_shape=shapes,
        in_specs=[SMEM] + [VMEM] * (count + len(arrays)) + [ANY] * len(into),
        out_specs=[ANY] * len(shapes),
        scratch_shapes=new_here
        + [
            pltpu.VMEM((rank, total), f32),
            pltpu.SemaphoreType.DMA((parts * len(shapes),)),
        ],
        input_output_aliases=aliases,
        compiler_params=params(24),
        cost_estimate=cost(owned * rank * total * 20, owned * rank * total * 20),
    )(facts, *came, *arrays, *into)


def after(value, *others):
    return lax.optimization_barrier((value, *others))[0]


def swap(block, axes, flips):
    sizes = [lax.axis_size(a) for a in axes]
    route = []
    for t in range(sizes[0]):
        for s in range(sizes[1]):
            source = (t ^ flips[0]) * sizes[1] + (s ^ flips[1])
            route.append((source, t * sizes[1] + s))
    return lax.ppermute(block, axes, route)


def per_device(
    tokens,
    frozen_key_weight,
    output_gradient,
    counts,
    placement,
    adapter_sequence,
    adapter_down,
    adapter_up,
    down_first_moment,
    down_second_moment,
    down_average,
    up_first_moment,
    up_second_moment,
    up_average,
):
    tok_size = lax.axis_size("tok")
    tp_size, sub_size = lax.axis_size("tp"), lax.axis_size("sub")
    shards = ("tp", "sub")
    square = tp_size == 2 and sub_size == 2
    rows, wide = tokens.shape
    narrow = output_gradient.shape[1]
    key_width = frozen_key_weight.shape[1]
    owned = adapter_down.shape[0]
    slots = placement.shape[1]
    rank = ADAPTER_RANK
    flip = lambda a: jnp.swapaxes(a, 1, 2)
    down, down_m, down_v, down_a = map(
        flip, (adapter_down, down_first_moment, down_second_moment, down_average)
    )
    up, up_m, up_v, up_a = map(flip, (adapter_up, up_first_moment, up_second_moment, up_average))

    def fetch(block, slot):
        return lax.ppermute(block, "tok", [((i + slot) % tok_size, i) for i in range(tok_size)])

    def give_back(block, slot):
        return lax.ppermute(block, "tok", [((i - slot) % tok_size, i) for i in range(tok_size)])

    def shared(part):
        if not square:
            return [lax.psum(part, shards)]
        both = part + swap(part, shards, (0, 1))
        return [both, swap(both, shards, (1, 0))]

    step = min(256, wide)
    first = wide - step
    second = wide - first + narrow

    facts, *sent = pl.pallas_call(
        functools.partial(select_kernel, slots, owned, tok_size),
        out_shape=[shape_of((2 * slots,), jnp.int32)]
        + [shape_of((rank, narrow), bf16)] * slots
        + [shape_of((rank, wide), bf16)] * slots,
        in_specs=[SMEM, SMEM, SMEM, ANY, ANY],
        out_specs=[SMEM] + [VMEM] * (2 * slots),
        scratch_shapes=[pltpu.SemaphoreType.DMA((2 * slots,))],
        compiler_params=params(56),
        cost_estimate=cost(0, 4 * slots * rank * (wide + narrow)),
    )(counts, placement, adapter_sequence, down, up)
    up_send, down_send = sent[:slots], sent[slots:]
    ready = counts[0, 0] > 0
    early = fetch(down_send[1], 1)
    up_tables = [up_send[0]] + [fetch(up_send[s], s) for s in range(1, slots)]
    up_tables[0] = after(up_tables[0], early)
    down_tables = [down_send[0], early] + [
        fetch(after(down_send[s], ready, *up_tables), s) for s in range(2, slots)
    ]

    def group(work):
        shapes = jax.eval_shape(work)
        nothing = lambda: jax.tree.map(lambda a: jnp.zeros(a.shape, a.dtype), shapes)
        return lax.cond(ready, work, nothing)

    def back_work():
        part = pl.pallas_call(
            functools.partial(back_kernel, slots),
            out_shape=shape_of((rank, rows), f32),
            in_specs=[SMEM, VMEM] + [VMEM] * slots,
            out_specs=VMEM,
            compiler_params=params(16),
            cost_estimate=cost(2 * rows * narrow * rank * slots, 2 * rows * narrow),
        )(facts, output_gradient, *up_tables)
        parts = shared(part)
        if square:
            across = swap(output_gradient, shards, (1, 0))
            base = pl.pallas_call(
                functools.partial(base_kernel, narrow),
                out_shape=[shape_of((2, rows, narrow), f32)] * 2,
                in_specs=[VMEM, VMEM],
                out_specs=[VMEM, VMEM],
                compiler_params=params(16),
                cost_estimate=cost(2 * rows * wide * key_width, 2 * wide * (rows + key_width)),
            )(tokens, after(frozen_key_weight, parts[0]))
            pair = jnp.stack([output_gradient, after(across, base[0], parts[1])])
            grads = [across, swap(pair, shards, (0, 1))]
            parts = [after(parts[0], base[0]), parts[1]]
        else:
            base = []
            grads = [lax.all_gather(output_gradient, shards, axis=1, tiled=True)]
        spread, *sends = pl.pallas_call(
            functools.partial(part_down_kernel, slots, len(parts), first),
            out_shape=[shape_of((slots * rank, rows), bf16)] + [shape_of((rank, first), bf16)] * slots,
            in_specs=[SMEM, VMEM] + [VMEM] * len(parts),
            out_specs=[VMEM] * (1 + slots),
            compiler_params=params(16),
            cost_estimate=cost(2 * rows * first * rank * slots, 2 * rows * first),
        )(facts, tokens, *parts)
        return grads, base, spread, sends

    grads, base, spread_back, part_first = group(back_work)
    if square:
        grads = [output_gradient] + grads
    came_first = [part_first[0]] + [
        give_back(after(part_first[s], *down_tables[1:]), s) for s in range(1, slots)
    ]

    def input_whole(spread):
        return pl.pallas_call(
            functools.partial(input_kernel, slots, narrow),
            grid=(wide // step,),
            out_shape=shape_of((rows, wide), bf16),
            in_specs=[
                pl.BlockSpec((slots * rank, rows), lambda i: (0, 0)),
                pl.BlockSpec((step, key_width), lambda i: (i, 0)),
            ]
            + [pl.BlockSpec((rank, step), lambda i: (0, i))] * slots
            + [pl.BlockSpec(g.shape, lambda i, r=g.ndim: (0,) * r) for g in grads],
            out_specs=pl.BlockSpec((rows, step), lambda i: (0, i)),
            scratch_shapes=[
                pltpu.VMEM((rows, key_width), bf16),
                pltpu.VMEM((rows, slots * rank), bf16),
            ],
            compiler_params=params(16),
            cost_estimate=cost(
                2 * rows * wide * (key_width + rank * slots), 2 * wide * (rows + key_width)
            ),
        )(spread, frozen_key_weight, *down_tables, *grads)

    def low_work():
        part = pl.pallas_call(
            functools.partial(low_kernel, slots),
            out_shape=shape_of((rank, rows), f32),
            in_specs=[SMEM, VMEM] + [VMEM] * slots,
            out_specs=VMEM,
            compiler_params=params(16),
            cost_estimate=cost(2 * rows * wide * rank * slots, 2 * rows * wide),
        )(facts, tokens, *down_tables)
        parts = shared(part)
        input_gradient = input_whole(after(spread_back, parts[0]))
        if square:
            keep, send = base
            got = swap(send, shards, (0, 1))
            frozen, passing = keep[1] + got[1], (keep[0] + got[0]).astype(bf16)
            parts = [after(parts[0], input_gradient, frozen, passing), parts[1]]
        else:
            whole = jnp.dot(tokens, frozen_key_weight, preferred_element_type=f32)
            frozen = lax.psum_scatter(whole, shards, scatter_dimension=1, tiled=True)
            passing = ()
        spread, *sends = pl.pallas_call(
            functools.partial(second_kernel, slots, len(parts), first),
            out_shape=[shape_of((slots * rank, rows), bf16)] + [shape_of((rank, second), bf16)] * slots,
            in_specs=[SMEM] + [VMEM] * (3 + len(parts)),
            out_specs=[VMEM] * (1 + slots),
            compiler_params=params(16),
            cost_estimate=cost(2 * rows * narrow * rank * slots, 14 * rows * narrow),
        )(facts, tokens, output_gradient, spread_back, *parts)
        return spread, sends, frozen, passing, input_gradient

    spread_low, part_second, frozen, passing, input_gradient = group(low_work)
    frozen = [frozen, swap(passing, shards, (1, 0))] if square else [frozen]
    came_second = [part_second[0]] + [
        give_back(after(part_second[s], *came_first[1:]), s) for s in range(1, slots)
    ]

    key_output = pl.pallas_call(
        functools.partial(key_kernel, slots),
        out_shape=shape_of((rows, narrow), bf16),
        in_specs=[VMEM] * (1 + slots + len(frozen)),
        out_specs=VMEM,
        compiler_params=params(16),
        cost_estimate=cost(2 * rows * narrow * rank * slots, 14 * rows * narrow),
    )(spread_low, *up_tables, *frozen)

    down_old, up_old = (down, down_m, down_v, down_a), (up, up_m, up_v, up_a)
    done = adam(facts, came_first, [(down_old, 0, first, 0)], ())
    late = [came_second[0]] + [after(c, key_output, done[0]) for c in came_second[1:]]
    fresh_down, average_down, fresh_up, average_up = adam(
        facts,
        late,
        [(down_old, first, wide - first, 0), (up_old, 0, narrow, wide - first)],
        done,
    )
    return (
        key_output,
        input_gradient,
        flip(fresh_down),
        flip(fresh_up),
        flip(average_down),
        flip(average_up),
    )


def solution(mesh):
    rows = P(("groups", "tok"), ("tp", "sub"))
    cube = P(("groups", "tok"), ("tp", "sub"), None)
    return jax.shard_map(
        per_device,
        mesh=mesh,
        in_specs=(rows, P(("tp", "sub"), None), rows, P("groups", None), P("groups", None), P("groups"))
        + (cube,) * 8,
        out_specs=(rows, rows, cube, cube, cube, cube),
        check_vma=False,
    )
```

```python
import functools

import jax
import jax.numpy as jnp
from jax import lax
from jax.experimental import pallas as pl
from jax.experimental.pallas import tpu as pltpu
from jax.sharding import PartitionSpec as P

MODEL_WIDTH = 8192
ADAPTER_RANK = 64

adapter_scale = 0.5
learn_rate = 0.3
beta_one = 0.9
beta_two = 0.99
adam_eps = 1e-08
ema_decay = 0.9

LOW_SCALE = MODEL_WIDTH ** (-0.5)
BACK_SCALE = ADAPTER_RANK ** (-0.5)
MIB = 1024 * 1024

f32 = jnp.float32
bf16 = jnp.bfloat16

SMEM = pl.BlockSpec(memory_space=pltpu.SMEM)
VMEM = pl.BlockSpec(memory_space=pltpu.VMEM)
ANY = pl.BlockSpec(memory_space=pl.ANY)
HBM = pl.BlockSpec(memory_space=pltpu.HBM)


def shape_of(shape, dtype):
    return jax.ShapeDtypeStruct(tuple(shape), dtype)


SCHEDULE_SCALE = 3


def cost(flops, bytes_accessed):
    return pl.CostEstimate(
        flops=int(flops * SCHEDULE_SCALE),
        bytes_accessed=int(bytes_accessed * SCHEDULE_SCALE),
        transcendentals=0,
    )


def params(mib):
    return pltpu.CompilerParams(vmem_limit_bytes=mib * MIB)


def nt(a, b):
    return lax.dot_general(a, b, (((1,), (1,)), ((), ())), preferred_element_type=f32)


def nn(a, b):
    return lax.dot_general(a, b, (((1,), (0,)), ((), ())), preferred_element_type=f32)


def tn(a, b):
    return lax.dot_general(a, b, (((0,), (0,)), ((), ())), preferred_element_type=f32)


def facts_kernel(slots, owned, tok_size, counts, placement, sequence, facts):
    me = lax.axis_index("tok")
    total = jnp.int32(0)
    for s in range(slots):
        total = total + counts[me, s]
        facts[s] = total
        tenant = placement[lax.rem(me - s + tok_size, tok_size), s]
        place = jnp.int32(0)
        for k in range(1, owned):
            place = place + jnp.where(sequence[me * owned + k] == tenant, k, 0)
        facts[slots + s] = place


def slot_ends(facts, slots):
    return [facts[s] for s in range(slots)]


def slot_mask(ends, slot, shape):
    rows = lax.broadcasted_iota(jnp.int32, shape, 1)
    inside = rows < ends[slot]
    if slot:
        inside = inside & (rows >= ends[slot - 1])
    return inside


def pick_slot(ends, products, rank):
    rows = lax.broadcasted_iota(jnp.int32, (rank, products.shape[1]), 1)
    slots = products.shape[0] // rank
    out = products[(slots - 1) * rank :]
    for s in range(slots - 2, -1, -1):
        out = jnp.where(rows < ends[s], products[s * rank : (s + 1) * rank], out)
    return out


def spread_slots(ends, values):
    wide = values.astype(f32)
    return jnp.concatenate(
        [jnp.where(slot_mask(ends, s, wide.shape), wide, 0.0) for s in range(len(ends))], axis=0
    ).astype(bf16)


def paired_sum(refs):
    parts = [ref[...] for ref in refs]
    while len(parts) > 1:
        parts = [parts[i] + parts[i + 1] for i in range(0, len(parts), 2)]
    return parts[0]


def select_kernel(slots, owned, tok_size, counts, placement, sequence, down, up, facts, *rest):
    ups, downs, sems = rest[:slots], rest[slots : 2 * slots], rest[2 * slots]
    facts_kernel(slots, owned, tok_size, counts, placement, sequence, facts)
    copies = []
    order = list(range(1, slots)) + [0]
    for s in order:
        copies.append(pltpu.make_async_copy(up.at[facts[slots + s]], ups[s], sems.at[s]))
    for s in order:
        copies.append(pltpu.make_async_copy(down.at[facts[slots + s]], downs[s], sems.at[slots + s]))
    for copy in copies:
        copy.start()
    for copy in copies:
        copy.wait()


def base_kernel(width, tokens, weight, keep, send):
    tp, sub = lax.axis_index("tp"), lax.axis_index("sub")
    mine, other = tp, 1 - tp
    for ref, s in ((send, 1 - sub), (keep, sub)):
        for i, t in enumerate((other, mine)):
            start = pl.multiple_of((t * 2 + s) * width, width)
            ref[i] = nn(tokens[...], weight[:, pl.ds(start, width)])


def stacked(tables):
    return jnp.concatenate([t[...] for t in tables], axis=0)


def back_kernel(slots, facts, grad, *rest):
    tables, out = rest[:slots], rest[slots]
    out[...] = pick_slot(slot_ends(facts, slots), nt(stacked(tables), grad[...]), ADAPTER_RANK)


def part_down_kernel(slots, pieces, width, facts, tokens, *rest):
    parts, spread_out, outs = rest[:pieces], rest[pieces], rest[pieces + 1 :]
    ends = slot_ends(facts, slots)
    back = (paired_sum(parts) * BACK_SCALE).astype(bf16)
    spread = spread_slots(ends, back)
    spread_out[...] = spread
    for c in range(0, width, 256):
        columns = slice(c, min(c + 256, width))
        product = (nn(spread, tokens[:, columns]) * (adapter_scale * LOW_SCALE)).astype(bf16)
        for s in range(slots):
            outs[s][:, columns] = product[s * ADAPTER_RANK : (s + 1) * ADAPTER_RANK]


def low_kernel(slots, facts, tokens, *rest):
    tables, out = rest[:slots], rest[slots]
    out[...] = pick_slot(slot_ends(facts, slots), nt(stacked(tables), tokens[...]), ADAPTER_RANK)


def input_kernel(slots, width, spread, weight, *rest):
    tables, grads, (out, whole, turned) = rest[:slots], rest[slots:-3], rest[-3:]

    @pl.when(pl.program_id(0) == 0)
    def _():
        turned[...] = spread[...].astype(f32).T.astype(bf16)
        if len(grads) == 1:
            whole[...] = grads[0][...]
        else:
            tp, sub = lax.axis_index("tp"), lax.axis_index("sub")
            pieces = (grads[0][...], grads[1][...], grads[2][0], grads[2][1])
            for piece, t, s in zip(pieces, (tp, 1 - tp, tp, 1 - tp), (sub, sub, 1 - sub, 1 - sub)):
                start = pl.multiple_of((t * 2 + s) * width, width)
                whole[:, pl.ds(start, width)] = piece

    frozen = None
    for start in range(0, whole.shape[1], 256):
        term = nt(whole[:, start : start + 256], weight[:, start : start + 256])
        frozen = term if frozen is None else frozen + term
    adapter = nn(turned[...], stacked(tables))
    out[...] = (frozen + (adapter_scale * LOW_SCALE) * adapter).astype(bf16)


def second_kernel(slots, pieces, first, facts, tokens, grad, spread_back, *rest):
    rank = ADAPTER_RANK
    parts, spread_low, outs = rest[:pieces], rest[pieces], rest[pieces + 1 :]
    split = tokens.shape[1] - first
    ends = slot_ends(facts, slots)
    low = (paired_sum(parts) * LOW_SCALE).astype(bf16)
    spread = spread_slots(ends, low)
    spread_low[...] = spread
    product = (nn(spread, grad[...]) * (adapter_scale * BACK_SCALE)).astype(bf16)
    for s in range(slots):
        outs[s][:, split:] = product[s * rank : (s + 1) * rank]
    for c in range(0, split, 256):
        end = min(c + 256, split)
        product = nn(spread_back[...], tokens[:, first + c : first + end])
        product = (product * (adapter_scale * LOW_SCALE)).astype(bf16)
        for s in range(slots):
            outs[s][:, c:end] = product[s * rank : (s + 1) * rank]


def adam_kernel(slots, spans, extras, parts, frozen_count, facts, *rest):
    count = len(spans)
    key_count = 1 + slots + frozen_count if frozen_count else 0
    came, rest = rest[:slots], rest[slots:]
    key_in, rest = rest[:key_count], rest[key_count:]
    old, rest = rest[: 4 * count], rest[4 * count + extras :]
    new, rest = rest[: 2 * count], rest[2 * count :]
    key_out, rest = rest[: min(1, key_count)], rest[min(1, key_count) :]
    came_here, rest = rest[0], rest[1:]
    old_here, rest = rest[: 4 * count], rest[4 * count :]
    new_here, (gradient_ref, in_sems, out_sems) = rest[: 2 * count], rest[2 * count : 2 * count + 3]
    key_here = rest[2 * count + 3 :]
    owned, rank = old_here[0].shape[:2]
    total = gradient_ref.shape[1]
    start = spans[0][1]
    rows = 16

    arrivals = [
        pltpu.make_async_copy(came[s].at[:, pl.ds(start, total)], came_here.at[s], in_sems.at[s])
        for s in range(slots)
    ]
    loads, stores = [], []
    held = owned // parts
    for p in range(parts):
        group = pl.ds(p * held, held)
        for i in range(4 * count):
            first, _, width = spans[i // 4]
            block = old[i].at[group, :, pl.ds(first, width)]
            sem = in_sems.at[slots + p * 4 * count + i]
            loads.append(pltpu.make_async_copy(block, old_here[i].at[group], sem))
        for i in range(2 * count):
            first, _, width = spans[i // 2]
            block = new[i].at[group, :, pl.ds(first, width)]
            sem = out_sems.at[p * 2 * count + i]
            stores.append(pltpu.make_async_copy(new_here[i].at[group], block, sem))
    key_loads = []
    if frozen_count:
        spread_here, table_here, key_done = key_here[0], key_here[1], key_here[-1]
        frozen_here = key_here[2:-1]
        places = [spread_here]
        places += [table_here.at[pl.ds(s * rank, rank)] for s in range(slots)]
        places += list(frozen_here)
        base = slots + parts * 4 * count
        for i, (source, place) in enumerate(zip(key_in, places)):
            key_loads.append(pltpu.make_async_copy(source, place, in_sems.at[base + i]))
    for copy in key_loads + arrivals + loads:
        copy.start()

    if frozen_count:
        for copy in key_loads:
            copy.wait()
        raised = nn(spread_here[...].astype(f32).T.astype(bf16), table_here[...])
        whole = frozen_here[0][...]
        for part in frozen_here[1:]:
            whole = whole + part[...].astype(f32)
        key_done[...] = (whole + (adapter_scale * BACK_SCALE) * raised).astype(bf16)
        sem = out_sems.at[parts * 2 * count]
        stores.append(pltpu.make_async_copy(key_done, key_out[0], sem))
        stores[-1].start()

    def over_rows(body):
        def step(i, _):
            body(pl.ds(pl.multiple_of(i * rows, rows), rows))
            return 0

        lax.fori_loop(0, rank // rows, step, 0)

    def update(k, refs, news, r, begin, columns):
        weights, mean_old, var_old, avg_old = refs
        gradient = gradient_ref[r, begin + columns.start : begin + columns.stop]
        mean_new = beta_one * mean_old[k, r, columns] + (1.0 - beta_one) * gradient
        var_new = beta_two * var_old[k, r, columns] + (1.0 - beta_two) * gradient * gradient
        root = var_new * lax.rsqrt(var_new) + adam_eps
        inverse = pl.reciprocal(root, approx=True)
        inverse = inverse * (2.0 - root * inverse)
        updated = weights[k, r, columns].astype(f32) - learn_rate * mean_new * inverse
        news[0][k, r, columns] = updated.astype(bf16)
        news[1][k, r, columns] = ema_decay * avg_old[k, r, columns] + (1.0 - ema_decay) * updated

    for copy in arrivals:
        copy.wait()
    for k in range(owned):

        @over_rows
        def _(r):
            gradient_ref[r, :] = jnp.zeros((rows, total), f32)

        for s in range(slots):

            @pl.when(facts[slots + s] == k)
            def _():
                @over_rows
                def _(r):
                    gradient_ref[r, :] += came_here[s, r, :].astype(f32)

        if k % held == 0:
            for copy in loads[k // held * 4 * count : (k // held + 1) * 4 * count]:
                copy.wait()

        @over_rows
        def _(r):
            begin = 0
            for t, (_, _, width) in enumerate(spans):
                for c in range(0, width, 512):
                    columns = slice(c, min(c + 512, width))
                    refs, news = old_here[4 * t : 4 * t + 4], new_here[2 * t : 2 * t + 2]
                    update(k, refs, news, r, begin, columns)
                begin += width

        if (k + 1) % held == 0:
            for copy in stores[k // held * 2 * count : (k // held + 1) * 2 * count]:
                copy.start()
    for copy in stores:
        copy.wait()


def adam(facts, came, targets, into, spread=None, tables=(), frozen=()):
    owned, rank, _ = targets[0][0][0].shape
    arrays, shapes, spans, old_here, new_here = [], [], [], [], []
    for old, first, width, start in targets:
        arrays += list(old)
        shapes += [shape_of(old[0].shape, bf16), shape_of(old[0].shape, f32)]
        spans.append((first, start, width))
        old_here += [pltpu.VMEM((owned, rank, width), a.dtype) for a in old]
        new_here += [pltpu.VMEM((owned, rank, width), t) for t in (bf16, f32)]
    total = sum(span[2] for span in spans)
    count = len(came)
    parts = 2 if total > 1024 and owned % 2 == 0 else 1
    key_in = [spread, *tables, *frozen] if frozen else []
    key_here = []
    stores = parts * len(shapes)
    if frozen:
        rows, narrow = frozen[0].shape
        shapes.append(shape_of((rows, narrow), bf16))
        key_here = [pltpu.VMEM(spread.shape, bf16), pltpu.VMEM((count * rank, narrow), bf16)]
        key_here += [pltpu.VMEM(f.shape, f.dtype) for f in frozen]
        key_here += [pltpu.VMEM((rows, narrow), bf16)]
    first_extra = 1 + count + len(key_in) + len(arrays)
    return pl.pallas_call(
        functools.partial(adam_kernel, count, tuple(spans), len(into), parts, len(frozen)),
        out_shape=shapes,
        in_specs=[SMEM] + [HBM] * (count + len(key_in) + len(arrays) + len(into)),
        out_specs=[HBM] * len(shapes),
        scratch_shapes=[pltpu.VMEM((count, rank, total), bf16)]
        + old_here
        + new_here
        + [
            pltpu.VMEM((rank, total), f32),
            pltpu.SemaphoreType.DMA((count + parts * len(arrays) + len(key_in),)),
            pltpu.SemaphoreType.DMA((stores + 1,)),
        ]
        + key_here,
        input_output_aliases={first_extra + i: i for i in range(len(into))},
        compiler_params=params(60),
        cost_estimate=cost(owned * rank * total * 20, owned * rank * total * 20),
    )(facts, *came, *key_in, *arrays, *into)


def after(value, *others):
    return lax.optimization_barrier((value, *others))[0]


def swap(block, axes, flips):
    sizes = [lax.axis_size(a) for a in axes]
    route = []
    for t in range(sizes[0]):
        for s in range(sizes[1]):
            source = (t ^ flips[0]) * sizes[1] + (s ^ flips[1])
            route.append((source, t * sizes[1] + s))
    return lax.ppermute(block, axes, route)


def per_device(
    tokens,
    frozen_key_weight,
    output_gradient,
    counts,
    placement,
    adapter_sequence,
    adapter_down,
    adapter_up,
    down_first_moment,
    down_second_moment,
    down_average,
    up_first_moment,
    up_second_moment,
    up_average,
):
    tok_size = lax.axis_size("tok")
    tp_size, sub_size = lax.axis_size("tp"), lax.axis_size("sub")
    shards = ("tp", "sub")
    square = tp_size == 2 and sub_size == 2
    rows, wide = tokens.shape
    narrow = output_gradient.shape[1]
    key_width = frozen_key_weight.shape[1]
    owned = adapter_down.shape[0]
    slots = placement.shape[1]
    rank = ADAPTER_RANK
    flip = lambda a: jnp.swapaxes(a, 1, 2)
    down, down_m, down_v, down_a = map(
        flip, (adapter_down, down_first_moment, down_second_moment, down_average)
    )
    up, up_m, up_v, up_a = map(flip, (adapter_up, up_first_moment, up_second_moment, up_average))

    def fetch(block, slot):
        return lax.ppermute(block, "tok", [((i + slot) % tok_size, i) for i in range(tok_size)])

    def give_back(block, slot):
        return lax.ppermute(block, "tok", [((i - slot) % tok_size, i) for i in range(tok_size)])

    def shared(part):
        if not square:
            return [lax.psum(part, shards)]
        both = part + swap(part, shards, (0, 1))
        return [both, swap(both, shards, (1, 0))]

    step = min(256, wide)
    first = wide - step
    second = wide - first + narrow

    facts, *sent = pl.pallas_call(
        functools.partial(select_kernel, slots, owned, tok_size),
        out_shape=[shape_of((2 * slots,), jnp.int32)]
        + [shape_of((rank, narrow), bf16)] * slots
        + [shape_of((rank, wide), bf16)] * slots,
        in_specs=[SMEM, SMEM, SMEM, ANY, ANY],
        out_specs=[SMEM] + [VMEM] * (2 * slots),
        scratch_shapes=[pltpu.SemaphoreType.DMA((2 * slots,))],
        compiler_params=params(56),
        cost_estimate=cost(0, 4 * slots * rank * (wide + narrow)),
    )(counts, placement, adapter_sequence, down, up)
    up_send, down_send = sent[:slots], sent[slots:]
    ready = counts[0, 0] > 0
    early = fetch(down_send[1], 1)
    up_tables = [up_send[0]] + [fetch(up_send[s], s) for s in range(1, slots)]
    if square:
        across = swap(output_gradient, shards, (1, 0))
        pair = jnp.stack([output_gradient, across])
        up_tables[0] = after(up_tables[0], early, pair)
    else:
        up_tables[0] = after(up_tables[0], early)
    down_tables = [down_send[0], early] + [
        fetch(after(down_send[s], ready, *up_tables), s) for s in range(2, slots)
    ]

    def group(work):
        shapes = jax.eval_shape(work)
        nothing = lambda: jax.tree.map(lambda a: jnp.zeros(a.shape, a.dtype), shapes)
        return lax.cond(ready, work, nothing)

    def back_work():
        part = pl.pallas_call(
            functools.partial(back_kernel, slots),
            out_shape=shape_of((rank, rows), f32),
            in_specs=[SMEM, VMEM] + [VMEM] * slots,
            out_specs=VMEM,
            compiler_params=params(16),
            cost_estimate=cost(2 * rows * narrow * rank * slots, 2 * rows * narrow),
        )(facts, output_gradient, *up_tables)
        parts = shared(part)
        if square:
            base = pl.pallas_call(
                functools.partial(base_kernel, narrow),
                out_shape=[shape_of((2, rows, narrow), f32)] * 2,
                in_specs=[VMEM, VMEM],
                out_specs=[VMEM, VMEM],
                compiler_params=params(16),
                cost_estimate=cost(2 * rows * wide * key_width, 2 * wide * (rows + key_width)),
            )(tokens, after(frozen_key_weight, parts[0]))
            grads = [swap(pair, shards, (0, 1))]
            parts = [after(parts[0], base[0]), parts[1]]
        else:
            base = []
            grads = [lax.all_gather(output_gradient, shards, axis=1, tiled=True)]
        spread, *sends = pl.pallas_call(
            functools.partial(part_down_kernel, slots, len(parts), first),
            out_shape=[shape_of((slots * rank, rows), bf16)] + [shape_of((rank, first), bf16)] * slots,
            in_specs=[SMEM, VMEM] + [VMEM] * len(parts),
            out_specs=[VMEM] * (1 + slots),
            compiler_params=params(16),
            cost_estimate=cost(2 * rows * first * rank * slots, 2 * rows * first),
        )(facts, tokens, *parts)
        return grads, base, spread, sends

    grads, base, spread_back, part_first = group(back_work)
    if square:
        grads = [output_gradient, across] + grads
    came_first = [part_first[0]] + [
        give_back(after(part_first[s], *down_tables[1:]), s) for s in range(1, slots)
    ]

    def input_whole(spread):
        return pl.pallas_call(
            functools.partial(input_kernel, slots, narrow),
            grid=(wide // step,),
            out_shape=shape_of((rows, wide), bf16),
            in_specs=[
                pl.BlockSpec((slots * rank, rows), lambda i: (0, 0)),
                pl.BlockSpec((step, key_width), lambda i: (i, 0)),
            ]
            + [pl.BlockSpec((rank, step), lambda i: (0, i))] * slots
            + [pl.BlockSpec(g.shape, lambda i, r=g.ndim: (0,) * r) for g in grads],
            out_specs=pl.BlockSpec((rows, step), lambda i: (0, i)),
            scratch_shapes=[
                pltpu.VMEM((rows, key_width), bf16),
                pltpu.VMEM((rows, slots * rank), bf16),
            ],
            compiler_params=params(16),
            cost_estimate=cost(
                2 * rows * wide * (key_width + rank * slots), 2 * wide * (rows + key_width)
            ),
        )(spread, frozen_key_weight, *down_tables, *grads)

    def low_work():
        part = pl.pallas_call(
            functools.partial(low_kernel, slots),
            out_shape=shape_of((rank, rows), f32),
            in_specs=[SMEM, VMEM] + [VMEM] * slots,
            out_specs=VMEM,
            compiler_params=params(16),
            cost_estimate=cost(2 * rows * wide * rank * slots, 2 * rows * wide),
        )(facts, tokens, *down_tables)
        parts = shared(part)
        input_gradient = input_whole(after(spread_back, parts[0]))
        if square:
            keep, send = base
            got = swap(send, shards, (0, 1))
            frozen, passing = keep[1] + got[1], (keep[0] + got[0]).astype(bf16)
            parts = [after(parts[0], input_gradient, frozen, passing), parts[1]]
        else:
            whole = jnp.dot(tokens, frozen_key_weight, preferred_element_type=f32)
            frozen = lax.psum_scatter(whole, shards, scatter_dimension=1, tiled=True)
            passing = ()
        spread, *sends = pl.pallas_call(
            functools.partial(second_kernel, slots, len(parts), first),
            out_shape=[shape_of((slots * rank, rows), bf16)] + [shape_of((rank, second), bf16)] * slots,
            in_specs=[SMEM] + [VMEM] * (3 + len(parts)),
            out_specs=[VMEM] * (1 + slots),
            compiler_params=params(16),
            cost_estimate=cost(2 * rows * narrow * rank * slots, 14 * rows * narrow),
        )(facts, tokens, output_gradient, spread_back, *parts)
        return spread, sends, frozen, passing, input_gradient

    spread_low, part_second, frozen, passing, input_gradient = group(low_work)
    frozen = [frozen, swap(passing, shards, (1, 0))] if square else [frozen]
    came_second = [part_second[0]] + [
        give_back(after(part_second[s], *came_first[1:]), s) for s in range(1, slots)
    ]

    down_old, up_old = (down, down_m, down_v, down_a), (up, up_m, up_v, up_a)
    *done, key_output = adam(
        facts, came_first, [(down_old, 0, first, 0)], (), spread_low, up_tables, frozen
    )
    late = [came_second[0]] + [after(c, done[0]) for c in came_second[1:]]
    fresh_down, average_down, fresh_up, average_up = adam(
        facts,
        late,
        [(down_old, first, wide - first, 0), (up_old, 0, narrow, wide - first)],
        done,
    )
    return (
        key_output,
        input_gradient,
        flip(fresh_down),
        flip(fresh_up),
        flip(average_down),
        flip(average_up),
    )


def solution(mesh):
    rows = P(("groups", "tok"), ("tp", "sub"))
    cube = P(("groups", "tok"), ("tp", "sub"), None)
    return jax.shard_map(
        per_device,
        mesh=mesh,
        in_specs=(rows, P(("tp", "sub"), None), rows, P("groups", None), P("groups", None), P("groups"))
        + (cube,) * 8,
        out_specs=(rows, rows, cube, cube, cube, cube),
        check_vma=False,
    )
```

```python
import functools

import jax
import jax.numpy as jnp
from jax import lax
from jax.experimental import pallas as pl
from jax.experimental.pallas import tpu as pltpu
from jax.sharding import PartitionSpec as P

MODEL_WIDTH = 8192
ADAPTER_RANK = 64

adapter_scale = 0.5
learn_rate = 0.3
beta_one = 0.9
beta_two = 0.99
adam_eps = 1e-08
ema_decay = 0.9

LOW_SCALE = MODEL_WIDTH ** (-0.5)
BACK_SCALE = ADAPTER_RANK ** (-0.5)
MIB = 1024 * 1024

f32 = jnp.float32
bf16 = jnp.bfloat16

SMEM = pl.BlockSpec(memory_space=pltpu.SMEM)
VMEM = pl.BlockSpec(memory_space=pltpu.VMEM)
ANY = pl.BlockSpec(memory_space=pl.ANY)
HBM = pl.BlockSpec(memory_space=pltpu.HBM)


def shape_of(shape, dtype):
    return jax.ShapeDtypeStruct(tuple(shape), dtype)


SCHEDULE_SCALE = 3


def cost(flops, bytes_accessed):
    return pl.CostEstimate(
        flops=int(flops * SCHEDULE_SCALE),
        bytes_accessed=int(bytes_accessed * SCHEDULE_SCALE),
        transcendentals=0,
    )


def params(mib):
    return pltpu.CompilerParams(vmem_limit_bytes=mib * MIB)


def nt(a, b):
    return lax.dot_general(a, b, (((1,), (1,)), ((), ())), preferred_element_type=f32)


def nn(a, b):
    return lax.dot_general(a, b, (((1,), (0,)), ((), ())), preferred_element_type=f32)


def tn(a, b):
    return lax.dot_general(a, b, (((0,), (0,)), ((), ())), preferred_element_type=f32)


def facts_kernel(slots, owned, tok_size, counts, placement, sequence, facts):
    me = lax.axis_index("tok")
    total = jnp.int32(0)
    for s in range(slots):
        total = total + counts[me, s]
        facts[s] = total
        tenant = placement[lax.rem(me - s + tok_size, tok_size), s]
        place = jnp.int32(0)
        for k in range(1, owned):
            place = place + jnp.where(sequence[me * owned + k] == tenant, k, 0)
        facts[slots + s] = place


def slot_ends(facts, slots):
    return [facts[s] for s in range(slots)]


def slot_mask(ends, slot, shape):
    rows = lax.broadcasted_iota(jnp.int32, shape, 1)
    inside = rows < ends[slot]
    if slot:
        inside = inside & (rows >= ends[slot - 1])
    return inside


def pick_slot(ends, products, rank):
    rows = lax.broadcasted_iota(jnp.int32, (rank, products.shape[1]), 1)
    slots = products.shape[0] // rank
    out = products[(slots - 1) * rank :]
    for s in range(slots - 2, -1, -1):
        out = jnp.where(rows < ends[s], products[s * rank : (s + 1) * rank], out)
    return out


def spread_slots(ends, values):
    wide = values.astype(f32)
    return jnp.concatenate(
        [jnp.where(slot_mask(ends, s, wide.shape), wide, 0.0) for s in range(len(ends))], axis=0
    ).astype(bf16)


def paired_sum(refs):
    parts = [ref[...] for ref in refs]
    while len(parts) > 1:
        parts = [parts[i] + parts[i + 1] for i in range(0, len(parts), 2)]
    return parts[0]


def select_kernel(slots, owned, tok_size, counts, placement, sequence, down, up, facts, *rest):
    ups, downs, sems = rest[:slots], rest[slots : 2 * slots], rest[2 * slots]
    facts_kernel(slots, owned, tok_size, counts, placement, sequence, facts)
    copies = []
    order = list(range(1, slots)) + [0]
    for s in order:
        copies.append(pltpu.make_async_copy(up.at[facts[slots + s]], ups[s], sems.at[s]))
    for s in order:
        copies.append(pltpu.make_async_copy(down.at[facts[slots + s]], downs[s], sems.at[slots + s]))
    for copy in copies:
        copy.start()
    for copy in copies:
        copy.wait()


def base_kernel(width, tokens, weight, keep, send):
    tp, sub = lax.axis_index("tp"), lax.axis_index("sub")
    mine, other = tp, 1 - tp
    for ref, s in ((send, 1 - sub), (keep, sub)):
        for i, t in enumerate((other, mine)):
            start = pl.multiple_of((t * 2 + s) * width, width)
            ref[i] = nn(tokens[...], weight[:, pl.ds(start, width)])


def stacked(tables):
    return jnp.concatenate([t[...] for t in tables], axis=0)


def back_kernel(slots, facts, grad, *rest):
    tables, out = rest[:slots], rest[slots]
    out[...] = pick_slot(slot_ends(facts, slots), nt(stacked(tables), grad[...]), ADAPTER_RANK)


def part_down_kernel(slots, pieces, facts, tokens, *rest):
    parts, spread_out, outs = rest[:pieces], rest[pieces], rest[pieces + 1 :]
    ends = slot_ends(facts, slots)
    back = (paired_sum(parts) * BACK_SCALE).astype(bf16)
    spread = spread_slots(ends, back)
    spread_out[...] = spread
    for c in range(0, tokens.shape[1], 256):
        columns = slice(c, min(c + 256, tokens.shape[1]))
        product = (nn(spread, tokens[:, columns]) * (adapter_scale * LOW_SCALE)).astype(bf16)
        for s in range(slots):
            outs[s][:, columns] = product[s * ADAPTER_RANK : (s + 1) * ADAPTER_RANK]


def low_kernel(slots, facts, tokens, *rest):
    tables, out = rest[:slots], rest[slots]
    out[...] = pick_slot(slot_ends(facts, slots), nt(stacked(tables), tokens[...]), ADAPTER_RANK)


def input_kernel(slots, width, spread, weight, *rest):
    tables, grads, (out, whole, turned) = rest[:slots], rest[slots:-3], rest[-3:]

    @pl.when(pl.program_id(0) == 0)
    def _():
        turned[...] = spread[...].astype(f32).T.astype(bf16)
        if len(grads) == 1:
            whole[...] = grads[0][...]
        else:
            tp, sub = lax.axis_index("tp"), lax.axis_index("sub")
            pieces = (grads[0][...], grads[1][...], grads[2][0], grads[2][1])
            for piece, t, s in zip(pieces, (tp, 1 - tp, tp, 1 - tp), (sub, sub, 1 - sub, 1 - sub)):
                start = pl.multiple_of((t * 2 + s) * width, width)
                whole[:, pl.ds(start, width)] = piece

    frozen = None
    for start in range(0, whole.shape[1], 256):
        term = nt(whole[:, start : start + 256], weight[:, start : start + 256])
        frozen = term if frozen is None else frozen + term
    adapter = nn(turned[...], stacked(tables))
    out[...] = (frozen + (adapter_scale * LOW_SCALE) * adapter).astype(bf16)


def second_kernel(slots, tok_size, pieces, facts, grad, *rest):
    parts, (spread_low, out) = rest[:pieces], rest[pieces:]
    me = lax.axis_index("tok")
    low = (paired_sum(parts) * LOW_SCALE).astype(bf16)
    spread = spread_slots(slot_ends(facts, slots), low)
    spread_low[...] = spread
    product = (nn(spread, grad[...]) * (adapter_scale * BACK_SCALE)).astype(bf16)
    for s in range(slots):
        out[lax.rem(me + s, tok_size)] = product[s * ADAPTER_RANK : (s + 1) * ADAPTER_RANK]


def adam_step(weights, mean_old, var_old, avg_old, gradient):
    mean_new = beta_one * mean_old + (1.0 - beta_one) * gradient
    var_new = beta_two * var_old + (1.0 - beta_two) * gradient * gradient
    root = var_new * lax.rsqrt(var_new) + adam_eps
    inverse = pl.reciprocal(root, approx=True)
    inverse = inverse * (2.0 - root * inverse)
    updated = weights.astype(f32) - learn_rate * mean_new * inverse
    return updated.astype(bf16), ema_decay * avg_old + (1.0 - ema_decay) * updated


def each_rows(count, body):
    rows = 16

    def step(i, _):
        body(pl.ds(pl.multiple_of(i * rows, rows), rows), rows)
        return 0

    lax.fori_loop(0, count // rows, step, 0)


def adam_kernel(slots, facts, *rest):
    came, old, rest = rest[:slots], rest[slots : slots + 4], rest[slots + 4 :]
    fresh, average, came_here = rest[:3]
    old_here, rest = rest[3:7], rest[7:]
    fresh_here, average_here, gradient_ref, in_sems, out_sems = rest
    owned, rank, width = fresh_here.shape

    arrivals = [
        pltpu.make_async_copy(came[s], came_here.at[s], in_sems.at[s]) for s in range(slots)
    ]
    loads, stores = [], []
    for k in range(owned):
        for i in range(4):
            sem = in_sems.at[slots + 4 * k + i]
            loads.append(pltpu.make_async_copy(old[i].at[k], old_here[i].at[k], sem))
        for i, (here, there) in enumerate(((fresh_here, fresh), (average_here, average))):
            sem = out_sems.at[2 * k + i]
            stores.append(pltpu.make_async_copy(here.at[k], there.at[k], sem))
    for copy in arrivals + loads:
        copy.start()

    for copy in arrivals:
        copy.wait()
    for k in range(owned):

        def clear(r, rows):
            gradient_ref[r, :] = jnp.zeros((rows, width), f32)

        each_rows(rank, clear)
        for s in range(slots):

            @pl.when(facts[slots + s] == k)
            def _():
                def add(r, rows):
                    gradient_ref[r, :] += came_here[s, r, :].astype(f32)

                each_rows(rank, add)

        for copy in loads[4 * k : 4 * k + 4]:
            copy.wait()

        def update(r, rows):
            for c in range(0, width, 512):
                columns = slice(c, min(c + 512, width))
                fresh_here[k, r, columns], average_here[k, r, columns] = adam_step(
                    *[ref[k, r, columns] for ref in old_here], gradient_ref[r, columns]
                )

        each_rows(rank, update)
        for copy in stores[2 * k : 2 * k + 2]:
            copy.start()
    for copy in stores:
        copy.wait()


def adam_down(facts, came, old):
    owned, rank, width = old[0].shape
    slots = len(came)
    shapes = [shape_of(old[0].shape, bf16), shape_of(old[0].shape, f32)]
    return pl.pallas_call(
        functools.partial(adam_kernel, slots),
        out_shape=shapes,
        in_specs=[SMEM] + [ANY] * (slots + 4),
        out_specs=[ANY] * 2,
        scratch_shapes=[pltpu.VMEM((slots, rank, width), bf16)]
        + [pltpu.VMEM(a.shape, a.dtype) for a in old]
        + [
            pltpu.VMEM(old[0].shape, bf16),
            pltpu.VMEM(old[0].shape, f32),
            pltpu.VMEM((rank, width), f32),
            pltpu.SemaphoreType.DMA((slots + 4 * owned,)),
            pltpu.SemaphoreType.DMA((2 * owned,)),
        ],
        compiler_params=params(60),
        cost_estimate=cost(owned * rank * width * 20, owned * rank * width * 20),
    )(facts, *came, *old)


def last_kernel(slots, tok_size, facts, came, *rest):
    old, rest = rest[:4], rest[4:]
    spread, tables, frozen = rest[0], rest[1 : 1 + slots], rest[1 + slots : -4]
    fresh, average, key_out, gradients = rest[-4:]
    raised = nn(spread[...].astype(f32).T.astype(bf16), stacked(tables))
    whole = frozen[0][...]
    for part in frozen[1:]:
        whole = whole + part[...].astype(f32)
    key_out[...] = (whole + (adapter_scale * BACK_SCALE) * raised).astype(bf16)
    me = lax.axis_index("tok")
    gradients[...] = jnp.zeros(gradients.shape, f32)
    for s in range(slots):
        gradients[facts[slots + s]] += came[lax.rem(me - s + tok_size, tok_size)].astype(f32)
    owned, rank, _ = gradients.shape
    for k in range(owned):

        def update(r, rows):
            fresh[k, r, :], average[k, r, :] = adam_step(
                *[ref[k, r, :] for ref in old], gradients[k, r, :]
            )

        each_rows(rank, update)


def last_step(facts, came, old, spread, tables, frozen, tok_size):
    shape = old[0].shape
    slots = len(tables)
    return pl.pallas_call(
        functools.partial(last_kernel, slots, tok_size),
        out_shape=[
            shape_of(shape, bf16),
            shape_of(shape, f32),
            shape_of(frozen[0].shape, bf16),
        ],
        in_specs=[SMEM] + [VMEM] * (6 + slots + len(frozen)),
        out_specs=[VMEM] * 3,
        scratch_shapes=[pltpu.VMEM(shape, f32)],
        compiler_params=params(16),
        cost_estimate=cost(old[0].size * 20, old[0].size * 20),
    )(facts, came, *old, spread, *tables, *frozen)


def after(value, *others):
    return lax.optimization_barrier((value, *others))[0]


def swap(block, axes, flips):
    sizes = [lax.axis_size(a) for a in axes]
    route = []
    for t in range(sizes[0]):
        for s in range(sizes[1]):
            source = (t ^ flips[0]) * sizes[1] + (s ^ flips[1])
            route.append((source, t * sizes[1] + s))
    return lax.ppermute(block, axes, route)


def per_device(
    tokens,
    frozen_key_weight,
    output_gradient,
    counts,
    placement,
    adapter_sequence,
    adapter_down,
    adapter_up,
    down_first_moment,
    down_second_moment,
    down_average,
    up_first_moment,
    up_second_moment,
    up_average,
):
    tok_size = lax.axis_size("tok")
    tp_size, sub_size = lax.axis_size("tp"), lax.axis_size("sub")
    shards = ("tp", "sub")
    square = tp_size == 2 and sub_size == 2
    rows, wide = tokens.shape
    narrow = output_gradient.shape[1]
    key_width = frozen_key_weight.shape[1]
    owned = adapter_down.shape[0]
    slots = placement.shape[1]
    rank = ADAPTER_RANK
    flip = lambda a: jnp.swapaxes(a, 1, 2)
    down, down_m, down_v, down_a = map(
        flip, (adapter_down, down_first_moment, down_second_moment, down_average)
    )
    up, up_m, up_v, up_a = map(flip, (adapter_up, up_first_moment, up_second_moment, up_average))

    def fetch(block, slot):
        return lax.ppermute(block, "tok", [((i + slot) % tok_size, i) for i in range(tok_size)])

    def give_back(block, slot):
        return lax.ppermute(block, "tok", [((i - slot) % tok_size, i) for i in range(tok_size)])

    def shared(part):
        if not square:
            return [lax.psum(part, shards)]
        both = part + swap(part, shards, (0, 1))
        return [both, swap(both, shards, (1, 0))]

    step = min(256, wide)

    facts, *sent = pl.pallas_call(
        functools.partial(select_kernel, slots, owned, tok_size),
        out_shape=[shape_of((2 * slots,), jnp.int32)]
        + [shape_of((rank, narrow), bf16)] * slots
        + [shape_of((rank, wide), bf16)] * slots,
        in_specs=[SMEM, SMEM, SMEM, ANY, ANY],
        out_specs=[SMEM] + [VMEM] * (2 * slots),
        scratch_shapes=[pltpu.SemaphoreType.DMA((2 * slots,))],
        compiler_params=params(56),
        cost_estimate=cost(0, 4 * slots * rank * (wide + narrow)),
    )(counts, placement, adapter_sequence, down, up)
    up_send, down_send = sent[:slots], sent[slots:]
    ready = counts[0, 0] > 0
    ahead = [s for s in (1, 3) if s < slots]
    down_tables = {0: down_send[0]}
    down_tables.update((s, fetch(down_send[s], s)) for s in ahead)
    up_tables = [up_send[0]] + [fetch(up_send[s], s) for s in range(1, slots)]
    if square:
        across = swap(after(output_gradient, facts), shards, (1, 0))
        pair = jnp.stack([output_gradient, across])
        up_tables[0] = after(up_tables[0], pair, *[down_tables[s] for s in ahead])
    for s in range(2, slots):
        if s not in ahead:
            down_tables[s] = fetch(after(down_send[s], ready, *up_tables), s)
    down_tables = [down_tables[s] for s in range(slots)]

    def group(work):
        shapes = jax.eval_shape(work)
        nothing = lambda: jax.tree.map(lambda a: jnp.zeros(a.shape, a.dtype), shapes)
        return lax.cond(ready, work, nothing)

    def back_work():
        part = pl.pallas_call(
            functools.partial(back_kernel, slots),
            out_shape=shape_of((rank, rows), f32),
            in_specs=[SMEM, VMEM] + [VMEM] * slots,
            out_specs=VMEM,
            compiler_params=params(16),
            cost_estimate=cost(2 * rows * narrow * rank * slots, 2 * rows * narrow),
        )(facts, output_gradient, *up_tables)
        parts = shared(part)
        if square:
            base = pl.pallas_call(
                functools.partial(base_kernel, narrow),
                out_shape=[shape_of((2, rows, narrow), f32)] * 2,
                in_specs=[VMEM, VMEM],
                out_specs=[VMEM, VMEM],
                compiler_params=params(16),
                cost_estimate=cost(2 * rows * wide * key_width, 2 * wide * (rows + key_width)),
            )(tokens, after(frozen_key_weight, parts[0]))
            grads = [swap(pair, shards, (0, 1))]
            parts = [after(parts[0], base[0]), parts[1]]
        else:
            base = []
            grads = [lax.all_gather(output_gradient, shards, axis=1, tiled=True)]
        spread, *sends = pl.pallas_call(
            functools.partial(part_down_kernel, slots, len(parts)),
            out_shape=[shape_of((slots * rank, rows), bf16)] + [shape_of((rank, wide), bf16)] * slots,
            in_specs=[SMEM, VMEM] + [VMEM] * len(parts),
            out_specs=[VMEM] * (1 + slots),
            compiler_params=params(16),
            cost_estimate=cost(2 * rows * wide * rank * slots, 2 * rows * wide),
        )(facts, tokens, *parts)
        return grads, base, spread, sends

    grads, base, spread_back, part_down = group(back_work)
    if square:
        grads = [output_gradient, across] + grads
    came = [part_down[0]] + [
        give_back(after(part_down[s], *down_tables[1:]), s) for s in range(1, slots)
    ]

    def input_whole(spread):
        return pl.pallas_call(
            functools.partial(input_kernel, slots, narrow),
            grid=(wide // step,),
            out_shape=shape_of((rows, wide), bf16),
            in_specs=[
                pl.BlockSpec((slots * rank, rows), lambda i: (0, 0)),
                pl.BlockSpec((step, key_width), lambda i: (i, 0)),
            ]
            + [pl.BlockSpec((rank, step), lambda i: (0, i))] * slots
            + [pl.BlockSpec(g.shape, lambda i, r=g.ndim: (0,) * r) for g in grads],
            out_specs=pl.BlockSpec((rows, step), lambda i: (0, i)),
            scratch_shapes=[
                pltpu.VMEM((rows, key_width), bf16),
                pltpu.VMEM((rows, slots * rank), bf16),
            ],
            compiler_params=params(16),
            cost_estimate=cost(
                2 * rows * wide * (key_width + rank * slots), 2 * wide * (rows + key_width)
            ),
        )(spread, frozen_key_weight, *down_tables, *grads)

    def low_work():
        part = pl.pallas_call(
            functools.partial(low_kernel, slots),
            out_shape=shape_of((rank, rows), f32),
            in_specs=[SMEM, VMEM] + [VMEM] * slots,
            out_specs=VMEM,
            compiler_params=params(16),
            cost_estimate=cost(2 * rows * wide * rank * slots, 2 * rows * wide),
        )(facts, tokens, *down_tables)
        parts = shared(part)
        input_gradient = input_whole(after(spread_back, parts[0]))
        if square:
            keep, send = base
            got = swap(send, shards, (0, 1))
            frozen, passing = keep[1] + got[1], (keep[0] + got[0]).astype(bf16)
            parts = [after(parts[0], input_gradient, frozen, passing), parts[1]]
        else:
            whole = jnp.dot(tokens, frozen_key_weight, preferred_element_type=f32)
            frozen = lax.psum_scatter(whole, shards, scatter_dimension=1, tiled=True)
            passing = ()
        spread, send = pl.pallas_call(
            functools.partial(second_kernel, slots, tok_size, len(parts)),
            out_shape=[
                shape_of((slots * rank, rows), bf16),
                shape_of((tok_size, rank, narrow), bf16),
            ],
            in_specs=[SMEM] + [VMEM] * (1 + len(parts)),
            out_specs=[VMEM] * 2,
            compiler_params=params(16),
            cost_estimate=cost(2 * rows * narrow * rank * slots, 2 * rows * narrow),
        )(facts, output_gradient, *parts)
        return spread, send, frozen, passing, input_gradient

    spread_low, part_up, frozen, passing, input_gradient = group(low_work)
    came_up = lax.all_to_all(part_up, "tok", split_axis=0, concat_axis=0, tiled=True)
    frozen = [frozen]
    if square:
        frozen.append(swap(after(passing, *came[1:]), shards, (1, 0)))

    fresh_down, average_down = adam_down(facts, came, (down, down_m, down_v, down_a))
    fresh_up, average_up, key_output = last_step(
        facts,
        after(came_up, fresh_down),
        (up, up_m, up_v, up_a),
        spread_low,
        up_tables,
        frozen,
        tok_size,
    )
    return (
        key_output,
        input_gradient,
        flip(fresh_down),
        flip(fresh_up),
        flip(average_down),
        flip(average_up),
    )


def solution(mesh):
    rows = P(("groups", "tok"), ("tp", "sub"))
    cube = P(("groups", "tok"), ("tp", "sub"), None)
    return jax.shard_map(
        per_device,
        mesh=mesh,
        in_specs=(rows, P(("tp", "sub"), None), rows, P("groups", None), P("groups", None), P("groups"))
        + (cube,) * 8,
        out_specs=(rows, rows, cube, cube, cube, cube),
        check_vma=False,
    )
```

```python
import functools

import jax
import jax.numpy as jnp
from jax import lax
from jax.experimental import pallas as pl
from jax.experimental.pallas import tpu as pltpu
from jax.sharding import PartitionSpec as P

MODEL_WIDTH = 8192
ADAPTER_RANK = 64

adapter_scale = 0.5
learn_rate = 0.3
beta_one = 0.9
beta_two = 0.99
adam_eps = 1e-08
ema_decay = 0.9

LOW_SCALE = MODEL_WIDTH ** (-0.5)
BACK_SCALE = ADAPTER_RANK ** (-0.5)
MIB = 1024 * 1024

f32 = jnp.float32
bf16 = jnp.bfloat16

SMEM = pl.BlockSpec(memory_space=pltpu.SMEM)
VMEM = pl.BlockSpec(memory_space=pltpu.VMEM)
ANY = pl.BlockSpec(memory_space=pl.ANY)
HBM = pl.BlockSpec(memory_space=pltpu.HBM)


def shape_of(shape, dtype):
    return jax.ShapeDtypeStruct(tuple(shape), dtype)


SCHEDULE_SCALE = 3


def cost(flops, bytes_accessed):
    return pl.CostEstimate(
        flops=int(flops * SCHEDULE_SCALE),
        bytes_accessed=int(bytes_accessed * SCHEDULE_SCALE),
        transcendentals=0,
    )


def params(mib):
    return pltpu.CompilerParams(vmem_limit_bytes=mib * MIB)


def nt(a, b):
    return lax.dot_general(a, b, (((1,), (1,)), ((), ())), preferred_element_type=f32)


def nn(a, b):
    return lax.dot_general(a, b, (((1,), (0,)), ((), ())), preferred_element_type=f32)


def tn(a, b):
    return lax.dot_general(a, b, (((0,), (0,)), ((), ())), preferred_element_type=f32)


def facts_kernel(slots, owned, tok_size, counts, placement, sequence, facts):
    me = lax.axis_index("tok")
    total = jnp.int32(0)
    for s in range(slots):
        total = total + counts[me, s]
        facts[s] = total
        tenant = placement[lax.rem(me - s + tok_size, tok_size), s]
        place = jnp.int32(0)
        for k in range(1, owned):
            place = place + jnp.where(sequence[me * owned + k] == tenant, k, 0)
        facts[slots + s] = place


def slot_ends(facts, slots):
    return [facts[s] for s in range(slots)]


def slot_mask(ends, slot, shape):
    rows = lax.broadcasted_iota(jnp.int32, shape, 1)
    inside = rows < ends[slot]
    if slot:
        inside = inside & (rows >= ends[slot - 1])
    return inside


def pick_slot(ends, products, rank):
    rows = lax.broadcasted_iota(jnp.int32, (rank, products.shape[1]), 1)
    slots = products.shape[0] // rank
    out = products[(slots - 1) * rank :]
    for s in range(slots - 2, -1, -1):
        out = jnp.where(rows < ends[s], products[s * rank : (s + 1) * rank], out)
    return out


def spread_slots(ends, values):
    wide = values.astype(f32)
    return jnp.concatenate(
        [jnp.where(slot_mask(ends, s, wide.shape), wide, 0.0) for s in range(len(ends))], axis=0
    ).astype(bf16)


def paired_sum(refs):
    parts = [ref[...] for ref in refs]
    while len(parts) > 1:
        parts = [parts[i] + parts[i + 1] for i in range(0, len(parts), 2)]
    return parts[0]


def select_kernel(slots, owned, tok_size, counts, placement, sequence, down, up, facts, *rest):
    ups, downs, sems = rest[:slots], rest[slots : 2 * slots], rest[2 * slots]
    facts_kernel(slots, owned, tok_size, counts, placement, sequence, facts)
    copies = []
    order = list(range(1, slots)) + [0]
    for s in order:
        copies.append(pltpu.make_async_copy(up.at[facts[slots + s]], ups[s], sems.at[s]))
    for s in order:
        copies.append(pltpu.make_async_copy(down.at[facts[slots + s]], downs[s], sems.at[slots + s]))
    for copy in copies:
        copy.start()
    for copy in copies:
        copy.wait()


def base_kernel(width, tokens, weight, keep, send):
    tp, sub = lax.axis_index("tp"), lax.axis_index("sub")
    mine, other = tp, 1 - tp
    for ref, s in ((send, 1 - sub), (keep, sub)):
        for i, t in enumerate((other, mine)):
            start = pl.multiple_of((t * 2 + s) * width, width)
            ref[i] = nn(tokens[...], weight[:, pl.ds(start, width)])


def stacked(tables):
    return jnp.concatenate([t[...] for t in tables], axis=0)


def back_kernel(slots, facts, grad, *rest):
    tables, out = rest[:slots], rest[slots]
    out[...] = pick_slot(slot_ends(facts, slots), nt(stacked(tables), grad[...]), ADAPTER_RANK)


def part_down_kernel(slots, tok_size, pieces, facts, tokens, *rest):
    parts, spread_out, outs, stack = rest[:pieces], rest[pieces], rest[pieces + 1 : -1], rest[-1]
    me = lax.axis_index("tok")
    ends = slot_ends(facts, slots)
    back = (paired_sum(parts) * BACK_SCALE).astype(bf16)
    spread = spread_slots(ends, back)
    spread_out[...] = spread
    first = outs[0].shape[1]
    for c in range(0, tokens.shape[1], 256):
        end = min(c + 256, tokens.shape[1])
        product = (nn(spread, tokens[:, c:end]) * (adapter_scale * LOW_SCALE)).astype(bf16)
        for s in range(slots):
            piece = product[s * ADAPTER_RANK : (s + 1) * ADAPTER_RANK]
            if c < first:
                outs[s][:, c:end] = piece
            else:
                stack[lax.rem(me + s, tok_size), :, c - first : end - first] = piece


def low_kernel(slots, facts, tokens, *rest):
    tables, out = rest[:slots], rest[slots]
    out[...] = pick_slot(slot_ends(facts, slots), nt(stacked(tables), tokens[...]), ADAPTER_RANK)


def input_kernel(slots, width, spread, weight, *rest):
    tables, grads, (out, whole, turned) = rest[:slots], rest[slots:-3], rest[-3:]

    @pl.when(pl.program_id(0) == 0)
    def _():
        turned[...] = spread[...].astype(f32).T.astype(bf16)
        if len(grads) == 1:
            whole[...] = grads[0][...]
        else:
            tp, sub = lax.axis_index("tp"), lax.axis_index("sub")
            pieces = (grads[0][...], grads[1][...], grads[2][0], grads[2][1])
            for piece, t, s in zip(pieces, (tp, 1 - tp, tp, 1 - tp), (sub, sub, 1 - sub, 1 - sub)):
                start = pl.multiple_of((t * 2 + s) * width, width)
                whole[:, pl.ds(start, width)] = piece

    frozen = None
    for start in range(0, whole.shape[1], 256):
        term = nt(whole[:, start : start + 256], weight[:, start : start + 256])
        frozen = term if frozen is None else frozen + term
    adapter = nn(turned[...], stacked(tables))
    out[...] = (frozen + (adapter_scale * LOW_SCALE) * adapter).astype(bf16)


def second_kernel(slots, pieces, facts, grad, *rest):
    parts, spread_low, outs = rest[:pieces], rest[pieces], rest[pieces + 1 :]
    low = (paired_sum(parts) * LOW_SCALE).astype(bf16)
    spread = spread_slots(slot_ends(facts, slots), low)
    spread_low[...] = spread
    product = (nn(spread, grad[...]) * (adapter_scale * BACK_SCALE)).astype(bf16)
    for s in range(slots):
        outs[s][...] = product[s * ADAPTER_RANK : (s + 1) * ADAPTER_RANK]


def adam_step(weights, mean_old, var_old, avg_old, gradient):
    mean_new = beta_one * mean_old + (1.0 - beta_one) * gradient
    var_new = beta_two * var_old + (1.0 - beta_two) * gradient * gradient
    root = var_new * lax.rsqrt(var_new) + adam_eps
    inverse = pl.reciprocal(root, approx=True)
    inverse = inverse * (2.0 - root * inverse)
    updated = weights.astype(f32) - learn_rate * mean_new * inverse
    return updated.astype(bf16), ema_decay * avg_old + (1.0 - ema_decay) * updated


def each_rows(count, body):
    rows = 16

    def step(i, _):
        body(pl.ds(pl.multiple_of(i * rows, rows), rows), rows)
        return 0

    lax.fori_loop(0, count // rows, step, 0)


def adam_kernel(slots, tok_size, first, extras, count, facts, *rest):
    came, old, rest = rest[:count], rest[count : count + 4], rest[count + 4 + extras :]
    fresh, average, came_here = rest[:3]
    old_here, rest = rest[3:7], rest[7:]
    fresh_here, average_here, gradient_ref, in_sems, out_sems = rest
    owned, rank, width = fresh_here.shape
    columns = pl.ds(first, width)
    me = lax.axis_index("tok")

    arrivals = []
    for s in range(slots):
        block = came[s] if count > 1 else came[0].at[lax.rem(me - s + tok_size, tok_size)]
        arrivals.append(pltpu.make_async_copy(block, came_here.at[s], in_sems.at[s]))
    loads, stores = [], []
    for k in range(owned):
        for i in range(4):
            sem = in_sems.at[slots + 4 * k + i]
            block = old[i].at[k, :, columns]
            loads.append(pltpu.make_async_copy(block, old_here[i].at[k], sem))
        for i, (here, there) in enumerate(((fresh_here, fresh), (average_here, average))):
            sem = out_sems.at[2 * k + i]
            stores.append(pltpu.make_async_copy(here.at[k], there.at[k, :, columns], sem))
    for copy in arrivals + loads:
        copy.start()

    for copy in arrivals:
        copy.wait()
    for k in range(owned):

        def clear(r, rows):
            gradient_ref[r, :] = jnp.zeros((rows, width), f32)

        each_rows(rank, clear)
        for s in range(slots):

            @pl.when(facts[slots + s] == k)
            def _():
                def add(r, rows):
                    gradient_ref[r, :] += came_here[s, r, :].astype(f32)

                each_rows(rank, add)

        for copy in loads[4 * k : 4 * k + 4]:
            copy.wait()

        def update(r, rows):
            for c in range(0, width, 512):
                columns = slice(c, min(c + 512, width))
                fresh_here[k, r, columns], average_here[k, r, columns] = adam_step(
                    *[ref[k, r, columns] for ref in old_here], gradient_ref[r, columns]
                )

        each_rows(rank, update)
        for copy in stores[2 * k : 2 * k + 2]:
            copy.start()
    for copy in stores:
        copy.wait()


def adam_down(facts, came, old, first, into, slots, tok_size):
    owned, rank, _ = old[0].shape
    width = came[0].shape[-1]
    count = len(came)
    shapes = [shape_of(old[0].shape, bf16), shape_of(old[0].shape, f32)]
    part = (owned, rank, width)
    return pl.pallas_call(
        functools.partial(adam_kernel, slots, tok_size, first, len(into), count),
        out_shape=shapes,
        in_specs=[SMEM] + [ANY] * (count + 4 + len(into)),
        out_specs=[ANY] * 2,
        scratch_shapes=[pltpu.VMEM((slots, rank, width), bf16)]
        + [pltpu.VMEM(part, a.dtype) for a in old]
        + [
            pltpu.VMEM(part, bf16),
            pltpu.VMEM(part, f32),
            pltpu.VMEM((rank, width), f32),
            pltpu.SemaphoreType.DMA((slots + 4 * owned,)),
            pltpu.SemaphoreType.DMA((2 * owned,)),
        ],
        input_output_aliases={5 + count + i: i for i in range(len(into))},
        compiler_params=params(60),
        cost_estimate=cost(owned * rank * width * 20, owned * rank * width * 40),
    )(facts, *came, *old, *into)


def last_kernel(slots, facts, *rest):
    came, old, rest = rest[:slots], rest[slots : slots + 4], rest[slots + 4 :]
    spread, tables, frozen = rest[0], rest[1 : 1 + slots], rest[1 + slots : -4]
    fresh, average, key_out, gradients = rest[-4:]
    raised = nn(spread[...].astype(f32).T.astype(bf16), stacked(tables))
    whole = frozen[0][...]
    for part in frozen[1:]:
        whole = whole + part[...].astype(f32)
    key_out[...] = (whole + (adapter_scale * BACK_SCALE) * raised).astype(bf16)
    gradients[...] = jnp.zeros(gradients.shape, f32)
    for s in range(slots):
        gradients[facts[slots + s]] += came[s][...].astype(f32)
    owned, rank, _ = gradients.shape
    for k in range(owned):

        def update(r, rows):
            fresh[k, r, :], average[k, r, :] = adam_step(
                *[ref[k, r, :] for ref in old], gradients[k, r, :]
            )

        each_rows(rank, update)


def last_step(facts, came, old, spread, tables, frozen):
    shape = old[0].shape
    slots = len(tables)
    return pl.pallas_call(
        functools.partial(last_kernel, slots),
        out_shape=[
            shape_of(shape, bf16),
            shape_of(shape, f32),
            shape_of(frozen[0].shape, bf16),
        ],
        in_specs=[SMEM] + [VMEM] * (5 + 2 * slots + len(frozen)),
        out_specs=[VMEM] * 3,
        scratch_shapes=[pltpu.VMEM(shape, f32)],
        compiler_params=params(16),
        cost_estimate=cost(old[0].size * 20, old[0].size * 20),
    )(facts, *came, *old, spread, *tables, *frozen)


def after(value, *others):
    return lax.optimization_barrier((value, *others))[0]


def swap(block, axes, flips):
    sizes = [lax.axis_size(a) for a in axes]
    route = []
    for t in range(sizes[0]):
        for s in range(sizes[1]):
            source = (t ^ flips[0]) * sizes[1] + (s ^ flips[1])
            route.append((source, t * sizes[1] + s))
    return lax.ppermute(block, axes, route)


def per_device(
    tokens,
    frozen_key_weight,
    output_gradient,
    counts,
    placement,
    adapter_sequence,
    adapter_down,
    adapter_up,
    down_first_moment,
    down_second_moment,
    down_average,
    up_first_moment,
    up_second_moment,
    up_average,
):
    tok_size = lax.axis_size("tok")
    tp_size, sub_size = lax.axis_size("tp"), lax.axis_size("sub")
    shards = ("tp", "sub")
    square = tp_size == 2 and sub_size == 2
    rows, wide = tokens.shape
    narrow = output_gradient.shape[1]
    key_width = frozen_key_weight.shape[1]
    owned = adapter_down.shape[0]
    slots = placement.shape[1]
    rank = ADAPTER_RANK
    flip = lambda a: jnp.swapaxes(a, 1, 2)
    down, down_m, down_v, down_a = map(
        flip, (adapter_down, down_first_moment, down_second_moment, down_average)
    )
    up, up_m, up_v, up_a = map(flip, (adapter_up, up_first_moment, up_second_moment, up_average))

    def fetch(block, slot):
        return lax.ppermute(block, "tok", [((i + slot) % tok_size, i) for i in range(tok_size)])

    def give_back(block, slot):
        return lax.ppermute(block, "tok", [((i - slot) % tok_size, i) for i in range(tok_size)])

    def shared(part):
        if not square:
            return [lax.psum(part, shards)]
        both = part + swap(part, shards, (0, 1))
        return [both, swap(both, shards, (1, 0))]

    step = min(256, wide)
    first = wide // 2

    facts, *sent = pl.pallas_call(
        functools.partial(select_kernel, slots, owned, tok_size),
        out_shape=[shape_of((2 * slots,), jnp.int32)]
        + [shape_of((rank, narrow), bf16)] * slots
        + [shape_of((rank, wide), bf16)] * slots,
        in_specs=[SMEM, SMEM, SMEM, ANY, ANY],
        out_specs=[SMEM] + [VMEM] * (2 * slots),
        scratch_shapes=[pltpu.SemaphoreType.DMA((2 * slots,))],
        compiler_params=params(56),
        cost_estimate=cost(0, 4 * slots * rank * (wide + narrow)),
    )(counts, placement, adapter_sequence, down, up)
    up_send, down_send = sent[:slots], sent[slots:]
    ready = counts[0, 0] > 0
    ahead = [s for s in (1, 3) if s < slots]
    down_tables = {0: down_send[0]}
    down_tables.update((s, fetch(down_send[s], s)) for s in ahead)
    up_tables = [up_send[0]] + [fetch(up_send[s], s) for s in range(1, slots)]
    if square:
        across = swap(after(output_gradient, facts), shards, (1, 0))
        pair = jnp.stack([output_gradient, across])
        up_tables[0] = after(up_tables[0], pair, *[down_tables[s] for s in ahead])
    for s in range(2, slots):
        if s not in ahead:
            down_tables[s] = fetch(after(down_send[s], ready, *up_tables), s)
    down_tables = [down_tables[s] for s in range(slots)]

    def group(work):
        shapes = jax.eval_shape(work)
        nothing = lambda: jax.tree.map(lambda a: jnp.zeros(a.shape, a.dtype), shapes)
        return lax.cond(ready, work, nothing)

    def back_work():
        part = pl.pallas_call(
            functools.partial(back_kernel, slots),
            out_shape=shape_of((rank, rows), f32),
            in_specs=[SMEM, VMEM] + [VMEM] * slots,
            out_specs=VMEM,
            compiler_params=params(16),
            cost_estimate=cost(2 * rows * narrow * rank * slots, 2 * rows * narrow),
        )(facts, output_gradient, *up_tables)
        parts = shared(part)
        if square:
            base = pl.pallas_call(
                functools.partial(base_kernel, narrow),
                out_shape=[shape_of((2, rows, narrow), f32)] * 2,
                in_specs=[VMEM, VMEM],
                out_specs=[VMEM, VMEM],
                compiler_params=params(16),
                cost_estimate=cost(2 * rows * wide * key_width, 2 * wide * (rows + key_width)),
            )(tokens, after(frozen_key_weight, parts[0]))
            grads = [swap(pair, shards, (0, 1))]
            parts = [after(parts[0], base[0]), parts[1]]
        else:
            base = []
            grads = [lax.all_gather(output_gradient, shards, axis=1, tiled=True)]
        spread, *sends = pl.pallas_call(
            functools.partial(part_down_kernel, slots, tok_size, len(parts)),
            out_shape=[shape_of((slots * rank, rows), bf16)]
            + [shape_of((rank, first), bf16)] * slots
            + [shape_of((tok_size, rank, wide - first), bf16)],
            in_specs=[SMEM, VMEM] + [VMEM] * len(parts),
            out_specs=[VMEM] * (2 + slots),
            compiler_params=params(16),
            cost_estimate=cost(2 * rows * wide * rank * slots, 2 * rows * wide),
        )(facts, tokens, *parts)
        return grads, base, spread, sends

    grads, base, spread_back, part_down = group(back_work)
    if square:
        grads = [output_gradient, across] + grads
    came_first = [part_down[0]] + [
        give_back(after(part_down[s], *down_tables[1:]), s) for s in range(1, slots)
    ]
    came_second = lax.all_to_all(
        after(part_down[-1], *down_tables[1:]), "tok", split_axis=0, concat_axis=0, tiled=True
    )

    def input_whole(spread):
        return pl.pallas_call(
            functools.partial(input_kernel, slots, narrow),
            grid=(wide // step,),
            out_shape=shape_of((rows, wide), bf16),
            in_specs=[
                pl.BlockSpec((slots * rank, rows), lambda i: (0, 0)),
                pl.BlockSpec((step, key_width), lambda i: (i, 0)),
            ]
            + [pl.BlockSpec((rank, step), lambda i: (0, i))] * slots
            + [pl.BlockSpec(g.shape, lambda i, r=g.ndim: (0,) * r) for g in grads],
            out_specs=pl.BlockSpec((rows, step), lambda i: (0, i)),
            scratch_shapes=[
                pltpu.VMEM((rows, key_width), bf16),
                pltpu.VMEM((rows, slots * rank), bf16),
            ],
            compiler_params=params(16),
            cost_estimate=cost(
                2 * rows * wide * (key_width + rank * slots), 2 * wide * (rows + key_width)
            ),
        )(spread, frozen_key_weight, *down_tables, *grads)

    def low_work():
        part = pl.pallas_call(
            functools.partial(low_kernel, slots),
            out_shape=shape_of((rank, rows), f32),
            in_specs=[SMEM, VMEM] + [VMEM] * slots,
            out_specs=VMEM,
            compiler_params=params(16),
            cost_estimate=cost(2 * rows * wide * rank * slots, 2 * rows * wide),
        )(facts, tokens, *down_tables)
        parts = shared(part)
        input_gradient = input_whole(after(spread_back, parts[0]))
        if square:
            keep, send = base
            got = swap(send, shards, (0, 1))
            frozen, passing = keep[1] + got[1], (keep[0] + got[0]).astype(bf16)
            parts = [after(parts[0], input_gradient, frozen, passing), parts[1]]
        else:
            whole = jnp.dot(tokens, frozen_key_weight, preferred_element_type=f32)
            frozen = lax.psum_scatter(whole, shards, scatter_dimension=1, tiled=True)
            passing = ()
        spread, *sends = pl.pallas_call(
            functools.partial(second_kernel, slots, len(parts)),
            out_shape=[shape_of((slots * rank, rows), bf16)] + [shape_of((rank, narrow), bf16)] * slots,
            in_specs=[SMEM] + [VMEM] * (1 + len(parts)),
            out_specs=[VMEM] * (1 + slots),
            compiler_params=params(16),
            cost_estimate=cost(2 * rows * narrow * rank * slots, 2 * rows * narrow),
        )(facts, output_gradient, *parts)
        return spread, sends, frozen, passing, input_gradient

    spread_low, part_up, frozen, passing, input_gradient = group(low_work)
    came_up = [part_up[0]] + [
        give_back(after(part_up[s], *came_first[1:]), s) for s in range(1, slots)
    ]
    frozen = [frozen]
    if square:
        frozen.append(swap(after(passing, *came_first[1:]), shards, (1, 0)))

    down_old = (down, down_m, down_v, down_a)
    done = adam_down(facts, came_first, down_old, 0, (), slots, tok_size)
    fresh_down, average_down = adam_down(
        facts, [after(came_second, done[0])], down_old, first, done, slots, tok_size
    )
    came_up[0] = after(came_up[0], fresh_down)
    fresh_up, average_up, key_output = last_step(
        facts, came_up, (up, up_m, up_v, up_a), spread_low, up_tables, frozen
    )
    return (
        key_output,
        input_gradient,
        flip(fresh_down),
        flip(fresh_up),
        flip(average_down),
        flip(average_up),
    )


def solution(mesh):
    rows = P(("groups", "tok"), ("tp", "sub"))
    cube = P(("groups", "tok"), ("tp", "sub"), None)
    return jax.shard_map(
        per_device,
        mesh=mesh,
        in_specs=(rows, P(("tp", "sub"), None), rows, P("groups", None), P("groups", None), P("groups"))
        + (cube,) * 8,
        out_specs=(rows, rows, cube, cube, cube, cube),
        check_vma=False,
    )
```

```python
import functools

import jax
import jax.numpy as jnp
from jax import lax
from jax.experimental import pallas as pl
from jax.experimental.pallas import tpu as pltpu
from jax.sharding import PartitionSpec as P

MODEL_WIDTH = 8192
ADAPTER_RANK = 64

adapter_scale = 0.5
learn_rate = 0.3
beta_one = 0.9
beta_two = 0.99
adam_eps = 1e-08
ema_decay = 0.9

LOW_SCALE = MODEL_WIDTH ** (-0.5)
BACK_SCALE = ADAPTER_RANK ** (-0.5)
MIB = 1024 * 1024

f32 = jnp.float32
bf16 = jnp.bfloat16

SMEM = pl.BlockSpec(memory_space=pltpu.SMEM)
VMEM = pl.BlockSpec(memory_space=pltpu.VMEM)
ANY = pl.BlockSpec(memory_space=pl.ANY)
HBM = pl.BlockSpec(memory_space=pltpu.HBM)


def shape_of(shape, dtype):
    return jax.ShapeDtypeStruct(tuple(shape), dtype)


SCHEDULE_SCALE = 3


def cost(flops, bytes_accessed):
    return pl.CostEstimate(
        flops=int(flops * SCHEDULE_SCALE),
        bytes_accessed=int(bytes_accessed * SCHEDULE_SCALE),
        transcendentals=0,
    )


def params(mib):
    return pltpu.CompilerParams(vmem_limit_bytes=mib * MIB)


def nt(a, b):
    return lax.dot_general(a, b, (((1,), (1,)), ((), ())), preferred_element_type=f32)


def nn(a, b):
    return lax.dot_general(a, b, (((1,), (0,)), ((), ())), preferred_element_type=f32)


def tn(a, b):
    return lax.dot_general(a, b, (((0,), (0,)), ((), ())), preferred_element_type=f32)


def facts_kernel(slots, owned, tok_size, counts, placement, sequence, facts):
    me = lax.axis_index("tok")
    total = jnp.int32(0)
    for s in range(slots):
        total = total + counts[me, s]
        facts[s] = total
        tenant = placement[lax.rem(me - s + tok_size, tok_size), s]
        place = jnp.int32(0)
        for k in range(1, owned):
            place = place + jnp.where(sequence[me * owned + k] == tenant, k, 0)
        facts[slots + s] = place


def slot_ends(facts, slots):
    return [facts[s] for s in range(slots)]


def slot_mask(ends, slot, shape):
    rows = lax.broadcasted_iota(jnp.int32, shape, 1)
    inside = rows < ends[slot]
    if slot:
        inside = inside & (rows >= ends[slot - 1])
    return inside


def pick_slot(ends, products, rank):
    rows = lax.broadcasted_iota(jnp.int32, (rank, products.shape[1]), 1)
    slots = products.shape[0] // rank
    out = products[(slots - 1) * rank :]
    for s in range(slots - 2, -1, -1):
        out = jnp.where(rows < ends[s], products[s * rank : (s + 1) * rank], out)
    return out


def spread_slots(ends, values):
    wide = values.astype(f32)
    return jnp.concatenate(
        [jnp.where(slot_mask(ends, s, wide.shape), wide, 0.0) for s in range(len(ends))], axis=0
    ).astype(bf16)


def paired_sum(refs):
    parts = [ref[...] for ref in refs]
    while len(parts) > 1:
        parts = [parts[i] + parts[i + 1] for i in range(0, len(parts), 2)]
    return parts[0]


def select_kernel(slots, owned, tok_size, counts, placement, sequence, down, up, facts, *rest):
    ups, downs, sems = rest[:slots], rest[slots : 2 * slots], rest[2 * slots]
    facts_kernel(slots, owned, tok_size, counts, placement, sequence, facts)
    copies = []
    order = list(range(1, slots)) + [0]
    for s in order:
        copies.append(pltpu.make_async_copy(up.at[facts[slots + s]], ups[s], sems.at[s]))
    for s in order:
        copies.append(pltpu.make_async_copy(down.at[facts[slots + s]], downs[s], sems.at[slots + s]))
    for copy in copies:
        copy.start()
    for copy in copies:
        copy.wait()


def base_kernel(width, tokens, weight, keep, send):
    tp, sub = lax.axis_index("tp"), lax.axis_index("sub")
    mine, other = tp, 1 - tp
    for ref, s in ((send, 1 - sub), (keep, sub)):
        for i, t in enumerate((other, mine)):
            start = pl.multiple_of((t * 2 + s) * width, width)
            ref[i] = nn(tokens[...], weight[:, pl.ds(start, width)])


def stacked(tables):
    return jnp.concatenate([t[...] for t in tables], axis=0)


def back_kernel(slots, facts, grad, *rest):
    tables, out = rest[:slots], rest[slots]
    out[...] = pick_slot(slot_ends(facts, slots), nt(stacked(tables), grad[...]), ADAPTER_RANK)


def part_down_kernel(slots, pieces, facts, tokens, *rest):
    parts, spread_out, outs = rest[:pieces], rest[pieces], rest[pieces + 1 :]
    ends = slot_ends(facts, slots)
    back = (paired_sum(parts) * BACK_SCALE).astype(bf16)
    spread = spread_slots(ends, back)
    spread_out[...] = spread
    for c in range(0, tokens.shape[1], 256):
        columns = slice(c, min(c + 256, tokens.shape[1]))
        product = (nn(spread, tokens[:, columns]) * (adapter_scale * LOW_SCALE)).astype(bf16)
        for s in range(slots):
            outs[s][:, columns] = product[s * ADAPTER_RANK : (s + 1) * ADAPTER_RANK]


def low_kernel(slots, facts, tokens, *rest):
    tables, out = rest[:slots], rest[slots]
    out[...] = pick_slot(slot_ends(facts, slots), nt(stacked(tables), tokens[...]), ADAPTER_RANK)


def input_kernel(slots, width, spread, weight, *rest):
    tables, grads, (out, whole, turned) = rest[:slots], rest[slots:-3], rest[-3:]

    @pl.when(pl.program_id(0) == 0)
    def _():
        turned[...] = spread[...].astype(f32).T.astype(bf16)
        if len(grads) == 1:
            whole[...] = grads[0][...]
        else:
            tp, sub = lax.axis_index("tp"), lax.axis_index("sub")
            pieces = (grads[0][...], grads[1][...], grads[2][0], grads[2][1])
            for piece, t, s in zip(pieces, (tp, 1 - tp, tp, 1 - tp), (sub, sub, 1 - sub, 1 - sub)):
                start = pl.multiple_of((t * 2 + s) * width, width)
                whole[:, pl.ds(start, width)] = piece

    frozen = None
    for start in range(0, whole.shape[1], 256):
        term = nt(whole[:, start : start + 256], weight[:, start : start + 256])
        frozen = term if frozen is None else frozen + term
    adapter = nn(turned[...], stacked(tables))
    out[...] = (frozen + (adapter_scale * LOW_SCALE) * adapter).astype(bf16)


def second_kernel(slots, tok_size, pieces, facts, grad, *rest):
    parts, (spread_low, out) = rest[:pieces], rest[pieces:]
    me = lax.axis_index("tok")
    low = (paired_sum(parts) * LOW_SCALE).astype(bf16)
    spread = spread_slots(slot_ends(facts, slots), low)
    spread_low[...] = spread
    product = (nn(spread, grad[...]) * (adapter_scale * BACK_SCALE)).astype(bf16)
    for s in range(slots):
        out[lax.rem(me + s, tok_size)] = product[s * ADAPTER_RANK : (s + 1) * ADAPTER_RANK]


def adam_step(weights, mean_old, var_old, avg_old, gradient):
    mean_new = beta_one * mean_old + (1.0 - beta_one) * gradient
    var_new = beta_two * var_old + (1.0 - beta_two) * gradient * gradient
    root = var_new * lax.rsqrt(var_new) + adam_eps
    inverse = pl.reciprocal(root, approx=True)
    inverse = inverse * (2.0 - root * inverse)
    updated = weights.astype(f32) - learn_rate * mean_new * inverse
    return updated.astype(bf16), ema_decay * avg_old + (1.0 - ema_decay) * updated


def each_rows(count, body):
    rows = 16

    def step(i, _):
        body(pl.ds(pl.multiple_of(i * rows, rows), rows), rows)
        return 0

    lax.fori_loop(0, count // rows, step, 0)


def adam_kernel(slots, facts, *rest):
    came, old, rest = rest[:slots], rest[slots : slots + 4], rest[slots + 4 :]
    fresh, average, fresh_here, average_here, gradient_ref, out_sems = rest
    owned, rank, width = fresh_here.shape
    stores = []
    for k in range(owned):
        for i, (here, there) in enumerate(((fresh_here, fresh), (average_here, average))):
            sem = out_sems.at[2 * k + i]
            stores.append(pltpu.make_async_copy(here.at[k], there.at[k], sem))
    for k in range(owned):

        def clear(r, rows):
            gradient_ref[r, :] = jnp.zeros((rows, width), f32)

        each_rows(rank, clear)
        for s in range(slots):

            @pl.when(facts[slots + s] == k)
            def _():
                def add(r, rows):
                    gradient_ref[r, :] += came[s][r, :].astype(f32)

                each_rows(rank, add)

        def update(r, rows):
            for c in range(0, width, 512):
                columns = slice(c, min(c + 512, width))
                fresh_here[k, r, columns], average_here[k, r, columns] = adam_step(
                    *[ref[k, r, columns] for ref in old], gradient_ref[r, columns]
                )

        each_rows(rank, update)
        for copy in stores[2 * k : 2 * k + 2]:
            copy.start()
    for copy in stores:
        copy.wait()


def adam_down(facts, came, old):
    owned, rank, width = old[0].shape
    slots = len(came)
    shapes = [shape_of(old[0].shape, bf16), shape_of(old[0].shape, f32)]
    return pl.pallas_call(
        functools.partial(adam_kernel, slots),
        out_shape=shapes,
        in_specs=[SMEM] + [VMEM] * (slots + 4),
        out_specs=[ANY] * 2,
        scratch_shapes=[
            pltpu.VMEM(old[0].shape, bf16),
            pltpu.VMEM(old[0].shape, f32),
            pltpu.VMEM((rank, width), f32),
            pltpu.SemaphoreType.DMA((2 * owned,)),
        ],
        compiler_params=params(20),
        cost_estimate=cost(owned * rank * width * 20, owned * rank * width * 60),
    )(facts, *came, *old)


def last_kernel(slots, tok_size, facts, came, *rest):
    old, rest = rest[:4], rest[4:]
    spread, tables, frozen = rest[0], rest[1 : 1 + slots], rest[1 + slots : -4]
    fresh, average, key_out, gradients = rest[-4:]
    raised = nn(spread[...].astype(f32).T.astype(bf16), stacked(tables))
    whole = frozen[0][...]
    for part in frozen[1:]:
        whole = whole + part[...].astype(f32)
    key_out[...] = (whole + (adapter_scale * BACK_SCALE) * raised).astype(bf16)
    me = lax.axis_index("tok")
    gradients[...] = jnp.zeros(gradients.shape, f32)
    for s in range(slots):
        gradients[facts[slots + s]] += came[lax.rem(me - s + tok_size, tok_size)].astype(f32)
    owned, rank, _ = gradients.shape
    for k in range(owned):

        def update(r, rows):
            fresh[k, r, :], average[k, r, :] = adam_step(
                *[ref[k, r, :] for ref in old], gradients[k, r, :]
            )

        each_rows(rank, update)


def last_step(facts, came, old, spread, tables, frozen, tok_size):
    shape = old[0].shape
    slots = len(tables)
    return pl.pallas_call(
        functools.partial(last_kernel, slots, tok_size),
        out_shape=[
            shape_of(shape, bf16),
            shape_of(shape, f32),
            shape_of(frozen[0].shape, bf16),
        ],
        in_specs=[SMEM] + [VMEM] * (6 + slots + len(frozen)),
        out_specs=[VMEM] * 3,
        scratch_shapes=[pltpu.VMEM(shape, f32)],
        compiler_params=params(16),
        cost_estimate=cost(old[0].size * 20, old[0].size * 20),
    )(facts, came, *old, spread, *tables, *frozen)


def after(value, *others):
    return lax.optimization_barrier((value, *others))[0]


def swap(block, axes, flips):
    sizes = [lax.axis_size(a) for a in axes]
    route = []
    for t in range(sizes[0]):
        for s in range(sizes[1]):
            source = (t ^ flips[0]) * sizes[1] + (s ^ flips[1])
            route.append((source, t * sizes[1] + s))
    return lax.ppermute(block, axes, route)


def per_device(
    tokens,
    frozen_key_weight,
    output_gradient,
    counts,
    placement,
    adapter_sequence,
    adapter_down,
    adapter_up,
    down_first_moment,
    down_second_moment,
    down_average,
    up_first_moment,
    up_second_moment,
    up_average,
):
    tok_size = lax.axis_size("tok")
    tp_size, sub_size = lax.axis_size("tp"), lax.axis_size("sub")
    shards = ("tp", "sub")
    square = tp_size == 2 and sub_size == 2
    rows, wide = tokens.shape
    narrow = output_gradient.shape[1]
    key_width = frozen_key_weight.shape[1]
    owned = adapter_down.shape[0]
    slots = placement.shape[1]
    rank = ADAPTER_RANK
    flip = lambda a: jnp.swapaxes(a, 1, 2)
    down, down_m, down_v, down_a = map(
        flip, (adapter_down, down_first_moment, down_second_moment, down_average)
    )
    up, up_m, up_v, up_a = map(flip, (adapter_up, up_first_moment, up_second_moment, up_average))

    def fetch(block, slot):
        return lax.ppermute(block, "tok", [((i + slot) % tok_size, i) for i in range(tok_size)])

    def give_back(block, slot):
        return lax.ppermute(block, "tok", [((i - slot) % tok_size, i) for i in range(tok_size)])

    def shared(part):
        if not square:
            return [lax.psum(part, shards)]
        both = part + swap(part, shards, (0, 1))
        return [both, swap(both, shards, (1, 0))]

    step = min(256, wide)

    facts, *sent = pl.pallas_call(
        functools.partial(select_kernel, slots, owned, tok_size),
        out_shape=[shape_of((2 * slots,), jnp.int32)]
        + [shape_of((rank, narrow), bf16)] * slots
        + [shape_of((rank, wide), bf16)] * slots,
        in_specs=[SMEM, SMEM, SMEM, ANY, ANY],
        out_specs=[SMEM] + [VMEM] * (2 * slots),
        scratch_shapes=[pltpu.SemaphoreType.DMA((2 * slots,))],
        compiler_params=params(56),
        cost_estimate=cost(0, 4 * slots * rank * (wide + narrow)),
    )(counts, placement, adapter_sequence, down, up)
    up_send, down_send = sent[:slots], sent[slots:]
    ready = counts[0, 0] > 0
    ahead = [s for s in (1, 3) if s < slots]
    down_tables = {0: down_send[0]}
    down_tables.update((s, fetch(down_send[s], s)) for s in ahead)
    up_tables = [up_send[0]] + [fetch(up_send[s], s) for s in range(1, slots)]
    if square:
        across = swap(after(output_gradient, facts), shards, (1, 0))
        pair = jnp.stack([output_gradient, across])
        up_tables[0] = after(up_tables[0], pair, *[down_tables[s] for s in ahead])
    for s in range(2, slots):
        if s not in ahead:
            down_tables[s] = fetch(after(down_send[s], ready, *up_tables), s)
    down_tables = [down_tables[s] for s in range(slots)]

    def group(work):
        shapes = jax.eval_shape(work)
        nothing = lambda: jax.tree.map(lambda a: jnp.zeros(a.shape, a.dtype), shapes)
        return lax.cond(ready, work, nothing)

    def back_work():
        part = pl.pallas_call(
            functools.partial(back_kernel, slots),
            out_shape=shape_of((rank, rows), f32),
            in_specs=[SMEM, VMEM] + [VMEM] * slots,
            out_specs=VMEM,
            compiler_params=params(16),
            cost_estimate=cost(2 * rows * narrow * rank * slots, 2 * rows * narrow),
        )(facts, output_gradient, *up_tables)
        parts = shared(part)
        if square:
            base = pl.pallas_call(
                functools.partial(base_kernel, narrow),
                out_shape=[shape_of((2, rows, narrow), f32)] * 2,
                in_specs=[VMEM, VMEM],
                out_specs=[VMEM, VMEM],
                compiler_params=params(16),
                cost_estimate=cost(2 * rows * wide * key_width, 2 * wide * (rows + key_width)),
            )(tokens, after(frozen_key_weight, parts[0]))
            grads = [swap(pair, shards, (0, 1))]
            parts = [after(parts[0], base[0]), parts[1]]
        else:
            base = []
            grads = [lax.all_gather(output_gradient, shards, axis=1, tiled=True)]
        spread, *sends = pl.pallas_call(
            functools.partial(part_down_kernel, slots, len(parts)),
            out_shape=[shape_of((slots * rank, rows), bf16)] + [shape_of((rank, wide), bf16)] * slots,
            in_specs=[SMEM, VMEM] + [VMEM] * len(parts),
            out_specs=[VMEM] * (1 + slots),
            compiler_params=params(16),
            cost_estimate=cost(2 * rows * wide * rank * slots, 2 * rows * wide),
        )(facts, tokens, *parts)
        return grads, base, spread, sends

    grads, base, spread_back, part_down = group(back_work)
    if square:
        grads = [output_gradient, across] + grads
    came = [part_down[0]] + [
        give_back(after(part_down[s], *down_tables[1:]), s) for s in range(1, slots)
    ]

    def input_whole(spread):
        return pl.pallas_call(
            functools.partial(input_kernel, slots, narrow),
            grid=(wide // step,),
            out_shape=shape_of((rows, wide), bf16),
            in_specs=[
                pl.BlockSpec((slots * rank, rows), lambda i: (0, 0)),
                pl.BlockSpec((step, key_width), lambda i: (i, 0)),
            ]
            + [pl.BlockSpec((rank, step), lambda i: (0, i))] * slots
            + [pl.BlockSpec(g.shape, lambda i, r=g.ndim: (0,) * r) for g in grads],
            out_specs=pl.BlockSpec((rows, step), lambda i: (0, i)),
            scratch_shapes=[
                pltpu.VMEM((rows, key_width), bf16),
                pltpu.VMEM((rows, slots * rank), bf16),
            ],
            compiler_params=params(16),
            cost_estimate=cost(
                2 * rows * wide * (key_width + rank * slots), 2 * wide * (rows + key_width)
            ),
        )(spread, frozen_key_weight, *down_tables, *grads)

    def low_work():
        part = pl.pallas_call(
            functools.partial(low_kernel, slots),
            out_shape=shape_of((rank, rows), f32),
            in_specs=[SMEM, VMEM] + [VMEM] * slots,
            out_specs=VMEM,
            compiler_params=params(16),
            cost_estimate=cost(2 * rows * wide * rank * slots, 2 * rows * wide),
        )(facts, tokens, *down_tables)
        parts = shared(part)
        input_gradient = input_whole(after(spread_back, parts[0]))
        if square:
            keep, send = base
            got = swap(send, shards, (0, 1))
            frozen, passing = keep[1] + got[1], (keep[0] + got[0]).astype(bf16)
            parts = [after(parts[0], input_gradient, frozen, passing), parts[1]]
        else:
            whole = jnp.dot(tokens, frozen_key_weight, preferred_element_type=f32)
            frozen = lax.psum_scatter(whole, shards, scatter_dimension=1, tiled=True)
            passing = ()
        spread, send = pl.pallas_call(
            functools.partial(second_kernel, slots, tok_size, len(parts)),
            out_shape=[
                shape_of((slots * rank, rows), bf16),
                shape_of((tok_size, rank, narrow), bf16),
            ],
            in_specs=[SMEM] + [VMEM] * (1 + len(parts)),
            out_specs=[VMEM] * 2,
            compiler_params=params(16),
            cost_estimate=cost(2 * rows * narrow * rank * slots, 2 * rows * narrow),
        )(facts, output_gradient, *parts)
        return spread, send, frozen, passing, input_gradient

    spread_low, part_up, frozen, passing, input_gradient = group(low_work)
    came_up = lax.all_to_all(part_up, "tok", split_axis=0, concat_axis=0, tiled=True)
    frozen = [frozen]
    if square:
        frozen.append(swap(passing, shards, (1, 0)))

    fresh_down, average_down = adam_down(facts, came, (down, down_m, down_v, down_a))
    fresh_up, average_up, key_output = last_step(
        facts,
        after(came_up, fresh_down),
        (up, up_m, up_v, up_a),
        spread_low,
        up_tables,
        frozen,
        tok_size,
    )
    return (
        key_output,
        input_gradient,
        flip(fresh_down),
        flip(fresh_up),
        flip(average_down),
        flip(average_up),
    )


def solution(mesh):
    rows = P(("groups", "tok"), ("tp", "sub"))
    cube = P(("groups", "tok"), ("tp", "sub"), None)
    return jax.shard_map(
        per_device,
        mesh=mesh,
        in_specs=(rows, P(("tp", "sub"), None), rows, P("groups", None), P("groups", None), P("groups"))
        + (cube,) * 8,
        out_specs=(rows, rows, cube, cube, cube, cube),
        check_vma=False,
    )
```

```python
import functools

import jax
import jax.numpy as jnp
from jax import lax
from jax.experimental import pallas as pl
from jax.experimental.pallas import tpu as pltpu
from jax.sharding import PartitionSpec as P

MODEL_WIDTH = 8192
ADAPTER_RANK = 64

adapter_scale = 0.5
learn_rate = 0.3
beta_one = 0.9
beta_two = 0.99
adam_eps = 1e-08
ema_decay = 0.9

LOW_SCALE = MODEL_WIDTH ** (-0.5)
BACK_SCALE = ADAPTER_RANK ** (-0.5)
MIB = 1024 * 1024

f32 = jnp.float32
bf16 = jnp.bfloat16

SMEM = pl.BlockSpec(memory_space=pltpu.SMEM)
VMEM = pl.BlockSpec(memory_space=pltpu.VMEM)
ANY = pl.BlockSpec(memory_space=pl.ANY)
HBM = pl.BlockSpec(memory_space=pltpu.HBM)


def shape_of(shape, dtype):
    return jax.ShapeDtypeStruct(tuple(shape), dtype)


SCHEDULE_SCALE = 3


def cost(flops, bytes_accessed):
    return pl.CostEstimate(
        flops=int(flops * SCHEDULE_SCALE),
        bytes_accessed=int(bytes_accessed * SCHEDULE_SCALE),
        transcendentals=0,
    )


def params(mib):
    return pltpu.CompilerParams(vmem_limit_bytes=mib * MIB)


def nt(a, b):
    return lax.dot_general(a, b, (((1,), (1,)), ((), ())), preferred_element_type=f32)


def nn(a, b):
    return lax.dot_general(a, b, (((1,), (0,)), ((), ())), preferred_element_type=f32)


def tn(a, b):
    return lax.dot_general(a, b, (((0,), (0,)), ((), ())), preferred_element_type=f32)


def facts_kernel(slots, owned, tok_size, counts, placement, sequence, facts):
    me = lax.axis_index("tok")
    total = jnp.int32(0)
    for s in range(slots):
        total = total + counts[me, s]
        facts[s] = total
        tenant = placement[lax.rem(me - s + tok_size, tok_size), s]
        place = jnp.int32(0)
        for k in range(1, owned):
            place = place + jnp.where(sequence[me * owned + k] == tenant, k, 0)
        facts[slots + s] = place


def slot_ends(facts, slots):
    return [facts[s] for s in range(slots)]


def slot_mask(ends, slot, shape):
    rows = lax.broadcasted_iota(jnp.int32, shape, 1)
    inside = rows < ends[slot]
    if slot:
        inside = inside & (rows >= ends[slot - 1])
    return inside


def pick_slot(ends, products, rank):
    rows = lax.broadcasted_iota(jnp.int32, (rank, products.shape[1]), 1)
    slots = products.shape[0] // rank
    out = products[(slots - 1) * rank :]
    for s in range(slots - 2, -1, -1):
        out = jnp.where(rows < ends[s], products[s * rank : (s + 1) * rank], out)
    return out


def spread_slots(ends, values):
    wide = values.astype(f32)
    return jnp.concatenate(
        [jnp.where(slot_mask(ends, s, wide.shape), wide, 0.0) for s in range(len(ends))], axis=0
    ).astype(bf16)


def paired_sum(refs):
    parts = [ref[...] for ref in refs]
    while len(parts) > 1:
        parts = [parts[i] + parts[i + 1] for i in range(0, len(parts), 2)]
    return parts[0]


def select_kernel(slots, owned, tok_size, counts, placement, sequence, down, up, facts, *rest):
    ups, downs, sems = rest[:slots], rest[slots : 2 * slots], rest[2 * slots]
    facts_kernel(slots, owned, tok_size, counts, placement, sequence, facts)
    copies = []
    order = list(range(1, slots)) + [0]
    for s in order:
        copies.append(pltpu.make_async_copy(up.at[facts[slots + s]], ups[s], sems.at[s]))
    for s in order:
        copies.append(pltpu.make_async_copy(down.at[facts[slots + s]], downs[s], sems.at[slots + s]))
    for copy in copies:
        copy.start()
    for copy in copies:
        copy.wait()


def base_kernel(width, tokens, weight, keep, send):
    tp, sub = lax.axis_index("tp"), lax.axis_index("sub")
    mine, other = tp, 1 - tp
    for ref, s in ((send, 1 - sub), (keep, sub)):
        for i, t in enumerate((other, mine)):
            start = pl.multiple_of((t * 2 + s) * width, width)
            ref[i] = nn(tokens[...], weight[:, pl.ds(start, width)])


def stacked(tables):
    return jnp.concatenate([t[...] for t in tables], axis=0)


def back_kernel(slots, facts, grad, *rest):
    tables, out = rest[:slots], rest[slots]
    out[...] = pick_slot(slot_ends(facts, slots), nt(stacked(tables), grad[...]), ADAPTER_RANK)


def part_down_kernel(slots, pieces, facts, tokens, *rest):
    parts, spread_out, outs = rest[:pieces], rest[pieces], rest[pieces + 1 :]
    ends = slot_ends(facts, slots)
    back = (paired_sum(parts) * BACK_SCALE).astype(bf16)
    spread = spread_slots(ends, back)
    spread_out[...] = spread
    for c in range(0, tokens.shape[1], 256):
        columns = slice(c, min(c + 256, tokens.shape[1]))
        product = (nn(spread, tokens[:, columns]) * (adapter_scale * LOW_SCALE)).astype(bf16)
        for s in range(slots):
            outs[s][:, columns] = product[s * ADAPTER_RANK : (s + 1) * ADAPTER_RANK]


def low_kernel(slots, facts, tokens, *rest):
    tables, out = rest[:slots], rest[slots]
    out[...] = pick_slot(slot_ends(facts, slots), nt(stacked(tables), tokens[...]), ADAPTER_RANK)


def input_kernel(slots, width, spread, weight, *rest):
    tables, grads, (out, whole, turned) = rest[:slots], rest[slots:-3], rest[-3:]

    @pl.when(pl.program_id(0) == 0)
    def _():
        turned[...] = spread[...].astype(f32).T.astype(bf16)
        if len(grads) == 1:
            whole[...] = grads[0][...]
        else:
            tp, sub = lax.axis_index("tp"), lax.axis_index("sub")
            pieces = (grads[0][...], grads[1][...], grads[2][0], grads[2][1])
            for piece, t, s in zip(pieces, (tp, 1 - tp, tp, 1 - tp), (sub, sub, 1 - sub, 1 - sub)):
                start = pl.multiple_of((t * 2 + s) * width, width)
                whole[:, pl.ds(start, width)] = piece

    frozen = None
    for start in range(0, whole.shape[1], 256):
        term = nt(whole[:, start : start + 256], weight[:, start : start + 256])
        frozen = term if frozen is None else frozen + term
    adapter = nn(turned[...], stacked(tables))
    out[...] = (frozen + (adapter_scale * LOW_SCALE) * adapter).astype(bf16)


def second_kernel(slots, tok_size, pieces, facts, grad, *rest):
    parts, (spread_low, out) = rest[:pieces], rest[pieces:]
    me = lax.axis_index("tok")
    low = (paired_sum(parts) * LOW_SCALE).astype(bf16)
    spread = spread_slots(slot_ends(facts, slots), low)
    spread_low[...] = spread
    product = (nn(spread, grad[...]) * (adapter_scale * BACK_SCALE)).astype(bf16)
    for s in range(slots):
        out[lax.rem(me + s, tok_size)] = product[s * ADAPTER_RANK : (s + 1) * ADAPTER_RANK]


def adam_step(weights, mean_old, var_old, avg_old, gradient):
    mean_new = beta_one * mean_old + (1.0 - beta_one) * gradient
    var_new = beta_two * var_old + (1.0 - beta_two) * gradient * gradient
    root = var_new * lax.rsqrt(var_new) + adam_eps
    inverse = pl.reciprocal(root, approx=True)
    inverse = inverse * (2.0 - root * inverse)
    updated = weights.astype(f32) - learn_rate * mean_new * inverse
    return updated.astype(bf16), ema_decay * avg_old + (1.0 - ema_decay) * updated


def each_rows(count, body):
    rows = 16

    def step(i, _):
        body(pl.ds(pl.multiple_of(i * rows, rows), rows), rows)
        return 0

    lax.fori_loop(0, count // rows, step, 0)


def adam_kernel(slots, facts, *rest):
    came, old, rest = rest[:slots], rest[slots : slots + 4], rest[slots + 4 :]
    fresh, average, came_here = rest[:3]
    old_here, rest = rest[3:7], rest[7:]
    fresh_here, average_here, gradient_ref, in_sems, out_sems = rest
    owned, rank, width = fresh_here.shape

    arrivals = [
        pltpu.make_async_copy(came[s], came_here.at[s], in_sems.at[s]) for s in range(slots)
    ]
    loads, stores = [], []
    for k in range(owned):
        for i in range(4):
            sem = in_sems.at[slots + 4 * k + i]
            loads.append(pltpu.make_async_copy(old[i].at[k], old_here[i].at[k], sem))
        for i, (here, there) in enumerate(((fresh_here, fresh), (average_here, average))):
            sem = out_sems.at[2 * k + i]
            stores.append(pltpu.make_async_copy(here.at[k], there.at[k], sem))
    for copy in arrivals + loads:
        copy.start()

    for copy in arrivals:
        copy.wait()
    for k in range(owned):

        def clear(r, rows):
            gradient_ref[r, :] = jnp.zeros((rows, width), f32)

        each_rows(rank, clear)
        for s in range(slots):

            @pl.when(facts[slots + s] == k)
            def _():
                def add(r, rows):
                    gradient_ref[r, :] += came_here[s, r, :].astype(f32)

                each_rows(rank, add)

        for copy in loads[4 * k : 4 * k + 4]:
            copy.wait()

        def update(r, rows):
            for c in range(0, width, 512):
                columns = slice(c, min(c + 512, width))
                fresh_here[k, r, columns], average_here[k, r, columns] = adam_step(
                    *[ref[k, r, columns] for ref in old_here], gradient_ref[r, columns]
                )

        each_rows(rank, update)
        for copy in stores[2 * k : 2 * k + 2]:
            copy.start()
    for copy in stores:
        copy.wait()


def adam_down(facts, came, old):
    owned, rank, width = old[0].shape
    slots = len(came)
    shapes = [shape_of(old[0].shape, bf16), shape_of(old[0].shape, f32)]
    return pl.pallas_call(
        functools.partial(adam_kernel, slots),
        out_shape=shapes,
        in_specs=[SMEM] + [ANY] * (slots + 4),
        out_specs=[ANY] * 2,
        scratch_shapes=[pltpu.VMEM((slots, rank, width), bf16)]
        + [pltpu.VMEM(a.shape, a.dtype) for a in old]
        + [
            pltpu.VMEM(old[0].shape, bf16),
            pltpu.VMEM(old[0].shape, f32),
            pltpu.VMEM((rank, width), f32),
            pltpu.SemaphoreType.DMA((slots + 4 * owned,)),
            pltpu.SemaphoreType.DMA((2 * owned,)),
        ],
        compiler_params=params(60),
        cost_estimate=cost(owned * rank * width * 20, owned * rank * width * 60),
    )(facts, *came, *old)


def last_kernel(slots, tok_size, facts, came, *rest):
    old, rest = rest[:4], rest[4:]
    spread, tables, frozen = rest[0], rest[1 : 1 + slots], rest[1 + slots : -4]
    fresh, average, key_out, gradients = rest[-4:]
    raised = nn(spread[...].astype(f32).T.astype(bf16), stacked(tables))
    whole = frozen[0][...]
    for part in frozen[1:]:
        whole = whole + part[...].astype(f32)
    key_out[...] = (whole + (adapter_scale * BACK_SCALE) * raised).astype(bf16)
    me = lax.axis_index("tok")
    gradients[...] = jnp.zeros(gradients.shape, f32)
    for s in range(slots):
        gradients[facts[slots + s]] += came[lax.rem(me - s + tok_size, tok_size)].astype(f32)
    owned, rank, _ = gradients.shape
    for k in range(owned):

        def update(r, rows):
            fresh[k, r, :], average[k, r, :] = adam_step(
                *[ref[k, r, :] for ref in old], gradients[k, r, :]
            )

        each_rows(rank, update)


def last_step(facts, came, old, spread, tables, frozen, tok_size):
    shape = old[0].shape
    slots = len(tables)
    return pl.pallas_call(
        functools.partial(last_kernel, slots, tok_size),
        out_shape=[
            shape_of(shape, bf16),
            shape_of(shape, f32),
            shape_of(frozen[0].shape, bf16),
        ],
        in_specs=[SMEM] + [VMEM] * (6 + slots + len(frozen)),
        out_specs=[VMEM] * 3,
        scratch_shapes=[pltpu.VMEM(shape, f32)],
        compiler_params=params(16),
        cost_estimate=cost(old[0].size * 20, old[0].size * 20),
    )(facts, came, *old, spread, *tables, *frozen)


def after(value, *others):
    return lax.optimization_barrier((value, *others))[0]


def swap(block, axes, flips):
    sizes = [lax.axis_size(a) for a in axes]
    route = []
    for t in range(sizes[0]):
        for s in range(sizes[1]):
            source = (t ^ flips[0]) * sizes[1] + (s ^ flips[1])
            route.append((source, t * sizes[1] + s))
    return lax.ppermute(block, axes, route)


def per_device(
    tokens,
    frozen_key_weight,
    output_gradient,
    counts,
    placement,
    adapter_sequence,
    adapter_down,
    adapter_up,
    down_first_moment,
    down_second_moment,
    down_average,
    up_first_moment,
    up_second_moment,
    up_average,
):
    tok_size = lax.axis_size("tok")
    tp_size, sub_size = lax.axis_size("tp"), lax.axis_size("sub")
    shards = ("tp", "sub")
    square = tp_size == 2 and sub_size == 2
    rows, wide = tokens.shape
    narrow = output_gradient.shape[1]
    key_width = frozen_key_weight.shape[1]
    owned = adapter_down.shape[0]
    slots = placement.shape[1]
    rank = ADAPTER_RANK
    flip = lambda a: jnp.swapaxes(a, 1, 2)
    down, down_m, down_v, down_a = map(
        flip, (adapter_down, down_first_moment, down_second_moment, down_average)
    )
    up, up_m, up_v, up_a = map(flip, (adapter_up, up_first_moment, up_second_moment, up_average))

    def fetch(block, slot):
        return lax.ppermute(block, "tok", [((i + slot) % tok_size, i) for i in range(tok_size)])

    def give_back(block, slot):
        return lax.ppermute(block, "tok", [((i - slot) % tok_size, i) for i in range(tok_size)])

    def shared(part):
        if not square:
            return [lax.psum(part, shards)]
        both = part + swap(part, shards, (0, 1))
        return [both, swap(both, shards, (1, 0))]

    step = min(256, wide)

    facts, *sent = pl.pallas_call(
        functools.partial(select_kernel, slots, owned, tok_size),
        out_shape=[shape_of((2 * slots,), jnp.int32)]
        + [shape_of((rank, narrow), bf16)] * slots
        + [shape_of((rank, wide), bf16)] * slots,
        in_specs=[SMEM, SMEM, SMEM, ANY, ANY],
        out_specs=[SMEM] + [VMEM] * (2 * slots),
        scratch_shapes=[pltpu.SemaphoreType.DMA((2 * slots,))],
        compiler_params=params(56),
        cost_estimate=cost(0, 4 * slots * rank * (wide + narrow)),
    )(counts, placement, adapter_sequence, down, up)
    up_send, down_send = sent[:slots], sent[slots:]
    ready = counts[0, 0] > 0
    ahead = [s for s in (1, 3) if s < slots]
    down_tables = {0: down_send[0]}
    down_tables.update((s, fetch(down_send[s], s)) for s in ahead)
    up_tables = [up_send[0]] + [fetch(up_send[s], s) for s in range(1, slots)]
    if square:
        across = swap(after(output_gradient, facts), shards, (1, 0))
        pair = jnp.stack([output_gradient, across])
        base = pl.pallas_call(
            functools.partial(base_kernel, narrow),
            out_shape=[shape_of((2, rows, narrow), f32)] * 2,
            in_specs=[VMEM, VMEM],
            out_specs=[VMEM, VMEM],
            compiler_params=params(16),
            cost_estimate=cost(2 * rows * wide * key_width, 2 * wide * (rows + key_width)),
        )(tokens, after(frozen_key_weight, pair))
        up_tables[0] = after(up_tables[0], base[0], *[down_tables[s] for s in ahead])
    for s in range(2, slots):
        if s not in ahead:
            down_tables[s] = fetch(after(down_send[s], ready, down_tables[1]), s)
    down_tables = [down_tables[s] for s in range(slots)]

    def group(work):
        shapes = jax.eval_shape(work)
        nothing = lambda: jax.tree.map(lambda a: jnp.zeros(a.shape, a.dtype), shapes)
        return lax.cond(ready, work, nothing)

    def back_work():
        part = pl.pallas_call(
            functools.partial(back_kernel, slots),
            out_shape=shape_of((rank, rows), f32),
            in_specs=[SMEM, VMEM] + [VMEM] * slots,
            out_specs=VMEM,
            compiler_params=params(16),
            cost_estimate=cost(2 * rows * narrow * rank * slots, 2 * rows * narrow),
        )(facts, output_gradient, *up_tables)
        parts = shared(part)
        if square:
            grads = [swap(pair, shards, (0, 1))]
        else:
            grads = [lax.all_gather(output_gradient, shards, axis=1, tiled=True)]
        spread, *sends = pl.pallas_call(
            functools.partial(part_down_kernel, slots, len(parts)),
            out_shape=[shape_of((slots * rank, rows), bf16)] + [shape_of((rank, wide), bf16)] * slots,
            in_specs=[SMEM, VMEM] + [VMEM] * len(parts),
            out_specs=[VMEM] * (1 + slots),
            compiler_params=params(16),
            cost_estimate=cost(2 * rows * wide * rank * slots, 2 * rows * wide),
        )(facts, tokens, *parts)
        return grads, spread, sends

    grads, spread_back, part_down = group(back_work)
    if square:
        grads = [output_gradient, across] + grads
    came = [part_down[0]] + [
        give_back(after(part_down[s], *down_tables[1:]), s) for s in range(1, slots)
    ]

    def input_whole(spread):
        return pl.pallas_call(
            functools.partial(input_kernel, slots, narrow),
            grid=(wide // step,),
            out_shape=shape_of((rows, wide), bf16),
            in_specs=[
                pl.BlockSpec((slots * rank, rows), lambda i: (0, 0)),
                pl.BlockSpec((step, key_width), lambda i: (i, 0)),
            ]
            + [pl.BlockSpec((rank, step), lambda i: (0, i))] * slots
            + [pl.BlockSpec(g.shape, lambda i, r=g.ndim: (0,) * r) for g in grads],
            out_specs=pl.BlockSpec((rows, step), lambda i: (0, i)),
            scratch_shapes=[
                pltpu.VMEM((rows, key_width), bf16),
                pltpu.VMEM((rows, slots * rank), bf16),
            ],
            compiler_params=params(16),
            cost_estimate=cost(
                2 * rows * wide * (key_width + rank * slots), 2 * wide * (rows + key_width)
            ),
        )(spread, frozen_key_weight, *down_tables, *grads)

    def low_work():
        part = pl.pallas_call(
            functools.partial(low_kernel, slots),
            out_shape=shape_of((rank, rows), f32),
            in_specs=[SMEM, VMEM] + [VMEM] * slots,
            out_specs=VMEM,
            compiler_params=params(16),
            cost_estimate=cost(2 * rows * wide * rank * slots, 2 * rows * wide),
        )(facts, tokens, *down_tables)
        parts = shared(part)
        input_gradient = input_whole(after(spread_back, parts[0]))
        if square:
            keep, send = base
            got = swap(send, shards, (0, 1))
            frozen, passing = keep[1] + got[1], (keep[0] + got[0]).astype(bf16)
            parts = [after(parts[0], input_gradient, frozen, passing), parts[1]]
        else:
            whole = jnp.dot(tokens, frozen_key_weight, preferred_element_type=f32)
            frozen = lax.psum_scatter(whole, shards, scatter_dimension=1, tiled=True)
            passing = ()
        spread, send = pl.pallas_call(
            functools.partial(second_kernel, slots, tok_size, len(parts)),
            out_shape=[
                shape_of((slots * rank, rows), bf16),
                shape_of((tok_size, rank, narrow), bf16),
            ],
            in_specs=[SMEM] + [VMEM] * (1 + len(parts)),
            out_specs=[VMEM] * 2,
            compiler_params=params(16),
            cost_estimate=cost(2 * rows * narrow * rank * slots, 2 * rows * narrow),
        )(facts, output_gradient, *parts)
        return spread, send, frozen, passing, input_gradient

    spread_low, part_up, frozen, passing, input_gradient = group(low_work)
    came_up = lax.all_to_all(part_up, "tok", split_axis=0, concat_axis=0, tiled=True)
    frozen = [frozen]
    if square:
        frozen.append(swap(passing, shards, (1, 0)))

    fresh_down, average_down = adam_down(facts, came, (down, down_m, down_v, down_a))
    fresh_up, average_up, key_output = last_step(
        facts,
        after(came_up, fresh_down),
        (up, up_m, up_v, up_a),
        spread_low,
        up_tables,
        frozen,
        tok_size,
    )
    return (
        key_output,
        input_gradient,
        flip(fresh_down),
        flip(fresh_up),
        flip(average_down),
        flip(average_up),
    )


def solution(mesh):
    rows = P(("groups", "tok"), ("tp", "sub"))
    cube = P(("groups", "tok"), ("tp", "sub"), None)
    return jax.shard_map(
        per_device,
        mesh=mesh,
        in_specs=(rows, P(("tp", "sub"), None), rows, P("groups", None), P("groups", None), P("groups"))
        + (cube,) * 8,
        out_specs=(rows, rows, cube, cube, cube, cube),
        check_vma=False,
    )
```

```python
import functools

import jax
import jax.numpy as jnp
from jax import lax
from jax.experimental import pallas as pl
from jax.experimental.pallas import tpu as pltpu
from jax.sharding import PartitionSpec as P

MODEL_WIDTH = 8192
ADAPTER_RANK = 64

adapter_scale = 0.5
learn_rate = 0.3
beta_one = 0.9
beta_two = 0.99
adam_eps = 1e-08
ema_decay = 0.9

LOW_SCALE = MODEL_WIDTH ** (-0.5)
BACK_SCALE = ADAPTER_RANK ** (-0.5)
MIB = 1024 * 1024

f32 = jnp.float32
bf16 = jnp.bfloat16

SMEM = pl.BlockSpec(memory_space=pltpu.SMEM)
VMEM = pl.BlockSpec(memory_space=pltpu.VMEM)
ANY = pl.BlockSpec(memory_space=pl.ANY)
HBM = pl.BlockSpec(memory_space=pltpu.HBM)


def shape_of(shape, dtype):
    return jax.ShapeDtypeStruct(tuple(shape), dtype)


SCHEDULE_SCALE = 3


def cost(flops, bytes_accessed):
    return pl.CostEstimate(
        flops=int(flops * SCHEDULE_SCALE),
        bytes_accessed=int(bytes_accessed * SCHEDULE_SCALE),
        transcendentals=0,
    )


def params(mib):
    return pltpu.CompilerParams(vmem_limit_bytes=mib * MIB)


def nt(a, b):
    return lax.dot_general(a, b, (((1,), (1,)), ((), ())), preferred_element_type=f32)


def nn(a, b):
    return lax.dot_general(a, b, (((1,), (0,)), ((), ())), preferred_element_type=f32)


def tn(a, b):
    return lax.dot_general(a, b, (((0,), (0,)), ((), ())), preferred_element_type=f32)


def facts_kernel(slots, owned, tok_size, counts, placement, sequence, facts):
    me = lax.axis_index("tok")
    total = jnp.int32(0)
    for s in range(slots):
        total = total + counts[me, s]
        facts[s] = total
        tenant = placement[lax.rem(me - s + tok_size, tok_size), s]
        place = jnp.int32(0)
        for k in range(1, owned):
            place = place + jnp.where(sequence[me * owned + k] == tenant, k, 0)
        facts[slots + s] = place


def slot_ends(facts, slots):
    return [facts[s] for s in range(slots)]


def slot_mask(ends, slot, shape):
    rows = lax.broadcasted_iota(jnp.int32, shape, 1)
    inside = rows < ends[slot]
    if slot:
        inside = inside & (rows >= ends[slot - 1])
    return inside


def pick_slot(ends, products, rank):
    rows = lax.broadcasted_iota(jnp.int32, (rank, products.shape[1]), 1)
    slots = products.shape[0] // rank
    out = products[(slots - 1) * rank :]
    for s in range(slots - 2, -1, -1):
        out = jnp.where(rows < ends[s], products[s * rank : (s + 1) * rank], out)
    return out


def spread_slots(ends, values):
    wide = values.astype(f32)
    return jnp.concatenate(
        [jnp.where(slot_mask(ends, s, wide.shape), wide, 0.0) for s in range(len(ends))], axis=0
    ).astype(bf16)


def paired_sum(refs):
    parts = [ref[...] for ref in refs]
    while len(parts) > 1:
        parts = [parts[i] + parts[i + 1] for i in range(0, len(parts), 2)]
    return parts[0]


def select_kernel(slots, owned, tok_size, counts, placement, sequence, down, up, facts, *rest):
    ups, downs, sems = rest[:slots], rest[slots : 2 * slots], rest[2 * slots]
    facts_kernel(slots, owned, tok_size, counts, placement, sequence, facts)
    copies = []
    order = list(range(1, slots)) + [0]
    for s in order:
        copies.append(pltpu.make_async_copy(up.at[facts[slots + s]], ups[s], sems.at[s]))
    for s in order:
        copies.append(pltpu.make_async_copy(down.at[facts[slots + s]], downs[s], sems.at[slots + s]))
    for copy in copies:
        copy.start()
    for copy in copies:
        copy.wait()


def base_kernel(width, tokens, weight, keep, send):
    tp, sub = lax.axis_index("tp"), lax.axis_index("sub")
    mine, other = tp, 1 - tp
    for ref, s in ((send, 1 - sub), (keep, sub)):
        for i, t in enumerate((other, mine)):
            start = pl.multiple_of((t * 2 + s) * width, width)
            ref[i] = nn(tokens[...], weight[:, pl.ds(start, width)])


def stacked(tables):
    return jnp.concatenate([t[...] for t in tables], axis=0)


def back_kernel(slots, facts, grad, *rest):
    tables, out = rest[:slots], rest[slots]
    out[...] = pick_slot(slot_ends(facts, slots), nt(stacked(tables), grad[...]), ADAPTER_RANK)


def part_down_kernel(slots, pieces, facts, tokens, *rest):
    parts, spread_out, outs = rest[:pieces], rest[pieces], rest[pieces + 1 :]
    ends = slot_ends(facts, slots)
    back = (paired_sum(parts) * BACK_SCALE).astype(bf16)
    spread = spread_slots(ends, back)
    spread_out[...] = spread
    for c in range(0, tokens.shape[1], 256):
        columns = slice(c, min(c + 256, tokens.shape[1]))
        product = (nn(spread, tokens[:, columns]) * (adapter_scale * LOW_SCALE)).astype(bf16)
        for s in range(slots):
            outs[s][:, columns] = product[s * ADAPTER_RANK : (s + 1) * ADAPTER_RANK]


def low_kernel(slots, facts, tokens, *rest):
    tables, out = rest[:slots], rest[slots]
    out[...] = pick_slot(slot_ends(facts, slots), nt(stacked(tables), tokens[...]), ADAPTER_RANK)


def input_kernel(slots, width, spread, weight, *rest):
    tables, grads, (out, whole, turned) = rest[:slots], rest[slots:-3], rest[-3:]

    @pl.when(pl.program_id(0) == 0)
    def _():
        turned[...] = spread[...].astype(f32).T.astype(bf16)
        if len(grads) == 1:
            whole[...] = grads[0][...]
        else:
            tp, sub = lax.axis_index("tp"), lax.axis_index("sub")
            pieces = (grads[0][...], grads[1][...], grads[2][0], grads[2][1])
            for piece, t, s in zip(pieces, (tp, 1 - tp, tp, 1 - tp), (sub, sub, 1 - sub, 1 - sub)):
                start = pl.multiple_of((t * 2 + s) * width, width)
                whole[:, pl.ds(start, width)] = piece

    frozen = None
    for start in range(0, whole.shape[1], 256):
        term = nt(whole[:, start : start + 256], weight[:, start : start + 256])
        frozen = term if frozen is None else frozen + term
    adapter = nn(turned[...], stacked(tables))
    out[...] = (frozen + (adapter_scale * LOW_SCALE) * adapter).astype(bf16)


def second_kernel(slots, tok_size, pieces, facts, grad, *rest):
    parts, (spread_low, out) = rest[:pieces], rest[pieces:]
    me = lax.axis_index("tok")
    low = (paired_sum(parts) * LOW_SCALE).astype(bf16)
    spread = spread_slots(slot_ends(facts, slots), low)
    spread_low[...] = spread
    product = (nn(spread, grad[...]) * (adapter_scale * BACK_SCALE)).astype(bf16)
    for s in range(slots):
        out[lax.rem(me + s, tok_size)] = product[s * ADAPTER_RANK : (s + 1) * ADAPTER_RANK]


def adam_step(weights, mean_old, var_old, avg_old, gradient):
    mean_new = beta_one * mean_old + (1.0 - beta_one) * gradient
    var_new = beta_two * var_old + (1.0 - beta_two) * gradient * gradient
    root = var_new * lax.rsqrt(var_new) + adam_eps
    inverse = pl.reciprocal(root, approx=True)
    inverse = inverse * (2.0 - root * inverse)
    updated = weights.astype(f32) - learn_rate * mean_new * inverse
    return updated.astype(bf16), ema_decay * avg_old + (1.0 - ema_decay) * updated


def each_rows(count, body):
    rows = 16

    def step(i, _):
        body(pl.ds(pl.multiple_of(i * rows, rows), rows), rows)
        return 0

    lax.fori_loop(0, count // rows, step, 0)


def adam_kernel(slots, facts, *rest):
    came, old, rest = rest[:slots], rest[slots : slots + 4], rest[slots + 4 :]
    fresh, average, came_here = rest[:3]
    old_here, rest = rest[3:7], rest[7:]
    fresh_here, average_here, gradient_ref, in_sems, out_sems = rest
    owned, rank, width = fresh_here.shape

    arrivals = [
        pltpu.make_async_copy(came[s], came_here.at[s], in_sems.at[s]) for s in range(slots)
    ]
    loads, stores = [], []
    for k in range(owned):
        for i in range(4):
            sem = in_sems.at[slots + 4 * k + i]
            loads.append(pltpu.make_async_copy(old[i].at[k], old_here[i].at[k], sem))
        for i, (here, there) in enumerate(((fresh_here, fresh), (average_here, average))):
            sem = out_sems.at[2 * k + i]
            stores.append(pltpu.make_async_copy(here.at[k], there.at[k], sem))
    for copy in arrivals + loads:
        copy.start()

    for copy in arrivals:
        copy.wait()
    for k in range(owned):

        def clear(r, rows):
            gradient_ref[r, :] = jnp.zeros((rows, width), f32)

        each_rows(rank, clear)
        for s in range(slots):

            @pl.when(facts[slots + s] == k)
            def _():
                def add(r, rows):
                    gradient_ref[r, :] += came_here[s, r, :].astype(f32)

                each_rows(rank, add)

        for copy in loads[4 * k : 4 * k + 4]:
            copy.wait()

        def update(r, rows):
            for c in range(0, width, 512):
                columns = slice(c, min(c + 512, width))
                fresh_here[k, r, columns], average_here[k, r, columns] = adam_step(
                    *[ref[k, r, columns] for ref in old_here], gradient_ref[r, columns]
                )

        each_rows(rank, update)
        for copy in stores[2 * k : 2 * k + 2]:
            copy.start()
    for copy in stores:
        copy.wait()


def adam_down(facts, came, old):
    owned, rank, width = old[0].shape
    slots = len(came)
    shapes = [shape_of(old[0].shape, bf16), shape_of(old[0].shape, f32)]
    return pl.pallas_call(
        functools.partial(adam_kernel, slots),
        out_shape=shapes,
        in_specs=[SMEM] + [ANY] * (slots + 4),
        out_specs=[ANY] * 2,
        scratch_shapes=[pltpu.VMEM((slots, rank, width), bf16)]
        + [pltpu.VMEM(a.shape, a.dtype) for a in old]
        + [
            pltpu.VMEM(old[0].shape, bf16),
            pltpu.VMEM(old[0].shape, f32),
            pltpu.VMEM((rank, width), f32),
            pltpu.SemaphoreType.DMA((slots + 4 * owned,)),
            pltpu.SemaphoreType.DMA((2 * owned,)),
        ],
        compiler_params=params(60),
        cost_estimate=cost(owned * rank * width * 20, owned * rank * width * 60),
    )(facts, *came, *old)


def stack_kernel(own, across, out):
    out[0] = own[...]
    out[1] = across[...]


def stack_pair(own, across, flops):
    return pl.pallas_call(
        stack_kernel,
        out_shape=shape_of((2,) + own.shape, own.dtype),
        in_specs=[VMEM] * 2,
        out_specs=VMEM,
        compiler_params=params(16),
        cost_estimate=cost(flops, 2 * flops // 256),
    )(own, across)


def last_kernel(slots, tok_size, facts, came, *rest):
    old, rest = rest[:4], rest[4:]
    spread, tables, frozen = rest[0], rest[1 : 1 + slots], rest[1 + slots : -4]
    fresh, average, key_out, gradients = rest[-4:]
    raised = nn(spread[...].astype(f32).T.astype(bf16), stacked(tables))
    whole = frozen[0][...]
    for part in frozen[1:]:
        whole = whole + part[...].astype(f32)
    key_out[...] = (whole + (adapter_scale * BACK_SCALE) * raised).astype(bf16)
    me = lax.axis_index("tok")
    gradients[...] = jnp.zeros(gradients.shape, f32)
    for s in range(slots):
        gradients[facts[slots + s]] += came[lax.rem(me - s + tok_size, tok_size)].astype(f32)
    owned, rank, _ = gradients.shape
    for k in range(owned):

        def update(r, rows):
            fresh[k, r, :], average[k, r, :] = adam_step(
                *[ref[k, r, :] for ref in old], gradients[k, r, :]
            )

        each_rows(rank, update)


def last_step(facts, came, old, spread, tables, frozen, tok_size):
    shape = old[0].shape
    slots = len(tables)
    return pl.pallas_call(
        functools.partial(last_kernel, slots, tok_size),
        out_shape=[
            shape_of(shape, bf16),
            shape_of(shape, f32),
            shape_of(frozen[0].shape, bf16),
        ],
        in_specs=[SMEM] + [VMEM] * (6 + slots + len(frozen)),
        out_specs=[VMEM] * 3,
        scratch_shapes=[pltpu.VMEM(shape, f32)],
        compiler_params=params(16),
        cost_estimate=cost(old[0].size * 20, old[0].size * 20),
    )(facts, came, *old, spread, *tables, *frozen)


def after(value, *others):
    return lax.optimization_barrier((value, *others))[0]


def swap(block, axes, flips):
    sizes = [lax.axis_size(a) for a in axes]
    route = []
    for t in range(sizes[0]):
        for s in range(sizes[1]):
            source = (t ^ flips[0]) * sizes[1] + (s ^ flips[1])
            route.append((source, t * sizes[1] + s))
    return lax.ppermute(block, axes, route)


def per_device(
    tokens,
    frozen_key_weight,
    output_gradient,
    counts,
    placement,
    adapter_sequence,
    adapter_down,
    adapter_up,
    down_first_moment,
    down_second_moment,
    down_average,
    up_first_moment,
    up_second_moment,
    up_average,
):
    tok_size = lax.axis_size("tok")
    tp_size, sub_size = lax.axis_size("tp"), lax.axis_size("sub")
    shards = ("tp", "sub")
    square = tp_size == 2 and sub_size == 2
    rows, wide = tokens.shape
    narrow = output_gradient.shape[1]
    key_width = frozen_key_weight.shape[1]
    owned = adapter_down.shape[0]
    slots = placement.shape[1]
    rank = ADAPTER_RANK
    flip = lambda a: jnp.swapaxes(a, 1, 2)
    down, down_m, down_v, down_a = map(
        flip, (adapter_down, down_first_moment, down_second_moment, down_average)
    )
    up, up_m, up_v, up_a = map(flip, (adapter_up, up_first_moment, up_second_moment, up_average))

    def fetch(block, slot):
        return lax.ppermute(block, "tok", [((i + slot) % tok_size, i) for i in range(tok_size)])

    def give_back(block, slot):
        return lax.ppermute(block, "tok", [((i - slot) % tok_size, i) for i in range(tok_size)])

    def shared(part):
        if not square:
            return [lax.psum(part, shards)]
        both = part + swap(part, shards, (0, 1))
        return [both, swap(both, shards, (1, 0))]

    step = min(256, wide)

    facts, *sent = pl.pallas_call(
        functools.partial(select_kernel, slots, owned, tok_size),
        out_shape=[shape_of((2 * slots,), jnp.int32)]
        + [shape_of((rank, narrow), bf16)] * slots
        + [shape_of((rank, wide), bf16)] * slots,
        in_specs=[SMEM, SMEM, SMEM, ANY, ANY],
        out_specs=[SMEM] + [VMEM] * (2 * slots),
        scratch_shapes=[pltpu.SemaphoreType.DMA((2 * slots,))],
        compiler_params=params(56),
        cost_estimate=cost(0, 4 * slots * rank * (wide + narrow)),
    )(counts, placement, adapter_sequence, down, up)
    up_send, down_send = sent[:slots], sent[slots:]
    ready = counts[0, 0] > 0
    early = fetch(down_send[1], 1)
    up_tables = [up_send[0]] + [fetch(up_send[s], s) for s in range(1, slots)]
    if square:
        across = swap(after(output_gradient, facts), shards, (1, 0))
        pair = stack_pair(output_gradient, across, 2 * rows * wide * key_width)
        up_tables[0] = after(up_tables[0], pair)
    down_tables = [down_send[0], early] + [
        fetch(after(down_send[s], ready, early), s) for s in range(2, slots)
    ]
    up_tables[0] = after(up_tables[0], early)

    def group(work):
        shapes = jax.eval_shape(work)
        nothing = lambda: jax.tree.map(lambda a: jnp.zeros(a.shape, a.dtype), shapes)
        return lax.cond(ready, work, nothing)

    def back_work():
        part = pl.pallas_call(
            functools.partial(back_kernel, slots),
            out_shape=shape_of((rank, rows), f32),
            in_specs=[SMEM, VMEM] + [VMEM] * slots,
            out_specs=VMEM,
            compiler_params=params(16),
            cost_estimate=cost(2 * rows * narrow * rank * slots, 2 * rows * narrow),
        )(facts, output_gradient, *up_tables)
        parts = shared(part)
        if square:
            base = pl.pallas_call(
                functools.partial(base_kernel, narrow),
                out_shape=[shape_of((2, rows, narrow), f32)] * 2,
                in_specs=[VMEM, VMEM],
                out_specs=[VMEM, VMEM],
                compiler_params=params(16),
                cost_estimate=cost(2 * rows * wide * key_width, 2 * wide * (rows + key_width)),
            )(tokens, after(frozen_key_weight, parts[0]))
            grads = [swap(pair, shards, (0, 1))]
            parts = [after(parts[0], base[0]), parts[1]]
        else:
            base = []
            grads = [lax.all_gather(output_gradient, shards, axis=1, tiled=True)]
        spread, *sends = pl.pallas_call(
            functools.partial(part_down_kernel, slots, len(parts)),
            out_shape=[shape_of((slots * rank, rows), bf16)] + [shape_of((rank, wide), bf16)] * slots,
            in_specs=[SMEM, VMEM] + [VMEM] * len(parts),
            out_specs=[VMEM] * (1 + slots),
            compiler_params=params(16),
            cost_estimate=cost(2 * rows * wide * rank * slots, 2 * rows * wide),
        )(facts, tokens, *parts)
        return grads, base, spread, sends

    grads, base, spread_back, part_down = group(back_work)
    if square:
        grads = [output_gradient, across] + grads
    came = [part_down[0]] + [
        give_back(after(part_down[s], *down_tables[1:]), s) for s in range(1, slots)
    ]

    def input_whole(spread):
        return pl.pallas_call(
            functools.partial(input_kernel, slots, narrow),
            grid=(wide // step,),
            out_shape=shape_of((rows, wide), bf16),
            in_specs=[
                pl.BlockSpec((slots * rank, rows), lambda i: (0, 0)),
                pl.BlockSpec((step, key_width), lambda i: (i, 0)),
            ]
            + [pl.BlockSpec((rank, step), lambda i: (0, i))] * slots
            + [pl.BlockSpec(g.shape, lambda i, r=g.ndim: (0,) * r) for g in grads],
            out_specs=pl.BlockSpec((rows, step), lambda i: (0, i)),
            scratch_shapes=[
                pltpu.VMEM((rows, key_width), bf16),
                pltpu.VMEM((rows, slots * rank), bf16),
            ],
            compiler_params=params(16),
            cost_estimate=cost(
                2 * rows * wide * (key_width + rank * slots), 2 * wide * (rows + key_width)
            ),
        )(spread, frozen_key_weight, *down_tables, *grads)

    def low_work():
        part = pl.pallas_call(
            functools.partial(low_kernel, slots),
            out_shape=shape_of((rank, rows), f32),
            in_specs=[SMEM, VMEM] + [VMEM] * slots,
            out_specs=VMEM,
            compiler_params=params(16),
            cost_estimate=cost(2 * rows * wide * rank * slots, 2 * rows * wide),
        )(facts, tokens, *down_tables)
        parts = shared(part)
        input_gradient = input_whole(after(spread_back, parts[0]))
        if square:
            keep, send = base
            got = swap(send, shards, (0, 1))
            frozen, passing = keep[1] + got[1], (keep[0] + got[0]).astype(bf16)
            parts = [after(parts[0], input_gradient, frozen, passing), parts[1]]
        else:
            whole = jnp.dot(tokens, frozen_key_weight, preferred_element_type=f32)
            frozen = lax.psum_scatter(whole, shards, scatter_dimension=1, tiled=True)
            passing = ()
        spread, send = pl.pallas_call(
            functools.partial(second_kernel, slots, tok_size, len(parts)),
            out_shape=[
                shape_of((slots * rank, rows), bf16),
                shape_of((tok_size, rank, narrow), bf16),
            ],
            in_specs=[SMEM] + [VMEM] * (1 + len(parts)),
            out_specs=[VMEM] * 2,
            compiler_params=params(16),
            cost_estimate=cost(2 * rows * narrow * rank * slots, 2 * rows * narrow),
        )(facts, output_gradient, *parts)
        return spread, send, frozen, passing, input_gradient

    spread_low, part_up, frozen, passing, input_gradient = group(low_work)
    came_up = lax.all_to_all(part_up, "tok", split_axis=0, concat_axis=0, tiled=True)
    frozen = [frozen]
    if square:
        frozen.append(swap(passing, shards, (1, 0)))

    fresh_down, average_down = adam_down(facts, came, (down, down_m, down_v, down_a))
    fresh_up, average_up, key_output = last_step(
        facts,
        after(came_up, fresh_down),
        (up, up_m, up_v, up_a),
        spread_low,
        up_tables,
        frozen,
        tok_size,
    )
    return (
        key_output,
        input_gradient,
        flip(fresh_down),
        flip(fresh_up),
        flip(average_down),
        flip(average_up),
    )


def solution(mesh):
    rows = P(("groups", "tok"), ("tp", "sub"))
    cube = P(("groups", "tok"), ("tp", "sub"), None)
    return jax.shard_map(
        per_device,
        mesh=mesh,
        in_specs=(rows, P(("tp", "sub"), None), rows, P("groups", None), P("groups", None), P("groups"))
        + (cube,) * 8,
        out_specs=(rows, rows, cube, cube, cube, cube),
        check_vma=False,
    )
```

```python
import functools

import jax
import jax.numpy as jnp
from jax import lax
from jax.experimental import pallas as pl
from jax.experimental.pallas import tpu as pltpu
from jax.sharding import PartitionSpec as P

MODEL_WIDTH = 8192
ADAPTER_RANK = 64

adapter_scale = 0.5
learn_rate = 0.3
beta_one = 0.9
beta_two = 0.99
adam_eps = 1e-08
ema_decay = 0.9

LOW_SCALE = MODEL_WIDTH ** (-0.5)
BACK_SCALE = ADAPTER_RANK ** (-0.5)
MIB = 1024 * 1024

f32 = jnp.float32
bf16 = jnp.bfloat16

SMEM = pl.BlockSpec(memory_space=pltpu.SMEM)
VMEM = pl.BlockSpec(memory_space=pltpu.VMEM)
ANY = pl.BlockSpec(memory_space=pl.ANY)
HBM = pl.BlockSpec(memory_space=pltpu.HBM)


def shape_of(shape, dtype):
    return jax.ShapeDtypeStruct(tuple(shape), dtype)


SCHEDULE_SCALE = 3


def cost(flops, bytes_accessed):
    return pl.CostEstimate(
        flops=int(flops * SCHEDULE_SCALE),
        bytes_accessed=int(bytes_accessed * SCHEDULE_SCALE),
        transcendentals=0,
    )


def params(mib):
    return pltpu.CompilerParams(vmem_limit_bytes=mib * MIB)


def nt(a, b):
    return lax.dot_general(a, b, (((1,), (1,)), ((), ())), preferred_element_type=f32)


def nn(a, b):
    return lax.dot_general(a, b, (((1,), (0,)), ((), ())), preferred_element_type=f32)


def tn(a, b):
    return lax.dot_general(a, b, (((0,), (0,)), ((), ())), preferred_element_type=f32)


def facts_kernel(slots, owned, tok_size, counts, placement, sequence, facts):
    me = lax.axis_index("tok")
    total = jnp.int32(0)
    for s in range(slots):
        total = total + counts[me, s]
        facts[s] = total
        tenant = placement[lax.rem(me - s + tok_size, tok_size), s]
        place = jnp.int32(0)
        for k in range(1, owned):
            place = place + jnp.where(sequence[me * owned + k] == tenant, k, 0)
        facts[slots + s] = place


def slot_ends(facts, slots):
    return [facts[s] for s in range(slots)]


def slot_mask(ends, slot, shape):
    rows = lax.broadcasted_iota(jnp.int32, shape, 1)
    inside = rows < ends[slot]
    if slot:
        inside = inside & (rows >= ends[slot - 1])
    return inside


def pick_slot(ends, products, rank):
    rows = lax.broadcasted_iota(jnp.int32, (rank, products.shape[1]), 1)
    slots = products.shape[0] // rank
    out = products[(slots - 1) * rank :]
    for s in range(slots - 2, -1, -1):
        out = jnp.where(rows < ends[s], products[s * rank : (s + 1) * rank], out)
    return out


def spread_slots(ends, values):
    wide = values.astype(f32)
    return jnp.concatenate(
        [jnp.where(slot_mask(ends, s, wide.shape), wide, 0.0) for s in range(len(ends))], axis=0
    ).astype(bf16)


def paired_sum(refs):
    parts = [ref[...] for ref in refs]
    while len(parts) > 1:
        parts = [parts[i] + parts[i + 1] for i in range(0, len(parts), 2)]
    return parts[0]


def select_kernel(slots, owned, tok_size, counts, placement, sequence, down, up, facts, *rest):
    ups, downs, sems = rest[:slots], rest[slots : 2 * slots], rest[2 * slots]
    facts_kernel(slots, owned, tok_size, counts, placement, sequence, facts)
    copies = []
    order = list(range(1, slots)) + [0]
    for s in order:
        copies.append(pltpu.make_async_copy(up.at[facts[slots + s]], ups[s], sems.at[s]))
    for s in order:
        copies.append(pltpu.make_async_copy(down.at[facts[slots + s]], downs[s], sems.at[slots + s]))
    for copy in copies:
        copy.start()
    for copy in copies:
        copy.wait()


def base_kernel(width, tokens, weight, keep, send):
    tp, sub = lax.axis_index("tp"), lax.axis_index("sub")
    mine, other = tp, 1 - tp
    for ref, s in ((send, 1 - sub), (keep, sub)):
        for i, t in enumerate((other, mine)):
            start = pl.multiple_of((t * 2 + s) * width, width)
            ref[i] = nn(tokens[...], weight[:, pl.ds(start, width)])


def stacked(tables):
    return jnp.concatenate([t[...] for t in tables], axis=0)


def back_kernel(slots, facts, grad, *rest):
    tables, out = rest[:slots], rest[slots]
    out[...] = pick_slot(slot_ends(facts, slots), nt(stacked(tables), grad[...]), ADAPTER_RANK)


def part_down_kernel(slots, pieces, facts, tokens, *rest):
    parts, spread_out, outs = rest[:pieces], rest[pieces], rest[pieces + 1 :]
    ends = slot_ends(facts, slots)
    back = (paired_sum(parts) * BACK_SCALE).astype(bf16)
    spread = spread_slots(ends, back)
    spread_out[...] = spread
    for c in range(0, tokens.shape[1], 256):
        columns = slice(c, min(c + 256, tokens.shape[1]))
        product = (nn(spread, tokens[:, columns]) * (adapter_scale * LOW_SCALE)).astype(bf16)
        for s in range(slots):
            outs[s][:, columns] = product[s * ADAPTER_RANK : (s + 1) * ADAPTER_RANK]


def low_kernel(slots, facts, tokens, *rest):
    tables, out = rest[:slots], rest[slots]
    out[...] = pick_slot(slot_ends(facts, slots), nt(stacked(tables), tokens[...]), ADAPTER_RANK)


def input_kernel(slots, width, spread, weight, *rest):
    tables, grads, (out, whole, turned) = rest[:slots], rest[slots:-3], rest[-3:]

    @pl.when(pl.program_id(0) == 0)
    def _():
        turned[...] = spread[...].astype(f32).T.astype(bf16)
        if len(grads) == 1:
            whole[...] = grads[0][...]
        else:
            tp, sub = lax.axis_index("tp"), lax.axis_index("sub")
            pieces = (grads[0][...], grads[1][...], grads[2][0], grads[2][1])
            for piece, t, s in zip(pieces, (tp, 1 - tp, tp, 1 - tp), (sub, sub, 1 - sub, 1 - sub)):
                start = pl.multiple_of((t * 2 + s) * width, width)
                whole[:, pl.ds(start, width)] = piece

    for c in range(0, out.shape[1], 256):
        columns = slice(c, min(c + 256, out.shape[1]))
        frozen = None
        for start in range(0, whole.shape[1], 256):
            term = nt(whole[:, start : start + 256], weight[columns, start : start + 256])
            frozen = term if frozen is None else frozen + term
        table = jnp.concatenate([t[:, columns] for t in tables], axis=0)
        adapter = nn(turned[...], table)
        out[:, columns] = (frozen + (adapter_scale * LOW_SCALE) * adapter).astype(bf16)


def second_kernel(slots, tok_size, pieces, facts, grad, *rest):
    parts, (spread_low, out) = rest[:pieces], rest[pieces:]
    me = lax.axis_index("tok")
    low = (paired_sum(parts) * LOW_SCALE).astype(bf16)
    spread = spread_slots(slot_ends(facts, slots), low)
    spread_low[...] = spread
    product = (nn(spread, grad[...]) * (adapter_scale * BACK_SCALE)).astype(bf16)
    for s in range(slots):
        out[lax.rem(me + s, tok_size)] = product[s * ADAPTER_RANK : (s + 1) * ADAPTER_RANK]


def adam_step(weights, mean_old, var_old, avg_old, gradient):
    mean_new = beta_one * mean_old + (1.0 - beta_one) * gradient
    var_new = beta_two * var_old + (1.0 - beta_two) * gradient * gradient
    root = var_new * lax.rsqrt(var_new) + adam_eps
    inverse = pl.reciprocal(root, approx=True)
    inverse = inverse * (2.0 - root * inverse)
    updated = weights.astype(f32) - learn_rate * mean_new * inverse
    return updated.astype(bf16), ema_decay * avg_old + (1.0 - ema_decay) * updated


def each_rows(count, body):
    rows = 16

    def step(i, _):
        body(pl.ds(pl.multiple_of(i * rows, rows), rows), rows)
        return 0

    lax.fori_loop(0, count // rows, step, 0)


def adam_kernel(slots, facts, *rest):
    came, old, rest = rest[:slots], rest[slots : slots + 4], rest[slots + 4 :]
    fresh, average, came_here = rest[:3]
    old_here, rest = rest[3:7], rest[7:]
    fresh_here, average_here, gradient_ref, in_sems, out_sems = rest
    owned, rank, width = fresh_here.shape
    ahead = min(2, owned)

    arrivals = [
        pltpu.make_async_copy(came[s], came_here.at[s], in_sems.at[s]) for s in range(slots)
    ]
    loads, stores = [], []
    for k in range(owned):
        for i in range(4):
            sem = in_sems.at[slots + 4 * k + i]
            loads.append(pltpu.make_async_copy(old[i].at[k], old_here[i].at[k], sem))
        for i, (here, there) in enumerate(((fresh_here, fresh), (average_here, average))):
            sem = out_sems.at[2 * k + i]
            stores.append(pltpu.make_async_copy(here.at[k], there.at[k], sem))
    for copy in arrivals + loads[: 4 * ahead]:
        copy.start()

    for copy in arrivals:
        copy.wait()
    for k in range(owned):

        def clear(r, rows):
            gradient_ref[r, :] = jnp.zeros((rows, width), f32)

        each_rows(rank, clear)
        for s in range(slots):

            @pl.when(facts[slots + s] == k)
            def _():
                def add(r, rows):
                    gradient_ref[r, :] += came_here[s, r, :].astype(f32)

                each_rows(rank, add)

        for copy in loads[4 * k : 4 * k + 4]:
            copy.wait()
        for copy in loads[4 * (k + ahead) : 4 * (k + ahead) + 4]:
            copy.start()

        def update(r, rows):
            for c in range(0, width, 512):
                columns = slice(c, min(c + 512, width))
                fresh_here[k, r, columns], average_here[k, r, columns] = adam_step(
                    *[ref[k, r, columns] for ref in old_here], gradient_ref[r, columns]
                )

        each_rows(rank, update)
        for copy in stores[2 * k : 2 * k + 2]:
            copy.start()
    for copy in stores:
        copy.wait()


def adam_down(facts, came, old):
    owned, rank, width = old[0].shape
    slots = len(came)
    shapes = [shape_of(old[0].shape, bf16), shape_of(old[0].shape, f32)]
    return pl.pallas_call(
        functools.partial(adam_kernel, slots),
        out_shape=shapes,
        in_specs=[SMEM] + [ANY] * (slots + 4),
        out_specs=[ANY] * 2,
        scratch_shapes=[pltpu.VMEM((slots, rank, width), bf16)]
        + [pltpu.VMEM(a.shape, a.dtype) for a in old]
        + [
            pltpu.VMEM(old[0].shape, bf16),
            pltpu.VMEM(old[0].shape, f32),
            pltpu.VMEM((rank, width), f32),
            pltpu.SemaphoreType.DMA((slots + 4 * owned,)),
            pltpu.SemaphoreType.DMA((2 * owned,)),
        ],
        compiler_params=params(60),
        cost_estimate=cost(owned * rank * width * 20, owned * rank * width * 60),
    )(facts, *came, *old)


def stack_kernel(own, across, out):
    out[0] = own[...]
    out[1] = across[...]


def stack_pair(own, across, flops):
    return pl.pallas_call(
        stack_kernel,
        out_shape=shape_of((2,) + own.shape, own.dtype),
        in_specs=[VMEM] * 2,
        out_specs=VMEM,
        compiler_params=params(16),
        cost_estimate=cost(flops, 2 * flops // 256),
    )(own, across)


def last_kernel(slots, tok_size, facts, came, *rest):
    old, rest = rest[:4], rest[4:]
    spread, tables, frozen = rest[0], rest[1 : 1 + slots], rest[1 + slots : -4]
    fresh, average, key_out, gradients = rest[-4:]
    raised = nn(spread[...].astype(f32).T.astype(bf16), stacked(tables))
    whole = frozen[0][...]
    for part in frozen[1:]:
        whole = whole + part[...].astype(f32)
    key_out[...] = (whole + (adapter_scale * BACK_SCALE) * raised).astype(bf16)
    me = lax.axis_index("tok")
    gradients[...] = jnp.zeros(gradients.shape, f32)
    for s in range(slots):
        gradients[facts[slots + s]] += came[lax.rem(me - s + tok_size, tok_size)].astype(f32)
    owned, rank, _ = gradients.shape
    for k in range(owned):

        def update(r, rows):
            fresh[k, r, :], average[k, r, :] = adam_step(
                *[ref[k, r, :] for ref in old], gradients[k, r, :]
            )

        each_rows(rank, update)


def last_step(facts, came, old, spread, tables, frozen, tok_size):
    shape = old[0].shape
    slots = len(tables)
    return pl.pallas_call(
        functools.partial(last_kernel, slots, tok_size),
        out_shape=[
            shape_of(shape, bf16),
            shape_of(shape, f32),
            shape_of(frozen[0].shape, bf16),
        ],
        in_specs=[SMEM] + [VMEM] * (6 + slots + len(frozen)),
        out_specs=[VMEM] * 3,
        scratch_shapes=[pltpu.VMEM(shape, f32)],
        compiler_params=params(16),
        cost_estimate=cost(old[0].size * 20, old[0].size * 20),
    )(facts, came, *old, spread, *tables, *frozen)


def after(value, *others):
    return lax.optimization_barrier((value, *others))[0]


def swap(block, axes, flips):
    sizes = [lax.axis_size(a) for a in axes]
    route = []
    for t in range(sizes[0]):
        for s in range(sizes[1]):
            source = (t ^ flips[0]) * sizes[1] + (s ^ flips[1])
            route.append((source, t * sizes[1] + s))
    return lax.ppermute(block, axes, route)


def per_device(
    tokens,
    frozen_key_weight,
    output_gradient,
    counts,
    placement,
    adapter_sequence,
    adapter_down,
    adapter_up,
    down_first_moment,
    down_second_moment,
    down_average,
    up_first_moment,
    up_second_moment,
    up_average,
):
    tok_size = lax.axis_size("tok")
    tp_size, sub_size = lax.axis_size("tp"), lax.axis_size("sub")
    shards = ("tp", "sub")
    square = tp_size == 2 and sub_size == 2
    rows, wide = tokens.shape
    narrow = output_gradient.shape[1]
    key_width = frozen_key_weight.shape[1]
    owned = adapter_down.shape[0]
    slots = placement.shape[1]
    rank = ADAPTER_RANK
    flip = lambda a: jnp.swapaxes(a, 1, 2)
    down, down_m, down_v, down_a = map(
        flip, (adapter_down, down_first_moment, down_second_moment, down_average)
    )
    up, up_m, up_v, up_a = map(flip, (adapter_up, up_first_moment, up_second_moment, up_average))

    def fetch(block, slot):
        return lax.ppermute(block, "tok", [((i + slot) % tok_size, i) for i in range(tok_size)])

    def give_back(block, slot):
        return lax.ppermute(block, "tok", [((i - slot) % tok_size, i) for i in range(tok_size)])

    def shared(part):
        if not square:
            return [lax.psum(part, shards)]
        both = part + swap(part, shards, (0, 1))
        return [both, swap(both, shards, (1, 0))]

    step = min(256, wide)

    facts, *sent = pl.pallas_call(
        functools.partial(select_kernel, slots, owned, tok_size),
        out_shape=[shape_of((2 * slots,), jnp.int32)]
        + [shape_of((rank, narrow), bf16)] * slots
        + [shape_of((rank, wide), bf16)] * slots,
        in_specs=[SMEM, SMEM, SMEM, ANY, ANY],
        out_specs=[SMEM] + [VMEM] * (2 * slots),
        scratch_shapes=[pltpu.SemaphoreType.DMA((2 * slots,))],
        compiler_params=params(56),
        cost_estimate=cost(0, 4 * slots * rank * (wide + narrow)),
    )(counts, placement, adapter_sequence, down, up)
    up_send, down_send = sent[:slots], sent[slots:]
    ready = counts[0, 0] > 0
    early = fetch(down_send[1], 1)
    up_tables = [up_send[0]] + [fetch(up_send[s], s) for s in range(1, slots)]
    if square:
        across = swap(after(output_gradient, facts), shards, (1, 0))
        pair = stack_pair(output_gradient, across, 2 * rows * wide * key_width)
        up_tables[0] = after(up_tables[0], pair)
    down_tables = [down_send[0], early] + [
        fetch(after(down_send[s], ready, early), s) for s in range(2, slots)
    ]
    up_tables[0] = after(up_tables[0], early)

    def group(work):
        shapes = jax.eval_shape(work)
        nothing = lambda: jax.tree.map(lambda a: jnp.zeros(a.shape, a.dtype), shapes)
        return lax.cond(ready, work, nothing)

    def back_work():
        part = pl.pallas_call(
            functools.partial(back_kernel, slots),
            out_shape=shape_of((rank, rows), f32),
            in_specs=[SMEM, VMEM] + [VMEM] * slots,
            out_specs=VMEM,
            compiler_params=params(16),
            cost_estimate=cost(2 * rows * narrow * rank * slots, 2 * rows * narrow),
        )(facts, output_gradient, *up_tables)
        parts = shared(part)
        if square:
            base = pl.pallas_call(
                functools.partial(base_kernel, narrow),
                out_shape=[shape_of((2, rows, narrow), f32)] * 2,
                in_specs=[VMEM, VMEM],
                out_specs=[VMEM, VMEM],
                compiler_params=params(16),
                cost_estimate=cost(2 * rows * wide * key_width, 2 * wide * (rows + key_width)),
            )(tokens, after(frozen_key_weight, parts[0]))
            grads = [swap(pair, shards, (0, 1))]
            parts = [after(parts[0], base[0]), parts[1]]
        else:
            base = []
            grads = [lax.all_gather(output_gradient, shards, axis=1, tiled=True)]
        spread, *sends = pl.pallas_call(
            functools.partial(part_down_kernel, slots, len(parts)),
            out_shape=[shape_of((slots * rank, rows), bf16)] + [shape_of((rank, wide), bf16)] * slots,
            in_specs=[SMEM, VMEM] + [VMEM] * len(parts),
            out_specs=[VMEM] * (1 + slots),
            compiler_params=params(16),
            cost_estimate=cost(2 * rows * wide * rank * slots, 2 * rows * wide),
        )(facts, tokens, *parts)
        return grads, base, spread, sends

    grads, base, spread_back, part_down = group(back_work)
    if square:
        grads = [output_gradient, across] + grads
    came = [part_down[0]] + [
        give_back(after(part_down[s], *down_tables[1:]), s) for s in range(1, slots)
    ]

    wide_step = min(512, wide)

    def input_whole(spread):
        return pl.pallas_call(
            functools.partial(input_kernel, slots, narrow),
            grid=(wide // wide_step,),
            out_shape=shape_of((rows, wide), bf16),
            in_specs=[
                pl.BlockSpec((slots * rank, rows), lambda i: (0, 0)),
                pl.BlockSpec((wide_step, key_width), lambda i: (i, 0)),
            ]
            + [pl.BlockSpec((rank, wide_step), lambda i: (0, i))] * slots
            + [pl.BlockSpec(g.shape, lambda i, r=g.ndim: (0,) * r) for g in grads],
            out_specs=pl.BlockSpec((rows, wide_step), lambda i: (0, i)),
            scratch_shapes=[
                pltpu.VMEM((rows, key_width), bf16),
                pltpu.VMEM((rows, slots * rank), bf16),
            ],
            compiler_params=params(16),
            cost_estimate=cost(
                2 * rows * wide * (key_width + rank * slots), 2 * wide * (rows + key_width)
            ),
        )(spread, frozen_key_weight, *down_tables, *grads)

    def low_work():
        part = pl.pallas_call(
            functools.partial(low_kernel, slots),
            out_shape=shape_of((rank, rows), f32),
            in_specs=[SMEM, VMEM] + [VMEM] * slots,
            out_specs=VMEM,
            compiler_params=params(16),
            cost_estimate=cost(2 * rows * wide * rank * slots, 2 * rows * wide),
        )(facts, tokens, *down_tables)
        parts = shared(part)
        input_gradient = input_whole(after(spread_back, parts[0]))
        if square:
            keep, send = base
            got = swap(send, shards, (0, 1))
            frozen, passing = keep[1] + got[1], (keep[0] + got[0]).astype(bf16)
            parts = [after(parts[0], input_gradient, frozen, passing), parts[1]]
        else:
            whole = jnp.dot(tokens, frozen_key_weight, preferred_element_type=f32)
            frozen = lax.psum_scatter(whole, shards, scatter_dimension=1, tiled=True)
            passing = ()
        spread, send = pl.pallas_call(
            functools.partial(second_kernel, slots, tok_size, len(parts)),
            out_shape=[
                shape_of((slots * rank, rows), bf16),
                shape_of((tok_size, rank, narrow), bf16),
            ],
            in_specs=[SMEM] + [VMEM] * (1 + len(parts)),
            out_specs=[VMEM] * 2,
            compiler_params=params(16),
            cost_estimate=cost(2 * rows * narrow * rank * slots, 2 * rows * narrow),
        )(facts, output_gradient, *parts)
        return spread, send, frozen, passing, input_gradient

    spread_low, part_up, frozen, passing, input_gradient = group(low_work)
    came_up = lax.all_to_all(part_up, "tok", split_axis=0, concat_axis=0, tiled=True)
    frozen = [frozen]
    if square:
        frozen.append(swap(passing, shards, (1, 0)))

    fresh_down, average_down = adam_down(facts, came, (down, down_m, down_v, down_a))
    fresh_up, average_up, key_output = last_step(
        facts,
        after(came_up, fresh_down),
        (up, up_m, up_v, up_a),
        spread_low,
        up_tables,
        frozen,
        tok_size,
    )
    return (
        key_output,
        input_gradient,
        flip(fresh_down),
        flip(fresh_up),
        flip(average_down),
        flip(average_up),
    )


def solution(mesh):
    rows = P(("groups", "tok"), ("tp", "sub"))
    cube = P(("groups", "tok"), ("tp", "sub"), None)
    return jax.shard_map(
        per_device,
        mesh=mesh,
        in_specs=(rows, P(("tp", "sub"), None), rows, P("groups", None), P("groups", None), P("groups"))
        + (cube,) * 8,
        out_specs=(rows, rows, cube, cube, cube, cube),
        check_vma=False,
    )
```

```python
import functools

import jax
import jax.numpy as jnp
from jax import lax
from jax.experimental import pallas as pl
from jax.experimental.pallas import tpu as pltpu
from jax.sharding import PartitionSpec as P

MODEL_WIDTH = 8192
ADAPTER_RANK = 64

adapter_scale = 0.5
learn_rate = 0.3
beta_one = 0.9
beta_two = 0.99
adam_eps = 1e-08
ema_decay = 0.9

LOW_SCALE = MODEL_WIDTH ** (-0.5)
BACK_SCALE = ADAPTER_RANK ** (-0.5)
MIB = 1024 * 1024

f32 = jnp.float32
bf16 = jnp.bfloat16

SMEM = pl.BlockSpec(memory_space=pltpu.SMEM)
VMEM = pl.BlockSpec(memory_space=pltpu.VMEM)
ANY = pl.BlockSpec(memory_space=pl.ANY)
HBM = pl.BlockSpec(memory_space=pltpu.HBM)


def shape_of(shape, dtype):
    return jax.ShapeDtypeStruct(tuple(shape), dtype)


SCHEDULE_SCALE = 3


def cost(flops, bytes_accessed):
    return pl.CostEstimate(
        flops=int(flops * SCHEDULE_SCALE),
        bytes_accessed=int(bytes_accessed * SCHEDULE_SCALE),
        transcendentals=0,
    )


def params(mib):
    return pltpu.CompilerParams(vmem_limit_bytes=mib * MIB)


def nt(a, b):
    return lax.dot_general(a, b, (((1,), (1,)), ((), ())), preferred_element_type=f32)


def nn(a, b):
    return lax.dot_general(a, b, (((1,), (0,)), ((), ())), preferred_element_type=f32)


def tn(a, b):
    return lax.dot_general(a, b, (((0,), (0,)), ((), ())), preferred_element_type=f32)


def facts_kernel(slots, owned, tok_size, counts, placement, sequence, facts):
    me = lax.axis_index("tok")
    total = jnp.int32(0)
    for s in range(slots):
        total = total + counts[me, s]
        facts[s] = total
        tenant = placement[lax.rem(me - s + tok_size, tok_size), s]
        place = jnp.int32(0)
        for k in range(1, owned):
            place = place + jnp.where(sequence[me * owned + k] == tenant, k, 0)
        facts[slots + s] = place


def slot_ends(facts, slots):
    return [facts[s] for s in range(slots)]


def slot_mask(ends, slot, shape):
    rows = lax.broadcasted_iota(jnp.int32, shape, 1)
    inside = rows < ends[slot]
    if slot:
        inside = inside & (rows >= ends[slot - 1])
    return inside


def pick_slot(ends, products, rank):
    rows = lax.broadcasted_iota(jnp.int32, (rank, products.shape[1]), 1)
    slots = products.shape[0] // rank
    out = products[(slots - 1) * rank :]
    for s in range(slots - 2, -1, -1):
        out = jnp.where(rows < ends[s], products[s * rank : (s + 1) * rank], out)
    return out


def spread_slots(ends, values):
    wide = values.astype(f32)
    return jnp.concatenate(
        [jnp.where(slot_mask(ends, s, wide.shape), wide, 0.0) for s in range(len(ends))], axis=0
    ).astype(bf16)


def paired_sum(refs):
    parts = [ref[...] for ref in refs]
    while len(parts) > 1:
        parts = [parts[i] + parts[i + 1] for i in range(0, len(parts), 2)]
    return parts[0]


def select_kernel(slots, owned, tok_size, counts, placement, sequence, down, up, facts, *rest):
    ups, downs, sems = rest[:slots], rest[slots : 2 * slots], rest[2 * slots]
    facts_kernel(slots, owned, tok_size, counts, placement, sequence, facts)
    copies = []
    order = list(range(1, slots)) + [0]
    for s in order:
        copies.append(pltpu.make_async_copy(up.at[facts[slots + s]], ups[s], sems.at[s]))
    for s in order:
        copies.append(pltpu.make_async_copy(down.at[facts[slots + s]], downs[s], sems.at[slots + s]))
    for copy in copies:
        copy.start()
    for copy in copies:
        copy.wait()


def base_kernel(width, tokens, weight, keep, send):
    tp, sub = lax.axis_index("tp"), lax.axis_index("sub")
    mine, other = tp, 1 - tp
    for ref, s in ((send, 1 - sub), (keep, sub)):
        for i, t in enumerate((other, mine)):
            start = pl.multiple_of((t * 2 + s) * width, width)
            ref[i] = nn(tokens[...], weight[:, pl.ds(start, width)])


def stacked(tables):
    return jnp.concatenate([t[...] for t in tables], axis=0)


def back_kernel(slots, facts, grad, *rest):
    tables, out = rest[:slots], rest[slots]
    out[...] = pick_slot(slot_ends(facts, slots), nt(stacked(tables), grad[...]), ADAPTER_RANK)


def part_down_kernel(slots, pieces, facts, tokens, *rest):
    parts, spread_out, outs = rest[:pieces], rest[pieces], rest[pieces + 1 :]
    ends = slot_ends(facts, slots)
    back = (paired_sum(parts) * BACK_SCALE).astype(bf16)
    spread = spread_slots(ends, back)
    spread_out[...] = spread
    for c in range(0, tokens.shape[1], 256):
        columns = slice(c, min(c + 256, tokens.shape[1]))
        product = (nn(spread, tokens[:, columns]) * (adapter_scale * LOW_SCALE)).astype(bf16)
        for s in range(slots):
            outs[s][:, columns] = product[s * ADAPTER_RANK : (s + 1) * ADAPTER_RANK]


def low_kernel(slots, facts, tokens, *rest):
    tables, out = rest[:slots], rest[slots]
    out[...] = pick_slot(slot_ends(facts, slots), nt(stacked(tables), tokens[...]), ADAPTER_RANK)


def input_kernel(slots, width, spread, weight, *rest):
    tables, grads, (out, whole, turned) = rest[:slots], rest[slots:-3], rest[-3:]

    @pl.when(pl.program_id(0) == 0)
    def _():
        turned[...] = spread[...].astype(f32).T.astype(bf16)
        if len(grads) == 1:
            whole[...] = grads[0][...]
        else:
            tp, sub = lax.axis_index("tp"), lax.axis_index("sub")
            pieces = (grads[0][...], grads[1][...], grads[2][0], grads[2][1])
            for piece, t, s in zip(pieces, (tp, 1 - tp, tp, 1 - tp), (sub, sub, 1 - sub, 1 - sub)):
                start = pl.multiple_of((t * 2 + s) * width, width)
                whole[:, pl.ds(start, width)] = piece

    for c in range(0, out.shape[1], 256):
        columns = slice(c, min(c + 256, out.shape[1]))
        frozen = None
        for start in range(0, whole.shape[1], 256):
            term = nt(whole[:, start : start + 256], weight[columns, start : start + 256])
            frozen = term if frozen is None else frozen + term
        table = jnp.concatenate([t[:, columns] for t in tables], axis=0)
        adapter = nn(turned[...], table)
        out[:, columns] = (frozen + (adapter_scale * LOW_SCALE) * adapter).astype(bf16)


def second_kernel(slots, tok_size, pieces, facts, grad, *rest):
    parts, (spread_low, out) = rest[:pieces], rest[pieces:]
    me = lax.axis_index("tok")
    low = (paired_sum(parts) * LOW_SCALE).astype(bf16)
    spread = spread_slots(slot_ends(facts, slots), low)
    spread_low[...] = spread
    product = (nn(spread, grad[...]) * (adapter_scale * BACK_SCALE)).astype(bf16)
    for s in range(slots):
        out[lax.rem(me + s, tok_size)] = product[s * ADAPTER_RANK : (s + 1) * ADAPTER_RANK]


def adam_step(weights, mean_old, var_old, avg_old, gradient):
    mean_new = beta_one * mean_old + (1.0 - beta_one) * gradient
    var_new = beta_two * var_old + (1.0 - beta_two) * gradient * gradient
    root = var_new * lax.rsqrt(var_new) + adam_eps
    inverse = pl.reciprocal(root, approx=True)
    inverse = inverse * (2.0 - root * inverse)
    updated = weights.astype(f32) - learn_rate * mean_new * inverse
    return updated.astype(bf16), ema_decay * avg_old + (1.0 - ema_decay) * updated


def each_rows(count, body):
    rows = 16

    def step(i, _):
        body(pl.ds(pl.multiple_of(i * rows, rows), rows), rows)
        return 0

    lax.fori_loop(0, count // rows, step, 0)


def adam_kernel(slots, facts, *rest):
    came, old, rest = rest[:slots], rest[slots : slots + 4], rest[slots + 4 :]
    fresh, average, came_here = rest[:3]
    old_here, rest = rest[3:7], rest[7:]
    fresh_here, average_here, gradient_ref, in_sems, out_sems = rest
    owned, rank, width = fresh_here.shape

    arrivals = [
        pltpu.make_async_copy(came[s], came_here.at[s], in_sems.at[s]) for s in range(slots)
    ]
    loads, stores = [], []
    for k in range(owned):
        for i in range(4):
            sem = in_sems.at[slots + 4 * k + i]
            loads.append(pltpu.make_async_copy(old[i].at[k], old_here[i].at[k], sem))
        for i, (here, there) in enumerate(((fresh_here, fresh), (average_here, average))):
            sem = out_sems.at[2 * k + i]
            stores.append(pltpu.make_async_copy(here.at[k], there.at[k], sem))
    for copy in arrivals + loads:
        copy.start()

    for copy in arrivals:
        copy.wait()
    for k in range(owned):

        def clear(r, rows):
            gradient_ref[r, :] = jnp.zeros((rows, width), f32)

        each_rows(rank, clear)
        for s in range(slots):

            @pl.when(facts[slots + s] == k)
            def _():
                def add(r, rows):
                    gradient_ref[r, :] += came_here[s, r, :].astype(f32)

                each_rows(rank, add)

        for copy in loads[4 * k : 4 * k + 4]:
            copy.wait()

        def update(r, rows):
            for c in range(0, width, 512):
                columns = slice(c, min(c + 512, width))
                fresh_here[k, r, columns], average_here[k, r, columns] = adam_step(
                    *[ref[k, r, columns] for ref in old_here], gradient_ref[r, columns]
                )

        each_rows(rank, update)
        for copy in stores[2 * k : 2 * k + 2]:
            copy.start()
    for copy in stores:
        copy.wait()


def adam_down(facts, came, old):
    owned, rank, width = old[0].shape
    slots = len(came)
    shapes = [shape_of(old[0].shape, bf16), shape_of(old[0].shape, f32)]
    return pl.pallas_call(
        functools.partial(adam_kernel, slots),
        out_shape=shapes,
        in_specs=[SMEM] + [ANY] * (slots + 4),
        out_specs=[ANY] * 2,
        scratch_shapes=[pltpu.VMEM((slots, rank, width), bf16)]
        + [pltpu.VMEM(a.shape, a.dtype) for a in old]
        + [
            pltpu.VMEM(old[0].shape, bf16),
            pltpu.VMEM(old[0].shape, f32),
            pltpu.VMEM((rank, width), f32),
            pltpu.SemaphoreType.DMA((slots + 4 * owned,)),
            pltpu.SemaphoreType.DMA((2 * owned,)),
        ],
        compiler_params=params(60),
        cost_estimate=cost(owned * rank * width * 20, owned * rank * width * 60),
    )(facts, *came, *old)


def stack_kernel(own, across, out):
    out[0] = own[...]
    out[1] = across[...]


def stack_pair(own, across, flops):
    return pl.pallas_call(
        stack_kernel,
        out_shape=shape_of((2,) + own.shape, own.dtype),
        in_specs=[VMEM] * 2,
        out_specs=VMEM,
        compiler_params=params(16),
        cost_estimate=cost(flops, 2 * flops // 256),
    )(own, across)


def last_kernel(slots, tok_size, facts, came, *rest):
    old, rest = rest[:4], rest[4:]
    spread, tables, frozen = rest[0], rest[1 : 1 + slots], rest[1 + slots : -4]
    fresh, average, key_out, gradients = rest[-4:]
    raised = nn(spread[...].astype(f32).T.astype(bf16), stacked(tables))
    whole = frozen[0][...]
    for part in frozen[1:]:
        whole = whole + part[...].astype(f32)
    key_out[...] = (whole + (adapter_scale * BACK_SCALE) * raised).astype(bf16)
    me = lax.axis_index("tok")
    gradients[...] = jnp.zeros(gradients.shape, f32)
    for s in range(slots):
        gradients[facts[slots + s]] += came[lax.rem(me - s + tok_size, tok_size)].astype(f32)
    owned, rank, _ = gradients.shape
    for k in range(owned):

        def update(r, rows):
            fresh[k, r, :], average[k, r, :] = adam_step(
                *[ref[k, r, :] for ref in old], gradients[k, r, :]
            )

        each_rows(rank, update)


def last_step(facts, came, old, spread, tables, frozen, tok_size):
    shape = old[0].shape
    slots = len(tables)
    return pl.pallas_call(
        functools.partial(last_kernel, slots, tok_size),
        out_shape=[
            shape_of(shape, bf16),
            shape_of(shape, f32),
            shape_of(frozen[0].shape, bf16),
        ],
        in_specs=[SMEM] + [VMEM] * (6 + slots + len(frozen)),
        out_specs=[VMEM] * 3,
        scratch_shapes=[pltpu.VMEM(shape, f32)],
        compiler_params=params(16),
        cost_estimate=cost(old[0].size * 20, old[0].size * 20),
    )(facts, came, *old, spread, *tables, *frozen)


def after(value, *others):
    return lax.optimization_barrier((value, *others))[0]


def swap(block, axes, flips):
    sizes = [lax.axis_size(a) for a in axes]
    route = []
    for t in range(sizes[0]):
        for s in range(sizes[1]):
            source = (t ^ flips[0]) * sizes[1] + (s ^ flips[1])
            route.append((source, t * sizes[1] + s))
    return lax.ppermute(block, axes, route)


def per_device(
    tokens,
    frozen_key_weight,
    output_gradient,
    counts,
    placement,
    adapter_sequence,
    adapter_down,
    adapter_up,
    down_first_moment,
    down_second_moment,
    down_average,
    up_first_moment,
    up_second_moment,
    up_average,
):
    tok_size = lax.axis_size("tok")
    tp_size, sub_size = lax.axis_size("tp"), lax.axis_size("sub")
    shards = ("tp", "sub")
    square = tp_size == 2 and sub_size == 2
    rows, wide = tokens.shape
    narrow = output_gradient.shape[1]
    key_width = frozen_key_weight.shape[1]
    owned = adapter_down.shape[0]
    slots = placement.shape[1]
    rank = ADAPTER_RANK
    flip = lambda a: jnp.swapaxes(a, 1, 2)
    down, down_m, down_v, down_a = map(
        flip, (adapter_down, down_first_moment, down_second_moment, down_average)
    )
    up, up_m, up_v, up_a = map(flip, (adapter_up, up_first_moment, up_second_moment, up_average))

    def fetch(block, slot):
        return lax.ppermute(block, "tok", [((i + slot) % tok_size, i) for i in range(tok_size)])

    def give_back(block, slot):
        return lax.ppermute(block, "tok", [((i - slot) % tok_size, i) for i in range(tok_size)])

    def shared(part):
        if not square:
            return [lax.psum(part, shards)]
        both = part + swap(part, shards, (0, 1))
        return [both, swap(both, shards, (1, 0))]

    step = min(256, wide)

    facts, *sent = pl.pallas_call(
        functools.partial(select_kernel, slots, owned, tok_size),
        out_shape=[shape_of((2 * slots,), jnp.int32)]
        + [shape_of((rank, narrow), bf16)] * slots
        + [shape_of((rank, wide), bf16)] * slots,
        in_specs=[SMEM, SMEM, SMEM, ANY, ANY],
        out_specs=[SMEM] + [VMEM] * (2 * slots),
        scratch_shapes=[pltpu.SemaphoreType.DMA((2 * slots,))],
        compiler_params=params(56),
        cost_estimate=cost(0, 4 * slots * rank * (wide + narrow)),
    )(counts, placement, adapter_sequence, down, up)
    up_send, down_send = sent[:slots], sent[slots:]
    ready = counts[0, 0] > 0
    early = fetch(down_send[1], 1)
    up_tables = [up_send[0]] + [fetch(up_send[s], s) for s in range(1, slots)]
    if square:
        across = swap(after(output_gradient, facts), shards, (1, 0))
        pair = stack_pair(output_gradient, across, 2 * rows * wide * key_width)
        up_tables[0] = after(up_tables[0], pair)
    down_tables = [down_send[0], early] + [
        fetch(after(down_send[s], ready, early), s) for s in range(2, slots)
    ]
    up_tables[0] = after(up_tables[0], early)

    def group(work):
        shapes = jax.eval_shape(work)
        nothing = lambda: jax.tree.map(lambda a: jnp.zeros(a.shape, a.dtype), shapes)
        return lax.cond(ready, work, nothing)

    def back_work():
        part = pl.pallas_call(
            functools.partial(back_kernel, slots),
            out_shape=shape_of((rank, rows), f32),
            in_specs=[SMEM, VMEM] + [VMEM] * slots,
            out_specs=VMEM,
            compiler_params=params(16),
            cost_estimate=cost(2 * rows * narrow * rank * slots, 2 * rows * narrow),
        )(facts, output_gradient, *up_tables)
        parts = shared(part)
        if square:
            base = pl.pallas_call(
                functools.partial(base_kernel, narrow),
                out_shape=[shape_of((2, rows, narrow), f32)] * 2,
                in_specs=[VMEM, VMEM],
                out_specs=[VMEM, VMEM],
                compiler_params=params(16),
                cost_estimate=cost(2 * rows * wide * key_width, 2 * wide * (rows + key_width)),
            )(tokens, after(frozen_key_weight, parts[0]))
            grads = [swap(pair, shards, (0, 1))]
            parts = [after(parts[0], base[0]), parts[1]]
        else:
            base = []
            grads = [lax.all_gather(output_gradient, shards, axis=1, tiled=True)]
        spread, *sends = pl.pallas_call(
            functools.partial(part_down_kernel, slots, len(parts)),
            out_shape=[shape_of((slots * rank, rows), bf16)] + [shape_of((rank, wide), bf16)] * slots,
            in_specs=[SMEM, VMEM] + [VMEM] * len(parts),
            out_specs=[VMEM] * (1 + slots),
            compiler_params=params(16),
            cost_estimate=cost(2 * rows * wide * rank * slots, 2 * rows * wide),
        )(facts, tokens, *parts)
        return grads, base, spread, sends

    grads, base, spread_back, part_down = group(back_work)
    if square:
        grads = [output_gradient, across] + grads
    came = {0: part_down[0]}
    for s in sorted(range(1, slots), key=lambda s: s == 2):
        early = [] if s == 2 else down_tables[1:]
        came[s] = give_back(after(part_down[s], *early), s)
    came = [came[s] for s in range(slots)]

    wide_step = min(512, wide)

    def input_whole(spread):
        return pl.pallas_call(
            functools.partial(input_kernel, slots, narrow),
            grid=(wide // wide_step,),
            out_shape=shape_of((rows, wide), bf16),
            in_specs=[
                pl.BlockSpec((slots * rank, rows), lambda i: (0, 0)),
                pl.BlockSpec((wide_step, key_width), lambda i: (i, 0)),
            ]
            + [pl.BlockSpec((rank, wide_step), lambda i: (0, i))] * slots
            + [pl.BlockSpec(g.shape, lambda i, r=g.ndim: (0,) * r) for g in grads],
            out_specs=pl.BlockSpec((rows, wide_step), lambda i: (0, i)),
            scratch_shapes=[
                pltpu.VMEM((rows, key_width), bf16),
                pltpu.VMEM((rows, slots * rank), bf16),
            ],
            compiler_params=params(16),
            cost_estimate=cost(
                2 * rows * wide * (key_width + rank * slots), 2 * wide * (rows + key_width)
            ),
        )(spread, frozen_key_weight, *down_tables, *grads)

    def low_work():
        part = pl.pallas_call(
            functools.partial(low_kernel, slots),
            out_shape=shape_of((rank, rows), f32),
            in_specs=[SMEM, VMEM] + [VMEM] * slots,
            out_specs=VMEM,
            compiler_params=params(16),
            cost_estimate=cost(2 * rows * wide * rank * slots, 2 * rows * wide),
        )(facts, tokens, *down_tables)
        parts = shared(part)
        input_gradient = input_whole(after(spread_back, parts[0]))
        if square:
            keep, send = base
            got = swap(send, shards, (0, 1))
            frozen, passing = keep[1] + got[1], (keep[0] + got[0]).astype(bf16)
            parts = [after(parts[0], input_gradient, frozen, passing), parts[1]]
        else:
            whole = jnp.dot(tokens, frozen_key_weight, preferred_element_type=f32)
            frozen = lax.psum_scatter(whole, shards, scatter_dimension=1, tiled=True)
            passing = ()
        spread, send = pl.pallas_call(
            functools.partial(second_kernel, slots, tok_size, len(parts)),
            out_shape=[
                shape_of((slots * rank, rows), bf16),
                shape_of((tok_size, rank, narrow), bf16),
            ],
            in_specs=[SMEM] + [VMEM] * (1 + len(parts)),
            out_specs=[VMEM] * 2,
            compiler_params=params(16),
            cost_estimate=cost(2 * rows * narrow * rank * slots, 2 * rows * narrow),
        )(facts, output_gradient, *parts)
        return spread, send, frozen, passing, input_gradient

    spread_low, part_up, frozen, passing, input_gradient = group(low_work)
    came_up = lax.all_to_all(part_up, "tok", split_axis=0, concat_axis=0, tiled=True)
    frozen = [frozen]
    if square:
        frozen.append(swap(passing, shards, (1, 0)))

    fresh_down, average_down = adam_down(facts, came, (down, down_m, down_v, down_a))
    fresh_up, average_up, key_output = last_step(
        facts,
        after(came_up, fresh_down),
        (up, up_m, up_v, up_a),
        spread_low,
        up_tables,
        frozen,
        tok_size,
    )
    return (
        key_output,
        input_gradient,
        flip(fresh_down),
        flip(fresh_up),
        flip(average_down),
        flip(average_up),
    )


def solution(mesh):
    rows = P(("groups", "tok"), ("tp", "sub"))
    cube = P(("groups", "tok"), ("tp", "sub"), None)
    return jax.shard_map(
        per_device,
        mesh=mesh,
        in_specs=(rows, P(("tp", "sub"), None), rows, P("groups", None), P("groups", None), P("groups"))
        + (cube,) * 8,
        out_specs=(rows, rows, cube, cube, cube, cube),
        check_vma=False,
    )
```

```python
import functools

import jax
import jax.numpy as jnp
from jax import lax
from jax.experimental import pallas as pl
from jax.experimental.pallas import tpu as pltpu
from jax.sharding import PartitionSpec as P

MODEL_WIDTH = 8192
ADAPTER_RANK = 64

adapter_scale = 0.5
learn_rate = 0.3
beta_one = 0.9
beta_two = 0.99
adam_eps = 1e-08
ema_decay = 0.9

LOW_SCALE = MODEL_WIDTH ** (-0.5)
BACK_SCALE = ADAPTER_RANK ** (-0.5)
MIB = 1024 * 1024

f32 = jnp.float32
bf16 = jnp.bfloat16

SMEM = pl.BlockSpec(memory_space=pltpu.SMEM)
VMEM = pl.BlockSpec(memory_space=pltpu.VMEM)
ANY = pl.BlockSpec(memory_space=pl.ANY)
HBM = pl.BlockSpec(memory_space=pltpu.HBM)


def shape_of(shape, dtype):
    return jax.ShapeDtypeStruct(tuple(shape), dtype)


SCHEDULE_SCALE = 3


def cost(flops, bytes_accessed):
    return pl.CostEstimate(
        flops=int(flops * SCHEDULE_SCALE),
        bytes_accessed=int(bytes_accessed * SCHEDULE_SCALE),
        transcendentals=0,
    )


def params(mib):
    return pltpu.CompilerParams(vmem_limit_bytes=mib * MIB)


def nt(a, b):
    return lax.dot_general(a, b, (((1,), (1,)), ((), ())), preferred_element_type=f32)


def nn(a, b):
    return lax.dot_general(a, b, (((1,), (0,)), ((), ())), preferred_element_type=f32)


def tn(a, b):
    return lax.dot_general(a, b, (((0,), (0,)), ((), ())), preferred_element_type=f32)


def facts_kernel(slots, owned, tok_size, counts, placement, sequence, facts):
    me = lax.axis_index("tok")
    total = jnp.int32(0)
    for s in range(slots):
        total = total + counts[me, s]
        facts[s] = total
        tenant = placement[lax.rem(me - s + tok_size, tok_size), s]
        place = jnp.int32(0)
        for k in range(1, owned):
            place = place + jnp.where(sequence[me * owned + k] == tenant, k, 0)
        facts[slots + s] = place


def slot_ends(facts, slots):
    return [facts[s] for s in range(slots)]


def slot_mask(ends, slot, shape):
    rows = lax.broadcasted_iota(jnp.int32, shape, 1)
    inside = rows < ends[slot]
    if slot:
        inside = inside & (rows >= ends[slot - 1])
    return inside


def pick_slot(ends, products, rank):
    rows = lax.broadcasted_iota(jnp.int32, (rank, products.shape[1]), 1)
    slots = products.shape[0] // rank
    out = products[(slots - 1) * rank :]
    for s in range(slots - 2, -1, -1):
        out = jnp.where(rows < ends[s], products[s * rank : (s + 1) * rank], out)
    return out


def spread_slots(ends, values):
    wide = values.astype(f32)
    return jnp.concatenate(
        [jnp.where(slot_mask(ends, s, wide.shape), wide, 0.0) for s in range(len(ends))], axis=0
    ).astype(bf16)


def paired_sum(refs):
    parts = [ref[...] for ref in refs]
    while len(parts) > 1:
        parts = [parts[i] + parts[i + 1] for i in range(0, len(parts), 2)]
    return parts[0]


def select_kernel(slots, owned, tok_size, counts, placement, sequence, down, up, facts, *rest):
    ups, downs, sems = rest[:slots], rest[slots : 2 * slots], rest[2 * slots]
    facts_kernel(slots, owned, tok_size, counts, placement, sequence, facts)
    copies = []
    order = list(range(1, slots)) + [0]
    for s in order:
        copies.append(pltpu.make_async_copy(up.at[facts[slots + s]], ups[s], sems.at[s]))
    for s in order:
        copies.append(pltpu.make_async_copy(down.at[facts[slots + s]], downs[s], sems.at[slots + s]))
    for copy in copies:
        copy.start()
    for copy in copies:
        copy.wait()


def base_kernel(width, tokens, weight, keep, send):
    tp, sub = lax.axis_index("tp"), lax.axis_index("sub")
    mine, other = tp, 1 - tp
    for ref, s in ((send, 1 - sub), (keep, sub)):
        for i, t in enumerate((other, mine)):
            start = pl.multiple_of((t * 2 + s) * width, width)
            ref[i] = nn(tokens[...], weight[:, pl.ds(start, width)])


def stacked(tables):
    return jnp.concatenate([t[...] for t in tables], axis=0)


def back_kernel(slots, facts, grad, *rest):
    tables, out = rest[:slots], rest[slots]
    out[...] = pick_slot(slot_ends(facts, slots), nt(stacked(tables), grad[...]), ADAPTER_RANK)


def part_down_kernel(slots, pieces, facts, tokens, *rest):
    parts, spread_out, outs = rest[:pieces], rest[pieces], rest[pieces + 1 :]
    ends = slot_ends(facts, slots)
    back = (paired_sum(parts) * BACK_SCALE).astype(bf16)
    spread = spread_slots(ends, back)
    spread_out[...] = spread
    for c in range(0, tokens.shape[1], 256):
        columns = slice(c, min(c + 256, tokens.shape[1]))
        product = (nn(spread, tokens[:, columns]) * (adapter_scale * LOW_SCALE)).astype(bf16)
        for s in range(slots):
            outs[s][:, columns] = product[s * ADAPTER_RANK : (s + 1) * ADAPTER_RANK]


def low_kernel(slots, facts, tokens, *rest):
    tables, out = rest[:slots], rest[slots]
    out[...] = pick_slot(slot_ends(facts, slots), nt(stacked(tables), tokens[...]), ADAPTER_RANK)


def input_kernel(slots, width, spread, weight, *rest):
    tables, grads, (out, whole, turned) = rest[:slots], rest[slots:-3], rest[-3:]

    @pl.when(pl.program_id(0) == 0)
    def _():
        turned[...] = spread[...].astype(f32).T.astype(bf16)
        if len(grads) == 1:
            whole[...] = grads[0][...]
        else:
            tp, sub = lax.axis_index("tp"), lax.axis_index("sub")
            pieces = (grads[0][...], grads[1][...], grads[2][0], grads[2][1])
            for piece, t, s in zip(pieces, (tp, 1 - tp, tp, 1 - tp), (sub, sub, 1 - sub, 1 - sub)):
                start = pl.multiple_of((t * 2 + s) * width, width)
                whole[:, pl.ds(start, width)] = piece

    for c in range(0, out.shape[1], 256):
        columns = slice(c, min(c + 256, out.shape[1]))
        frozen = None
        for start in range(0, whole.shape[1], 256):
            term = nt(whole[:, start : start + 256], weight[columns, start : start + 256])
            frozen = term if frozen is None else frozen + term
        table = jnp.concatenate([t[:, columns] for t in tables], axis=0)
        adapter = nn(turned[...], table)
        out[:, columns] = (frozen + (adapter_scale * LOW_SCALE) * adapter).astype(bf16)


def second_kernel(slots, tok_size, pieces, facts, grad, *rest):
    parts, (spread_low, out) = rest[:pieces], rest[pieces:]
    me = lax.axis_index("tok")
    low = (paired_sum(parts) * LOW_SCALE).astype(bf16)
    spread = spread_slots(slot_ends(facts, slots), low)
    spread_low[...] = spread
    product = (nn(spread, grad[...]) * (adapter_scale * BACK_SCALE)).astype(bf16)
    for s in range(slots):
        out[lax.rem(me + s, tok_size)] = product[s * ADAPTER_RANK : (s + 1) * ADAPTER_RANK]


def adam_step(weights, mean_old, var_old, avg_old, gradient):
    mean_new = beta_one * mean_old + (1.0 - beta_one) * gradient
    var_new = beta_two * var_old + (1.0 - beta_two) * gradient * gradient
    root = var_new * lax.rsqrt(var_new) + adam_eps
    inverse = pl.reciprocal(root, approx=True)
    inverse = inverse * (2.0 - root * inverse)
    updated = weights.astype(f32) - learn_rate * mean_new * inverse
    return updated.astype(bf16), ema_decay * avg_old + (1.0 - ema_decay) * updated


def each_rows(count, body):
    rows = 16

    for i in range(count // rows):
        body(slice(i * rows, (i + 1) * rows), rows)


def adam_kernel(slots, facts, *rest):
    came, old, rest = rest[:slots], rest[slots : slots + 4], rest[slots + 4 :]
    fresh, average, came_here = rest[:3]
    old_here, rest = rest[3:7], rest[7:]
    fresh_here, average_here, gradient_ref, in_sems, out_sems = rest
    owned, rank, width = fresh_here.shape

    arrivals = [
        pltpu.make_async_copy(came[s], came_here.at[s], in_sems.at[s]) for s in range(slots)
    ]
    loads, stores = [], []
    for k in range(owned):
        for i in range(4):
            sem = in_sems.at[slots + 4 * k + i]
            loads.append(pltpu.make_async_copy(old[i].at[k], old_here[i].at[k], sem))
        for i, (here, there) in enumerate(((fresh_here, fresh), (average_here, average))):
            sem = out_sems.at[2 * k + i]
            stores.append(pltpu.make_async_copy(here.at[k], there.at[k], sem))
    for copy in arrivals + loads:
        copy.start()

    for copy in arrivals:
        copy.wait()
    for k in range(owned):

        def clear(r, rows):
            gradient_ref[r, :] = jnp.zeros((rows, width), f32)

        each_rows(rank, clear)
        for s in range(slots):

            @pl.when(facts[slots + s] == k)
            def _():
                def add(r, rows):
                    gradient_ref[r, :] += came_here[s, r, :].astype(f32)

                each_rows(rank, add)

        for copy in loads[4 * k : 4 * k + 4]:
            copy.wait()

        def update(r, rows):
            for c in range(0, width, 512):
                columns = slice(c, min(c + 512, width))
                fresh_here[k, r, columns], average_here[k, r, columns] = adam_step(
                    *[ref[k, r, columns] for ref in old_here], gradient_ref[r, columns]
                )

        each_rows(rank, update)
        for copy in stores[2 * k : 2 * k + 2]:
            copy.start()
    for copy in stores:
        copy.wait()


def adam_down(facts, came, old):
    owned, rank, width = old[0].shape
    slots = len(came)
    shapes = [shape_of(old[0].shape, bf16), shape_of(old[0].shape, f32)]
    return pl.pallas_call(
        functools.partial(adam_kernel, slots),
        out_shape=shapes,
        in_specs=[SMEM] + [ANY] * (slots + 4),
        out_specs=[ANY] * 2,
        scratch_shapes=[pltpu.VMEM((slots, rank, width), bf16)]
        + [pltpu.VMEM(a.shape, a.dtype) for a in old]
        + [
            pltpu.VMEM(old[0].shape, bf16),
            pltpu.VMEM(old[0].shape, f32),
            pltpu.VMEM((rank, width), f32),
            pltpu.SemaphoreType.DMA((slots + 4 * owned,)),
            pltpu.SemaphoreType.DMA((2 * owned,)),
        ],
        compiler_params=params(60),
        cost_estimate=cost(owned * rank * width * 20, owned * rank * width * 60),
    )(facts, *came, *old)


def stack_kernel(own, across, out):
    out[0] = own[...]
    out[1] = across[...]


def stack_pair(own, across, flops):
    return pl.pallas_call(
        stack_kernel,
        out_shape=shape_of((2,) + own.shape, own.dtype),
        in_specs=[VMEM] * 2,
        out_specs=VMEM,
        compiler_params=params(16),
        cost_estimate=cost(flops, 2 * flops // 256),
    )(own, across)


def last_kernel(slots, tok_size, facts, came, *rest):
    old, rest = rest[:4], rest[4:]
    spread, tables, frozen = rest[0], rest[1 : 1 + slots], rest[1 + slots : -4]
    fresh, average, key_out, gradients = rest[-4:]
    raised = nn(spread[...].astype(f32).T.astype(bf16), stacked(tables))
    whole = frozen[0][...]
    for part in frozen[1:]:
        whole = whole + part[...].astype(f32)
    key_out[...] = (whole + (adapter_scale * BACK_SCALE) * raised).astype(bf16)
    me = lax.axis_index("tok")
    gradients[...] = jnp.zeros(gradients.shape, f32)
    for s in range(slots):
        gradients[facts[slots + s]] += came[lax.rem(me - s + tok_size, tok_size)].astype(f32)
    owned, rank, _ = gradients.shape
    for k in range(owned):

        def update(r, rows):
            fresh[k, r, :], average[k, r, :] = adam_step(
                *[ref[k, r, :] for ref in old], gradients[k, r, :]
            )

        each_rows(rank, update)


def last_step(facts, came, old, spread, tables, frozen, tok_size):
    shape = old[0].shape
    slots = len(tables)
    return pl.pallas_call(
        functools.partial(last_kernel, slots, tok_size),
        out_shape=[
            shape_of(shape, bf16),
            shape_of(shape, f32),
            shape_of(frozen[0].shape, bf16),
        ],
        in_specs=[SMEM] + [VMEM] * (6 + slots + len(frozen)),
        out_specs=[VMEM] * 3,
        scratch_shapes=[pltpu.VMEM(shape, f32)],
        compiler_params=params(16),
        cost_estimate=cost(old[0].size * 20, old[0].size * 20),
    )(facts, came, *old, spread, *tables, *frozen)


def after(value, *others):
    return lax.optimization_barrier((value, *others))[0]


def swap(block, axes, flips):
    sizes = [lax.axis_size(a) for a in axes]
    route = []
    for t in range(sizes[0]):
        for s in range(sizes[1]):
            source = (t ^ flips[0]) * sizes[1] + (s ^ flips[1])
            route.append((source, t * sizes[1] + s))
    return lax.ppermute(block, axes, route)


def per_device(
    tokens,
    frozen_key_weight,
    output_gradient,
    counts,
    placement,
    adapter_sequence,
    adapter_down,
    adapter_up,
    down_first_moment,
    down_second_moment,
    down_average,
    up_first_moment,
    up_second_moment,
    up_average,
):
    tok_size = lax.axis_size("tok")
    tp_size, sub_size = lax.axis_size("tp"), lax.axis_size("sub")
    shards = ("tp", "sub")
    square = tp_size == 2 and sub_size == 2
    rows, wide = tokens.shape
    narrow = output_gradient.shape[1]
    key_width = frozen_key_weight.shape[1]
    owned = adapter_down.shape[0]
    slots = placement.shape[1]
    rank = ADAPTER_RANK
    flip = lambda a: jnp.swapaxes(a, 1, 2)
    down, down_m, down_v, down_a = map(
        flip, (adapter_down, down_first_moment, down_second_moment, down_average)
    )
    up, up_m, up_v, up_a = map(flip, (adapter_up, up_first_moment, up_second_moment, up_average))

    def fetch(block, slot):
        return lax.ppermute(block, "tok", [((i + slot) % tok_size, i) for i in range(tok_size)])

    def give_back(block, slot):
        return lax.ppermute(block, "tok", [((i - slot) % tok_size, i) for i in range(tok_size)])

    def shared(part):
        if not square:
            return [lax.psum(part, shards)]
        both = part + swap(part, shards, (0, 1))
        return [both, swap(both, shards, (1, 0))]

    step = min(256, wide)

    facts, *sent = pl.pallas_call(
        functools.partial(select_kernel, slots, owned, tok_size),
        out_shape=[shape_of((2 * slots,), jnp.int32)]
        + [shape_of((rank, narrow), bf16)] * slots
        + [shape_of((rank, wide), bf16)] * slots,
        in_specs=[SMEM, SMEM, SMEM, ANY, ANY],
        out_specs=[SMEM] + [VMEM] * (2 * slots),
        scratch_shapes=[pltpu.SemaphoreType.DMA((2 * slots,))],
        compiler_params=params(56),
        cost_estimate=cost(0, 4 * slots * rank * (wide + narrow)),
    )(counts, placement, adapter_sequence, down, up)
    up_send, down_send = sent[:slots], sent[slots:]
    ready = counts[0, 0] > 0
    early = fetch(down_send[1], 1)
    up_tables = [up_send[0]] + [fetch(up_send[s], s) for s in range(1, slots)]
    if square:
        across = swap(after(output_gradient, facts), shards, (1, 0))
        pair = stack_pair(output_gradient, across, 2 * rows * wide * key_width)
        up_tables[0] = after(up_tables[0], pair)
    down_tables = [down_send[0], early] + [
        fetch(after(down_send[s], ready, early), s) for s in range(2, slots)
    ]
    up_tables[0] = after(up_tables[0], early)

    def group(work):
        shapes = jax.eval_shape(work)
        nothing = lambda: jax.tree.map(lambda a: jnp.zeros(a.shape, a.dtype), shapes)
        return lax.cond(ready, work, nothing)

    def back_work():
        part = pl.pallas_call(
            functools.partial(back_kernel, slots),
            out_shape=shape_of((rank, rows), f32),
            in_specs=[SMEM, VMEM] + [VMEM] * slots,
            out_specs=VMEM,
            compiler_params=params(16),
            cost_estimate=cost(2 * rows * narrow * rank * slots, 2 * rows * narrow),
        )(facts, output_gradient, *up_tables)
        parts = shared(part)
        if square:
            base = pl.pallas_call(
                functools.partial(base_kernel, narrow),
                out_shape=[shape_of((2, rows, narrow), f32)] * 2,
                in_specs=[VMEM, VMEM],
                out_specs=[VMEM, VMEM],
                compiler_params=params(16),
                cost_estimate=cost(2 * rows * wide * key_width, 2 * wide * (rows + key_width)),
            )(tokens, after(frozen_key_weight, parts[0]))
            grads = [swap(pair, shards, (0, 1))]
            parts = [after(parts[0], base[0]), parts[1]]
        else:
            base = []
            grads = [lax.all_gather(output_gradient, shards, axis=1, tiled=True)]
        spread, *sends = pl.pallas_call(
            functools.partial(part_down_kernel, slots, len(parts)),
            out_shape=[shape_of((slots * rank, rows), bf16)] + [shape_of((rank, wide), bf16)] * slots,
            in_specs=[SMEM, VMEM] + [VMEM] * len(parts),
            out_specs=[VMEM] * (1 + slots),
            compiler_params=params(16),
            cost_estimate=cost(2 * rows * wide * rank * slots, 2 * rows * wide),
        )(facts, tokens, *parts)
        return grads, base, spread, sends

    grads, base, spread_back, part_down = group(back_work)
    if square:
        grads = [output_gradient, across] + grads
    came = {0: part_down[0]}
    for s in sorted(range(1, slots), key=lambda s: s == 2):
        early = [] if s == 2 else down_tables[1:]
        came[s] = give_back(after(part_down[s], *early), s)
    came = [came[s] for s in range(slots)]

    wide_step = min(512, wide)

    def input_whole(spread):
        return pl.pallas_call(
            functools.partial(input_kernel, slots, narrow),
            grid=(wide // wide_step,),
            out_shape=shape_of((rows, wide), bf16),
            in_specs=[
                pl.BlockSpec((slots * rank, rows), lambda i: (0, 0)),
                pl.BlockSpec((wide_step, key_width), lambda i: (i, 0)),
            ]
            + [pl.BlockSpec((rank, wide_step), lambda i: (0, i))] * slots
            + [pl.BlockSpec(g.shape, lambda i, r=g.ndim: (0,) * r) for g in grads],
            out_specs=pl.BlockSpec((rows, wide_step), lambda i: (0, i)),
            scratch_shapes=[
                pltpu.VMEM((rows, key_width), bf16),
                pltpu.VMEM((rows, slots * rank), bf16),
            ],
            compiler_params=params(16),
            cost_estimate=cost(
                2 * rows * wide * (key_width + rank * slots), 2 * wide * (rows + key_width)
            ),
        )(spread, frozen_key_weight, *down_tables, *grads)

    def low_work():
        part = pl.pallas_call(
            functools.partial(low_kernel, slots),
            out_shape=shape_of((rank, rows), f32),
            in_specs=[SMEM, VMEM] + [VMEM] * slots,
            out_specs=VMEM,
            compiler_params=params(16),
            cost_estimate=cost(2 * rows * wide * rank * slots, 2 * rows * wide),
        )(facts, tokens, *down_tables)
        parts = shared(part)
        input_gradient = input_whole(after(spread_back, parts[0]))
        if square:
            keep, send = base
            got = swap(send, shards, (0, 1))
            frozen, passing = keep[1] + got[1], (keep[0] + got[0]).astype(bf16)
            parts = [after(parts[0], input_gradient, frozen, passing), parts[1]]
        else:
            whole = jnp.dot(tokens, frozen_key_weight, preferred_element_type=f32)
            frozen = lax.psum_scatter(whole, shards, scatter_dimension=1, tiled=True)
            passing = ()
        spread, send = pl.pallas_call(
            functools.partial(second_kernel, slots, tok_size, len(parts)),
            out_shape=[
                shape_of((slots * rank, rows), bf16),
                shape_of((tok_size, rank, narrow), bf16),
            ],
            in_specs=[SMEM] + [VMEM] * (1 + len(parts)),
            out_specs=[VMEM] * 2,
            compiler_params=params(16),
            cost_estimate=cost(2 * rows * narrow * rank * slots, 2 * rows * narrow),
        )(facts, output_gradient, *parts)
        return spread, send, frozen, passing, input_gradient

    spread_low, part_up, frozen, passing, input_gradient = group(low_work)
    came_up = lax.all_to_all(part_up, "tok", split_axis=0, concat_axis=0, tiled=True)
    frozen = [frozen]
    if square:
        frozen.append(swap(passing, shards, (1, 0)))

    fresh_down, average_down = adam_down(facts, came, (down, down_m, down_v, down_a))
    fresh_up, average_up, key_output = last_step(
        facts,
        after(came_up, fresh_down),
        (up, up_m, up_v, up_a),
        spread_low,
        up_tables,
        frozen,
        tok_size,
    )
    return (
        key_output,
        input_gradient,
        flip(fresh_down),
        flip(fresh_up),
        flip(average_down),
        flip(average_up),
    )


def solution(mesh):
    rows = P(("groups", "tok"), ("tp", "sub"))
    cube = P(("groups", "tok"), ("tp", "sub"), None)
    return jax.shard_map(
        per_device,
        mesh=mesh,
        in_specs=(rows, P(("tp", "sub"), None), rows, P("groups", None), P("groups", None), P("groups"))
        + (cube,) * 8,
        out_specs=(rows, rows, cube, cube, cube, cube),
        check_vma=False,
    )
```

```python
import functools

import jax
import jax.numpy as jnp
from jax import lax
from jax.experimental import pallas as pl
from jax.experimental.pallas import tpu as pltpu
from jax.sharding import PartitionSpec as P

MODEL_WIDTH = 8192
ADAPTER_RANK = 64

adapter_scale = 0.5
learn_rate = 0.3
beta_one = 0.9
beta_two = 0.99
adam_eps = 1e-08
ema_decay = 0.9

LOW_SCALE = MODEL_WIDTH ** (-0.5)
BACK_SCALE = ADAPTER_RANK ** (-0.5)
MIB = 1024 * 1024

f32 = jnp.float32
bf16 = jnp.bfloat16

SMEM = pl.BlockSpec(memory_space=pltpu.SMEM)
VMEM = pl.BlockSpec(memory_space=pltpu.VMEM)
ANY = pl.BlockSpec(memory_space=pl.ANY)
HBM = pl.BlockSpec(memory_space=pltpu.HBM)


def shape_of(shape, dtype):
    return jax.ShapeDtypeStruct(tuple(shape), dtype)


SCHEDULE_SCALE = 3


def cost(flops, bytes_accessed):
    return pl.CostEstimate(
        flops=int(flops * SCHEDULE_SCALE),
        bytes_accessed=int(bytes_accessed * SCHEDULE_SCALE),
        transcendentals=0,
    )


def params(mib):
    return pltpu.CompilerParams(vmem_limit_bytes=mib * MIB)


def nt(a, b):
    return lax.dot_general(a, b, (((1,), (1,)), ((), ())), preferred_element_type=f32)


def nn(a, b):
    return lax.dot_general(a, b, (((1,), (0,)), ((), ())), preferred_element_type=f32)


def tn(a, b):
    return lax.dot_general(a, b, (((0,), (0,)), ((), ())), preferred_element_type=f32)


def facts_kernel(slots, owned, tok_size, counts, placement, sequence, facts):
    me = lax.axis_index("tok")
    total = jnp.int32(0)
    for s in range(slots):
        total = total + counts[me, s]
        facts[s] = total
        tenant = placement[lax.rem(me - s + tok_size, tok_size), s]
        place = jnp.int32(0)
        for k in range(1, owned):
            place = place + jnp.where(sequence[me * owned + k] == tenant, k, 0)
        facts[slots + s] = place


def slot_ends(facts, slots):
    return [facts[s] for s in range(slots)]


def slot_mask(ends, slot, shape):
    rows = lax.broadcasted_iota(jnp.int32, shape, 1)
    inside = rows < ends[slot]
    if slot:
        inside = inside & (rows >= ends[slot - 1])
    return inside


def pick_slot(ends, products, rank):
    rows = lax.broadcasted_iota(jnp.int32, (rank, products.shape[1]), 1)
    slots = products.shape[0] // rank
    out = products[(slots - 1) * rank :]
    for s in range(slots - 2, -1, -1):
        out = jnp.where(rows < ends[s], products[s * rank : (s + 1) * rank], out)
    return out


def spread_slots(ends, values):
    wide = values.astype(f32)
    return jnp.concatenate(
        [jnp.where(slot_mask(ends, s, wide.shape), wide, 0.0) for s in range(len(ends))], axis=0
    ).astype(bf16)


def paired_sum(refs):
    parts = [ref[...] for ref in refs]
    while len(parts) > 1:
        parts = [parts[i] + parts[i + 1] for i in range(0, len(parts), 2)]
    return parts[0]


def select_kernel(slots, owned, tok_size, counts, placement, sequence, down, up, facts, *rest):
    ups, downs, sems = rest[:slots], rest[slots : 2 * slots], rest[2 * slots]
    facts_kernel(slots, owned, tok_size, counts, placement, sequence, facts)
    copies = []
    order = list(range(1, slots)) + [0]
    for s in order:
        copies.append(pltpu.make_async_copy(up.at[facts[slots + s]], ups[s], sems.at[s]))
    for s in order:
        copies.append(pltpu.make_async_copy(down.at[facts[slots + s]], downs[s], sems.at[slots + s]))
    for copy in copies:
        copy.start()
    for copy in copies:
        copy.wait()


def base_kernel(width, tokens, weight, keep, send):
    tp, sub = lax.axis_index("tp"), lax.axis_index("sub")
    mine, other = tp, 1 - tp
    for ref, s in ((send, 1 - sub), (keep, sub)):
        for i, t in enumerate((other, mine)):
            start = pl.multiple_of((t * 2 + s) * width, width)
            ref[i] = nn(tokens[...], weight[:, pl.ds(start, width)])


def stacked(tables):
    return jnp.concatenate([t[...] for t in tables], axis=0)


def back_kernel(slots, facts, grad, *rest):
    tables, out = rest[:slots], rest[slots]
    out[...] = pick_slot(slot_ends(facts, slots), nt(stacked(tables), grad[...]), ADAPTER_RANK)


def part_down_kernel(slots, pieces, facts, tokens, *rest):
    parts, spread_out, outs = rest[:pieces], rest[pieces], rest[pieces + 1 :]
    ends = slot_ends(facts, slots)
    back = (paired_sum(parts) * BACK_SCALE).astype(bf16)
    spread = spread_slots(ends, back)
    spread_out[...] = spread
    for c in range(0, tokens.shape[1], 256):
        columns = slice(c, min(c + 256, tokens.shape[1]))
        product = (nn(spread, tokens[:, columns]) * (adapter_scale * LOW_SCALE)).astype(bf16)
        for s in range(slots):
            outs[s][:, columns] = product[s * ADAPTER_RANK : (s + 1) * ADAPTER_RANK]


def low_kernel(slots, facts, tokens, *rest):
    tables, out = rest[:slots], rest[slots]
    out[...] = pick_slot(slot_ends(facts, slots), nt(stacked(tables), tokens[...]), ADAPTER_RANK)


def input_kernel(slots, width, spread, weight, *rest):
    tables, grads, (out, whole, turned) = rest[:slots], rest[slots:-3], rest[-3:]

    @pl.when(pl.program_id(0) == 0)
    def _():
        turned[...] = spread[...].astype(f32).T.astype(bf16)
        if len(grads) == 1:
            whole[...] = grads[0][...]
        else:
            tp, sub = lax.axis_index("tp"), lax.axis_index("sub")
            pieces = (grads[0][...], grads[1][...], grads[2][0], grads[2][1])
            for piece, t, s in zip(pieces, (tp, 1 - tp, tp, 1 - tp), (sub, sub, 1 - sub, 1 - sub)):
                start = pl.multiple_of((t * 2 + s) * width, width)
                whole[:, pl.ds(start, width)] = piece

    for c in range(0, out.shape[1], 256):
        columns = slice(c, min(c + 256, out.shape[1]))
        frozen = None
        for start in range(0, whole.shape[1], 256):
            term = nt(whole[:, start : start + 256], weight[columns, start : start + 256])
            frozen = term if frozen is None else frozen + term
        table = jnp.concatenate([t[:, columns] for t in tables], axis=0)
        adapter = nn(turned[...], table)
        out[:, columns] = (frozen + (adapter_scale * LOW_SCALE) * adapter).astype(bf16)


def second_kernel(slots, tok_size, pieces, facts, grad, *rest):
    parts, (spread_low, out) = rest[:pieces], rest[pieces:]
    me = lax.axis_index("tok")
    low = (paired_sum(parts) * LOW_SCALE).astype(bf16)
    spread = spread_slots(slot_ends(facts, slots), low)
    spread_low[...] = spread
    product = (nn(spread, grad[...]) * (adapter_scale * BACK_SCALE)).astype(bf16)
    for s in range(slots):
        out[lax.rem(me + s, tok_size)] = product[s * ADAPTER_RANK : (s + 1) * ADAPTER_RANK]


def adam_step(weights, mean_old, var_old, avg_old, gradient):
    mean_new = beta_one * mean_old + (1.0 - beta_one) * gradient
    var_new = beta_two * var_old + (1.0 - beta_two) * gradient * gradient
    root = var_new * lax.rsqrt(var_new) + adam_eps
    inverse = pl.reciprocal(root, approx=True)
    inverse = inverse * (2.0 - root * inverse)
    updated = weights.astype(f32) - learn_rate * mean_new * inverse
    return updated.astype(bf16), ema_decay * avg_old + (1.0 - ema_decay) * updated


def each_rows(count, body):
    rows = 16

    for i in range(count // rows):
        body(slice(i * rows, (i + 1) * rows), rows)


def adam_kernel(slots, facts, *rest):
    came, old, rest = rest[:slots], rest[slots : slots + 4], rest[slots + 4 :]
    fresh, average, came_here = rest[:3]
    old_here, rest = rest[3:7], rest[7:]
    fresh_here, average_here, gradient_ref, in_sems, out_sems = rest
    owned, rank, width = fresh_here.shape

    arrivals = [
        pltpu.make_async_copy(came[s], came_here.at[s], in_sems.at[s]) for s in range(slots)
    ]
    loads, stores = [], []
    for k in range(owned):
        for i in range(4):
            sem = in_sems.at[slots + 4 * k + i]
            loads.append(pltpu.make_async_copy(old[i].at[k], old_here[i].at[k], sem))
        for i, (here, there) in enumerate(((fresh_here, fresh), (average_here, average))):
            sem = out_sems.at[2 * k + i]
            stores.append(pltpu.make_async_copy(here.at[k], there.at[k], sem))
    for copy in arrivals + loads:
        copy.start()

    for copy in arrivals:
        copy.wait()
    for k in range(owned):

        def clear(r, rows):
            gradient_ref[r, :] = jnp.zeros((rows, width), f32)

        each_rows(rank, clear)
        for s in range(slots):

            @pl.when(facts[slots + s] == k)
            def _():
                def add(r, rows):
                    gradient_ref[r, :] += came_here[s, r, :].astype(f32)

                each_rows(rank, add)

        for copy in loads[4 * k : 4 * k + 4]:
            copy.wait()

        def update(r, rows):
            for c in range(0, width, 512):
                columns = slice(c, min(c + 512, width))
                fresh_here[k, r, columns], average_here[k, r, columns] = adam_step(
                    *[ref[k, r, columns] for ref in old_here], gradient_ref[r, columns]
                )

        each_rows(rank, update)
        for copy in stores[2 * k : 2 * k + 2]:
            copy.start()
    for copy in stores:
        copy.wait()


def adam_down(facts, came, old):
    owned, rank, width = old[0].shape
    slots = len(came)
    shapes = [shape_of(old[0].shape, bf16), shape_of(old[0].shape, f32)]
    return pl.pallas_call(
        functools.partial(adam_kernel, slots),
        out_shape=shapes,
        in_specs=[SMEM] + [ANY] * (slots + 4),
        out_specs=[ANY] * 2,
        scratch_shapes=[pltpu.VMEM((slots, rank, width), bf16)]
        + [pltpu.VMEM(a.shape, a.dtype) for a in old]
        + [
            pltpu.VMEM(old[0].shape, bf16),
            pltpu.VMEM(old[0].shape, f32),
            pltpu.VMEM((rank, width), f32),
            pltpu.SemaphoreType.DMA((slots + 4 * owned,)),
            pltpu.SemaphoreType.DMA((2 * owned,)),
        ],
        compiler_params=params(60),
        cost_estimate=cost(owned * rank * width * 20, owned * rank * width * 60),
    )(facts, *came, *old)


def stack_kernel(own, across, out):
    out[0] = own[...]
    out[1] = across[...]


def stack_pair(own, across, flops):
    return pl.pallas_call(
        stack_kernel,
        out_shape=shape_of((2,) + own.shape, own.dtype),
        in_specs=[VMEM] * 2,
        out_specs=VMEM,
        compiler_params=params(16),
        cost_estimate=cost(flops, 2 * flops // 256),
    )(own, across)


def last_kernel(slots, tok_size, facts, came, *rest):
    old, rest = rest[:4], rest[4:]
    spread, tables, frozen = rest[0], rest[1 : 1 + slots], rest[1 + slots : -4]
    fresh, average, key_out, gradients = rest[-4:]
    raised = nn(spread[...].astype(f32).T.astype(bf16), stacked(tables))
    whole = frozen[0][...]
    for part in frozen[1:]:
        whole = whole + part[...].astype(f32)
    key_out[...] = (whole + (adapter_scale * BACK_SCALE) * raised).astype(bf16)
    me = lax.axis_index("tok")
    gradients[...] = jnp.zeros(gradients.shape, f32)
    for s in range(slots):
        gradients[facts[slots + s]] += came[lax.rem(me - s + tok_size, tok_size)].astype(f32)
    owned, rank, _ = gradients.shape
    for k in range(owned):

        def update(r, rows):
            fresh[k, r, :], average[k, r, :] = adam_step(
                *[ref[k, r, :] for ref in old], gradients[k, r, :]
            )

        each_rows(rank, update)


def last_step(facts, came, old, spread, tables, frozen, tok_size):
    shape = old[0].shape
    slots = len(tables)
    return pl.pallas_call(
        functools.partial(last_kernel, slots, tok_size),
        out_shape=[
            shape_of(shape, bf16),
            shape_of(shape, f32),
            shape_of(frozen[0].shape, bf16),
        ],
        in_specs=[SMEM] + [VMEM] * (6 + slots + len(frozen)),
        out_specs=[VMEM] * 3,
        scratch_shapes=[pltpu.VMEM(shape, f32)],
        compiler_params=params(16),
        cost_estimate=cost(old[0].size * 20, old[0].size * 20),
    )(facts, came, *old, spread, *tables, *frozen)


def after(value, *others):
    return lax.optimization_barrier((value, *others))[0]


def swap(block, axes, flips):
    sizes = [lax.axis_size(a) for a in axes]
    route = []
    for t in range(sizes[0]):
        for s in range(sizes[1]):
            source = (t ^ flips[0]) * sizes[1] + (s ^ flips[1])
            route.append((source, t * sizes[1] + s))
    return lax.ppermute(block, axes, route)


def per_device(
    tokens,
    frozen_key_weight,
    output_gradient,
    counts,
    placement,
    adapter_sequence,
    adapter_down,
    adapter_up,
    down_first_moment,
    down_second_moment,
    down_average,
    up_first_moment,
    up_second_moment,
    up_average,
):
    tok_size = lax.axis_size("tok")
    tp_size, sub_size = lax.axis_size("tp"), lax.axis_size("sub")
    shards = ("tp", "sub")
    square = tp_size == 2 and sub_size == 2
    rows, wide = tokens.shape
    narrow = output_gradient.shape[1]
    key_width = frozen_key_weight.shape[1]
    owned = adapter_down.shape[0]
    slots = placement.shape[1]
    rank = ADAPTER_RANK
    flip = lambda a: jnp.swapaxes(a, 1, 2)
    down, down_m, down_v, down_a = map(
        flip, (adapter_down, down_first_moment, down_second_moment, down_average)
    )
    up, up_m, up_v, up_a = map(flip, (adapter_up, up_first_moment, up_second_moment, up_average))

    def fetch(block, slot):
        return lax.ppermute(block, "tok", [((i + slot) % tok_size, i) for i in range(tok_size)])

    def give_back(block, slot):
        return lax.ppermute(block, "tok", [((i - slot) % tok_size, i) for i in range(tok_size)])

    def shared(part):
        if not square:
            return [lax.psum(part, shards)]
        both = part + swap(part, shards, (0, 1))
        return [both, swap(both, shards, (1, 0))]

    step = min(256, wide)

    facts, *sent = pl.pallas_call(
        functools.partial(select_kernel, slots, owned, tok_size),
        out_shape=[shape_of((2 * slots,), jnp.int32)]
        + [shape_of((rank, narrow), bf16)] * slots
        + [shape_of((rank, wide), bf16)] * slots,
        in_specs=[SMEM, SMEM, SMEM, ANY, ANY],
        out_specs=[SMEM] + [VMEM] * (2 * slots),
        scratch_shapes=[pltpu.SemaphoreType.DMA((2 * slots,))],
        compiler_params=params(56),
        cost_estimate=cost(0, 4 * slots * rank * (wide + narrow)),
    )(counts, placement, adapter_sequence, down, up)
    up_send, down_send = sent[:slots], sent[slots:]
    ready = counts[0, 0] > 0
    early = fetch(down_send[1], 1)
    up_tables = [up_send[0]] + [fetch(up_send[s], s) for s in range(1, slots)]
    if square:
        across = swap(after(output_gradient, facts), shards, (1, 0))
        pair = stack_pair(output_gradient, across, 2 * rows * wide * key_width)
        up_tables[0] = after(up_tables[0], pair)
    down_tables = [down_send[0], early] + [
        fetch(after(down_send[s], ready, early), s) for s in range(2, slots)
    ]
    up_tables[0] = after(up_tables[0], early)

    def group(work):
        shapes = jax.eval_shape(work)
        nothing = lambda: jax.tree.map(lambda a: jnp.zeros(a.shape, a.dtype), shapes)
        return lax.cond(ready, work, nothing)

    def back_work():
        part = pl.pallas_call(
            functools.partial(back_kernel, slots),
            out_shape=shape_of((rank, rows), f32),
            in_specs=[SMEM, VMEM] + [VMEM] * slots,
            out_specs=VMEM,
            compiler_params=params(16),
            cost_estimate=cost(2 * rows * narrow * rank * slots, 2 * rows * narrow),
        )(facts, output_gradient, *up_tables)
        parts = shared(part)
        if square:
            base = pl.pallas_call(
                functools.partial(base_kernel, narrow),
                out_shape=[shape_of((2, rows, narrow), f32)] * 2,
                in_specs=[VMEM, VMEM],
                out_specs=[VMEM, VMEM],
                compiler_params=params(16),
                cost_estimate=cost(2 * rows * wide * key_width, 2 * wide * (rows + key_width)),
            )(tokens, after(frozen_key_weight, parts[0]))
            grads = [swap(pair, shards, (0, 1))]
            parts = [after(parts[0], base[0]), parts[1]]
        else:
            base = []
            grads = [lax.all_gather(output_gradient, shards, axis=1, tiled=True)]
        spread, *sends = pl.pallas_call(
            functools.partial(part_down_kernel, slots, len(parts)),
            out_shape=[shape_of((slots * rank, rows), bf16)] + [shape_of((rank, wide), bf16)] * slots,
            in_specs=[SMEM, VMEM] + [VMEM] * len(parts),
            out_specs=[VMEM] * (1 + slots),
            compiler_params=params(16),
            cost_estimate=cost(2 * rows * wide * rank * slots, 2 * rows * wide),
        )(facts, tokens, *parts)
        return grads, base, spread, sends

    grads, base, spread_back, part_down = group(back_work)
    if square:
        grads = [output_gradient, across] + grads
    came = {0: part_down[0]}
    for s in sorted(range(1, slots), key=lambda s: s == 2):
        early = [] if s == 2 else down_tables[1:]
        came[s] = give_back(after(part_down[s], *early), s)
    came = [came[s] for s in range(slots)]

    wide_step = min(1024, wide)

    def input_whole(spread):
        return pl.pallas_call(
            functools.partial(input_kernel, slots, narrow),
            grid=(wide // wide_step,),
            out_shape=shape_of((rows, wide), bf16),
            in_specs=[
                pl.BlockSpec((slots * rank, rows), lambda i: (0, 0)),
                pl.BlockSpec((wide_step, key_width), lambda i: (i, 0)),
            ]
            + [pl.BlockSpec((rank, wide_step), lambda i: (0, i))] * slots
            + [pl.BlockSpec(g.shape, lambda i, r=g.ndim: (0,) * r) for g in grads],
            out_specs=pl.BlockSpec((rows, wide_step), lambda i: (0, i)),
            scratch_shapes=[
                pltpu.VMEM((rows, key_width), bf16),
                pltpu.VMEM((rows, slots * rank), bf16),
            ],
            compiler_params=params(20),
            cost_estimate=cost(
                2 * rows * wide * (key_width + rank * slots), 2 * wide * (rows + key_width)
            ),
        )(spread, frozen_key_weight, *down_tables, *grads)

    def low_work():
        part = pl.pallas_call(
            functools.partial(low_kernel, slots),
            out_shape=shape_of((rank, rows), f32),
            in_specs=[SMEM, VMEM] + [VMEM] * slots,
            out_specs=VMEM,
            compiler_params=params(16),
            cost_estimate=cost(2 * rows * wide * rank * slots, 2 * rows * wide),
        )(facts, tokens, *down_tables)
        parts = shared(part)
        input_gradient = input_whole(after(spread_back, parts[0]))
        if square:
            keep, send = base
            got = swap(send, shards, (0, 1))
            frozen, passing = keep[1] + got[1], (keep[0] + got[0]).astype(bf16)
            parts = [after(parts[0], input_gradient, frozen, passing), parts[1]]
        else:
            whole = jnp.dot(tokens, frozen_key_weight, preferred_element_type=f32)
            frozen = lax.psum_scatter(whole, shards, scatter_dimension=1, tiled=True)
            passing = ()
        spread, send = pl.pallas_call(
            functools.partial(second_kernel, slots, tok_size, len(parts)),
            out_shape=[
                shape_of((slots * rank, rows), bf16),
                shape_of((tok_size, rank, narrow), bf16),
            ],
            in_specs=[SMEM] + [VMEM] * (1 + len(parts)),
            out_specs=[VMEM] * 2,
            compiler_params=params(16),
            cost_estimate=cost(2 * rows * narrow * rank * slots, 2 * rows * narrow),
        )(facts, output_gradient, *parts)
        return spread, send, frozen, passing, input_gradient

    spread_low, part_up, frozen, passing, input_gradient = group(low_work)
    came_up = lax.all_to_all(part_up, "tok", split_axis=0, concat_axis=0, tiled=True)
    frozen = [frozen]
    if square:
        frozen.append(swap(passing, shards, (1, 0)))

    fresh_down, average_down = adam_down(facts, came, (down, down_m, down_v, down_a))
    fresh_up, average_up, key_output = last_step(
        facts,
        after(came_up, fresh_down),
        (up, up_m, up_v, up_a),
        spread_low,
        up_tables,
        frozen,
        tok_size,
    )
    return (
        key_output,
        input_gradient,
        flip(fresh_down),
        flip(fresh_up),
        flip(average_down),
        flip(average_up),
    )


def solution(mesh):
    rows = P(("groups", "tok"), ("tp", "sub"))
    cube = P(("groups", "tok"), ("tp", "sub"), None)
    return jax.shard_map(
        per_device,
        mesh=mesh,
        in_specs=(rows, P(("tp", "sub"), None), rows, P("groups", None), P("groups", None), P("groups"))
        + (cube,) * 8,
        out_specs=(rows, rows, cube, cube, cube, cube),
        check_vma=False,
    )
```
